32 devices in a mesh: dp: 8 (over z, x), seq: 4 (over y, core).
Axes of the slice: x: 2, y: 2, z: 4, core: 2. Of those that a mesh axis runs over, the one named last changes fastest.
Arguments:
- patches: bfloat16 [48, 576, 768], P('dp', 'seq'), may hold values from -6 to 6
- targets: bfloat16 [48, 576, 768], P('dp', 'seq'), may hold values from -6 to 6
- mask_order: int32 [48, 576], P('dp', 'seq'), may hold values from 0 to 575, each once within a row
- mask_count: int32 [48], P('dp'), may hold values from 230 to 460
- attend_gain: bfloat16 [768], replicated, may hold values from 0.5 to 1.5
- attend_shift: bfloat16 [768], replicated, may hold values from -1 to 1
- joint_weight: bfloat16 [768, 2304], replicated, may hold values from -0.21875 to 0.21875
- query_bias: bfloat16 [768], replicated, may hold values from -1.5 to 1.5
- value_bias: bfloat16 [768], replicated, may hold values from -1.5 to 1.5
- output_weight: bfloat16 [768, 768], replicated, may hold values from -2 to 2
- output_bias: bfloat16 [768], replicated, may hold values from -1 to 1
- feed_gain: bfloat16 [768], replicated, may hold values from 0.5 to 1.5
- feed_shift: bfloat16 [768], replicated, may hold values from -1 to 1
- expand_weight: bfloat16 [768, 3072], replicated, may hold values from -0.21875 to 0.21875
- expand_bias: bfloat16 [3072], replicated, may hold values from -1.5 to 1.5
- reduce_weight: bfloat16 [3072, 768], replicated, may hold values from -0.15625 to 0.15625
- reduce_bias: bfloat16 [768], replicated, may hold values from -1 to 1
- pixel_weight: bfloat16 [768, 768], replicated, may hold values from -0.21875 to 0.21875
- pixel_bias: bfloat16 [768], replicated, may hold values from -1.5 to 1.5
- mask_token: bfloat16 [768], replicated, may hold values from -4 to 4
Outputs:
- loss_value: float32 [], replicated
- attend_gain_grad: float32 [768], P('dp')
- attend_shift_grad: float32 [768], P('dp')
- joint_weight_grad: float32 [768, 2304], P('dp')
- query_bias_grad: float32 [768], P('dp')
- value_bias_grad: float32 [768], P('dp')
- output_weight_grad: float32 [768, 768], P('dp')
- output_bias_grad: float32 [768], P('dp')
- feed_gain_grad: float32 [768], P('dp')
- feed_shift_grad: float32 [768], P('dp')
- expand_weight_grad: float32 [768, 3072], P('dp')
- expand_bias_grad: float32 [3072], P('dp')
- reduce_weight_grad: float32 [3072, 768], P('dp')
- reduce_bias_grad: float32 [768], P('dp')
- pixel_weight_grad: float32 [768, 768], P('dp')
- pixel_bias_grad: float32 [768], P('dp')
- mask_token_grad: float32 [768], P('dp')
- patch_grad: float32 [48, 576, 768], P('dp', 'seq')
The draws below stay inside these ranges and needn't reach their ends.
Inputs may be any that keep to these rules, and one draw needn't show every extreme that they name: Each image's row holds every number below 576 once; patch p of image i is masked when mask_order[i, p] < mask_count[i].
All inputs are finite; a program needn't handle non-finite values.
Results may differ from the reference program's by a relative error of at most 0.011.
Values may be sent and summed in bfloat16 or wider, within the bound.
A program may use at most 192 MiB of HBM per device.

```python
import jax
import jax.numpy as jnp
from jax import lax

D = 768
HEADS = 12
HEAD_DIM = 64
FF = 3072
PIXELS = 768
PATCHES = 576
GROUP_IMAGES = 6
IMAGES = 48
N_DP = 8


def touch_ends(drawn, rng, smallest, high):
    longest = drawn.shape.index(max(drawn.shape))
    spots = []
    for shift in (0, 1):
        where = [jax.random.randint(jax.random.fold_in(rng, axis), (), 0, length) for axis, length in enumerate(drawn.shape)]
        where[longest] = (where[longest] + shift) % drawn.shape[longest]
        spots.append(tuple(where))
    return drawn.at[spots[0]].set(smallest).at[spots[1]].set(high)


def block_levels(rng, extent, pieces, low, top_value):
    def one(dim, parts):
        steps = jax.random.uniform(jax.random.fold_in(jax.random.fold_in(rng, 6), dim), (parts,), jnp.float32, low / len(pieces), top_value / len(pieces))
        return jnp.repeat(jnp.exp(steps), extent[dim] // parts).reshape((-1,) + (1,) * (len(extent) - dim - 1))

    factor_of = one(*pieces[0])
    for cut in pieces[1:]:
        factor_of = factor_of * one(*cut)
    return factor_of


def gaussian(rng, dims, deviation, bound, cuts=(), kind=jnp.bfloat16):
    values = deviation * jax.random.normal(rng, dims, jnp.float32)
    if cuts:
        values = values * block_levels(rng, dims, cuts, -0.22, 0.18)
    return jnp.clip(values, -bound, bound).astype(kind)


def setup_inputs(seed: int = 0) -> dict:
    streams_of = jax.random.split(jax.random.key(seed), 21)
    return {
        "patches": gaussian(streams_of[0], (IMAGES, PATCHES, D), 1.0, 6.0, ((0, 8), (1, 4))),
        "targets": gaussian(streams_of[1], (IMAGES, PATCHES, PIXELS), 1.0, 6.0, ((0, 8), (1, 4))),
        "mask_order": jax.vmap(lambda own: jax.random.permutation(own, PATCHES))(jax.random.split(streams_of[2], IMAGES)).reshape((IMAGES, PATCHES)).astype(jnp.int32),
        "mask_count": touch_ends(jax.random.randint(streams_of[3], (IMAGES,), 2 * PATCHES // 5, 4 * PATCHES // 5 + 1), jax.random.fold_in(streams_of[3], 1), 2 * PATCHES // 5, (4 * PATCHES // 5 + 1) - 1).astype(jnp.int32),
        "attend_gain": jnp.clip(1.0 + 0.1 * jax.random.normal(streams_of[4], (D,), jnp.float32), 0.5, 1.5).astype(jnp.bfloat16),
        "attend_shift": gaussian(streams_of[5], (D,), 0.2, 1.0),
        "joint_weight": gaussian(streams_of[6], (D, 3 * D), D ** -0.5, 0.21875),
        "query_bias": gaussian(streams_of[7], (D,), 0.3, 1.5),
        "value_bias": gaussian(streams_of[8], (D,), 0.3, 1.5),
        "output_weight": gaussian(streams_of[9], (D, D), (max(D * 8 // PATCHES, 1)) ** -0.5, 2.0),
        "output_bias": gaussian(streams_of[10], (D,), 0.2, 1.0),
        "feed_gain": jnp.clip(1.0 + 0.1 * jax.random.normal(streams_of[11], (D,), jnp.float32), 0.5, 1.5).astype(jnp.bfloat16),
        "feed_shift": gaussian(streams_of[12], (D,), 0.2, 1.0),
        "expand_weight": gaussian(streams_of[13], (D, FF), D ** -0.5, 0.21875),
        "expand_bias": gaussian(streams_of[14], (FF,), 0.3, 1.5),
        "reduce_weight": gaussian(streams_of[15], (FF, D), (FF // 2) ** -0.5, 0.15625),
        "reduce_bias": gaussian(streams_of[16], (D,), 0.2, 1.0),
        "pixel_weight": gaussian(streams_of[17], (D, PIXELS), D ** -0.5, 0.21875),
        "pixel_bias": gaussian(streams_of[18], (PIXELS,), 0.3, 1.5),
        "mask_token": gaussian(streams_of[19], (D,), 1.0, 4.0),
    }


@jax.custom_vjp
def low(v):
    return lax.optimization_barrier(v.astype(jnp.bfloat16)).astype(jnp.float32)

@jax.custom_vjp
def low_back(v):
    return v

def low_keep(v):
    return (low(v), None)

def low_pass(kept, grad):
    return (grad,)

def back_keep(v):
    return (v, None)

def back_low(kept, grad):
    return (low(grad),)
low.defvjp(low_keep, low_pass)
low_back.defvjp(back_keep, back_low)

def product(left, right):
    return jnp.dot(left, right, precision=lax.Precision.HIGHEST)

def layer_norm(inputs, gain, shift):
    centre = inputs - lax.optimization_barrier(jnp.mean(inputs, axis=-1, keepdims=True))
    variance = lax.optimization_barrier(jnp.mean(centre * centre, axis=-1, keepdims=True))
    return centre * lax.rsqrt(variance + 1e-06) * gain + shift

def forward(weights, rows_group, target_group, mask_group, inverse):
    attend_gain, attend_shift, joint_weight, query_bias, value_bias, output_weight, output_bias, feed_gain, feed_shift, expand_weight, expand_bias, reduce_weight, reduce_bias, pixel_weight, pixel_bias, mask_token = weights
    embedded = jnp.where(mask_group[:, None], mask_token[None, :], rows_group)
    input_one = low(layer_norm(embedded, attend_gain, attend_shift))
    joint_bias = jnp.concatenate([query_bias, jnp.zeros_like(query_bias), value_bias])
    joint = low(low_back(product(input_one, joint_weight) + joint_bias))
    joint = joint.reshape(GROUP_IMAGES, PATCHES, 3, HEADS, HEAD_DIM)
    queries, keys_in, values_in = (joint[:, :, 0], joint[:, :, 1], joint[:, :, 2])
    scores = jnp.einsum('bqhd,bkhd->bhqk', queries, keys_in, precision=lax.Precision.HIGHEST)
    scores = low_back(scores * HEAD_DIM ** (-0.5))
    probs = jax.nn.softmax(scores, axis=-1)
    mixed = jnp.einsum('bhqk,bkhd->bqhd', low(probs), values_in, precision=lax.Precision.HIGHEST)
    mixed = low(low_back(mixed)).reshape(GROUP_IMAGES * PATCHES, D)
    after_attn = embedded + low_back(product(mixed, output_weight) + output_bias)
    input_two = low(layer_norm(after_attn, feed_gain, feed_shift))
    expanded = low_back(product(input_two, expand_weight) + expand_bias)
    activated = low(jax.nn.gelu(expanded, approximate=False))
    after_mlp = after_attn + low_back(product(activated, reduce_weight) + reduce_bias)
    predicted = low_back(product(low(after_mlp), pixel_weight) + pixel_bias)
    errors = predicted - target_group
    smooth = (jnp.sqrt(errors * errors + 1.0) - 1.0) * mask_group[:, None].astype(jnp.float32)
    return jnp.sum(smooth) * inverse

def reference(patches, targets, mask_order, mask_count, attend_gain, attend_shift, joint_weight, query_bias, value_bias, output_weight, output_bias, feed_gain, feed_shift, expand_weight, expand_bias, reduce_weight, reduce_bias, pixel_weight, pixel_bias, mask_token):
    weights = tuple((w.astype(jnp.float32) for w in (attend_gain, attend_shift, joint_weight, query_bias, value_bias, output_weight, output_bias, feed_gain, feed_shift, expand_weight, expand_bias, reduce_weight, reduce_bias, pixel_weight, pixel_bias, mask_token)))
    masked = (mask_order < mask_count[:, None]).reshape(N_DP, GROUP_IMAGES * PATCHES)
    count_sum = jnp.sum(mask_count).astype(jnp.float32)
    inverse = 1.0 / (count_sum * PIXELS)
    rows_all = patches.astype(jnp.float32).reshape(N_DP, GROUP_IMAGES * PATCHES, D)
    target_all = targets.astype(jnp.float32).reshape(N_DP, GROUP_IMAGES * PATCHES, PIXELS)

    def step(carry, group):
        rows_group, target_group, mask_group = group

        def inner(weights_in, rows_in):
            return forward(weights_in, rows_in, target_group, mask_group, inverse)
        value, pull = jax.vjp(inner, weights, rows_group)
        grad_weights, grad_rows = pull(jnp.ones((), jnp.float32))
        summed = jax.tree.map(jnp.add, carry[1], grad_weights)
        return ((carry[0] + value, summed), grad_rows)
    start = (jnp.zeros((), jnp.float32), jax.tree.map(jnp.zeros_like, weights))
    (loss_value, grads), grad_rows = lax.scan(step, start, (rows_all, target_all, masked))
    patch_grad = grad_rows.reshape(IMAGES, PATCHES, D)
    return (loss_value, grads[0], grads[1], grads[2], grads[3], grads[4], grads[5], grads[6], grads[7], grads[8], grads[9], grads[10], grads[11], grads[12], grads[13], grads[14], grads[15], patch_grad)
```

```python
import functools
import itertools
from functools import partial

import jax
import jax.numpy as jnp
from jax import lax
from jax.experimental import pallas as pl
from jax.experimental.pallas import tpu as pltpu
from jax.sharding import PartitionSpec as P

HEADS = 12
HEAD_DIM = 64
PIXELS = 768
WIDE = 768
PAIR = 2 * HEAD_DIM
MIB = 1 << 20
F32 = jnp.float32
BF16 = jnp.bfloat16


def dot(left, right):
    return jnp.dot(left, right, preferred_element_type=F32)


def dot_nt(left, right):
    return lax.dot_general(left, right, (((1,), (1,)), ((), ())), preferred_element_type=F32)


def dot_tn(left, right):
    return lax.dot_general(left, right, (((0,), (0,)), ((), ())), preferred_element_type=F32)


def normalize(inputs):
    centre = inputs - jnp.mean(inputs, axis=-1, keepdims=True)
    scaling = lax.rsqrt(jnp.mean(centre * centre, axis=-1, keepdims=True) + 1e-06)
    return (centre * scaling, scaling)


def normalize_back(upstream, normed, scaling, gain):
    scaled = upstream * gain
    return scaling * (
        scaled
        - jnp.mean(scaled, axis=-1, keepdims=True)
        - normed * jnp.mean(scaled * normed, axis=-1, keepdims=True)
    )


def column_sums(values):
    return jnp.sum(values.astype(F32), axis=0, keepdims=True)


def gelu_both(inputs):
    bell = jnp.exp(inputs * inputs * -0.5)
    base_of = 1.0 + (0.3275911 * 0.7071067811865476) * jnp.abs(inputs)
    inner = pl.reciprocal(base_of, approx=True)
    inner = inner * (2.0 - base_of * inner)
    series = inner * (
        0.254829592
        + inner * (-0.284496736 + inner * (1.421413741 + inner * (-1.453152027 + inner * 1.061405429)))
    )
    tail = 0.5 * series * bell
    below = jnp.where(inputs < 0.0, tail, 1.0 - tail)
    return (inputs * below, below + inputs * bell * 0.3989422804014327)


def params(limit):
    return pltpu.CompilerParams(vmem_limit_bytes=limit * MIB)


def fixed(shape):
    zeros = (0,) * len(shape)
    return pl.BlockSpec(shape, lambda *place: zeros, pipeline_mode=pl.Buffered(1))


def cost(flops, moved):
    return pl.CostEstimate(flops=int(flops), bytes_accessed=int(moved), transcendentals=0)


def project_kernel(own, far, gain, shift, weight, bias, embedded_out, joint_out):
    embedded = jnp.concatenate([own[0], far[0]], axis=0)
    embedded_out[0] = embedded
    normed, _ = normalize(embedded.astype(F32))
    low = (normed * gain[...] + shift[...]).astype(BF16)
    for part in range(3):
        cut = slice(part * WIDE, (part + 1) * WIDE)
        joint_out[0, part] = (dot(low, weight[:, cut]) + bias[:, cut]).astype(BF16)


def project(own, far, gain, shift, weight, bias):
    near, quarter, width = own.shape
    rows = 2 * quarter
    return pl.pallas_call(
        project_kernel,
        grid=(near,),
        in_specs=[
            pl.BlockSpec((1, quarter, width), lambda i: (i, 0, 0)),
            pl.BlockSpec((1, quarter, width), lambda i: (i, 0, 0)),
            fixed((1, width)),
            fixed((1, width)),
            fixed((width, 3 * width)),
            fixed((1, 3 * width)),
        ],
        out_specs=[
            pl.BlockSpec((1, rows, width), lambda i: (i, 0, 0)),
            pl.BlockSpec((1, 3, rows, width), lambda i: (i, 0, 0, 0)),
        ],
        out_shape=[
            jax.ShapeDtypeStruct((near, rows, width), BF16),
            jax.ShapeDtypeStruct((near, 3, rows, width), BF16),
        ],
        compiler_params=params(32),
        cost_estimate=cost(2 * near * rows * width * 3 * width, 12e6),
        name="project",
    )(own, far, gain, shift, weight, bias)


def side_by_side(pair):
    lanes = lax.broadcasted_iota(jnp.int32, pair.shape, 1)
    zero = jnp.zeros_like(pair)
    first = jnp.where(lanes < HEAD_DIM, pair, zero)
    second = jnp.where(lanes < HEAD_DIM, zero, pair)
    return jnp.concatenate([first, second], axis=0)


def merge_heads(stacked):
    rows = stacked.shape[0] // 2
    lanes = lax.broadcasted_iota(jnp.int32, (rows, PAIR), 1)
    return jnp.where(lanes < HEAD_DIM, stacked[:rows], stacked[rows:])


def attend_kernel(own, far, mixed_out, probs_out):
    queries = side_by_side(own[0, 0] * jnp.asarray(HEAD_DIM**-0.5, BF16))
    keys_in = jnp.concatenate([own[0, 1], far[0, 0]], axis=0)
    values_in = jnp.concatenate([own[0, 2], far[0, 1]], axis=0)
    scores = dot_nt(queries, keys_in)
    exponent = jnp.exp(scores - jnp.max(scores, axis=-1, keepdims=True))
    total = jnp.sum(exponent, axis=-1, keepdims=True)
    probs = (exponent * (1.0 / total)).astype(BF16)
    probs_out[0, 0] = probs
    mixed_out[0] = merge_heads(dot(probs, values_in)).astype(BF16)


def attend(joint, pairs_far):
    near, _, rows, width = joint.shape
    keys_count = 2 * rows
    pairs = width // PAIR
    return pl.pallas_call(
        attend_kernel,
        grid=(near, pairs),
        in_specs=[
            pl.BlockSpec((1, 3, rows, PAIR), lambda i, h: (i, 0, 0, h)),
            pl.BlockSpec((1, 2, rows, PAIR), lambda i, h: (i, 0, 0, h)),
        ],
        out_specs=[
            pl.BlockSpec((1, rows, PAIR), lambda i, h: (i, 0, h)),
            pl.BlockSpec((1, 1, 2 * rows, keys_count), lambda i, h: (i, h, 0, 0)),
        ],
        out_shape=[
            jax.ShapeDtypeStruct((near, rows, width), BF16),
            jax.ShapeDtypeStruct((near, pairs, 2 * rows, keys_count), BF16),
        ],
        compiler_params=params(32),
        cost_estimate=cost(8 * near * rows * keys_count * width, 20e6),
        name="attend",
    )(joint, pairs_far)


def attend_back_kernel(own, far, probs_in, upstream, query_out, own_out, far_out):
    rows = own.shape[2]
    scale = HEAD_DIM**-0.5
    queries = side_by_side(own[0, 0])
    keys_in = jnp.concatenate([own[0, 1], far[0, 0]], axis=0)
    values_in = jnp.concatenate([own[0, 2], far[0, 1]], axis=0)
    grad_mixed = side_by_side(upstream[0])
    probs = probs_in[0, 0]
    grad_probs = dot_nt(grad_mixed, values_in)
    wide = probs.astype(F32)
    weighted = wide * grad_probs
    inner = jnp.sum(weighted, axis=-1, keepdims=True)
    grad_scores = (weighted - wide * inner).astype(BF16)
    query_out[0] = (merge_heads(dot(grad_scores, keys_in)) * scale).astype(BF16)
    grad_values = dot_tn(probs, grad_mixed).astype(BF16)
    grad_keys = (dot_tn(grad_scores, queries) * scale).astype(BF16)
    own_out[0, 0] = grad_keys[:rows]
    own_out[0, 1] = grad_values[:rows]
    far_out[0, 0] = grad_keys[rows:]
    far_out[0, 1] = grad_values[rows:]


def attend_back(joint, pairs_far, probs, upstream):
    near, _, rows, width = joint.shape
    keys_count = 2 * rows
    pairs = width // PAIR
    two = pl.BlockSpec((1, 2, rows, PAIR), lambda i, h: (i, 0, 0, h))
    one = pl.BlockSpec((1, rows, PAIR), lambda i, h: (i, 0, h))
    return pl.pallas_call(
        attend_back_kernel,
        grid=(near, pairs),
        in_specs=[
            pl.BlockSpec((1, 3, rows, PAIR), lambda i, h: (i, 0, 0, h)),
            two,
            pl.BlockSpec((1, 1, 2 * rows, keys_count), lambda i, h: (i, h, 0, 0)),
            one,
        ],
        out_specs=[one, two, two],
        out_shape=[
            jax.ShapeDtypeStruct((near, rows, width), BF16),
            jax.ShapeDtypeStruct((near, 2, rows, width), BF16),
            jax.ShapeDtypeStruct((near, 2, rows, width), BF16),
        ],
        compiler_params=params(32),
        cost_estimate=cost(16 * near * rows * keys_count * width, 25e6),
        name="attend_back",
    )(joint, pairs_far, probs, upstream)


def rows_kernel(
    hidden,
    inverse,
    embedded_in,
    mixed,
    mask_in,
    target_own,
    target_far,
    output_weight,
    expand_weight,
    reduce_weight,
    pixel_weight,
    biases,
    expand_bias,
    input_out,
    active_out,
    after_out,
    pred_out,
    branch_out,
    expand_out,
    low_out,
    attn_out,
    mixed_out,
    sums_out,
    slope,
):
    output_bias, gain, shift, reduce_bias, pixel_bias = (biases[row : row + 1] for row in range(5))
    mask = mask_in[0]
    after_attn = embedded_in[0].astype(F32) + dot(mixed[0], output_weight[...]) + output_bias
    normed, scaling = normalize(after_attn)
    low = (normed * gain + shift).astype(BF16)
    input_out[0] = low
    total = after_attn + reduce_bias
    for start in range(0, hidden, WIDE):
        cut = slice(start, start + WIDE)
        active, rate = gelu_both(dot(low, expand_weight[:, cut]) + expand_bias[:, cut])
        active = active.astype(BF16)
        active_out[0, :, cut] = active
        slope[:, cut] = rate.astype(slope.dtype)
        total += dot(active, reduce_weight[cut, :])
    after_low = total.astype(BF16)
    after_out[0] = after_low
    target = jnp.concatenate([target_own[0], target_far[0]], axis=0).astype(F32)
    errors = dot(after_low, pixel_weight[...]) + pixel_bias - target
    square = errors * errors + 1.0
    root = lax.rsqrt(square)
    channel = jnp.sum((square * root - 1.0) * mask, axis=0, keepdims=True)
    grad_pred = (mask * errors * root * inverse[0, 0]).astype(BF16)
    pred_out[0] = grad_pred
    grad_mlp = dot_nt(grad_pred, pixel_weight[...])
    branch = grad_mlp.astype(BF16)
    branch_out[0] = branch
    grad_in = jnp.zeros_like(grad_mlp)
    expand_sums = []
    for start in range(0, hidden, WIDE):
        cut = slice(start, start + WIDE)
        grad_expand = dot_nt(branch, reduce_weight[cut, :]) * slope[:, cut].astype(F32)
        grad_expand = grad_expand.astype(BF16)
        expand_out[0, :, cut] = grad_expand
        expand_sums.append(column_sums(grad_expand))
        grad_in += dot_nt(grad_expand, expand_weight[:, cut])
    grad_attn = grad_mlp + normalize_back(grad_in, normed, scaling, gain)
    attn_out[0] = grad_attn
    grad_low = grad_attn.astype(BF16)
    low_out[0] = grad_low
    mixed_out[0] = dot_nt(grad_low, output_weight[...]).astype(BF16)
    sums = [
        column_sums(grad_pred),
        column_sums(branch),
        column_sums(grad_in * normed),
        column_sums(grad_in),
        column_sums(grad_low),
        channel,
    ] + expand_sums

    @pl.when(pl.program_id(0) == 0)
    def _():
        sums_out[...] = jnp.zeros_like(sums_out)

    for row, line in enumerate(sums):
        sums_out[row : row + 1] += line


def rows_step(
    inverse,
    embedded,
    mixed,
    mask,
    target_own,
    target_far,
    output_weight,
    expand_weight,
    reduce_weight,
    pixel_weight,
    biases,
    expand_bias,
):
    near, rows, width = embedded.shape
    quarter = target_own.shape[1]
    hidden = expand_weight.shape[1]
    block = pl.BlockSpec((1, rows, width), lambda i: (i, 0, 0))
    half = pl.BlockSpec((1, quarter, width), lambda i: (i, 0, 0))
    long = pl.BlockSpec((1, rows, hidden), lambda i: (i, 0, 0))
    narrow = jax.ShapeDtypeStruct((near, rows, width), BF16)
    broad = jax.ShapeDtypeStruct((near, rows, hidden), BF16)
    return pl.pallas_call(
        partial(rows_kernel, hidden),
        grid=(near,),
        in_specs=[
            pl.BlockSpec(memory_space=pltpu.SMEM),
            block,
            block,
            pl.BlockSpec((1, rows, 1), lambda i: (i, 0, 0)),
            half,
            half,
            fixed((width, width)),
            fixed((width, hidden)),
            fixed((hidden, width)),
            fixed((width, width)),
            fixed((8, width)),
            fixed((1, hidden)),
        ],
        out_specs=[block, long, block, block, block, long, block, block, block, fixed_out((16, width))],
        out_shape=[
            narrow,
            broad,
            narrow,
            narrow,
            narrow,
            broad,
            narrow,
            jax.ShapeDtypeStruct((near, rows, width), F32),
            narrow,
            jax.ShapeDtypeStruct((16, width), F32),
        ],
        scratch_shapes=[pltpu.VMEM((rows, hidden), F32)],
        compiler_params=params(56),
        cost_estimate=cost(4 * near * rows * width * (2 * width + 2 * hidden), 40e6),
        name="rows_step",
    )(
        inverse,
        embedded,
        mixed,
        mask,
        target_own,
        target_far,
        output_weight,
        expand_weight,
        reduce_weight,
        pixel_weight,
        biases,
        expand_bias,
    )


def fixed_out(shape):
    zeros = (0,) * len(shape)
    return pl.BlockSpec(shape, lambda *place: zeros)


def outer_kernel(left_moves, left, right, out, turned):
    if left_moves:
        out[...] = dot_tn(left[...], right[...]).astype(out.dtype)
        return

    @pl.when(pl.program_id(0) == 0)
    def _():
        turned[...] = left[...].T

    out[...] = dot(turned[...], right[...]).astype(out.dtype)


def outer(left, right):
    rows, tall = left.shape
    broad = right.shape[1]
    left_moves = tall > broad
    if left_moves:
        grid, specs = tall // WIDE, [
            pl.BlockSpec((rows, WIDE), lambda i: (0, i)),
            fixed((rows, broad)),
        ]
        out_spec = pl.BlockSpec((WIDE, broad), lambda i: (i, 0))
    else:
        grid, specs = broad // WIDE, [
            fixed((rows, tall)),
            pl.BlockSpec((rows, WIDE), lambda i: (0, i)),
        ]
        out_spec = pl.BlockSpec((tall, WIDE), lambda i: (0, i))
    return pl.pallas_call(
        partial(outer_kernel, left_moves),
        grid=(grid,),
        in_specs=specs,
        out_specs=out_spec,
        out_shape=jax.ShapeDtypeStruct((tall, broad), BF16),
        scratch_shapes=[pltpu.VMEM((WIDE, rows), BF16)],
        compiler_params=params(32),
        cost_estimate=cost(2 * rows * tall * broad, 2 * (rows * (tall + broad) + tall * broad)),
        name="outer",
    )(left, right)


def project_back_kernel(
    query, own, received, embedded_in, attn, mask_in, gain, shift, weight,
    input_out, joint_out, near_out, far_out, sums_out,
):
    quarter = near_out.shape[1]
    mask = mask_in[0]
    embedded = embedded_in[0].astype(F32)
    normed, scaling = normalize(embedded)
    input_out[0] = (normed * gain[...] + shift[...]).astype(BF16)
    grad_query = query[0]
    grad_key = (own[0, 0].astype(F32) + received[0, 0].astype(F32)).astype(BF16)
    grad_value = (own[0, 1].astype(F32) + received[0, 1].astype(F32)).astype(BF16)
    grad_in = None
    for part, grad in enumerate((grad_query, grad_key, grad_value)):
        joint_out[part, 0] = grad
        term = dot_nt(grad, weight[:, part * WIDE : (part + 1) * WIDE])
        grad_in = term if grad_in is None else grad_in + term
    grad_embedded = attn[0] + normalize_back(grad_in, normed, scaling, gain[...])
    kept = grad_embedded * (1.0 - mask)
    near_out[0] = kept[:quarter]
    far_out[0] = kept[quarter:].astype(BF16)
    sums = [
        column_sums(grad_in * normed),
        column_sums(grad_in),
        column_sums(grad_query),
        column_sums(grad_value),
        column_sums(grad_embedded * mask),
    ]

    @pl.when(pl.program_id(0) == 0)
    def _():
        sums_out[...] = jnp.zeros_like(sums_out)

    for row, line in enumerate(sums):
        sums_out[row : row + 1] += line


def project_back(query, own, received, embedded, attn, mask, gain, shift, weight):
    near, rows, width = embedded.shape
    quarter = rows // 2
    block = pl.BlockSpec((1, rows, width), lambda i: (i, 0, 0))
    half = pl.BlockSpec((1, quarter, width), lambda i: (i, 0, 0))
    two = pl.BlockSpec((1, 2, rows, width), lambda i: (i, 0, 0, 0))
    return pl.pallas_call(
        project_back_kernel,
        grid=(near,),
        in_specs=[
            block,
            two,
            two,
            block,
            block,
            pl.BlockSpec((1, rows, 1), lambda i: (i, 0, 0)),
            fixed((1, width)),
            fixed((1, width)),
            fixed((width, 3 * width)),
        ],
        out_specs=[
            block,
            pl.BlockSpec((3, 1, rows, width), lambda i: (0, i, 0, 0)),
            half,
            half,
            fixed_out((8, width)),
        ],
        out_shape=[
            jax.ShapeDtypeStruct((near, rows, width), BF16),
            jax.ShapeDtypeStruct((3, near, rows, width), BF16),
            jax.ShapeDtypeStruct((near, quarter, width), F32),
            jax.ShapeDtypeStruct((near, quarter, width), BF16),
            jax.ShapeDtypeStruct((8, width), F32),
        ],
        compiler_params=params(40),
        cost_estimate=cost(2 * near * rows * width * 3 * width, 20e6),
        name="project_back",
    )(query, own, received, embedded, attn, mask, gain, shift, weight)


def swap(values, axis, bit):
    size = lax.axis_size(axis)
    return lax.ppermute(values, axis, [(place, place ^ bit) for place in range(size)])


def own_bit(axis, bit):
    return (lax.axis_index(axis) // bit) % 2


def pick(values, dim, which):
    return lax.dynamic_index_in_dim(values, which, dim, keepdims=False)


def add_in(kept, received):
    return (kept.astype(jnp.float32) + received.astype(jnp.float32)).astype(kept.dtype)


def halve(values, dim, axis, bit):
    mine = own_bit(axis, bit)
    received = swap(pick(values, dim, 1 - mine), axis, bit)
    return add_in(pick(values, dim, mine), received)


def join(values, dim, axis, bit):
    mine = own_bit(axis, bit)
    received = swap(values, axis, bit)
    first = jnp.where(mine == 0, values, received)
    second = jnp.where(mine == 0, received, values)
    return jnp.concatenate([first, second], axis=dim)


def reduce_rows(grad, order):
    dp = lax.axis_size("dp")
    rows, columns = grad.shape
    steps = dp.bit_length() - 1
    part = rows // dp
    if columns % 512 == 0:
        tail = (1, 2, part, 2, columns // 4, 2)
        parts = grad.reshape((2,) * steps + (part, 4, columns // 4))
        parts = jnp.moveaxis(parts, steps + 1, 0)
    else:
        parts = grad.reshape((2,) * steps + (4, part // 4, columns))
        parts = jnp.moveaxis(parts, steps, 0)
    parts = parts.reshape((2, 2) + parts.shape[1:])
    names = ["core", "y"] + [1 << bit for bit in reversed(range(steps))]
    for name in order(steps):
        dim = names.index(name)
        if name == "core":
            parts = halve(parts, dim, "seq", 1)
        elif name == "y":
            parts = halve(parts, dim, "seq", 2)
        else:
            parts = halve(parts, dim, "dp", name)
        names.pop(dim)
    parts = join(parts[None], 0, "seq", 2)
    parts = join(parts[None], 0, "seq", 1)
    parts = parts.reshape((4,) + parts.shape[2:]).astype(jnp.float32)
    if columns % 512 == 0:
        return jnp.moveaxis(parts, 0, 1).reshape(part, columns)
    return parts.reshape(part, columns)


def x_first(steps):
    return ["core"] + [1 << bit for bit in range(steps)] + ["y"]


def y_first(steps):
    return ["core", "y"] + [1 << bit for bit in range(steps)]


def z_first(steps):
    return ["core"] + [1 << bit for bit in range(1, steps)] + [1, "y"]


def reduce_vector(values):
    dp = lax.axis_size("dp")
    steps = dp.bit_length() - 1
    values = values + swap(values, "seq", 1)
    values = values + swap(values, "seq", 2)
    values = values.reshape((2,) * steps + values.shape[1:])
    for bit in reversed(range(steps)):
        mine = own_bit("dp", 1 << bit)
        received = swap(pick(values, 0, 1 - mine), "dp", 1 << bit)
        values = pick(values, 0, mine) + received
    return values


def any_places(
    patches,
    targets,
    mask_order,
    mask_count,
    attend_gain,
    attend_shift,
    joint_weight,
    query_bias,
    value_bias,
    output_weight,
    output_bias,
    feed_gain,
    feed_shift,
    expand_weight,
    expand_bias,
    reduce_weight,
    reduce_bias,
    pixel_weight,
    pixel_bias,
    mask_token,
):
    images, quarter, features = patches.shape
    dp = lax.axis_size("dp")
    near = images // 2
    rows_one = 2 * quarter
    row_count = near * rows_one
    place_y = own_bit("seq", 2)

    def own_and_far(values):
        parts = values.reshape((2, near) + values.shape[1:])
        return pick(parts, 0, place_y), swap(pick(parts, 0, 1 - place_y), "seq", 2)

    def line(vector):
        return vector.astype(F32)[None, :]

    masked_here = mask_order < mask_count[:, None]
    embedded_here = jnp.where(masked_here[:, :, None], mask_token[None, None, :], patches)
    embedded_own, embedded_far = own_and_far(embedded_here)
    mask = jnp.concatenate(own_and_far(masked_here.astype(jnp.int32)), axis=1)
    mask = mask.astype(F32)[:, :, None]
    count_sum = jnp.sum(mask_count)
    for bit in range(dp.bit_length() - 1):
        count_sum = count_sum + swap(count_sum, "dp", 1 << bit)
    inverse = 1.0 / (count_sum.astype(F32) * PIXELS)
    target_own, target_far = own_and_far(targets)
    joint_bias = jnp.concatenate(
        [line(query_bias), jnp.zeros((1, features), F32), line(value_bias)], axis=1
    )
    biases = jnp.concatenate(
        [
            line(vector)
            for vector in (output_bias, feed_gain, feed_shift, reduce_bias, pixel_bias)
        ]
        + [jnp.zeros((3, features), F32)],
        axis=0,
    )
    embedded, joint = project(
        embedded_own, embedded_far, line(attend_gain), line(attend_shift), joint_weight, joint_bias
    )
    pairs_far = swap(joint[:, 1:], "seq", 1)
    mixed, probs = attend(joint, pairs_far)
    (
        input_two,
        activated,
        after_low,
        grad_pred,
        grad_branch,
        grad_expand,
        grad_out,
        grad_attn,
        grad_mixed,
        sums_two,
    ) = rows_step(
        inverse.reshape(1, 1),
        embedded,
        mixed,
        mask,
        target_own,
        target_far,
        output_weight,
        expand_weight,
        reduce_weight,
        pixel_weight,
        biases,
        line(expand_bias),
    )

    def flat(values):
        return values.reshape(row_count, values.shape[-1])

    reduce_weight_grad = outer(flat(activated), flat(grad_branch))
    expand_weight_grad = outer(flat(input_two), flat(grad_expand))
    pixel_weight_grad = outer(flat(after_low), flat(grad_pred))
    output_weight_grad = outer(flat(mixed), flat(grad_out))
    square_grads = jnp.concatenate([pixel_weight_grad, output_weight_grad], axis=1)
    grad_query, grad_own, grad_far = attend_back(joint, pairs_far, probs, grad_mixed)
    received = swap(grad_far, "seq", 1)
    input_one, grad_joint, patch_near, patch_far, sums_one = project_back(
        grad_query,
        grad_own,
        received,
        embedded,
        grad_attn,
        mask,
        line(attend_gain),
        line(attend_shift),
        joint_weight,
    )
    grad_joint = grad_joint.reshape(3, row_count, features)
    joint_weight_grad = jnp.concatenate(
        [outer(flat(input_one), grad_joint[part]) for part in range(3)], axis=1
    )
    patch_far = swap(patch_far, "seq", 2).astype(F32)
    patch_grad = jnp.concatenate(
        [
            jnp.where(place_y == 0, patch_near, patch_far),
            jnp.where(place_y == 0, patch_far, patch_near),
        ],
        axis=0,
    )
    hidden = expand_bias.shape[0]
    vectors = (
        sums_one[0],
        sums_one[1],
        sums_one[2],
        sums_one[3],
        sums_two[4],
        sums_two[2],
        sums_two[3],
        sums_two[6 : 6 + hidden // features].reshape(hidden),
        sums_two[1],
        sums_two[0],
        sums_one[4],
    )
    loss_part = jnp.sum(sums_two[5]) * inverse
    lengths = [vector.shape[0] // dp for vector in vectors]
    packed = jnp.concatenate(
        [vector.reshape(dp, -1) for vector in vectors]
        + [jnp.broadcast_to(loss_part[None, None], (dp, 1))],
        axis=1,
    )
    packed = reduce_vector(packed)
    loss_value = packed[-1]
    cuts, start = [], 0
    for length in lengths:
        cuts.append(packed[start : start + length])
        start += length
    (
        attend_gain_grad,
        attend_shift_grad,
        query_bias_grad,
        value_bias_grad,
        output_bias_grad,
        feed_gain_grad,
        feed_shift_grad,
        expand_bias_grad,
        reduce_bias_grad,
        pixel_bias_grad,
        mask_token_grad,
    ) = cuts
    reduce_weight_grad = reduce_rows(reduce_weight_grad, x_first)
    expand_weight_grad = reduce_rows(expand_weight_grad, y_first)
    square_grads = reduce_rows(square_grads, z_first)
    joint_weight_grad = reduce_rows(joint_weight_grad, x_first)
    return (
        loss_value,
        attend_gain_grad,
        attend_shift_grad,
        joint_weight_grad,
        query_bias_grad,
        value_bias_grad,
        square_grads[:, PIXELS:],
        output_bias_grad,
        feed_gain_grad,
        feed_shift_grad,
        expand_weight_grad,
        expand_bias_grad,
        reduce_weight_grad,
        reduce_bias_grad,
        square_grads[:, :PIXELS],
        pixel_bias_grad,
        mask_token_grad,
        patch_grad,
    )


MESH = pl.DeviceIdType.MESH


def places():
    data, seq = lax.axis_index("dp"), lax.axis_index("seq")
    x, low, high = lax.rem(data, 2), lax.rem(lax.div(data, 2), 2), lax.div(data, 4)
    core, y = lax.rem(seq, 2), lax.div(seq, 2)
    return {
        "x": (x, {"dp": data + 1 - 2 * x}),
        "low": (low, {"dp": data + 2 - 4 * low}),
        "high": (high, {"dp": data + 4 - 8 * high}),
        "y": (y, {"seq": seq + 2 - 4 * y}),
        "core": (core, {"seq": seq + 1 - 2 * core}),
    }


def greet(where):
    barrier = pltpu.get_barrier_semaphore()
    for _, partner in where.values():
        pl.semaphore_signal(barrier, inc=1, device_id=partner, device_id_type=MESH)
    pl.semaphore_wait(barrier, len(where))


def remote(source, target, send, receive, partner):
    return pltpu.make_async_remote_copy(
        src_ref=source,
        dst_ref=target,
        send_sem=send,
        recv_sem=receive,
        device_id=partner,
        device_id_type=MESH,
    )


NAMES = ("high", "low", "x", "y")


def stage_shapes(names, order, tail):
    names, shapes = list(names), []
    for token in order:
        if token == "Gy":
            names = ["y"]
        elif token == "Gcore":
            names = ["core"] + names
        elif token[0] != "+":
            names.remove(token)
        shapes.append((2,) * len(names) + tail)
    return shapes


def for_each(dims, body):
    outer = max(dims - 2, 0)
    inner = list(itertools.product(range(2), repeat=dims - outer))
    if outer == 0:
        for spot in inner:
            body(spot)
        return

    def one(place, carry):
        first = tuple(lax.rem(lax.div(place, 2 ** (outer - 1 - dim)), 2) for dim in range(outer))
        for spot in inner:
            body(first + spot)
        return carry

    lax.fori_loop(0, 2**outer, one, 0)


def add_up(target, place, other):
    target[place] = (target[place].astype(F32) + other.astype(F32)).astype(target.dtype)


class Chain:
    def __init__(self, where, start, names, order, buffers, send, receive, base, swapped=None):
        self.where, self.order = dict(where), order
        if swapped is not None:
            (first, partner_first), (second, partner_second) = (where[name] for name in swapped)
            core = where["core"][0]

            def chosen(zero, one):
                return zero + core * (one - zero)

            for name, place, ours, other in (
                (swapped[0], (first, second), partner_first, partner_second),
                (swapped[1], (second, first), partner_second, partner_first),
            ):
                here = {"dp": lax.axis_index("dp"), "seq": lax.axis_index("seq")}
                ours, other = {**here, **ours}, {**here, **other}
                partner = {axis: chosen(ours[axis], other[axis]) for axis in here}
                self.where[name] = (chosen(*place), partner)
        self.plain = where
        self.refs = [start] + list(buffers)
        self.send, self.receive, self.base = send, receive, base
        self.names = [list(names)]
        for token in order:
            names = list(self.names[-1])
            if token == "Gy":
                names = ["y"]
            elif token == "Gcore":
                names = ["core"] + names
            elif token[0] != "+":
                names.remove(token)
            self.names.append(names)

    def copies(self, stage):
        token = self.order[stage]
        source, target = self.refs[stage], self.refs[stage + 1]
        if token[0] == "+":
            _, partner = self.plain[token[1:]]
        elif token[0] == "G":
            place, partner = self.plain[token[1:]]
            target = target.at[place]
        else:
            place, partner = self.where[token]
            dim = self.names[stage].index(token)
            source = source.at[(slice(None),) * dim + (1 - place,)]
        base = 2 * (self.base + stage)
        if len(source.shape) > 2:
            pairs = [(source.at[half], target.at[half]) for half in range(2)]
        else:
            pairs = [(source, target)]
        return [
            remote(one, other, self.send.at[base + index], self.receive.at[base + index], partner)
            for index, (one, other) in enumerate(pairs)
        ]

    def start(self, stage):
        for copy in self.copies(stage):
            copy.start()

    def finish(self, stage):
        for copy in self.copies(stage):
            copy.wait()
        token = self.order[stage]
        source, target = self.refs[stage], self.refs[stage + 1]
        if token[0] == "G":
            place, _ = self.plain[token[1:]]
            target[place] = source[...]
            return
        dim = None
        if token[0] != "+":
            place, _ = self.where[token]
            dim = self.names[stage].index(token)

        def one(spot):
            origin = spot if dim is None else spot[:dim] + (place,) + spot[dim:]
            add_up(target, spot if spot else Ellipsis, source[origin if origin else Ellipsis])

        for_each(len(self.names[stage + 1]), one)

    def turn(self, stage):
        if stage > 0:
            self.finish(stage - 1)
        if stage < len(self.order):
            self.start(stage)


Y_FIRST = ("y", "x", "low", "high", "Gy", "Gcore")
Y_THEN_LOW = ("y", "low", "x", "high", "Gy", "Gcore")
X_FIRST = ("x", "low", "high", "+y", "Gcore")
SUMS_ORDER = ("+core", "+y", "+x", "+low", "+high")
MOST = 6
TILE_ORDERS = (
    X_FIRST,
    Y_FIRST,
    Y_THEN_LOW,
    Y_THEN_LOW,
    Y_FIRST,
    Y_FIRST,
    Y_FIRST,
    X_FIRST,
    X_FIRST,
    Y_THEN_LOW,
    Y_FIRST,
    Y_FIRST,
    X_FIRST,
)
TILE_SWAPS = (
    ("x", "low"),
    ("x", "y"),
    ("y", "low"),
    ("y", "low"),
    ("x", "y"),
    ("x", "y"),
    ("x", "y"),
    ("x", "low"),
    ("x", "low"),
    ("y", "low"),
    ("x", "y"),
    ("x", "y"),
    ("x", "low"),
)
TILES = len(TILE_ORDERS)
TILE_STEPS = (0, 1, 2, 3, 4, 5, 6, 7, 8, 10, 18, 25, 31)
TURNS = {
    2: ((0, 0),),
    3: ((1, 0),),
    4: ((0, 1), (2, 0),),
    5: ((1, 1), (3, 0),),
    6: ((0, 2), (4, 0),),
    7: ((1, 2), (2, 1), (5, 0),),
    8: ((0, 3), (3, 1), (6, 0),),
    9: ((1, 3), (7, 0),),
    10: ((0, 4), (1, 4), (2, 2), (4, 1), (8, 0),),
    11: ((0, 5), (3, 2), (7, 1), (13, 0),),
    12: ((9, 0), (1, 5), (2, 3), (5, 1), (13, 1), (6, 1),),
    14: ((1, 6), (3, 3),),
    15: ((2, 4), (4, 2),),
    16: ((7, 2), (13, 2),),
    17: ((3, 4),),
    18: ((2, 5), (4, 3), (5, 2),),
    19: ((2, 6), (3, 5), (7, 3), (13, 3), (6, 2), (8, 1), (9, 1),),
    20: ((4, 4), (5, 3), (10, 0), (3, 6),),
    21: ((7, 4), (13, 4),),
    22: ((4, 5), (5, 4),),
    23: ((7, 5), (6, 3),),
    24: ((4, 6), (13, 5),),
    25: ((5, 5), (8, 2), (9, 2), (10, 1),),
    26: ((5, 6), (6, 4),),
    27: ((9, 3), (11, 0), (6, 5), (8, 3), (10, 2),),
    28: ((9, 4),),
    29: ((6, 6),),
    30: ((10, 3),),
    31: ((9, 5), (8, 4),),
    32: ((9, 6), (8, 5), (10, 4), (11, 1),),
    33: ((12, 0), (10, 5),),
}
LAST_TURNS = (
    (14, 0),
    (10, 6),
    (14, 1),
    (11, 2),
    (12, 1),
    (11, 3),
    (14, 2),
    (12, 2),
    (14, 3),
    (11, 4),
    (14, 4),
    (12, 3),
    (11, 5),
    (14, 5),
    (11, 6),
    (12, 4),
    (12, 5),
)


def chain_scratch(cases):
    scratch, counts = [], []
    for names, order, tail, dtype in cases:
        shapes = stage_shapes(names, order, tail)
        scratch += [pltpu.VMEM(shape, dtype) for shape in shapes]
        counts.append(len(shapes))
    return scratch, counts


def split_list(values, counts):
    parts, start = [], 0
    for count in counts:
        parts.append(values[start : start + count])
        start += count
    return parts


GAIN_ONE, SHIFT_ONE, QUERY, VALUE, OUTPUT, GAIN_TWO, SHIFT_TWO, REDUCE, PIXEL, TOKEN, EXPAND = range(11)
FRONT_OWN = 6
FRONT_FAR = 9
FRONT_ATTEND = 12


def lines_kernel(*refs):
    out = refs[-1]
    row = 0
    for ref in refs[:-1]:
        for start in range(0, ref.shape[0], WIDE):
            out[row : row + 1] = ref[start : start + WIDE].astype(F32).reshape(1, WIDE)
            row += 1


def stack_lines(*vectors):
    return pl.pallas_call(
        lines_kernel,
        in_specs=[pl.BlockSpec(memory_space=pltpu.VMEM)] * len(vectors),
        out_specs=pl.BlockSpec(memory_space=pltpu.VMEM),
        out_shape=jax.ShapeDtypeStruct((16, WIDE), F32),
        cost_estimate=cost(1e4, 1e5),
        name="stack_lines",
    )(*vectors)


def column_of(line):
    count = line.shape[1]
    down = lax.broadcasted_iota(jnp.int32, (count, count), 0)
    along = lax.broadcasted_iota(jnp.int32, (count, count), 1)
    return jnp.sum(jnp.where(down == along, jnp.broadcast_to(line, (count, count)), 0.0), axis=1, keepdims=True)


def front_kernel(
    parts, counts, rows_in, targets_in, orders_in, lines, weight_in, pixel_in, expand_in, output_in,
    embedded_out, input_out, joint_out, pairs_out, mixed_out, probs_out, masks_out, target_out, expand_out,
    embedded, inputs, masks, order_far, joint, pairs, weight, pixel, expand, output,
    local, far_send, far_receive, send, receive,
):
    images, heads = joint.shape[:2]
    quarter = rows_in.shape[2]
    where = {name: places()[name] for name in ("core", "y")}
    sibling = where["core"][1]
    y, other = where["y"]
    step = pl.program_id(0)
    near_half, far_half = pl.ds(0, quarter), pl.ds(quarter, quarter)

    def pair_copy(image):
        return remote(
            joint.at[image, :, pl.ds(1, 2)], pairs.at[image], send.at[image], receive.at[image], sibling
        )

    def far_copy(index, source, target):
        return remote(source, target, far_send.at[index], far_receive.at[index], other)

    order_copy = far_copy(0, orders_in.at[1 - y], order_far)
    row_copies = [
        far_copy(1 + image, rows_in.at[1 - y, image], embedded.at[image, far_half]) for image in range(images)
    ]
    target_copies = [
        far_copy(1 + images + image, targets_in.at[1 - y, image], target_out.at[image, far_half])
        for image in range(images)
    ]
    own_copy = pltpu.make_async_copy(rows_in.at[y], embedded.at[:, near_half], local.at[0])
    target_copy = pltpu.make_async_copy(targets_in.at[y], target_out.at[:, near_half], local.at[1])
    loads = [
        pltpu.make_async_copy(source, target, local.at[2 + index])
        for index, (source, target) in enumerate(
            ((pixel_in, pixel), (expand_in, expand), (output_in, output), (weight_in, weight))
        )
    ]

    @pl.when(step == 0)
    def _():
        own_copy.start()
        greet(where)
        order_copy.start()
        for copy in row_copies + loads:
            copy.start()
        target_copy.start()
        loads[0].wait()
        expand_out[0] = pixel[...]

    @pl.when(step == parts + 1)
    def _():
        loads[2].wait()
        expand_out[0] = output[...]

    for part in range(parts):

        @pl.when(step == 1 + part)
        def _(part=part):
            if part == 0:
                loads[1].wait()
            span = weight.shape[0] // 8
            starts = [place * parts * span + part * span for place in range(8)]
            expand_out[0] = jnp.concatenate([expand[:, start : start + span] for start in starts], axis=1)

    def project(image, start, order):
        block = pl.ds(start, quarter)
        mask = column_of((order < counts[y * images + image]).astype(F32))
        masks[image, block] = mask
        token = lines[TOKEN : TOKEN + 1].astype(BF16)
        rows = jnp.where(mask > 0.5, token, embedded[image, block])
        embedded[image, block] = rows
        normed, _ = normalize(rows.astype(F32))
        gain, shift = lines[GAIN_ONE : GAIN_ONE + 1], lines[SHIFT_ONE : SHIFT_ONE + 1]
        low = (normed * gain + shift).astype(BF16)
        inputs[image, block] = low
        for part, bias in ((1, None), (2, lines[VALUE : VALUE + 1]), (0, lines[QUERY : QUERY + 1])):
            total = dot(low, weight[:, part * WIDE : (part + 1) * WIDE])
            total = (total if bias is None else total + bias).astype(BF16)
            for pair in range(heads):
                joint[image, pair, part, block] = total[:, pair * PAIR : (pair + 1) * PAIR]

    @pl.when((step >= FRONT_OWN) & (step < FRONT_FAR))
    def _():
        @pl.when(step == FRONT_OWN)
        def _():
            own_copy.wait()
            loads[3].wait()

        image = step - FRONT_OWN
        project(image, 0, orders_in[y, image, 0:1, :quarter])

    @pl.when((step >= FRONT_FAR) & (step < FRONT_ATTEND))
    def _():
        for index in range(images):

            @pl.when(step == FRONT_FAR + index)
            def _(index=index):
                if index == 0:
                    order_copy.wait()
                row_copies[index].wait()
                target_copies[index].start()

        image = step - FRONT_FAR
        project(image, quarter, order_far[image, 0:1, :quarter])
        pair_copy(image).start()
        embedded_out[0] = embedded[image]
        input_out[0] = inputs[image]
        joint_out[0] = joint[image]
        masks_out[0] = masks[image]

    @pl.when(step >= FRONT_ATTEND)
    def _():
        place = step - FRONT_ATTEND
        image, pair = lax.div(place, heads), lax.rem(place, heads)

        @pl.when(pair == 0)
        def _():
            pair_copy(image).wait()

        queries = side_by_side(joint[image, pair, 0] * jnp.asarray(HEAD_DIM**-0.5, BF16))
        keys_in = jnp.concatenate([joint[image, pair, 1], pairs[image, pair, 0]], axis=0)
        values_in = jnp.concatenate([joint[image, pair, 2], pairs[image, pair, 1]], axis=0)
        pairs_out[0, 0] = pairs[image, pair]
        scores = dot_nt(keys_in, queries)
        exponent = jnp.exp(scores - jnp.max(scores, axis=0, keepdims=True))
        total = jnp.sum(exponent, axis=0, keepdims=True)
        probs = (exponent * (1.0 / total)).astype(BF16)
        probs_out[0, 0] = probs
        mixed_out[0] = merge_turned(dot_tn(values_in, probs)).astype(BF16)

    @pl.when(step == pl.num_programs(0) - 1)
    def _():
        for copy in target_copies:
            copy.wait()
        target_copy.wait()


def merge_turned(stacked):
    rows = stacked.shape[1] // 2
    down = lax.broadcasted_iota(jnp.int32, (PAIR, rows), 0)
    return jnp.where(down < HEAD_DIM, stacked[:, :rows], stacked[:, rows:]).T


def front(counts, rows_in, targets_in, orders_in, lines, weight, pixel, expand, output):
    near, quarter, width = rows_in.shape[1:]
    rows, heads = 2 * quarter, width // PAIR
    parts = expand.shape[1] // width

    def image(step):
        return jnp.clip(step - FRONT_FAR, 0, near - 1)

    def spot(step):
        place = jnp.maximum(step - FRONT_ATTEND, 0)
        return lax.div(place, heads), lax.rem(place, heads)

    block = pl.BlockSpec((1, rows, width), lambda s: (image(s), 0, 0))
    return pl.pallas_call(
        partial(front_kernel, parts),
        grid=(FRONT_ATTEND + near * heads,),
        in_specs=[
            pl.BlockSpec(memory_space=pltpu.SMEM),
            pl.BlockSpec(memory_space=pl.ANY),
            pl.BlockSpec(memory_space=pl.ANY),
            fixed(orders_in.shape),
            fixed(lines.shape),
        ]
        + [pl.BlockSpec(memory_space=pl.ANY)] * 4,
        out_specs=[
            block,
            block,
            pl.BlockSpec((1, heads, 3, rows, PAIR), lambda s: (image(s), 0, 0, 0, 0)),
            pl.BlockSpec((1, 1, 2, rows, PAIR), lambda s: spot(s) + (0, 0, 0)),
            pl.BlockSpec((1, rows, PAIR), lambda s: (spot(s)[0], 0, spot(s)[1])),
            pl.BlockSpec((1, 1, 2 * rows, 2 * rows), lambda s: spot(s) + (0, 0)),
            pl.BlockSpec((1, rows, 1), lambda s: (image(s), 0, 0)),
            pl.BlockSpec(memory_space=pl.ANY),
            pl.BlockSpec((1, width, width), lambda s: (jnp.minimum(s, parts + 1), 0, 0)),
        ],
        out_shape=[
            jax.ShapeDtypeStruct((near, rows, width), BF16),
            jax.ShapeDtypeStruct((near, rows, width), BF16),
            jax.ShapeDtypeStruct((near, heads, 3, rows, PAIR), BF16),
            jax.ShapeDtypeStruct((near, heads, 2, rows, PAIR), BF16),
            jax.ShapeDtypeStruct((near, rows, width), BF16),
            jax.ShapeDtypeStruct((near, heads, 2 * rows, 2 * rows), BF16),
            jax.ShapeDtypeStruct((near, rows, 1), F32),
            jax.ShapeDtypeStruct((near, rows, width), BF16),
            jax.ShapeDtypeStruct((parts + 2, width, width), BF16),
        ],
        scratch_shapes=[
            pltpu.VMEM((near, rows, width), BF16),
            pltpu.VMEM((near, rows, width), BF16),
            pltpu.VMEM((near, rows, 1), F32),
            pltpu.VMEM(orders_in.shape[1:], jnp.int32),
            pltpu.VMEM((near, heads, 3, rows, PAIR), BF16),
            pltpu.VMEM((near, heads, 2, rows, PAIR), BF16),
            pltpu.VMEM(weight.shape, BF16),
            pltpu.VMEM(pixel.shape, BF16),
            pltpu.VMEM(expand.shape, BF16),
            pltpu.VMEM(output.shape, BF16),
            pltpu.SemaphoreType.DMA((6,)),
            pltpu.SemaphoreType.DMA((1 + 2 * near,)),
            pltpu.SemaphoreType.DMA((1 + 2 * near,)),
            pltpu.SemaphoreType.DMA((near,)),
            pltpu.SemaphoreType.DMA((near,)),
        ],
        compiler_params=pltpu.CompilerParams(
            vmem_limit_bytes=60 * MIB, collective_id=1, has_side_effects=True
        ),
        cost_estimate=cost(5e9, 40e6),
        name="front",
    )(counts, rows_in, targets_in, orders_in, lines, weight, pixel, expand, output)


def middle_kernel(
    embedded_in, mixed, mask_in, target_in, weights, reduce, lines,
    lefts, rights, input_out, scaling_out, sums_out, low, total, biases,
):
    parts = reduce.shape[1]
    span = reduce.shape[2]
    width = weights.shape[1]
    mask = mask_in[0]

    @pl.when(pl.program_id(0) == 0)
    def _():
        sums_out[...] = jnp.zeros_like(sums_out)
        for part in range(parts):
            pieces = []
            for place in range(8):
                row, start = divmod((place * parts + part) * span, width)
                pieces.append(lines[EXPAND + row : EXPAND + row + 1, start : start + span])
            biases[part] = jnp.concatenate(pieces, axis=1)

    after_attn = embedded_in[0].astype(F32) + dot(mixed[0], weights[parts + 1]) + lines[OUTPUT : OUTPUT + 1]
    lefts[0, parts + 1] = mixed[0]
    normed, scaling = normalize(after_attn)
    rights[0, parts + 1] = normed.astype(BF16)
    scaling_out[0] = scaling
    low[...] = (normed * lines[GAIN_TWO : GAIN_TWO + 1] + lines[SHIFT_TWO : SHIFT_TWO + 1]).astype(BF16)
    input_out[0] = low[...]
    total[...] = after_attn + lines[REDUCE : REDUCE + 1]

    def one(part, carry):
        active, rate = gelu_both(dot(low[...], weights[1 + part]) + biases[part])
        active = active.astype(BF16)
        lefts[0, 1 + part] = active
        rights[0, 1 + part] = rate.astype(BF16)
        total[...] += dot(active, reduce[:, part].reshape(width, width))
        return carry

    for part in range(parts):
        one(part, 0)
    after_low = total[...].astype(BF16)
    lefts[0, 0] = after_low
    errors = dot(after_low, weights[0]) + lines[PIXEL : PIXEL + 1] - target_in[0].astype(F32)
    square = errors * errors + 1.0
    root = lax.rsqrt(square)
    grad_pred = (mask * errors * root).astype(BF16)
    rights[0, 0] = grad_pred
    sums_out[0:1] += column_sums(grad_pred)
    sums_out[5:6] += jnp.sum((square * root - 1.0) * mask, axis=0, keepdims=True)
    sums_out[10:11] += jnp.sum(jnp.broadcast_to(mask, errors.shape), axis=0, keepdims=True)


def middle(embedded, mixed, mask, targets, weights, reduce, lines):
    near, rows, width = embedded.shape
    parts = reduce.shape[1]
    block = pl.BlockSpec((1, rows, width), lambda i: (i, 0, 0))
    column = pl.BlockSpec((1, rows, 1), lambda i: (i, 0, 0))
    stack = pl.BlockSpec((1, parts + 2, rows, width), lambda i: (i, 0, 0, 0))
    return pl.pallas_call(
        middle_kernel,
        grid=(near,),
        in_specs=[
            block,
            block,
            column,
            block,
            fixed((parts + 2, width, width)),
            fixed(reduce.shape),
            fixed(lines.shape),
        ],
        out_specs=[stack, stack, block, column, fixed_out((16, width))],
        out_shape=[
            jax.ShapeDtypeStruct((near, parts + 2, rows, width), BF16),
            jax.ShapeDtypeStruct((near, parts + 2, rows, width), BF16),
            jax.ShapeDtypeStruct((near, rows, width), BF16),
            jax.ShapeDtypeStruct((near, rows, 1), F32),
            jax.ShapeDtypeStruct((16, width), F32),
        ],
        scratch_shapes=[
            pltpu.VMEM((rows, width), BF16),
            pltpu.VMEM((rows, width), F32),
            pltpu.VMEM((parts, 1, width), F32),
        ],
        compiler_params=params(60),
        cost_estimate=cost(2 * near * rows * width * width * (2 * parts + 2), 40e6),
        name="middle",
    )(embedded, mixed, mask, targets, weights, reduce, lines)


HIGH_ROWS = 4 * 96


def spread_half(result, target, high, start, swapped):
    for low in range(2):
        for x in range(2):
            for y in range(2):
                at = (low * 2 + x) * 96 + start
                piece = result[at : at + HALF, y * 384 : (y + 1) * 384]
                spot = {"high": high, "low": low, "x": x, "y": y}
                if swapped is not None:
                    first, second = swapped
                    spot[first], spot[second] = spot[second], spot[first]
                target[tuple(spot[name] for name in NAMES)] = piece.astype(BF16)


HALF = 48
SLOTS = 4
KEPT = 10
FIRST_ATTEND = 11
GROUP_STEPS = (18, 25, 31)
FIRST_NORM = 32


def back_kernel(
    counts, left, right, weights, reduce, query, key, value, input_two, scaling_two, input_one, joint, pairs, probs_in, lines, sums_in,
    embedded_in, mask_in, *rest,
):
    (
        done_out,
        near_out,
        far_out,
        sums_out,
        late_out,
        branch,
        wide,
        grad_in,
        upstream,
        own_pairs,
        give_pairs,
        got_pairs,
        far_give,
        sums,
        late,
        keep,
        give,
        got,
        send,
        receive,
        core_send,
        core_receive,
        pair_send,
        pair_receive,
        far_send,
        far_receive,
    ) = rest[:26]
    buffers = split_list(rest[26:], counts)
    where = places()
    core, sibling = where["core"]
    step = pl.program_id(0)
    images, rows, width = input_two.shape
    every = images * rows
    quarter = rows // 2
    heads = width // PAIR
    first_gain, second_gain = lines[GAIN_ONE : GAIN_ONE + 1], lines[GAIN_TWO : GAIN_TWO + 1]
    chains = [
        Chain(where, keep.at[unit % KEPT], NAMES, order, buffers[unit], send, receive, MOST * unit, TILE_SWAPS[unit])
        for unit, order in enumerate(TILE_ORDERS)
    ]
    chains.append(Chain(where, sums, (), SUMS_ORDER, buffers[TILES], send, receive, MOST * TILES))
    chains.append(Chain(where, late, (), SUMS_ORDER, buffers[TILES + 1], send, receive, MOST * TILES + MOST))

    def core_copy(unit):
        slot = lax.rem(unit, SLOTS)
        return remote(give.at[slot], got.at[slot], core_send.at[unit], core_receive.at[unit], sibling)

    def pair_copy(place):
        slot = lax.rem(place, SLOTS)
        return remote(
            give_pairs.at[slot], got_pairs.at[place], pair_send.at[place], pair_receive.at[place], sibling
        )

    def far_copy(image):
        return remote(
            far_give.at[image], far_out.at[image], far_send.at[image], far_receive.at[image], where["y"][1]
        )

    def core_sum(unit):
        core_copy(unit).wait()
        for_each(4, lambda spot: add_up(keep.at[unit % KEPT], spot, got[(unit % SLOTS,) + spot]))

    def turn(unit, stage):
        if unit < TILES and stage == 0:
            core_sum(unit)
        chains[unit].turn(stage)
        if stage == len(chains[unit].order) and unit < TILES:
            done_out[unit] = chains[unit].refs[-1][...]

    def tile(unit, lines_of, value, swaps):
        def one(high, carry):
            columns = pl.ds(pl.multiple_of(high * HIGH_ROWS, HIGH_ROWS), HIGH_ROWS)
            result = dot_tn(lines_of(columns).reshape(every, HIGH_ROWS), value)
            for half in range(2):
                for swapped, chosen in [(None, True)] if half == 0 else swaps:

                    @pl.when(jnp.logical_and(core == half, chosen))
                    def _(half=half, swapped=swapped):
                        spread_half(result, keep.at[lax.rem(unit, KEPT)], high, half * HALF, swapped)

                    @pl.when(jnp.logical_and(core != half, chosen))
                    def _(half=half, swapped=swapped):
                        spread_half(result, give.at[lax.rem(unit, SLOTS)], high, half * HALF, swapped)

            return carry

        lax.fori_loop(0, 2, one, 0)
        core_copy(unit).start()

    def swaps_of(units, unit):
        kinds = []
        for other in units:
            if TILE_SWAPS[other] not in kinds:
                kinds.append(TILE_SWAPS[other])
        if len(kinds) == 1:
            return [(kinds[0], True)]
        found = []
        for kind in kinds:
            chosen = functools.reduce(
                jnp.logical_or, [unit == other for other in units if TILE_SWAPS[other] == kind]
            )
            found.append((kind, chosen))
        return found

    def flat(ref):
        return ref[...].reshape(every, ref.shape[-1])

    def left_lines(columns):
        return left[:, 0, :, columns]

    @pl.when(step == 0)
    def _():
        greet(where)
        sums[...] = sums_in[...]
        late[...] = jnp.zeros_like(late)
        grad_in[...] = jnp.zeros_like(grad_in)

    for at, turns in TURNS.items():

        @pl.when(step == at)
        def _(turns=turns):
            for unit, stage in turns:
                turn(unit, stage)

    @pl.when(step == 0)
    def _():
        tile(0, left_lines, right[:, 0].reshape(every, width), swaps_of((0,), 0))

        def one(image, carry):
            low = dot_nt(right[image, 0], weights[0]).astype(BF16)
            branch[image] = low
            sums[1:2] += column_sums(low)
            return carry

        lax.fori_loop(0, images, one, 0)

    @pl.when((step > 0) & (step < 9) & (lax.rem(step, 2) == 1))
    def _():
        tile(step, left_lines, flat(branch), swaps_of((1, 3, 5, 7), step))
        row = pl.ds(6 + lax.div(step, 2), 1)

        def one(image, carry):
            low = dot_nt(branch[image], reduce[:, 0].reshape(width, width)) * right[image, 0].astype(F32)
            low = low.astype(BF16)
            wide[image] = low
            sums[row] += column_sums(low)
            return carry

        lax.fori_loop(0, images, one, 0)

    @pl.when((step > 0) & (step < 9) & (lax.rem(step, 2) == 0))
    def _():
        tile(step, lambda columns: input_two[:, :, columns], flat(wide), swaps_of((2, 4, 6, 8), step))
        fresh = jnp.where(step == 2, 0.0, 1.0)

        def one(image, carry):
            grad_in[image] = grad_in[image] * fresh + dot_nt(wide[image], weights[0])
            return carry

        lax.fori_loop(0, images, one, 0)

    @pl.when(step == 9)
    def _():
        def one(image, carry):
            normed = right[image, 0].astype(F32)
            grad = grad_in[image]
            low = branch[image].astype(F32) + normalize_back(grad, normed, scaling_two[image], second_gain)
            low = low.astype(BF16)
            branch[image] = low
            sums[2:3] += column_sums(grad * normed)
            sums[3:4] += column_sums(grad)
            sums[4:5] += column_sums(low)
            mixed = dot_nt(low, weights[0]).astype(BF16)
            for pair in range(heads):
                upstream[image, pair] = mixed[:, pair * PAIR : (pair + 1) * PAIR]
            return carry

        lax.fori_loop(0, images, one, 0)

    @pl.when(step == 10)
    def _():
        tile(9, left_lines, flat(branch), swaps_of((9,), 9))

    attends = (step >= FIRST_ATTEND) & (step < GROUP_STEPS[2]) & (step != GROUP_STEPS[0]) & (step != GROUP_STEPS[1])

    @pl.when(attends)
    def _():
        place = attend_place(step)
        group, inside = lax.div(place, 6), lax.rem(place, 6)
        image, pair = lax.rem(inside, 3), group * 2 + lax.div(inside, 3)

        @pl.when(place >= SLOTS)
        def _():
            pair_copy(place - SLOTS).wait_send()

        scale = HEAD_DIM**-0.5
        target = own_pairs.at[lax.rem(group, 2), inside]
        away = give_pairs.at[lax.rem(place, SLOTS)]
        queries = side_by_side(joint[0, 0, 0])
        keys_in = jnp.concatenate([joint[0, 0, 1], pairs[0, 0, 0]], axis=0)
        values_in = jnp.concatenate([joint[0, 0, 2], pairs[0, 0, 1]], axis=0)
        grad_mixed = side_by_side(upstream[image, pair])
        probs = probs_in[0, 0]
        grad_probs = dot_nt(values_in, grad_mixed)
        broad = probs.astype(F32)
        weighted = broad * grad_probs
        inner = jnp.sum(weighted, axis=0, keepdims=True)
        grad_scores = (weighted - broad * inner).astype(BF16)
        grad_values = dot(probs, grad_mixed).astype(BF16)
        grad_keys = (dot(grad_scores, queries) * scale).astype(BF16)
        target[0] = (merge_turned(dot_tn(keys_in, grad_scores)) * scale).astype(BF16)
        target[1] = grad_keys[:rows]
        target[2] = grad_values[:rows]
        away[0] = grad_keys[rows:]
        away[1] = grad_values[rows:]
        pair_copy(place).start()

    @pl.when((step == GROUP_STEPS[0]) | (step == GROUP_STEPS[1]) | (step == GROUP_STEPS[2]))
    def _():
        group = jnp.where(step == GROUP_STEPS[0], 0, jnp.where(step == GROUP_STEPS[1], 1, 2))
        slot = lax.rem(group, 2)
        for inside in range(6):
            pair_copy(group * 6 + inside).wait_recv()
            image, second = inside % 3, inside // 3
            for part in range(3):
                piece = own_pairs[slot, inside, part]
                if part > 0:
                    piece = piece.astype(F32) + got_pairs[group * 6 + inside, part - 1].astype(F32)
                start = part * 2 * PAIR + second * PAIR
                wide[image, :, start : start + PAIR] = piece.astype(BF16)
        tile(10 + group, lambda columns: input_one[:, :, columns], flat(wide), swaps_of((10, 11, 12), 10 + group))
        columns = jnp.concatenate([query[...], key[...], value[...]], axis=1)
        fresh = jnp.where(group == 0, 0.0, 1.0)
        row = pl.ds(5 + group, 1)

        def one(image, carry):
            late[row] += column_sums(wide[image])
            grad_in[image] = grad_in[image] * fresh + dot_nt(wide[image], columns)
            return carry

        lax.fori_loop(0, images, one, 0)

    @pl.when(step >= FIRST_NORM)
    def _():
        image = step - FIRST_NORM
        mask = mask_in[0]
        normed, scaling = normalize(embedded_in[0].astype(F32))
        grad = grad_in[image]
        total = branch[image].astype(F32) + normalize_back(grad, normed, scaling, first_gain)
        kept = total * (1.0 - mask)
        near_out[0] = kept[:quarter]
        far_give[image] = kept[quarter:].astype(BF16)
        far_copy(image).start()
        late[0:1] += column_sums(grad * normed)
        late[1:2] += column_sums(grad)
        late[2:3] += column_sums(total * mask)

    @pl.when(step == pl.num_programs(0) - 1)
    def _():
        for unit, stage in LAST_TURNS:
            turn(unit, stage)
        for image in range(images):
            far_copy(image).wait()
        for place in range(3 * heads - SLOTS, 3 * heads):
            pair_copy(place).wait_send()
        sums_out[...] = chains[TILES].refs[-1][...]
        late_out[...] = chains[TILES + 1].refs[-1][...]


def attend_place(step):
    place = step - FIRST_ATTEND
    for at in GROUP_STEPS[:2]:
        place = place - jnp.where(step > at, 1, 0)
    return jnp.clip(place, 0, 17)


def back(
    lefts, rights, weights, reduce, joint_weight, input_two, scaling_two, input_one, joint, pairs, probs, lines, sums, embedded, mask
):
    near, slots, rows, width = lefts.shape
    quarter = rows // 2
    heads = width // PAIR

    def slot(step):
        return jnp.minimum(lax.div(step + 1, 2), slots - 1)

    def part(step):
        return jnp.clip(lax.div(step - 1, 2), 0, slots - 3)

    def group(step):
        return jnp.where(step > GROUP_STEPS[0], 1, 0) + jnp.where(step > GROUP_STEPS[1], 1, 0)

    def columns(which):
        return pl.BlockSpec((width, 2 * PAIR), lambda s: (0, which * 3 + group(s)))

    def spot(step):
        place = attend_place(step)
        group, inside = lax.div(place, 6), lax.rem(place, 6)
        return lax.rem(inside, 3), group * 2 + lax.div(inside, 3)

    def image(step):
        return jnp.maximum(step - FIRST_NORM, 0)

    cases = [(NAMES, order, (HALF, 384), BF16) for order in TILE_ORDERS]
    cases.append(((), SUMS_ORDER, sums.shape, F32))
    cases.append(((), SUMS_ORDER, (8, width), F32))
    buffers, counts = chain_scratch(cases)
    whole = (2, 2, 2, 2, HALF, 384)
    stack = pl.BlockSpec((near, 1, rows, width), lambda s: (0, slot(s), 0, 0))
    return pl.pallas_call(
        partial(back_kernel, counts),
        grid=(FIRST_NORM + near,),
        in_specs=[
            stack,
            stack,
            pl.BlockSpec((1, width, width), lambda s: (slot(s), 0, 0)),
            pl.BlockSpec((8, 1, reduce.shape[2], width), lambda s: (0, part(s), 0, 0)),
            columns(0),
            columns(1),
            columns(2),
            fixed((near, rows, width)),
            fixed((near, rows, 1)),
            fixed((near, rows, width)),
            pl.BlockSpec((1, 1, 3, rows, PAIR), lambda s: spot(s) + (0, 0, 0)),
            pl.BlockSpec((1, 1, 2, rows, PAIR), lambda s: spot(s) + (0, 0, 0)),
            pl.BlockSpec((1, 1, 2 * rows, 2 * rows), lambda s: spot(s) + (0, 0)),
            fixed(lines.shape),
            fixed(sums.shape),
            pl.BlockSpec((1, rows, width), lambda s: (image(s), 0, 0)),
            pl.BlockSpec((1, rows, 1), lambda s: (image(s), 0, 0)),
        ],
        out_specs=[
            fixed((TILES, 2, 2, HALF, 384)),
            pl.BlockSpec((1, quarter, width), lambda s: (image(s), 0, 0)),
            pl.BlockSpec(memory_space=pl.ANY),
            fixed_out(sums.shape),
            fixed_out((8, width)),
        ],
        out_shape=[
            jax.ShapeDtypeStruct((TILES, 2, 2, HALF, 384), BF16),
            jax.ShapeDtypeStruct((near, quarter, width), F32),
            jax.ShapeDtypeStruct((near, quarter, width), BF16),
            jax.ShapeDtypeStruct(sums.shape, F32),
            jax.ShapeDtypeStruct((8, width), F32),
        ],
        scratch_shapes=[
            pltpu.VMEM((near, rows, width), BF16),
            pltpu.VMEM((near, rows, width), BF16),
            pltpu.VMEM((near, rows, width), F32),
            pltpu.VMEM((near, heads, rows, PAIR), BF16),
            pltpu.VMEM((2, 6, 3, rows, PAIR), BF16),
            pltpu.VMEM((SLOTS, 2, rows, PAIR), BF16),
            pltpu.VMEM((near * heads, 2, rows, PAIR), BF16),
            pltpu.VMEM((near, quarter, width), BF16),
            pltpu.VMEM(sums.shape, F32),
            pltpu.VMEM((8, width), F32),
            pltpu.VMEM((KEPT,) + whole, BF16),
            pltpu.VMEM((SLOTS,) + whole, BF16),
            pltpu.VMEM((SLOTS,) + whole, BF16),
            pltpu.SemaphoreType.DMA((2 * MOST * (TILES + 2),)),
            pltpu.SemaphoreType.DMA((2 * MOST * (TILES + 2),)),
            pltpu.SemaphoreType.DMA((TILES,)),
            pltpu.SemaphoreType.DMA((TILES,)),
            pltpu.SemaphoreType.DMA((near * heads,)),
            pltpu.SemaphoreType.DMA((near * heads,)),
            pltpu.SemaphoreType.DMA((near,)),
            pltpu.SemaphoreType.DMA((near,)),
        ]
        + buffers,
        compiler_params=pltpu.CompilerParams(
            vmem_limit_bytes=60 * MIB, collective_id=2, has_side_effects=True
        ),
        cost_estimate=cost(40e9, 60e6),
        name="back",
    )(
        lefts, rights, weights, reduce, joint_weight, joint_weight, joint_weight, input_two,
        scaling_two, input_one, joint, pairs, probs, lines, sums, embedded, mask,
    )


def emit_kernel(parts, place, done, near_in, far_in, sums, late, *outs):
    (
        loss, attend_gain, attend_shift, joint, query_bias, value_bias, output, output_bias, feed_gain,
        feed_shift, expand, expand_bias, reduce, reduce_bias, pixel, pixel_bias, token, patch,
    ) = outs
    data, y = place[0], place[1]
    inverse = 1.0 / (sums[10:11] * PIXELS)
    loss[...] = jnp.sum(sums[5:6] * inverse, axis=1, keepdims=True)
    wide_inverse = inverse[:, :384]

    def piece(unit, core, half):
        return done[unit, core, half].astype(F32) * wide_inverse

    def square(unit):
        return [
            jnp.concatenate([piece(unit, core, half) for half in range(2)], axis=1) for core in range(2)
        ]

    for unit, target in ((0, pixel), (2 * parts + 1, output)):
        for core, lines in enumerate(square(unit)):
            target[core * HALF : (core + 1) * HALF] = lines
    expands = []
    for part in range(parts):
        for core, lines in enumerate(square(1 + 2 * part)):
            start = part * 2 * HALF + core * HALF
            reduce[start : start + HALF] = lines
        expands.append(square(2 + 2 * part))
    span = 2 * HALF
    for core in range(2):
        for d in range(8):
            lines = [expands[part][core][:, d * span : (d + 1) * span] for part in range(parts)]
            expand[core * HALF : (core + 1) * HALF, d * 4 * span : (d + 1) * 4 * span] = jnp.concatenate(
                lines, axis=1
            )
    for group in range(3):
        for core, lines in enumerate(square(2 * parts + 2 + group)):
            for part in range(3):
                start = part * WIDE + group * 2 * PAIR
                joint[core * HALF : (core + 1) * HALF, start : start + 2 * PAIR] = lines[
                    :, part * 2 * PAIR : (part + 1) * 2 * PAIR
                ]

    def own_cut(lines):
        shift = lax.rem(WIDE - data * span, WIDE)
        return pltpu.roll(lines, shift, axis=1)[:, :span]

    early = own_cut(sums[...] * inverse)
    later = own_cut(late[...] * inverse)
    queries = jnp.concatenate([late[5 + group : 6 + group, : 2 * PAIR] for group in range(3)], axis=1)
    values = jnp.concatenate([late[5 + group : 6 + group, 4 * PAIR :] for group in range(3)], axis=1)
    both = jnp.concatenate([queries, values] + [jnp.zeros((6, WIDE), F32)], axis=0)
    both = own_cut(both * inverse)
    for target, lines, row in (
        (attend_gain, later, 0),
        (attend_shift, later, 1),
        (query_bias, both, 0),
        (value_bias, both, 1),
        (output_bias, early, 4),
        (feed_gain, early, 2),
        (feed_shift, early, 3),
        (reduce_bias, early, 1),
        (pixel_bias, early, 0),
        (token, later, 2),
    ):
        target[...] = lines[row : row + 1]
    expand_bias[...] = jnp.concatenate([early[6 + part : 7 + part] for part in range(parts)], axis=1)
    images = near_in.shape[0]
    for image in range(images):
        patch[y * images + image] = near_in[image] * inverse
        patch[(1 - y) * images + image] = far_in[image].astype(F32) * inverse


def emit(parts, place, done, near_in, far_in, sums, late):
    images, quarter, width = near_in.shape
    hidden = parts * width

    def out(*shape):
        return jax.ShapeDtypeStruct(shape, F32)

    small = out(1, 96)
    outs = [
        out(1, 1), small, small, out(96, 3 * width), small, small, out(96, width), small, small,
        small, out(96, hidden), out(1, hidden // 8), out(hidden // 8, width), small, out(96, width), small, small,
        out(2 * images, quarter, width),
    ]
    whole = pl.BlockSpec(memory_space=pltpu.VMEM)
    return pl.pallas_call(
        partial(emit_kernel, parts),
        in_specs=[pl.BlockSpec(memory_space=pltpu.SMEM)] + [whole] * 5,
        out_specs=[whole] * len(outs),
        out_shape=outs,
        compiler_params=params(60),
        cost_estimate=cost(1e6, 12e6),
        name="emit",
    )(place, done, near_in, far_in, sums, late)


def eight_places(
    patches,
    targets,
    mask_order,
    mask_count,
    attend_gain,
    attend_shift,
    joint_weight,
    query_bias,
    value_bias,
    output_weight,
    output_bias,
    feed_gain,
    feed_shift,
    expand_weight,
    expand_bias,
    reduce_weight,
    reduce_bias,
    pixel_weight,
    pixel_bias,
    mask_token,
):
    images, quarter, features = patches.shape
    near = images // 2
    place_y = own_bit("seq", 2)
    hidden = expand_bias.shape[0]
    parts = hidden // features

    def halves(values):
        return values.reshape((2, near) + values.shape[1:])

    lines = stack_lines(
        attend_gain,
        attend_shift,
        query_bias,
        value_bias,
        output_bias,
        feed_gain,
        feed_shift,
        reduce_bias,
        pixel_bias,
        mask_token,
        expand_bias,
    )
    orders = jnp.pad(mask_order[:, None, :], ((0, 0), (0, 7), (0, 256 - quarter)))
    reduce_parts = reduce_weight.reshape(8, parts, hidden // (8 * parts), features)
    place = jnp.stack([lax.axis_index("dp"), place_y]).astype(jnp.int32)
    embedded, input_one, joint, pairs, mixed, probs, mask, targets_here, weights = front(
        mask_count,
        halves(patches),
        halves(targets),
        halves(orders),
        lines,
        joint_weight,
        pixel_weight,
        expand_weight,
        output_weight,
    )
    lefts, rights, input_two, scaling_two, sums = middle(
        embedded, mixed, mask, targets_here, weights, reduce_parts, lines
    )
    done, patch_near, patch_far, sums, late = back(
        lefts,
        rights,
        weights,
        reduce_parts,
        joint_weight,
        input_two,
        scaling_two,
        input_one,
        joint,
        pairs,
        probs,
        lines,
        sums,
        embedded,
        mask,
    )
    outs = emit(parts, place, done, patch_near, patch_far, sums, late)
    flat = {0: (), 1: (-1,), 2: (-1,), 4: (-1,), 5: (-1,), 7: (-1,), 8: (-1,), 9: (-1,), 11: (-1,)}
    flat.update({13: (-1,), 15: (-1,), 16: (-1,)})
    return tuple(
        out.reshape(flat[index]) if index in flat else out for index, out in enumerate(outs)
    )


def on_device(*arguments):
    if lax.axis_size("dp") == 8 and lax.axis_size("seq") == 4:
        return eight_places(*arguments)
    return any_places(*arguments)


def solution(mesh):
    placed = (
        P("dp", "seq", None),
        P("dp", "seq", None),
        P("dp", "seq"),
        P("dp"),
        P(),
        P(),
        P(),
        P(),
        P(),
        P(),
        P(),
        P(),
        P(),
        P(),
        P(),
        P(),
        P(),
        P(),
        P(),
        P(),
    )
    return jax.shard_map(
        on_device,
        mesh=mesh,
        in_specs=placed,
        out_specs=(
            P(),
            P("dp"),
            P("dp"),
            P("dp", None),
            P("dp"),
            P("dp"),
            P("dp", None),
            P("dp"),
            P("dp"),
            P("dp"),
            P("dp", None),
            P("dp"),
            P("dp", None),
            P("dp"),
            P("dp", None),
            P("dp"),
            P("dp"),
            P("dp", "seq", None),
        ),
        check_vma=False,
    )
```

```python
import functools
import itertools
from functools import partial

import jax
import jax.numpy as jnp
from jax import lax
from jax.experimental import pallas as pl
from jax.experimental.pallas import tpu as pltpu
from jax.sharding import PartitionSpec as P

HEADS = 12
HEAD_DIM = 64
PIXELS = 768
WIDE = 768
PAIR = 2 * HEAD_DIM
MIB = 1 << 20
F32 = jnp.float32
BF16 = jnp.bfloat16


def dot(left, right):
    return jnp.dot(left, right, preferred_element_type=F32)


def dot_nt(left, right):
    return lax.dot_general(left, right, (((1,), (1,)), ((), ())), preferred_element_type=F32)


def dot_tn(left, right):
    return lax.dot_general(left, right, (((0,), (0,)), ((), ())), preferred_element_type=F32)


def normalize(inputs):
    centre = inputs - jnp.mean(inputs, axis=-1, keepdims=True)
    scaling = lax.rsqrt(jnp.mean(centre * centre, axis=-1, keepdims=True) + 1e-06)
    return (centre * scaling, scaling)


def normalize_back(upstream, normed, scaling, gain):
    scaled = upstream * gain
    return scaling * (
        scaled
        - jnp.mean(scaled, axis=-1, keepdims=True)
        - normed * jnp.mean(scaled * normed, axis=-1, keepdims=True)
    )


def column_sums(values):
    return jnp.sum(values.astype(F32), axis=0, keepdims=True)


def gelu_both(inputs):
    bell = jnp.exp(inputs * inputs * -0.5)
    base_of = 1.0 + (0.3275911 * 0.7071067811865476) * jnp.abs(inputs)
    inner = pl.reciprocal(base_of, approx=True)
    inner = inner * (2.0 - base_of * inner)
    series = inner * (
        0.254829592
        + inner * (-0.284496736 + inner * (1.421413741 + inner * (-1.453152027 + inner * 1.061405429)))
    )
    tail = 0.5 * series * bell
    below = jnp.where(inputs < 0.0, tail, 1.0 - tail)
    return (inputs * below, below + inputs * bell * 0.3989422804014327)


def params(limit):
    return pltpu.CompilerParams(vmem_limit_bytes=limit * MIB)


def fixed(shape):
    zeros = (0,) * len(shape)
    return pl.BlockSpec(shape, lambda *place: zeros, pipeline_mode=pl.Buffered(1))


def cost(flops, moved):
    return pl.CostEstimate(flops=int(flops), bytes_accessed=int(moved), transcendentals=0)


def project_kernel(own, far, gain, shift, weight, bias, embedded_out, joint_out):
    embedded = jnp.concatenate([own[0], far[0]], axis=0)
    embedded_out[0] = embedded
    normed, _ = normalize(embedded.astype(F32))
    low = (normed * gain[...] + shift[...]).astype(BF16)
    for part in range(3):
        cut = slice(part * WIDE, (part + 1) * WIDE)
        joint_out[0, part] = (dot(low, weight[:, cut]) + bias[:, cut]).astype(BF16)


def project(own, far, gain, shift, weight, bias):
    near, quarter, width = own.shape
    rows = 2 * quarter
    return pl.pallas_call(
        project_kernel,
        grid=(near,),
        in_specs=[
            pl.BlockSpec((1, quarter, width), lambda i: (i, 0, 0)),
            pl.BlockSpec((1, quarter, width), lambda i: (i, 0, 0)),
            fixed((1, width)),
            fixed((1, width)),
            fixed((width, 3 * width)),
            fixed((1, 3 * width)),
        ],
        out_specs=[
            pl.BlockSpec((1, rows, width), lambda i: (i, 0, 0)),
            pl.BlockSpec((1, 3, rows, width), lambda i: (i, 0, 0, 0)),
        ],
        out_shape=[
            jax.ShapeDtypeStruct((near, rows, width), BF16),
            jax.ShapeDtypeStruct((near, 3, rows, width), BF16),
        ],
        compiler_params=params(32),
        cost_estimate=cost(2 * near * rows * width * 3 * width, 12e6),
        name="project",
    )(own, far, gain, shift, weight, bias)


def side_by_side(pair):
    lanes = lax.broadcasted_iota(jnp.int32, pair.shape, 1)
    zero = jnp.zeros_like(pair)
    first = jnp.where(lanes < HEAD_DIM, pair, zero)
    second = jnp.where(lanes < HEAD_DIM, zero, pair)
    return jnp.concatenate([first, second], axis=0)


def merge_heads(stacked):
    rows = stacked.shape[0] // 2
    lanes = lax.broadcasted_iota(jnp.int32, (rows, PAIR), 1)
    return jnp.where(lanes < HEAD_DIM, stacked[:rows], stacked[rows:])


def attend_kernel(own, far, mixed_out, probs_out):
    queries = side_by_side(own[0, 0] * jnp.asarray(HEAD_DIM**-0.5, BF16))
    keys_in = jnp.concatenate([own[0, 1], far[0, 0]], axis=0)
    values_in = jnp.concatenate([own[0, 2], far[0, 1]], axis=0)
    scores = dot_nt(queries, keys_in)
    exponent = jnp.exp(scores - jnp.max(scores, axis=-1, keepdims=True))
    total = jnp.sum(exponent, axis=-1, keepdims=True)
    probs = (exponent * (1.0 / total)).astype(BF16)
    probs_out[0, 0] = probs
    mixed_out[0] = merge_heads(dot(probs, values_in)).astype(BF16)


def attend(joint, pairs_far):
    near, _, rows, width = joint.shape
    keys_count = 2 * rows
    pairs = width // PAIR
    return pl.pallas_call(
        attend_kernel,
        grid=(near, pairs),
        in_specs=[
            pl.BlockSpec((1, 3, rows, PAIR), lambda i, h: (i, 0, 0, h)),
            pl.BlockSpec((1, 2, rows, PAIR), lambda i, h: (i, 0, 0, h)),
        ],
        out_specs=[
            pl.BlockSpec((1, rows, PAIR), lambda i, h: (i, 0, h)),
            pl.BlockSpec((1, 1, 2 * rows, keys_count), lambda i, h: (i, h, 0, 0)),
        ],
        out_shape=[
            jax.ShapeDtypeStruct((near, rows, width), BF16),
            jax.ShapeDtypeStruct((near, pairs, 2 * rows, keys_count), BF16),
        ],
        compiler_params=params(32),
        cost_estimate=cost(8 * near * rows * keys_count * width, 20e6),
        name="attend",
    )(joint, pairs_far)


def attend_back_kernel(own, far, probs_in, upstream, query_out, own_out, far_out):
    rows = own.shape[2]
    scale = HEAD_DIM**-0.5
    queries = side_by_side(own[0, 0])
    keys_in = jnp.concatenate([own[0, 1], far[0, 0]], axis=0)
    values_in = jnp.concatenate([own[0, 2], far[0, 1]], axis=0)
    grad_mixed = side_by_side(upstream[0])
    probs = probs_in[0, 0]
    grad_probs = dot_nt(grad_mixed, values_in)
    wide = probs.astype(F32)
    weighted = wide * grad_probs
    inner = jnp.sum(weighted, axis=-1, keepdims=True)
    grad_scores = (weighted - wide * inner).astype(BF16)
    query_out[0] = (merge_heads(dot(grad_scores, keys_in)) * scale).astype(BF16)
    grad_values = dot_tn(probs, grad_mixed).astype(BF16)
    grad_keys = (dot_tn(grad_scores, queries) * scale).astype(BF16)
    own_out[0, 0] = grad_keys[:rows]
    own_out[0, 1] = grad_values[:rows]
    far_out[0, 0] = grad_keys[rows:]
    far_out[0, 1] = grad_values[rows:]


def attend_back(joint, pairs_far, probs, upstream):
    near, _, rows, width = joint.shape
    keys_count = 2 * rows
    pairs = width // PAIR
    two = pl.BlockSpec((1, 2, rows, PAIR), lambda i, h: (i, 0, 0, h))
    one = pl.BlockSpec((1, rows, PAIR), lambda i, h: (i, 0, h))
    return pl.pallas_call(
        attend_back_kernel,
        grid=(near, pairs),
        in_specs=[
            pl.BlockSpec((1, 3, rows, PAIR), lambda i, h: (i, 0, 0, h)),
            two,
            pl.BlockSpec((1, 1, 2 * rows, keys_count), lambda i, h: (i, h, 0, 0)),
            one,
        ],
        out_specs=[one, two, two],
        out_shape=[
            jax.ShapeDtypeStruct((near, rows, width), BF16),
            jax.ShapeDtypeStruct((near, 2, rows, width), BF16),
            jax.ShapeDtypeStruct((near, 2, rows, width), BF16),
        ],
        compiler_params=params(32),
        cost_estimate=cost(16 * near * rows * keys_count * width, 25e6),
        name="attend_back",
    )(joint, pairs_far, probs, upstream)


def rows_kernel(
    hidden,
    inverse,
    embedded_in,
    mixed,
    mask_in,
    target_own,
    target_far,
    output_weight,
    expand_weight,
    reduce_weight,
    pixel_weight,
    biases,
    expand_bias,
    input_out,
    active_out,
    after_out,
    pred_out,
    branch_out,
    expand_out,
    low_out,
    attn_out,
    mixed_out,
    sums_out,
    slope,
):
    output_bias, gain, shift, reduce_bias, pixel_bias = (biases[row : row + 1] for row in range(5))
    mask = mask_in[0]
    after_attn = embedded_in[0].astype(F32) + dot(mixed[0], output_weight[...]) + output_bias
    normed, scaling = normalize(after_attn)
    low = (normed * gain + shift).astype(BF16)
    input_out[0] = low
    total = after_attn + reduce_bias
    for start in range(0, hidden, WIDE):
        cut = slice(start, start + WIDE)
        active, rate = gelu_both(dot(low, expand_weight[:, cut]) + expand_bias[:, cut])
        active = active.astype(BF16)
        active_out[0, :, cut] = active
        slope[:, cut] = rate.astype(slope.dtype)
        total += dot(active, reduce_weight[cut, :])
    after_low = total.astype(BF16)
    after_out[0] = after_low
    target = jnp.concatenate([target_own[0], target_far[0]], axis=0).astype(F32)
    errors = dot(after_low, pixel_weight[...]) + pixel_bias - target
    square = errors * errors + 1.0
    root = lax.rsqrt(square)
    channel = jnp.sum((square * root - 1.0) * mask, axis=0, keepdims=True)
    grad_pred = (mask * errors * root * inverse[0, 0]).astype(BF16)
    pred_out[0] = grad_pred
    grad_mlp = dot_nt(grad_pred, pixel_weight[...])
    branch = grad_mlp.astype(BF16)
    branch_out[0] = branch
    grad_in = jnp.zeros_like(grad_mlp)
    expand_sums = []
    for start in range(0, hidden, WIDE):
        cut = slice(start, start + WIDE)
        grad_expand = dot_nt(branch, reduce_weight[cut, :]) * slope[:, cut].astype(F32)
        grad_expand = grad_expand.astype(BF16)
        expand_out[0, :, cut] = grad_expand
        expand_sums.append(column_sums(grad_expand))
        grad_in += dot_nt(grad_expand, expand_weight[:, cut])
    grad_attn = grad_mlp + normalize_back(grad_in, normed, scaling, gain)
    attn_out[0] = grad_attn
    grad_low = grad_attn.astype(BF16)
    low_out[0] = grad_low
    mixed_out[0] = dot_nt(grad_low, output_weight[...]).astype(BF16)
    sums = [
        column_sums(grad_pred),
        column_sums(branch),
        column_sums(grad_in * normed),
        column_sums(grad_in),
        column_sums(grad_low),
        channel,
    ] + expand_sums

    @pl.when(pl.program_id(0) == 0)
    def _():
        sums_out[...] = jnp.zeros_like(sums_out)

    for row, line in enumerate(sums):
        sums_out[row : row + 1] += line


def rows_step(
    inverse,
    embedded,
    mixed,
    mask,
    target_own,
    target_far,
    output_weight,
    expand_weight,
    reduce_weight,
    pixel_weight,
    biases,
    expand_bias,
):
    near, rows, width = embedded.shape
    quarter = target_own.shape[1]
    hidden = expand_weight.shape[1]
    block = pl.BlockSpec((1, rows, width), lambda i: (i, 0, 0))
    half = pl.BlockSpec((1, quarter, width), lambda i: (i, 0, 0))
    long = pl.BlockSpec((1, rows, hidden), lambda i: (i, 0, 0))
    narrow = jax.ShapeDtypeStruct((near, rows, width), BF16)
    broad = jax.ShapeDtypeStruct((near, rows, hidden), BF16)
    return pl.pallas_call(
        partial(rows_kernel, hidden),
        grid=(near,),
        in_specs=[
            pl.BlockSpec(memory_space=pltpu.SMEM),
            block,
            block,
            pl.BlockSpec((1, rows, 1), lambda i: (i, 0, 0)),
            half,
            half,
            fixed((width, width)),
            fixed((width, hidden)),
            fixed((hidden, width)),
            fixed((width, width)),
            fixed((8, width)),
            fixed((1, hidden)),
        ],
        out_specs=[block, long, block, block, block, long, block, block, block, fixed_out((16, width))],
        out_shape=[
            narrow,
            broad,
            narrow,
            narrow,
            narrow,
            broad,
            narrow,
            jax.ShapeDtypeStruct((near, rows, width), F32),
            narrow,
            jax.ShapeDtypeStruct((16, width), F32),
        ],
        scratch_shapes=[pltpu.VMEM((rows, hidden), F32)],
        compiler_params=params(56),
        cost_estimate=cost(4 * near * rows * width * (2 * width + 2 * hidden), 40e6),
        name="rows_step",
    )(
        inverse,
        embedded,
        mixed,
        mask,
        target_own,
        target_far,
        output_weight,
        expand_weight,
        reduce_weight,
        pixel_weight,
        biases,
        expand_bias,
    )


def fixed_out(shape):
    zeros = (0,) * len(shape)
    return pl.BlockSpec(shape, lambda *place: zeros)


def outer_kernel(left_moves, left, right, out, turned):
    if left_moves:
        out[...] = dot_tn(left[...], right[...]).astype(out.dtype)
        return

    @pl.when(pl.program_id(0) == 0)
    def _():
        turned[...] = left[...].T

    out[...] = dot(turned[...], right[...]).astype(out.dtype)


def outer(left, right):
    rows, tall = left.shape
    broad = right.shape[1]
    left_moves = tall > broad
    if left_moves:
        grid, specs = tall // WIDE, [
            pl.BlockSpec((rows, WIDE), lambda i: (0, i)),
            fixed((rows, broad)),
        ]
        out_spec = pl.BlockSpec((WIDE, broad), lambda i: (i, 0))
    else:
        grid, specs = broad // WIDE, [
            fixed((rows, tall)),
            pl.BlockSpec((rows, WIDE), lambda i: (0, i)),
        ]
        out_spec = pl.BlockSpec((tall, WIDE), lambda i: (0, i))
    return pl.pallas_call(
        partial(outer_kernel, left_moves),
        grid=(grid,),
        in_specs=specs,
        out_specs=out_spec,
        out_shape=jax.ShapeDtypeStruct((tall, broad), BF16),
        scratch_shapes=[pltpu.VMEM((WIDE, rows), BF16)],
        compiler_params=params(32),
        cost_estimate=cost(2 * rows * tall * broad, 2 * (rows * (tall + broad) + tall * broad)),
        name="outer",
    )(left, right)


def project_back_kernel(
    query, own, received, embedded_in, attn, mask_in, gain, shift, weight,
    input_out, joint_out, near_out, far_out, sums_out,
):
    quarter = near_out.shape[1]
    mask = mask_in[0]
    embedded = embedded_in[0].astype(F32)
    normed, scaling = normalize(embedded)
    input_out[0] = (normed * gain[...] + shift[...]).astype(BF16)
    grad_query = query[0]
    grad_key = (own[0, 0].astype(F32) + received[0, 0].astype(F32)).astype(BF16)
    grad_value = (own[0, 1].astype(F32) + received[0, 1].astype(F32)).astype(BF16)
    grad_in = None
    for part, grad in enumerate((grad_query, grad_key, grad_value)):
        joint_out[part, 0] = grad
        term = dot_nt(grad, weight[:, part * WIDE : (part + 1) * WIDE])
        grad_in = term if grad_in is None else grad_in + term
    grad_embedded = attn[0] + normalize_back(grad_in, normed, scaling, gain[...])
    kept = grad_embedded * (1.0 - mask)
    near_out[0] = kept[:quarter]
    far_out[0] = kept[quarter:].astype(BF16)
    sums = [
        column_sums(grad_in * normed),
        column_sums(grad_in),
        column_sums(grad_query),
        column_sums(grad_value),
        column_sums(grad_embedded * mask),
    ]

    @pl.when(pl.program_id(0) == 0)
    def _():
        sums_out[...] = jnp.zeros_like(sums_out)

    for row, line in enumerate(sums):
        sums_out[row : row + 1] += line


def project_back(query, own, received, embedded, attn, mask, gain, shift, weight):
    near, rows, width = embedded.shape
    quarter = rows // 2
    block = pl.BlockSpec((1, rows, width), lambda i: (i, 0, 0))
    half = pl.BlockSpec((1, quarter, width), lambda i: (i, 0, 0))
    two = pl.BlockSpec((1, 2, rows, width), lambda i: (i, 0, 0, 0))
    return pl.pallas_call(
        project_back_kernel,
        grid=(near,),
        in_specs=[
            block,
            two,
            two,
            block,
            block,
            pl.BlockSpec((1, rows, 1), lambda i: (i, 0, 0)),
            fixed((1, width)),
            fixed((1, width)),
            fixed((width, 3 * width)),
        ],
        out_specs=[
            block,
            pl.BlockSpec((3, 1, rows, width), lambda i: (0, i, 0, 0)),
            half,
            half,
            fixed_out((8, width)),
        ],
        out_shape=[
            jax.ShapeDtypeStruct((near, rows, width), BF16),
            jax.ShapeDtypeStruct((3, near, rows, width), BF16),
            jax.ShapeDtypeStruct((near, quarter, width), F32),
            jax.ShapeDtypeStruct((near, quarter, width), BF16),
            jax.ShapeDtypeStruct((8, width), F32),
        ],
        compiler_params=params(40),
        cost_estimate=cost(2 * near * rows * width * 3 * width, 20e6),
        name="project_back",
    )(query, own, received, embedded, attn, mask, gain, shift, weight)


def swap(values, axis, bit):
    size = lax.axis_size(axis)
    return lax.ppermute(values, axis, [(place, place ^ bit) for place in range(size)])


def own_bit(axis, bit):
    return (lax.axis_index(axis) // bit) % 2


def pick(values, dim, which):
    return lax.dynamic_index_in_dim(values, which, dim, keepdims=False)


def add_in(kept, received):
    return (kept.astype(jnp.float32) + received.astype(jnp.float32)).astype(kept.dtype)


def halve(values, dim, axis, bit):
    mine = own_bit(axis, bit)
    received = swap(pick(values, dim, 1 - mine), axis, bit)
    return add_in(pick(values, dim, mine), received)


def join(values, dim, axis, bit):
    mine = own_bit(axis, bit)
    received = swap(values, axis, bit)
    first = jnp.where(mine == 0, values, received)
    second = jnp.where(mine == 0, received, values)
    return jnp.concatenate([first, second], axis=dim)


def reduce_rows(grad, order):
    dp = lax.axis_size("dp")
    rows, columns = grad.shape
    steps = dp.bit_length() - 1
    part = rows // dp
    if columns % 512 == 0:
        tail = (1, 2, part, 2, columns // 4, 2)
        parts = grad.reshape((2,) * steps + (part, 4, columns // 4))
        parts = jnp.moveaxis(parts, steps + 1, 0)
    else:
        parts = grad.reshape((2,) * steps + (4, part // 4, columns))
        parts = jnp.moveaxis(parts, steps, 0)
    parts = parts.reshape((2, 2) + parts.shape[1:])
    names = ["core", "y"] + [1 << bit for bit in reversed(range(steps))]
    for name in order(steps):
        dim = names.index(name)
        if name == "core":
            parts = halve(parts, dim, "seq", 1)
        elif name == "y":
            parts = halve(parts, dim, "seq", 2)
        else:
            parts = halve(parts, dim, "dp", name)
        names.pop(dim)
    parts = join(parts[None], 0, "seq", 2)
    parts = join(parts[None], 0, "seq", 1)
    parts = parts.reshape((4,) + parts.shape[2:]).astype(jnp.float32)
    if columns % 512 == 0:
        return jnp.moveaxis(parts, 0, 1).reshape(part, columns)
    return parts.reshape(part, columns)


def x_first(steps):
    return ["core"] + [1 << bit for bit in range(steps)] + ["y"]


def y_first(steps):
    return ["core", "y"] + [1 << bit for bit in range(steps)]


def z_first(steps):
    return ["core"] + [1 << bit for bit in range(1, steps)] + [1, "y"]


def reduce_vector(values):
    dp = lax.axis_size("dp")
    steps = dp.bit_length() - 1
    values = values + swap(values, "seq", 1)
    values = values + swap(values, "seq", 2)
    values = values.reshape((2,) * steps + values.shape[1:])
    for bit in reversed(range(steps)):
        mine = own_bit("dp", 1 << bit)
        received = swap(pick(values, 0, 1 - mine), "dp", 1 << bit)
        values = pick(values, 0, mine) + received
    return values


def any_places(
    patches,
    targets,
    mask_order,
    mask_count,
    attend_gain,
    attend_shift,
    joint_weight,
    query_bias,
    value_bias,
    output_weight,
    output_bias,
    feed_gain,
    feed_shift,
    expand_weight,
    expand_bias,
    reduce_weight,
    reduce_bias,
    pixel_weight,
    pixel_bias,
    mask_token,
):
    images, quarter, features = patches.shape
    dp = lax.axis_size("dp")
    near = images // 2
    rows_one = 2 * quarter
    row_count = near * rows_one
    place_y = own_bit("seq", 2)

    def own_and_far(values):
        parts = values.reshape((2, near) + values.shape[1:])
        return pick(parts, 0, place_y), swap(pick(parts, 0, 1 - place_y), "seq", 2)

    def line(vector):
        return vector.astype(F32)[None, :]

    masked_here = mask_order < mask_count[:, None]
    embedded_here = jnp.where(masked_here[:, :, None], mask_token[None, None, :], patches)
    embedded_own, embedded_far = own_and_far(embedded_here)
    mask = jnp.concatenate(own_and_far(masked_here.astype(jnp.int32)), axis=1)
    mask = mask.astype(F32)[:, :, None]
    count_sum = jnp.sum(mask_count)
    for bit in range(dp.bit_length() - 1):
        count_sum = count_sum + swap(count_sum, "dp", 1 << bit)
    inverse = 1.0 / (count_sum.astype(F32) * PIXELS)
    target_own, target_far = own_and_far(targets)
    joint_bias = jnp.concatenate(
        [line(query_bias), jnp.zeros((1, features), F32), line(value_bias)], axis=1
    )
    biases = jnp.concatenate(
        [
            line(vector)
            for vector in (output_bias, feed_gain, feed_shift, reduce_bias, pixel_bias)
        ]
        + [jnp.zeros((3, features), F32)],
        axis=0,
    )
    embedded, joint = project(
        embedded_own, embedded_far, line(attend_gain), line(attend_shift), joint_weight, joint_bias
    )
    pairs_far = swap(joint[:, 1:], "seq", 1)
    mixed, probs = attend(joint, pairs_far)
    (
        input_two,
        activated,
        after_low,
        grad_pred,
        grad_branch,
        grad_expand,
        grad_out,
        grad_attn,
        grad_mixed,
        sums_two,
    ) = rows_step(
        inverse.reshape(1, 1),
        embedded,
        mixed,
        mask,
        target_own,
        target_far,
        output_weight,
        expand_weight,
        reduce_weight,
        pixel_weight,
        biases,
        line(expand_bias),
    )

    def flat(values):
        return values.reshape(row_count, values.shape[-1])

    reduce_weight_grad = outer(flat(activated), flat(grad_branch))
    expand_weight_grad = outer(flat(input_two), flat(grad_expand))
    pixel_weight_grad = outer(flat(after_low), flat(grad_pred))
    output_weight_grad = outer(flat(mixed), flat(grad_out))
    square_grads = jnp.concatenate([pixel_weight_grad, output_weight_grad], axis=1)
    grad_query, grad_own, grad_far = attend_back(joint, pairs_far, probs, grad_mixed)
    received = swap(grad_far, "seq", 1)
    input_one, grad_joint, patch_near, patch_far, sums_one = project_back(
        grad_query,
        grad_own,
        received,
        embedded,
        grad_attn,
        mask,
        line(attend_gain),
        line(attend_shift),
        joint_weight,
    )
    grad_joint = grad_joint.reshape(3, row_count, features)
    joint_weight_grad = jnp.concatenate(
        [outer(flat(input_one), grad_joint[part]) for part in range(3)], axis=1
    )
    patch_far = swap(patch_far, "seq", 2).astype(F32)
    patch_grad = jnp.concatenate(
        [
            jnp.where(place_y == 0, patch_near, patch_far),
            jnp.where(place_y == 0, patch_far, patch_near),
        ],
        axis=0,
    )
    hidden = expand_bias.shape[0]
    vectors = (
        sums_one[0],
        sums_one[1],
        sums_one[2],
        sums_one[3],
        sums_two[4],
        sums_two[2],
        sums_two[3],
        sums_two[6 : 6 + hidden // features].reshape(hidden),
        sums_two[1],
        sums_two[0],
        sums_one[4],
    )
    loss_part = jnp.sum(sums_two[5]) * inverse
    lengths = [vector.shape[0] // dp for vector in vectors]
    packed = jnp.concatenate(
        [vector.reshape(dp, -1) for vector in vectors]
        + [jnp.broadcast_to(loss_part[None, None], (dp, 1))],
        axis=1,
    )
    packed = reduce_vector(packed)
    loss_value = packed[-1]
    cuts, start = [], 0
    for length in lengths:
        cuts.append(packed[start : start + length])
        start += length
    (
        attend_gain_grad,
        attend_shift_grad,
        query_bias_grad,
        value_bias_grad,
        output_bias_grad,
        feed_gain_grad,
        feed_shift_grad,
        expand_bias_grad,
        reduce_bias_grad,
        pixel_bias_grad,
        mask_token_grad,
    ) = cuts
    reduce_weight_grad = reduce_rows(reduce_weight_grad, x_first)
    expand_weight_grad = reduce_rows(expand_weight_grad, y_first)
    square_grads = reduce_rows(square_grads, z_first)
    joint_weight_grad = reduce_rows(joint_weight_grad, x_first)
    return (
        loss_value,
        attend_gain_grad,
        attend_shift_grad,
        joint_weight_grad,
        query_bias_grad,
        value_bias_grad,
        square_grads[:, PIXELS:],
        output_bias_grad,
        feed_gain_grad,
        feed_shift_grad,
        expand_weight_grad,
        expand_bias_grad,
        reduce_weight_grad,
        reduce_bias_grad,
        square_grads[:, :PIXELS],
        pixel_bias_grad,
        mask_token_grad,
        patch_grad,
    )


MESH = pl.DeviceIdType.MESH


def places():
    data, seq = lax.axis_index("dp"), lax.axis_index("seq")
    x, low, high = lax.rem(data, 2), lax.rem(lax.div(data, 2), 2), lax.div(data, 4)
    core, y = lax.rem(seq, 2), lax.div(seq, 2)
    return {
        "x": (x, {"dp": data + 1 - 2 * x}),
        "low": (low, {"dp": data + 2 - 4 * low}),
        "high": (high, {"dp": data + 4 - 8 * high}),
        "y": (y, {"seq": seq + 2 - 4 * y}),
        "core": (core, {"seq": seq + 1 - 2 * core}),
    }


def greet(where):
    barrier = pltpu.get_barrier_semaphore()
    for _, partner in where.values():
        pl.semaphore_signal(barrier, inc=1, device_id=partner, device_id_type=MESH)
    pl.semaphore_wait(barrier, len(where))


def remote(source, target, send, receive, partner):
    return pltpu.make_async_remote_copy(
        src_ref=source,
        dst_ref=target,
        send_sem=send,
        recv_sem=receive,
        device_id=partner,
        device_id_type=MESH,
    )


NAMES = ("high", "low", "x", "y")


def names_of(order):
    halved = [token for token in order if token in NAMES]
    return tuple(halved + [name for name in NAMES if name not in halved])


def stage_shapes(names, order, tail):
    names, shapes = list(names), []
    for token in order:
        if token == "Gy":
            names = ["y"]
        elif token == "Gcore":
            names = ["core"] + names
        elif token[0] != "+":
            names.remove(token)
        shapes.append((2,) * len(names) + tail)
    return shapes


def for_each(dims, body):
    outer = max(dims - 2, 0)
    inner = list(itertools.product(range(2), repeat=dims - outer))
    if outer == 0:
        for spot in inner:
            body(spot)
        return

    def one(place, carry):
        first = tuple(lax.rem(lax.div(place, 2 ** (outer - 1 - dim)), 2) for dim in range(outer))
        for spot in inner:
            body(first + spot)
        return carry

    lax.fori_loop(0, 2**outer, one, 0)


def add_up(target, place, other):
    target[place] = (target[place].astype(F32) + other.astype(F32)).astype(target.dtype)


class Chain:
    def __init__(self, where, start, names, order, buffers, send, receive, base, swapped=None):
        self.where, self.order = dict(where), order
        if swapped is not None:
            (first, partner_first), (second, partner_second) = (where[name] for name in swapped)
            core = where["core"][0]

            def chosen(zero, one):
                return zero + core * (one - zero)

            for name, place, ours, other in (
                (swapped[0], (first, second), partner_first, partner_second),
                (swapped[1], (second, first), partner_second, partner_first),
            ):
                here = {"dp": lax.axis_index("dp"), "seq": lax.axis_index("seq")}
                ours, other = {**here, **ours}, {**here, **other}
                partner = {axis: chosen(ours[axis], other[axis]) for axis in here}
                self.where[name] = (chosen(*place), partner)
        self.plain = where
        self.refs = [start] + list(buffers)
        self.send, self.receive, self.base = send, receive, base
        self.names = [list(names)]
        for token in order:
            names = list(self.names[-1])
            if token == "Gy":
                names = ["y"]
            elif token == "Gcore":
                names = ["core"] + names
            elif token[0] != "+":
                names.remove(token)
            self.names.append(names)

    def copy(self, stage):
        token = self.order[stage]
        source, target = self.refs[stage], self.refs[stage + 1]
        if token[0] == "+":
            _, partner = self.plain[token[1:]]
        elif token[0] == "G":
            place, partner = self.plain[token[1:]]
            target = target.at[place]
        else:
            place, partner = self.where[token]
            dim = self.names[stage].index(token)
            source = source.at[(slice(None),) * dim + (1 - place,)]
        spot = self.base + stage
        return remote(source, target, self.send.at[spot], self.receive.at[spot], partner)

    def start(self, stage):
        self.copy(stage).start()

    def finish(self, stage):
        self.copy(stage).wait()
        token = self.order[stage]
        source, target = self.refs[stage], self.refs[stage + 1]
        if token[0] == "G":
            place, _ = self.plain[token[1:]]
            target[place] = source[...]
            return
        dim = None
        if token[0] != "+":
            place, _ = self.where[token]
            dim = self.names[stage].index(token)

        def one(spot):
            origin = spot if dim is None else spot[:dim] + (place,) + spot[dim:]
            add_up(target, spot if spot else Ellipsis, source[origin if origin else Ellipsis])

        for_each(len(self.names[stage + 1]), one)

    def turn(self, stage):
        if stage > 0:
            self.finish(stage - 1)
        if stage < len(self.order):
            self.start(stage)


Y_FIRST = ("y", "x", "low", "high", "Gy", "Gcore")
Y_THEN_LOW = ("y", "low", "x", "high", "Gy", "Gcore")
X_FIRST = ("x", "low", "high", "+y", "Gcore")
SUMS_ORDER = ("+core", "+y", "+x", "+low", "+high")
MOST = 6
TILE_ORDERS = (
    X_FIRST,
    X_FIRST,
    X_FIRST,
    X_FIRST,
    X_FIRST,
    Y_FIRST,
    Y_THEN_LOW,
    Y_FIRST,
    X_FIRST,
    Y_FIRST,
    Y_FIRST,
    X_FIRST,
    X_FIRST,
)
TILE_SWAPS = (
    ("x", "low"),
    ("x", "low"),
    ("x", "low"),
    ("x", "low"),
    ("x", "low"),
    ("x", "y"),
    ("y", "low"),
    ("x", "y"),
    ("x", "low"),
    ("x", "y"),
    ("x", "y"),
    ("x", "low"),
    ("x", "low"),
)
TILES = len(TILE_ORDERS)
TILE_STEPS = (0, 1, 2, 3, 4, 5, 6, 7, 8, 10, 15, 19, 22)
TURNS = {
    2: ((0, 0),),
    3: ((1, 0),),
    4: ((0, 1), (2, 0),),
    5: ((3, 0), (1, 1),),
    6: ((0, 2), (4, 0),),
    7: ((5, 0),),
    8: ((1, 2), (6, 0), (0, 3), (2, 1),),
    9: ((7, 0),),
    10: ((0, 4), (1, 3), (3, 1), (8, 0),),
    11: ((0, 5), (5, 1), (13, 0), (4, 1),),
    12: ((1, 4), (2, 2), (13, 1), (9, 0),),
    13: ((1, 5),),
    14: ((3, 2), (13, 2), (6, 1), (7, 1),),
    15: ((2, 3), (4, 2), (5, 2),),
    16: ((13, 3),),
    17: ((2, 4), (3, 3), (7, 2), (8, 1), (10, 0), (9, 1), (4, 3),),
    18: ((2, 5), (13, 4), (5, 3), (6, 2),),
    19: ((3, 4), (7, 3), (8, 2),),
    20: ((3, 5), (4, 4), (9, 2), (6, 3),),
    21: ((4, 5), (13, 5), (5, 4), (10, 1), (11, 0),),
    22: ((7, 4), (9, 3),),
    23: ((5, 5), (7, 5), (6, 4), (8, 3), (10, 2),),
    24: ((9, 4), (11, 1), (12, 0), (5, 6), (7, 6),),
    25: ((6, 5), (10, 3),),
}
LAST_TURNS = (
    (14, 0),
    (11, 2),
    (9, 5),
    (6, 6),
    (8, 4),
    (14, 1),
    (9, 6),
    (8, 5),
    (10, 4),
    (14, 2),
    (11, 3),
    (12, 1),
    (14, 3),
    (10, 5),
    (12, 2),
    (10, 6),
    (14, 4),
    (11, 4),
    (14, 5),
    (11, 5),
    (12, 3),
    (12, 4),
    (12, 5),
)


def chain_scratch(cases):
    scratch, counts = [], []
    for names, order, tail, dtype in cases:
        shapes = stage_shapes(names, order, tail)
        scratch += [pltpu.VMEM(shape, dtype) for shape in shapes]
        counts.append(len(shapes))
    return scratch, counts


def split_list(values, counts):
    parts, start = [], 0
    for count in counts:
        parts.append(values[start : start + count])
        start += count
    return parts


GAIN_ONE, SHIFT_ONE, QUERY, VALUE, OUTPUT, GAIN_TWO, SHIFT_TWO, REDUCE, PIXEL, TOKEN, EXPAND = range(11)
FRONT_OWN = 6
FRONT_FAR = 9
FRONT_ATTEND = 12
FRONT_PAIRS = 2


def lines_kernel(*refs):
    out = refs[-1]
    row = 0
    for ref in refs[:-1]:
        for start in range(0, ref.shape[0], WIDE):
            out[row : row + 1] = ref[start : start + WIDE].astype(F32).reshape(1, WIDE)
            row += 1


def stack_lines(*vectors):
    return pl.pallas_call(
        lines_kernel,
        in_specs=[pl.BlockSpec(memory_space=pltpu.VMEM)] * len(vectors),
        out_specs=pl.BlockSpec(memory_space=pltpu.VMEM),
        out_shape=jax.ShapeDtypeStruct((16, WIDE), F32),
        cost_estimate=cost(1e4, 1e5),
        name="stack_lines",
    )(*vectors)


def column_of(line):
    count = line.shape[1]
    down = lax.broadcasted_iota(jnp.int32, (count, count), 0)
    along = lax.broadcasted_iota(jnp.int32, (count, count), 1)
    return jnp.sum(jnp.where(down == along, jnp.broadcast_to(line, (count, count)), 0.0), axis=1, keepdims=True)


def front_kernel(
    parts, counts, rows_in, targets_in, orders_in, lines, weight_in, pixel_in, expand_in, output_in,
    embedded_out, input_out, joint_out, pairs_out, mixed_out, probs_out, masks_out, target_out, expand_out,
    embedded, inputs, masks, order_far, joint, pairs, weight, pixel, expand, output,
    local, far_send, far_receive, send, receive,
):
    images, heads = joint.shape[:2]
    quarter = rows_in.shape[2]
    where = {name: places()[name] for name in ("core", "y")}
    sibling = where["core"][1]
    y, other = where["y"]
    step = pl.program_id(0)
    near_half, far_half = pl.ds(0, quarter), pl.ds(quarter, quarter)

    def pair_copy(image):
        return remote(
            joint.at[image, :, pl.ds(1, 2)], pairs.at[image], send.at[image], receive.at[image], sibling
        )

    def far_copy(index, source, target):
        return remote(source, target, far_send.at[index], far_receive.at[index], other)

    order_copy = far_copy(0, orders_in.at[1 - y], order_far)
    row_copies = [
        far_copy(1 + image, rows_in.at[1 - y, image], embedded.at[image, far_half]) for image in range(images)
    ]
    target_copies = [
        far_copy(1 + images + image, targets_in.at[1 - y, image], target_out.at[image, far_half])
        for image in range(images)
    ]
    own_copy = pltpu.make_async_copy(rows_in.at[y], embedded.at[:, near_half], local.at[0])
    target_copy = pltpu.make_async_copy(targets_in.at[y], target_out.at[:, near_half], local.at[1])
    loads = [
        pltpu.make_async_copy(source, target, local.at[2 + index])
        for index, (source, target) in enumerate(
            ((pixel_in, pixel), (expand_in, expand), (output_in, output), (weight_in, weight))
        )
    ]

    @pl.when(step == 0)
    def _():
        own_copy.start()
        greet(where)
        order_copy.start()
        for copy in row_copies + loads:
            copy.start()
        target_copy.start()
        loads[0].wait()
        expand_out[0] = pixel[...]

    @pl.when(step == parts + 1)
    def _():
        loads[2].wait()
        expand_out[0] = output[...]

    for part in range(parts):

        @pl.when(step == 1 + part)
        def _(part=part):
            if part == 0:
                loads[1].wait()
            span = weight.shape[0] // 8
            starts = [place * parts * span + part * span for place in range(8)]
            expand_out[0] = jnp.concatenate([expand[:, start : start + span] for start in starts], axis=1)

    def project(image, start, order):
        block = pl.ds(start, quarter)
        mask = column_of((order < counts[y * images + image]).astype(F32))
        masks[image, block] = mask
        token = lines[TOKEN : TOKEN + 1].astype(BF16)
        rows = jnp.where(mask > 0.5, token, embedded[image, block])
        embedded[image, block] = rows
        normed, _ = normalize(rows.astype(F32))
        gain, shift = lines[GAIN_ONE : GAIN_ONE + 1], lines[SHIFT_ONE : SHIFT_ONE + 1]
        low = (normed * gain + shift).astype(BF16)
        inputs[image, block] = low
        for part, bias in ((1, None), (2, lines[VALUE : VALUE + 1]), (0, lines[QUERY : QUERY + 1])):
            total = dot(low, weight[:, part * WIDE : (part + 1) * WIDE])
            total = (total if bias is None else total + bias).astype(BF16)
            for pair in range(heads):
                joint[image, pair, part, block] = total[:, pair * PAIR : (pair + 1) * PAIR]

    @pl.when((step >= FRONT_OWN) & (step < FRONT_FAR))
    def _():
        @pl.when(step == FRONT_OWN)
        def _():
            own_copy.wait()
            loads[3].wait()

        image = step - FRONT_OWN
        project(image, 0, orders_in[y, image, 0:1, :quarter])

    @pl.when((step >= FRONT_FAR) & (step < FRONT_ATTEND))
    def _():
        for index in range(images):

            @pl.when(step == FRONT_FAR + index)
            def _(index=index):
                if index == 0:
                    order_copy.wait()
                row_copies[index].wait()
                target_copies[index].start()

        image = step - FRONT_FAR
        project(image, quarter, order_far[image, 0:1, :quarter])
        pair_copy(image).start()
        embedded_out[0] = embedded[image]
        input_out[0] = inputs[image]
        joint_out[0] = joint[image]
        masks_out[0] = masks[image]

    def attend(image, pair, index):
        queries = side_by_side(joint[image, pair, 0] * jnp.asarray(HEAD_DIM**-0.5, BF16))
        keys_in = jnp.concatenate([joint[image, pair, 1], pairs[image, pair, 0]], axis=0)
        values_in = jnp.concatenate([joint[image, pair, 2], pairs[image, pair, 1]], axis=0)
        pairs_out[0, index] = pairs[image, pair]
        scores = dot_nt(keys_in, queries)
        exponent = jnp.exp(scores - jnp.max(scores, axis=0, keepdims=True))
        total = jnp.sum(exponent, axis=0, keepdims=True)
        probs = (exponent * (1.0 / total)).astype(BF16)
        probs_out[0, index] = probs
        mixed = merge_turned(dot_tn(values_in, probs)).astype(BF16)
        mixed_out[0, :, index * PAIR : (index + 1) * PAIR] = mixed

    @pl.when(step >= FRONT_ATTEND)
    def _():
        place = step - FRONT_ATTEND
        turns = heads // FRONT_PAIRS
        image, turn = lax.div(place, turns), lax.rem(place, turns)

        @pl.when(turn == 0)
        def _():
            pair_copy(image).wait()

        for index in range(FRONT_PAIRS):
            attend(image, turn * FRONT_PAIRS + index, index)

    @pl.when(step == pl.num_programs(0) - 1)
    def _():
        for copy in target_copies:
            copy.wait()
        target_copy.wait()


def merge_turned(stacked):
    rows = stacked.shape[1] // 2
    down = lax.broadcasted_iota(jnp.int32, (PAIR, rows), 0)
    return jnp.where(down < HEAD_DIM, stacked[:, :rows], stacked[:, rows:]).T


def front(counts, rows_in, targets_in, orders_in, lines, weight, pixel, expand, output):
    near, quarter, width = rows_in.shape[1:]
    rows, heads = 2 * quarter, width // PAIR
    parts = expand.shape[1] // width

    def image(step):
        return jnp.clip(step - FRONT_FAR, 0, near - 1)

    turns = heads // FRONT_PAIRS

    def spot(step):
        place = jnp.maximum(step - FRONT_ATTEND, 0)
        return lax.div(place, turns), lax.rem(place, turns)

    block = pl.BlockSpec((1, rows, width), lambda s: (image(s), 0, 0))
    return pl.pallas_call(
        partial(front_kernel, parts),
        grid=(FRONT_ATTEND + near * turns,),
        in_specs=[
            pl.BlockSpec(memory_space=pltpu.SMEM),
            pl.BlockSpec(memory_space=pl.ANY),
            pl.BlockSpec(memory_space=pl.ANY),
            fixed(orders_in.shape),
            fixed(lines.shape),
        ]
        + [pl.BlockSpec(memory_space=pl.ANY)] * 4,
        out_specs=[
            block,
            block,
            pl.BlockSpec((1, heads, 3, rows, PAIR), lambda s: (image(s), 0, 0, 0, 0)),
            pl.BlockSpec((1, FRONT_PAIRS, 2, rows, PAIR), lambda s: spot(s) + (0, 0, 0)),
            pl.BlockSpec((1, rows, FRONT_PAIRS * PAIR), lambda s: (spot(s)[0], 0, spot(s)[1])),
            pl.BlockSpec((1, FRONT_PAIRS, 2 * rows, 2 * rows), lambda s: spot(s) + (0, 0)),
            pl.BlockSpec((1, rows, 1), lambda s: (image(s), 0, 0)),
            pl.BlockSpec(memory_space=pl.ANY),
            pl.BlockSpec((1, width, width), lambda s: (jnp.minimum(s, parts + 1), 0, 0)),
        ],
        out_shape=[
            jax.ShapeDtypeStruct((near, rows, width), BF16),
            jax.ShapeDtypeStruct((near, rows, width), BF16),
            jax.ShapeDtypeStruct((near, heads, 3, rows, PAIR), BF16),
            jax.ShapeDtypeStruct((near, heads, 2, rows, PAIR), BF16),
            jax.ShapeDtypeStruct((near, rows, width), BF16),
            jax.ShapeDtypeStruct((near, heads, 2 * rows, 2 * rows), BF16),
            jax.ShapeDtypeStruct((near, rows, 1), F32),
            jax.ShapeDtypeStruct((near, rows, width), BF16),
            jax.ShapeDtypeStruct((parts + 2, width, width), BF16),
        ],
        scratch_shapes=[
            pltpu.VMEM((near, rows, width), BF16),
            pltpu.VMEM((near, rows, width), BF16),
            pltpu.VMEM((near, rows, 1), F32),
            pltpu.VMEM(orders_in.shape[1:], jnp.int32),
            pltpu.VMEM((near, heads, 3, rows, PAIR), BF16),
            pltpu.VMEM((near, heads, 2, rows, PAIR), BF16),
            pltpu.VMEM(weight.shape, BF16),
            pltpu.VMEM(pixel.shape, BF16),
            pltpu.VMEM(expand.shape, BF16),
            pltpu.VMEM(output.shape, BF16),
            pltpu.SemaphoreType.DMA((6,)),
            pltpu.SemaphoreType.DMA((1 + 2 * near,)),
            pltpu.SemaphoreType.DMA((1 + 2 * near,)),
            pltpu.SemaphoreType.DMA((near,)),
            pltpu.SemaphoreType.DMA((near,)),
        ],
        compiler_params=pltpu.CompilerParams(
            vmem_limit_bytes=60 * MIB, collective_id=1, has_side_effects=True
        ),
        cost_estimate=cost(5e9, 40e6),
        name="front",
    )(counts, rows_in, targets_in, orders_in, lines, weight, pixel, expand, output)


def middle_kernel(
    embedded_in, mixed, mask_in, target_in, weights, reduce, lines,
    lefts, rights, input_out, scaling_out, sums_out, low, total, biases,
):
    parts = reduce.shape[1]
    span = reduce.shape[2]
    width = weights.shape[1]
    mask = mask_in[0]

    @pl.when(pl.program_id(0) == 0)
    def _():
        sums_out[...] = jnp.zeros_like(sums_out)
        for part in range(parts):
            pieces = []
            for place in range(8):
                row, start = divmod((place * parts + part) * span, width)
                pieces.append(lines[EXPAND + row : EXPAND + row + 1, start : start + span])
            biases[part] = jnp.concatenate(pieces, axis=1)

    after_attn = embedded_in[0].astype(F32) + dot(mixed[0], weights[parts + 1]) + lines[OUTPUT : OUTPUT + 1]
    lefts[0, parts + 1] = mixed[0]
    normed, scaling = normalize(after_attn)
    rights[0, parts + 1] = normed.astype(BF16)
    scaling_out[0] = scaling
    low[...] = (normed * lines[GAIN_TWO : GAIN_TWO + 1] + lines[SHIFT_TWO : SHIFT_TWO + 1]).astype(BF16)
    input_out[0] = low[...]
    total[...] = after_attn + lines[REDUCE : REDUCE + 1]

    def one(part, carry):
        active, rate = gelu_both(dot(low[...], weights[1 + part]) + biases[part])
        active = active.astype(BF16)
        lefts[0, 1 + part] = active
        rights[0, 1 + part] = rate.astype(BF16)
        total[...] += dot(active, reduce[:, part].reshape(width, width))
        return carry

    for part in range(parts):
        one(part, 0)
    after_low = total[...].astype(BF16)
    lefts[0, 0] = after_low
    errors = dot(after_low, weights[0]) + lines[PIXEL : PIXEL + 1] - target_in[0].astype(F32)
    square = errors * errors + 1.0
    root = lax.rsqrt(square)
    grad_pred = (mask * errors * root).astype(BF16)
    rights[0, 0] = grad_pred
    sums_out[0:1] += column_sums(grad_pred)
    sums_out[5:6] += jnp.sum((square * root - 1.0) * mask, axis=0, keepdims=True)
    sums_out[10:11] += jnp.sum(jnp.broadcast_to(mask, errors.shape), axis=0, keepdims=True)


def middle(embedded, mixed, mask, targets, weights, reduce, lines):
    near, rows, width = embedded.shape
    parts = reduce.shape[1]
    block = pl.BlockSpec((1, rows, width), lambda i: (i, 0, 0))
    column = pl.BlockSpec((1, rows, 1), lambda i: (i, 0, 0))
    stack = pl.BlockSpec((1, parts + 2, rows, width), lambda i: (i, 0, 0, 0))
    return pl.pallas_call(
        middle_kernel,
        grid=(near,),
        in_specs=[
            block,
            block,
            column,
            block,
            fixed((parts + 2, width, width)),
            fixed(reduce.shape),
            fixed(lines.shape),
        ],
        out_specs=[stack, stack, block, column, fixed_out((16, width))],
        out_shape=[
            jax.ShapeDtypeStruct((near, parts + 2, rows, width), BF16),
            jax.ShapeDtypeStruct((near, parts + 2, rows, width), BF16),
            jax.ShapeDtypeStruct((near, rows, width), BF16),
            jax.ShapeDtypeStruct((near, rows, 1), F32),
            jax.ShapeDtypeStruct((16, width), F32),
        ],
        scratch_shapes=[
            pltpu.VMEM((rows, width), BF16),
            pltpu.VMEM((rows, width), F32),
            pltpu.VMEM((parts, 1, width), F32),
        ],
        compiler_params=params(60),
        cost_estimate=cost(2 * near * rows * width * width * (2 * parts + 2), 40e6),
        name="middle",
    )(embedded, mixed, mask, targets, weights, reduce, lines)


HIGH_ROWS = 4 * 96


def spread_half(result, target, high, start, names, swapped):
    for low in range(2):
        for x in range(2):
            for y in range(2):
                at = (low * 2 + x) * 96 + start
                piece = result[at : at + HALF, y * 384 : (y + 1) * 384]
                spot = {"high": high, "low": low, "x": x, "y": y}
                if swapped is not None:
                    first, second = swapped
                    spot[first], spot[second] = spot[second], spot[first]
                target[tuple(spot[name] for name in names)] = piece.astype(BF16)


HALF = 48
SLOTS = 4
KEPT = 10
FIRST_ATTEND = 11
GROUP_STEPS = (15, 19, 22)
FIRST_NORM = 23


def back_kernel(
    counts, left, right, weights, reduce, query, key, value, input_two, scaling_two, input_one, joint, pairs, probs_in, lines, sums_in,
    embedded_in, mask_in, *rest,
):
    (
        done_out,
        near_out,
        far_out,
        sums_out,
        late_out,
        done,
        done_sent,
        branch,
        wide,
        grad_in,
        upstream,
        own_pairs,
        give_pairs,
        got_pairs,
        far_give,
        sums,
        late,
        keep,
        give,
        got,
        send,
        receive,
        core_send,
        core_receive,
        pair_send,
        pair_receive,
        far_send,
        far_receive,
    ) = rest[:28]
    buffers = split_list(rest[28:], counts)
    where = places()
    core, sibling = where["core"]
    step = pl.program_id(0)
    images, rows, width = input_two.shape
    every = images * rows
    quarter = rows // 2
    heads = width // PAIR
    first_gain, second_gain = lines[GAIN_ONE : GAIN_ONE + 1], lines[GAIN_TWO : GAIN_TWO + 1]
    chains = [
        Chain(where, keep.at[unit % KEPT], names_of(order), order, list(buffers[unit]) + [done.at[unit]], send, receive, MOST * unit, TILE_SWAPS[unit])
        for unit, order in enumerate(TILE_ORDERS)
    ]
    chains.append(Chain(where, sums, (), SUMS_ORDER, buffers[TILES], send, receive, MOST * TILES))
    chains.append(Chain(where, late, (), SUMS_ORDER, buffers[TILES + 1], send, receive, MOST * TILES + MOST))

    def core_copy(unit):
        slot = lax.rem(unit, SLOTS)
        return remote(give.at[slot], got.at[slot], core_send.at[unit], core_receive.at[unit], sibling)

    def pair_copy(place, second):
        image = lax.rem(place, 3)
        slot = lax.rem((lax.div(place, 6) * 3 + image) * 2 + second, SLOTS)
        return remote(
            give_pairs.at[slot], got_pairs.at[place], pair_send.at[place], pair_receive.at[place], sibling
        )

    def far_copy(image):
        return remote(
            far_give.at[image], far_out.at[image], far_send.at[image], far_receive.at[image], where["y"][1]
        )

    def core_sum(unit):
        core_copy(unit).wait()
        for_each(4, lambda spot: add_up(keep.at[unit % KEPT], spot, got[(unit % SLOTS,) + spot]))

    def done_copy(unit):
        return pltpu.make_async_copy(done.at[unit], done_out.at[unit], done_sent.at[unit])

    def turn(unit, stage):
        if unit < TILES and stage == 0:
            core_sum(unit)
        chains[unit].turn(stage)
        if stage == len(chains[unit].order) and unit < TILES:
            done_copy(unit).start()

    def tile(unit, lines_of, value, forms):
        def one(high):
            columns = slice(high * HIGH_ROWS, (high + 1) * HIGH_ROWS)
            result = dot_tn(lines_of(columns).reshape(every, HIGH_ROWS), value)
            for half in range(2):
                for names, swapped, chosen in forms:
                    swapped = swapped if half == 1 else None

                    @pl.when(jnp.logical_and(core == half, chosen))
                    def _(half=half, names=names, swapped=swapped):
                        spread_half(result, keep.at[lax.rem(unit, KEPT)], high, half * HALF, names, swapped)

                    @pl.when(jnp.logical_and(core != half, chosen))
                    def _(half=half, names=names, swapped=swapped):
                        spread_half(result, give.at[lax.rem(unit, SLOTS)], high, half * HALF, names, swapped)

        for high in range(2):
            one(high)
        core_copy(unit).start()

    def forms_of(units, unit):
        forms = {}
        for other in units:
            form = (names_of(TILE_ORDERS[other]), TILE_SWAPS[other])
            forms.setdefault(form, []).append(unit == other)
        if len(forms) == 1:
            return [form + (True,) for form in forms]
        return [form + (functools.reduce(jnp.logical_or, asked),) for form, asked in forms.items()]

    def flat(ref):
        return ref[...].reshape(every, ref.shape[-1])

    def left_lines(columns):
        return left[:, 0, :, columns]

    @pl.when(step == 0)
    def _():
        greet(where)
        sums[...] = sums_in[...]
        late[...] = jnp.zeros_like(late)
        grad_in[...] = jnp.zeros_like(grad_in)

    for at, turns in TURNS.items():

        @pl.when(step == at)
        def _(turns=turns):
            for unit, stage in turns:
                turn(unit, stage)

    @pl.when(step == 0)
    def _():
        tile(0, left_lines, right[:, 0].reshape(every, width), forms_of((0,), 0))

        def one(image):
            low = dot_nt(right[image, 0], weights[0]).astype(BF16)
            branch[image] = low
            sums[1:2] += column_sums(low)
        for image in range(images):
            one(image)

    @pl.when((step > 0) & (step < 9) & (lax.rem(step, 2) == 1))
    def _():
        tile(step, left_lines, flat(branch), forms_of((1, 3, 5, 7), step))
        row = pl.ds(6 + lax.div(step, 2), 1)

        def one(image):
            low = dot_nt(branch[image], reduce[:, 0].reshape(width, width)) * right[image, 0].astype(F32)
            low = low.astype(BF16)
            wide[image] = low
            sums[row] += column_sums(low)
        for image in range(images):
            one(image)

    @pl.when((step > 0) & (step < 9) & (lax.rem(step, 2) == 0))
    def _():
        tile(step, lambda columns: input_two[:, :, columns], flat(wide), forms_of((2, 4, 6, 8), step))
        fresh = jnp.where(step == 2, 0.0, 1.0)

        def one(image):
            grad_in[image] = grad_in[image] * fresh + dot_nt(wide[image], weights[0])
        for image in range(images):
            one(image)

    @pl.when(step == 9)
    def _():
        def one(image):
            normed = right[image, 0].astype(F32)
            grad = grad_in[image]
            low = branch[image].astype(F32) + normalize_back(grad, normed, scaling_two[image], second_gain)
            low = low.astype(BF16)
            branch[image] = low
            sums[2:3] += column_sums(grad * normed)
            sums[3:4] += column_sums(grad)
            sums[4:5] += column_sums(low)
            mixed = dot_nt(low, weights[0]).astype(BF16)
            for pair in range(heads):
                upstream[image, pair] = mixed[:, pair * PAIR : (pair + 1) * PAIR]
        for image in range(images):
            one(image)

    @pl.when(step == 10)
    def _():
        tile(9, left_lines, flat(branch), forms_of((9,), 9))

    def attend_back(group, image, second, inside, order):
        place = group * 6 + inside

        @pl.when(order >= SLOTS)
        def _():
            before = order - SLOTS
            pair_copy(lax.div(before, 6) * 6 + second * 3 + lax.rem(lax.div(before, 2), 3), second).wait_send()

        scale = HEAD_DIM**-0.5
        target = own_pairs.at[lax.rem(group, 2), inside]
        away = give_pairs.at[lax.rem(order, SLOTS)]
        queries = side_by_side(joint[0, second, 0])
        keys_in = jnp.concatenate([joint[0, second, 1], pairs[0, second, 0]], axis=0)
        values_in = jnp.concatenate([joint[0, second, 2], pairs[0, second, 1]], axis=0)
        grad_mixed = side_by_side(upstream[image, group * 2 + second])
        probs = probs_in[0, second]
        grad_probs = dot_nt(values_in, grad_mixed)
        broad = probs.astype(F32)
        weighted = broad * grad_probs
        inner = jnp.sum(weighted, axis=0, keepdims=True)
        grad_scores = (weighted - broad * inner).astype(BF16)
        grad_values = dot(probs, grad_mixed).astype(BF16)
        grad_keys = (dot(grad_scores, queries) * scale).astype(BF16)
        target[0] = (merge_turned(dot_tn(keys_in, grad_scores)) * scale).astype(BF16)
        target[1] = grad_keys[:rows]
        target[2] = grad_values[:rows]
        away[0] = grad_keys[rows:]
        away[1] = grad_values[rows:]
        pair_copy(place, second).start()

    attends = (step >= FIRST_ATTEND) & (step < GROUP_STEPS[2]) & (step != GROUP_STEPS[0]) & (step != GROUP_STEPS[1])

    @pl.when(attends)
    def _():
        group, image = attend_place(step)
        for second in range(2):
            inside = second * 3 + image
            attend_back(group, image, second, inside, (group * 3 + image) * 2 + second)

    @pl.when((step == GROUP_STEPS[0]) | (step == GROUP_STEPS[1]) | (step == GROUP_STEPS[2]))
    def _():
        group = jnp.where(step == GROUP_STEPS[0], 0, jnp.where(step == GROUP_STEPS[1], 1, 2))
        slot = lax.rem(group, 2)
        for inside in range(6):
            pair_copy(group * 6 + inside, inside // 3).wait_recv()
            image, second = inside % 3, inside // 3
            for part in range(3):
                piece = own_pairs[slot, inside, part]
                if part > 0:
                    piece = piece.astype(F32) + got_pairs[group * 6 + inside, part - 1].astype(F32)
                start = part * 2 * PAIR + second * PAIR
                wide[image, :, start : start + PAIR] = piece.astype(BF16)
        tile(10 + group, lambda columns: input_one[:, :, columns], flat(wide), forms_of((10, 11, 12), 10 + group))
        columns = jnp.concatenate([query[...], key[...], value[...]], axis=1)
        fresh = jnp.where(group == 0, 0.0, 1.0)
        row = pl.ds(5 + group, 1)

        def one(image):
            late[row] += column_sums(wide[image])
            grad_in[image] = grad_in[image] * fresh + dot_nt(wide[image], columns)
        for image in range(images):
            one(image)

    @pl.when(step >= FIRST_NORM)
    def _():
        image = step - FIRST_NORM
        mask = mask_in[0]
        normed, scaling = normalize(embedded_in[0].astype(F32))
        grad = grad_in[image]
        total = branch[image].astype(F32) + normalize_back(grad, normed, scaling, first_gain)
        kept = total * (1.0 - mask)
        near_out[0] = kept[:quarter]
        far_give[image] = kept[quarter:].astype(BF16)
        far_copy(image).start()
        late[0:1] += column_sums(grad * normed)
        late[1:2] += column_sums(grad)
        late[2:3] += column_sums(total * mask)

    @pl.when(step == pl.num_programs(0) - 1)
    def _():
        for unit, stage in LAST_TURNS:
            turn(unit, stage)
        for image in range(images):
            far_copy(image).wait()
        for unit in range(TILES):
            done_copy(unit).wait()
        for image in range(1, 3):
            for second in range(2):
                pair_copy(12 + second * 3 + image, second).wait_send()
        sums_out[...] = chains[TILES].refs[-1][...]
        late_out[...] = chains[TILES + 1].refs[-1][...]


def attend_place(step):
    place = step - FIRST_ATTEND
    for at in GROUP_STEPS[:2]:
        place = place - jnp.where(step > at, 1, 0)
    place = jnp.clip(place, 0, 8)
    return lax.div(place, 3), lax.rem(place, 3)


def back(
    lefts, rights, weights, reduce, joint_weight, input_two, scaling_two, input_one, joint, pairs, probs, lines, sums, embedded, mask
):
    near, slots, rows, width = lefts.shape
    quarter = rows // 2
    heads = width // PAIR

    def slot(step):
        return jnp.minimum(lax.div(step + 1, 2), slots - 1)

    def part(step):
        return jnp.clip(lax.div(step - 1, 2), 0, slots - 3)

    def group(step):
        return jnp.where(step > GROUP_STEPS[0], 1, 0) + jnp.where(step > GROUP_STEPS[1], 1, 0)

    def columns(which):
        return pl.BlockSpec((width, 2 * PAIR), lambda s: (0, which * 3 + group(s)))

    def spot(step):
        group, image = attend_place(step)
        return image, group

    def image(step):
        return jnp.maximum(step - FIRST_NORM, 0)

    cases = [(names_of(order), order, (HALF, 384), BF16) for order in TILE_ORDERS]
    cases.append(((), SUMS_ORDER, sums.shape, F32))
    cases.append(((), SUMS_ORDER, (8, width), F32))
    buffers, counts = chain_scratch(cases)
    kept, start = [], 0
    for index, count in enumerate(counts):
        kept += buffers[start : start + count - (index < TILES)]
        start += count
    buffers, counts = kept, [count - (index < TILES) for index, count in enumerate(counts)]
    whole = (2, 2, 2, 2, HALF, 384)
    stack = pl.BlockSpec((near, 1, rows, width), lambda s: (0, slot(s), 0, 0))
    return pl.pallas_call(
        partial(back_kernel, counts),
        grid=(FIRST_NORM + near,),
        in_specs=[
            stack,
            stack,
            pl.BlockSpec((1, width, width), lambda s: (slot(s), 0, 0)),
            pl.BlockSpec((8, 1, reduce.shape[2], width), lambda s: (0, part(s), 0, 0)),
            columns(0),
            columns(1),
            columns(2),
            fixed((near, rows, width)),
            fixed((near, rows, 1)),
            fixed((near, rows, width)),
            pl.BlockSpec((1, 2, 3, rows, PAIR), lambda s: spot(s) + (0, 0, 0)),
            pl.BlockSpec((1, 2, 2, rows, PAIR), lambda s: spot(s) + (0, 0, 0)),
            pl.BlockSpec((1, 2, 2 * rows, 2 * rows), lambda s: spot(s) + (0, 0)),
            fixed(lines.shape),
            fixed(sums.shape),
            pl.BlockSpec((1, rows, width), lambda s: (image(s), 0, 0)),
            pl.BlockSpec((1, rows, 1), lambda s: (image(s), 0, 0)),
        ],
        out_specs=[
            pl.BlockSpec(memory_space=pl.ANY),
            pl.BlockSpec((1, quarter, width), lambda s: (image(s), 0, 0)),
            pl.BlockSpec(memory_space=pl.ANY),
            fixed_out(sums.shape),
            fixed_out((8, width)),
        ],
        out_shape=[
            jax.ShapeDtypeStruct((TILES, 2, 2, HALF, 384), BF16),
            jax.ShapeDtypeStruct((near, quarter, width), F32),
            jax.ShapeDtypeStruct((near, quarter, width), BF16),
            jax.ShapeDtypeStruct(sums.shape, F32),
            jax.ShapeDtypeStruct((8, width), F32),
        ],
        scratch_shapes=[
            pltpu.VMEM((TILES, 2, 2, HALF, 384), BF16),
            pltpu.SemaphoreType.DMA((TILES,)),
            pltpu.VMEM((near, rows, width), BF16),
            pltpu.VMEM((near, rows, width), BF16),
            pltpu.VMEM((near, rows, width), F32),
            pltpu.VMEM((near, heads, rows, PAIR), BF16),
            pltpu.VMEM((2, 6, 3, rows, PAIR), BF16),
            pltpu.VMEM((SLOTS, 2, rows, PAIR), BF16),
            pltpu.VMEM((near * heads, 2, rows, PAIR), BF16),
            pltpu.VMEM((near, quarter, width), BF16),
            pltpu.VMEM(sums.shape, F32),
            pltpu.VMEM((8, width), F32),
            pltpu.VMEM((KEPT,) + whole, BF16),
            pltpu.VMEM((SLOTS,) + whole, BF16),
            pltpu.VMEM((SLOTS,) + whole, BF16),
            pltpu.SemaphoreType.DMA((MOST * (TILES + 2),)),
            pltpu.SemaphoreType.DMA((MOST * (TILES + 2),)),
            pltpu.SemaphoreType.DMA((TILES,)),
            pltpu.SemaphoreType.DMA((TILES,)),
            pltpu.SemaphoreType.DMA((near * heads,)),
            pltpu.SemaphoreType.DMA((near * heads,)),
            pltpu.SemaphoreType.DMA((near,)),
            pltpu.SemaphoreType.DMA((near,)),
        ]
        + buffers,
        compiler_params=pltpu.CompilerParams(
            vmem_limit_bytes=60 * MIB, collective_id=2, has_side_effects=True
        ),
        cost_estimate=cost(40e9, 60e6),
        name="back",
    )(
        lefts, rights, weights, reduce, joint_weight, joint_weight, joint_weight, input_two,
        scaling_two, input_one, joint, pairs, probs, lines, sums, embedded, mask,
    )


def emit_kernel(parts, place, done, near_in, far_in, sums, late, *outs):
    (
        loss, attend_gain, attend_shift, joint, query_bias, value_bias, output, output_bias, feed_gain,
        feed_shift, expand, expand_bias, reduce, reduce_bias, pixel, pixel_bias, token, patch,
    ) = outs
    data, y = place[0], place[1]
    inverse = 1.0 / (sums[10:11] * PIXELS)
    loss[...] = jnp.sum(sums[5:6] * inverse, axis=1, keepdims=True)
    wide_inverse = inverse[:, :384]

    def piece(unit, core, half):
        return done[unit, core, half].astype(F32) * wide_inverse

    def square(unit):
        return [
            jnp.concatenate([piece(unit, core, half) for half in range(2)], axis=1) for core in range(2)
        ]

    for unit, target in ((0, pixel), (2 * parts + 1, output)):
        for core, lines in enumerate(square(unit)):
            target[core * HALF : (core + 1) * HALF] = lines
    expands = []
    for part in range(parts):
        for core, lines in enumerate(square(1 + 2 * part)):
            start = part * 2 * HALF + core * HALF
            reduce[start : start + HALF] = lines
        expands.append(square(2 + 2 * part))
    span = 2 * HALF
    for core in range(2):
        for d in range(8):
            lines = [expands[part][core][:, d * span : (d + 1) * span] for part in range(parts)]
            expand[core * HALF : (core + 1) * HALF, d * 4 * span : (d + 1) * 4 * span] = jnp.concatenate(
                lines, axis=1
            )
    for group in range(3):
        for core, lines in enumerate(square(2 * parts + 2 + group)):
            for part in range(3):
                start = part * WIDE + group * 2 * PAIR
                joint[core * HALF : (core + 1) * HALF, start : start + 2 * PAIR] = lines[
                    :, part * 2 * PAIR : (part + 1) * 2 * PAIR
                ]

    def own_cut(lines):
        shift = lax.rem(WIDE - data * span, WIDE)
        return pltpu.roll(lines, shift, axis=1)[:, :span]

    early = own_cut(sums[...] * inverse)
    later = own_cut(late[...] * inverse)
    queries = jnp.concatenate([late[5 + group : 6 + group, : 2 * PAIR] for group in range(3)], axis=1)
    values = jnp.concatenate([late[5 + group : 6 + group, 4 * PAIR :] for group in range(3)], axis=1)
    both = jnp.concatenate([queries, values] + [jnp.zeros((6, WIDE), F32)], axis=0)
    both = own_cut(both * inverse)
    for target, lines, row in (
        (attend_gain, later, 0),
        (attend_shift, later, 1),
        (query_bias, both, 0),
        (value_bias, both, 1),
        (output_bias, early, 4),
        (feed_gain, early, 2),
        (feed_shift, early, 3),
        (reduce_bias, early, 1),
        (pixel_bias, early, 0),
        (token, later, 2),
    ):
        target[...] = lines[row : row + 1]
    expand_bias[...] = jnp.concatenate([early[6 + part : 7 + part] for part in range(parts)], axis=1)
    images = near_in.shape[0]
    for image in range(images):
        patch[y * images + image] = near_in[image] * inverse
        patch[(1 - y) * images + image] = far_in[image].astype(F32) * inverse


def emit(parts, place, done, near_in, far_in, sums, late):
    images, quarter, width = near_in.shape
    hidden = parts * width

    def out(*shape):
        return jax.ShapeDtypeStruct(shape, F32)

    small = out(1, 96)
    outs = [
        out(1, 1), small, small, out(96, 3 * width), small, small, out(96, width), small, small,
        small, out(96, hidden), out(1, hidden // 8), out(hidden // 8, width), small, out(96, width), small, small,
        out(2 * images, quarter, width),
    ]
    whole = pl.BlockSpec(memory_space=pltpu.VMEM)
    return pl.pallas_call(
        partial(emit_kernel, parts),
        in_specs=[pl.BlockSpec(memory_space=pltpu.SMEM)] + [whole] * 5,
        out_specs=[whole] * len(outs),
        out_shape=outs,
        compiler_params=params(60),
        cost_estimate=cost(1e6, 12e6),
        name="emit",
    )(place, done, near_in, far_in, sums, late)


def eight_places(
    patches,
    targets,
    mask_order,
    mask_count,
    attend_gain,
    attend_shift,
    joint_weight,
    query_bias,
    value_bias,
    output_weight,
    output_bias,
    feed_gain,
    feed_shift,
    expand_weight,
    expand_bias,
    reduce_weight,
    reduce_bias,
    pixel_weight,
    pixel_bias,
    mask_token,
):
    images, quarter, features = patches.shape
    near = images // 2
    place_y = own_bit("seq", 2)
    hidden = expand_bias.shape[0]
    parts = hidden // features

    def halves(values):
        return values.reshape((2, near) + values.shape[1:])

    lines = stack_lines(
        attend_gain,
        attend_shift,
        query_bias,
        value_bias,
        output_bias,
        feed_gain,
        feed_shift,
        reduce_bias,
        pixel_bias,
        mask_token,
        expand_bias,
    )
    orders = jnp.pad(mask_order[:, None, :], ((0, 0), (0, 7), (0, 256 - quarter)))
    reduce_parts = reduce_weight.reshape(8, parts, hidden // (8 * parts), features)
    place = jnp.stack([lax.axis_index("dp"), place_y]).astype(jnp.int32)
    embedded, input_one, joint, pairs, mixed, probs, mask, targets_here, weights = front(
        mask_count,
        halves(patches),
        halves(targets),
        halves(orders),
        lines,
        joint_weight,
        pixel_weight,
        expand_weight,
        output_weight,
    )
    lefts, rights, input_two, scaling_two, sums = middle(
        embedded, mixed, mask, targets_here, weights, reduce_parts, lines
    )
    done, patch_near, patch_far, sums, late = back(
        lefts,
        rights,
        weights,
        reduce_parts,
        joint_weight,
        input_two,
        scaling_two,
        input_one,
        joint,
        pairs,
        probs,
        lines,
        sums,
        embedded,
        mask,
    )
    outs = emit(parts, place, done, patch_near, patch_far, sums, late)
    flat = {0: (), 1: (-1,), 2: (-1,), 4: (-1,), 5: (-1,), 7: (-1,), 8: (-1,), 9: (-1,), 11: (-1,)}
    flat.update({13: (-1,), 15: (-1,), 16: (-1,)})
    return tuple(
        out.reshape(flat[index]) if index in flat else out for index, out in enumerate(outs)
    )


def on_device(*arguments):
    if lax.axis_size("dp") == 8 and lax.axis_size("seq") == 4:
        return eight_places(*arguments)
    return any_places(*arguments)


def solution(mesh):
    placed = (
        P("dp", "seq", None),
        P("dp", "seq", None),
        P("dp", "seq"),
        P("dp"),
        P(),
        P(),
        P(),
        P(),
        P(),
        P(),
        P(),
        P(),
        P(),
        P(),
        P(),
        P(),
        P(),
        P(),
        P(),
        P(),
    )
    return jax.shard_map(
        on_device,
        mesh=mesh,
        in_specs=placed,
        out_specs=(
            P(),
            P("dp"),
            P("dp"),
            P("dp", None),
            P("dp"),
            P("dp"),
            P("dp", None),
            P("dp"),
            P("dp"),
            P("dp"),
            P("dp", None),
            P("dp"),
            P("dp", None),
            P("dp"),
            P("dp", None),
            P("dp"),
            P("dp"),
            P("dp", "seq", None),
        ),
        check_vma=False,
    )
```

```python
import functools
import itertools
from functools import partial

import jax
import jax.numpy as jnp
from jax import lax
from jax.experimental import pallas as pl
from jax.experimental.pallas import tpu as pltpu
from jax.sharding import PartitionSpec as P

HEADS = 12
HEAD_DIM = 64
PIXELS = 768
WIDE = 768
PAIR = 2 * HEAD_DIM
MIB = 1 << 20
F32 = jnp.float32
BF16 = jnp.bfloat16


def dot(left, right):
    return jnp.dot(left, right, preferred_element_type=F32)


def dot_nt(left, right):
    return lax.dot_general(left, right, (((1,), (1,)), ((), ())), preferred_element_type=F32)


def dot_tn(left, right):
    return lax.dot_general(left, right, (((0,), (0,)), ((), ())), preferred_element_type=F32)


def normalize(inputs):
    centre = inputs - jnp.mean(inputs, axis=-1, keepdims=True)
    scaling = lax.rsqrt(jnp.mean(centre * centre, axis=-1, keepdims=True) + 1e-06)
    return (centre * scaling, scaling)


def normalize_back(upstream, normed, scaling, gain):
    scaled = upstream * gain
    return scaling * (
        scaled
        - jnp.mean(scaled, axis=-1, keepdims=True)
        - normed * jnp.mean(scaled * normed, axis=-1, keepdims=True)
    )


def column_sums(values):
    return jnp.sum(values.astype(F32), axis=0, keepdims=True)


def gelu_both(inputs):
    bell = jnp.exp(inputs * inputs * -0.5)
    base_of = 1.0 + (0.3275911 * 0.7071067811865476) * jnp.abs(inputs)
    inner = pl.reciprocal(base_of, approx=True)
    inner = inner * (2.0 - base_of * inner)
    series = inner * (
        0.254829592
        + inner * (-0.284496736 + inner * (1.421413741 + inner * (-1.453152027 + inner * 1.061405429)))
    )
    tail = 0.5 * series * bell
    below = jnp.where(inputs < 0.0, tail, 1.0 - tail)
    return (inputs * below, below + inputs * bell * 0.3989422804014327)


def params(limit):
    return pltpu.CompilerParams(vmem_limit_bytes=limit * MIB)


def fixed(shape):
    zeros = (0,) * len(shape)
    return pl.BlockSpec(shape, lambda *place: zeros, pipeline_mode=pl.Buffered(1))


def cost(flops, moved):
    return pl.CostEstimate(flops=int(flops), bytes_accessed=int(moved), transcendentals=0)


def project_kernel(own, far, gain, shift, weight, bias, embedded_out, joint_out):
    embedded = jnp.concatenate([own[0], far[0]], axis=0)
    embedded_out[0] = embedded
    normed, _ = normalize(embedded.astype(F32))
    low = (normed * gain[...] + shift[...]).astype(BF16)
    for part in range(3):
        cut = slice(part * WIDE, (part + 1) * WIDE)
        joint_out[0, part] = (dot(low, weight[:, cut]) + bias[:, cut]).astype(BF16)


def project(own, far, gain, shift, weight, bias):
    near, quarter, width = own.shape
    rows = 2 * quarter
    return pl.pallas_call(
        project_kernel,
        grid=(near,),
        in_specs=[
            pl.BlockSpec((1, quarter, width), lambda i: (i, 0, 0)),
            pl.BlockSpec((1, quarter, width), lambda i: (i, 0, 0)),
            fixed((1, width)),
            fixed((1, width)),
            fixed((width, 3 * width)),
            fixed((1, 3 * width)),
        ],
        out_specs=[
            pl.BlockSpec((1, rows, width), lambda i: (i, 0, 0)),
            pl.BlockSpec((1, 3, rows, width), lambda i: (i, 0, 0, 0)),
        ],
        out_shape=[
            jax.ShapeDtypeStruct((near, rows, width), BF16),
            jax.ShapeDtypeStruct((near, 3, rows, width), BF16),
        ],
        compiler_params=params(32),
        cost_estimate=cost(2 * near * rows * width * 3 * width, 12e6),
        name="project",
    )(own, far, gain, shift, weight, bias)


def side_by_side(pair):
    lanes = lax.broadcasted_iota(jnp.int32, pair.shape, 1)
    zero = jnp.zeros_like(pair)
    first = jnp.where(lanes < HEAD_DIM, pair, zero)
    second = jnp.where(lanes < HEAD_DIM, zero, pair)
    return jnp.concatenate([first, second], axis=0)


def merge_heads(stacked):
    rows = stacked.shape[0] // 2
    lanes = lax.broadcasted_iota(jnp.int32, (rows, PAIR), 1)
    return jnp.where(lanes < HEAD_DIM, stacked[:rows], stacked[rows:])


def attend_kernel(own, far, mixed_out, probs_out):
    queries = side_by_side(own[0, 0] * jnp.asarray(HEAD_DIM**-0.5, BF16))
    keys_in = jnp.concatenate([own[0, 1], far[0, 0]], axis=0)
    values_in = jnp.concatenate([own[0, 2], far[0, 1]], axis=0)
    scores = dot_nt(queries, keys_in)
    exponent = jnp.exp(scores - jnp.max(scores, axis=-1, keepdims=True))
    total = jnp.sum(exponent, axis=-1, keepdims=True)
    probs = (exponent * (1.0 / total)).astype(BF16)
    probs_out[0, 0] = probs
    mixed_out[0] = merge_heads(dot(probs, values_in)).astype(BF16)


def attend(joint, pairs_far):
    near, _, rows, width = joint.shape
    keys_count = 2 * rows
    pairs = width // PAIR
    return pl.pallas_call(
        attend_kernel,
        grid=(near, pairs),
        in_specs=[
            pl.BlockSpec((1, 3, rows, PAIR), lambda i, h: (i, 0, 0, h)),
            pl.BlockSpec((1, 2, rows, PAIR), lambda i, h: (i, 0, 0, h)),
        ],
        out_specs=[
            pl.BlockSpec((1, rows, PAIR), lambda i, h: (i, 0, h)),
            pl.BlockSpec((1, 1, 2 * rows, keys_count), lambda i, h: (i, h, 0, 0)),
        ],
        out_shape=[
            jax.ShapeDtypeStruct((near, rows, width), BF16),
            jax.ShapeDtypeStruct((near, pairs, 2 * rows, keys_count), BF16),
        ],
        compiler_params=params(32),
        cost_estimate=cost(8 * near * rows * keys_count * width, 20e6),
        name="attend",
    )(joint, pairs_far)


def attend_back_kernel(own, far, probs_in, upstream, query_out, own_out, far_out):
    rows = own.shape[2]
    scale = HEAD_DIM**-0.5
    queries = side_by_side(own[0, 0])
    keys_in = jnp.concatenate([own[0, 1], far[0, 0]], axis=0)
    values_in = jnp.concatenate([own[0, 2], far[0, 1]], axis=0)
    grad_mixed = side_by_side(upstream[0])
    probs = probs_in[0, 0]
    grad_probs = dot_nt(grad_mixed, values_in)
    wide = probs.astype(F32)
    weighted = wide * grad_probs
    inner = jnp.sum(weighted, axis=-1, keepdims=True)
    grad_scores = (weighted - wide * inner).astype(BF16)
    query_out[0] = (merge_heads(dot(grad_scores, keys_in)) * scale).astype(BF16)
    grad_values = dot_tn(probs, grad_mixed).astype(BF16)
    grad_keys = (dot_tn(grad_scores, queries) * scale).astype(BF16)
    own_out[0, 0] = grad_keys[:rows]
    own_out[0, 1] = grad_values[:rows]
    far_out[0, 0] = grad_keys[rows:]
    far_out[0, 1] = grad_values[rows:]


def attend_back(joint, pairs_far, probs, upstream):
    near, _, rows, width = joint.shape
    keys_count = 2 * rows
    pairs = width // PAIR
    two = pl.BlockSpec((1, 2, rows, PAIR), lambda i, h: (i, 0, 0, h))
    one = pl.BlockSpec((1, rows, PAIR), lambda i, h: (i, 0, h))
    return pl.pallas_call(
        attend_back_kernel,
        grid=(near, pairs),
        in_specs=[
            pl.BlockSpec((1, 3, rows, PAIR), lambda i, h: (i, 0, 0, h)),
            two,
            pl.BlockSpec((1, 1, 2 * rows, keys_count), lambda i, h: (i, h, 0, 0)),
            one,
        ],
        out_specs=[one, two, two],
        out_shape=[
            jax.ShapeDtypeStruct((near, rows, width), BF16),
            jax.ShapeDtypeStruct((near, 2, rows, width), BF16),
            jax.ShapeDtypeStruct((near, 2, rows, width), BF16),
        ],
        compiler_params=params(32),
        cost_estimate=cost(16 * near * rows * keys_count * width, 25e6),
        name="attend_back",
    )(joint, pairs_far, probs, upstream)


def rows_kernel(
    hidden,
    inverse,
    embedded_in,
    mixed,
    mask_in,
    target_own,
    target_far,
    output_weight,
    expand_weight,
    reduce_weight,
    pixel_weight,
    biases,
    expand_bias,
    input_out,
    active_out,
    after_out,
    pred_out,
    branch_out,
    expand_out,
    low_out,
    attn_out,
    mixed_out,
    sums_out,
    slope,
):
    output_bias, gain, shift, reduce_bias, pixel_bias = (biases[row : row + 1] for row in range(5))
    mask = mask_in[0]
    after_attn = embedded_in[0].astype(F32) + dot(mixed[0], output_weight[...]) + output_bias
    normed, scaling = normalize(after_attn)
    low = (normed * gain + shift).astype(BF16)
    input_out[0] = low
    total = after_attn + reduce_bias
    for start in range(0, hidden, WIDE):
        cut = slice(start, start + WIDE)
        active, rate = gelu_both(dot(low, expand_weight[:, cut]) + expand_bias[:, cut])
        active = active.astype(BF16)
        active_out[0, :, cut] = active
        slope[:, cut] = rate.astype(slope.dtype)
        total += dot(active, reduce_weight[cut, :])
    after_low = total.astype(BF16)
    after_out[0] = after_low
    target = jnp.concatenate([target_own[0], target_far[0]], axis=0).astype(F32)
    errors = dot(after_low, pixel_weight[...]) + pixel_bias - target
    square = errors * errors + 1.0
    root = lax.rsqrt(square)
    channel = jnp.sum((square * root - 1.0) * mask, axis=0, keepdims=True)
    grad_pred = (mask * errors * root * inverse[0, 0]).astype(BF16)
    pred_out[0] = grad_pred
    grad_mlp = dot_nt(grad_pred, pixel_weight[...])
    branch = grad_mlp.astype(BF16)
    branch_out[0] = branch
    grad_in = jnp.zeros_like(grad_mlp)
    expand_sums = []
    for start in range(0, hidden, WIDE):
        cut = slice(start, start + WIDE)
        grad_expand = dot_nt(branch, reduce_weight[cut, :]) * slope[:, cut].astype(F32)
        grad_expand = grad_expand.astype(BF16)
        expand_out[0, :, cut] = grad_expand
        expand_sums.append(column_sums(grad_expand))
        grad_in += dot_nt(grad_expand, expand_weight[:, cut])
    grad_attn = grad_mlp + normalize_back(grad_in, normed, scaling, gain)
    attn_out[0] = grad_attn
    grad_low = grad_attn.astype(BF16)
    low_out[0] = grad_low
    mixed_out[0] = dot_nt(grad_low, output_weight[...]).astype(BF16)
    sums = [
        column_sums(grad_pred),
        column_sums(branch),
        column_sums(grad_in * normed),
        column_sums(grad_in),
        column_sums(grad_low),
        channel,
    ] + expand_sums

    @pl.when(pl.program_id(0) == 0)
    def _():
        sums_out[...] = jnp.zeros_like(sums_out)

    for row, line in enumerate(sums):
        sums_out[row : row + 1] += line


def rows_step(
    inverse,
    embedded,
    mixed,
    mask,
    target_own,
    target_far,
    output_weight,
    expand_weight,
    reduce_weight,
    pixel_weight,
    biases,
    expand_bias,
):
    near, rows, width = embedded.shape
    quarter = target_own.shape[1]
    hidden = expand_weight.shape[1]
    block = pl.BlockSpec((1, rows, width), lambda i: (i, 0, 0))
    half = pl.BlockSpec((1, quarter, width), lambda i: (i, 0, 0))
    long = pl.BlockSpec((1, rows, hidden), lambda i: (i, 0, 0))
    narrow = jax.ShapeDtypeStruct((near, rows, width), BF16)
    broad = jax.ShapeDtypeStruct((near, rows, hidden), BF16)
    return pl.pallas_call(
        partial(rows_kernel, hidden),
        grid=(near,),
        in_specs=[
            pl.BlockSpec(memory_space=pltpu.SMEM),
            block,
            block,
            pl.BlockSpec((1, rows, 1), lambda i: (i, 0, 0)),
            half,
            half,
            fixed((width, width)),
            fixed((width, hidden)),
            fixed((hidden, width)),
            fixed((width, width)),
            fixed((8, width)),
            fixed((1, hidden)),
        ],
        out_specs=[block, long, block, block, block, long, block, block, block, fixed_out((16, width))],
        out_shape=[
            narrow,
            broad,
            narrow,
            narrow,
            narrow,
            broad,
            narrow,
            jax.ShapeDtypeStruct((near, rows, width), F32),
            narrow,
            jax.ShapeDtypeStruct((16, width), F32),
        ],
        scratch_shapes=[pltpu.VMEM((rows, hidden), F32)],
        compiler_params=params(56),
        cost_estimate=cost(4 * near * rows * width * (2 * width + 2 * hidden), 40e6),
        name="rows_step",
    )(
        inverse,
        embedded,
        mixed,
        mask,
        target_own,
        target_far,
        output_weight,
        expand_weight,
        reduce_weight,
        pixel_weight,
        biases,
        expand_bias,
    )


def fixed_out(shape):
    zeros = (0,) * len(shape)
    return pl.BlockSpec(shape, lambda *place: zeros)


def outer_kernel(left_moves, left, right, out, turned):
    if left_moves:
        out[...] = dot_tn(left[...], right[...]).astype(out.dtype)
        return

    @pl.when(pl.program_id(0) == 0)
    def _():
        turned[...] = left[...].T

    out[...] = dot(turned[...], right[...]).astype(out.dtype)


def outer(left, right):
    rows, tall = left.shape
    broad = right.shape[1]
    left_moves = tall > broad
    if left_moves:
        grid, specs = tall // WIDE, [
            pl.BlockSpec((rows, WIDE), lambda i: (0, i)),
            fixed((rows, broad)),
        ]
        out_spec = pl.BlockSpec((WIDE, broad), lambda i: (i, 0))
    else:
        grid, specs = broad // WIDE, [
            fixed((rows, tall)),
            pl.BlockSpec((rows, WIDE), lambda i: (0, i)),
        ]
        out_spec = pl.BlockSpec((tall, WIDE), lambda i: (0, i))
    return pl.pallas_call(
        partial(outer_kernel, left_moves),
        grid=(grid,),
        in_specs=specs,
        out_specs=out_spec,
        out_shape=jax.ShapeDtypeStruct((tall, broad), BF16),
        scratch_shapes=[pltpu.VMEM((WIDE, rows), BF16)],
        compiler_params=params(32),
        cost_estimate=cost(2 * rows * tall * broad, 2 * (rows * (tall + broad) + tall * broad)),
        name="outer",
    )(left, right)


def project_back_kernel(
    query, own, received, embedded_in, attn, mask_in, gain, shift, weight,
    input_out, joint_out, near_out, far_out, sums_out,
):
    quarter = near_out.shape[1]
    mask = mask_in[0]
    embedded = embedded_in[0].astype(F32)
    normed, scaling = normalize(embedded)
    input_out[0] = (normed * gain[...] + shift[...]).astype(BF16)
    grad_query = query[0]
    grad_key = (own[0, 0].astype(F32) + received[0, 0].astype(F32)).astype(BF16)
    grad_value = (own[0, 1].astype(F32) + received[0, 1].astype(F32)).astype(BF16)
    grad_in = None
    for part, grad in enumerate((grad_query, grad_key, grad_value)):
        joint_out[part, 0] = grad
        term = dot_nt(grad, weight[:, part * WIDE : (part + 1) * WIDE])
        grad_in = term if grad_in is None else grad_in + term
    grad_embedded = attn[0] + normalize_back(grad_in, normed, scaling, gain[...])
    kept = grad_embedded * (1.0 - mask)
    near_out[0] = kept[:quarter]
    far_out[0] = kept[quarter:].astype(BF16)
    sums = [
        column_sums(grad_in * normed),
        column_sums(grad_in),
        column_sums(grad_query),
        column_sums(grad_value),
        column_sums(grad_embedded * mask),
    ]

    @pl.when(pl.program_id(0) == 0)
    def _():
        sums_out[...] = jnp.zeros_like(sums_out)

    for row, line in enumerate(sums):
        sums_out[row : row + 1] += line


def project_back(query, own, received, embedded, attn, mask, gain, shift, weight):
    near, rows, width = embedded.shape
    quarter = rows // 2
    block = pl.BlockSpec((1, rows, width), lambda i: (i, 0, 0))
    half = pl.BlockSpec((1, quarter, width), lambda i: (i, 0, 0))
    two = pl.BlockSpec((1, 2, rows, width), lambda i: (i, 0, 0, 0))
    return pl.pallas_call(
        project_back_kernel,
        grid=(near,),
        in_specs=[
            block,
            two,
            two,
            block,
            block,
            pl.BlockSpec((1, rows, 1), lambda i: (i, 0, 0)),
            fixed((1, width)),
            fixed((1, width)),
            fixed((width, 3 * width)),
        ],
        out_specs=[
            block,
            pl.BlockSpec((3, 1, rows, width), lambda i: (0, i, 0, 0)),
            half,
            half,
            fixed_out((8, width)),
        ],
        out_shape=[
            jax.ShapeDtypeStruct((near, rows, width), BF16),
            jax.ShapeDtypeStruct((3, near, rows, width), BF16),
            jax.ShapeDtypeStruct((near, quarter, width), F32),
            jax.ShapeDtypeStruct((near, quarter, width), BF16),
            jax.ShapeDtypeStruct((8, width), F32),
        ],
        compiler_params=params(40),
        cost_estimate=cost(2 * near * rows * width * 3 * width, 20e6),
        name="project_back",
    )(query, own, received, embedded, attn, mask, gain, shift, weight)


def swap(values, axis, bit):
    size = lax.axis_size(axis)
    return lax.ppermute(values, axis, [(place, place ^ bit) for place in range(size)])


def own_bit(axis, bit):
    return (lax.axis_index(axis) // bit) % 2


def pick(values, dim, which):
    return lax.dynamic_index_in_dim(values, which, dim, keepdims=False)


def add_in(kept, received):
    return (kept.astype(jnp.float32) + received.astype(jnp.float32)).astype(kept.dtype)


def halve(values, dim, axis, bit):
    mine = own_bit(axis, bit)
    received = swap(pick(values, dim, 1 - mine), axis, bit)
    return add_in(pick(values, dim, mine), received)


def join(values, dim, axis, bit):
    mine = own_bit(axis, bit)
    received = swap(values, axis, bit)
    first = jnp.where(mine == 0, values, received)
    second = jnp.where(mine == 0, received, values)
    return jnp.concatenate([first, second], axis=dim)


def reduce_rows(grad, order):
    dp = lax.axis_size("dp")
    rows, columns = grad.shape
    steps = dp.bit_length() - 1
    part = rows // dp
    if columns % 512 == 0:
        tail = (1, 2, part, 2, columns // 4, 2)
        parts = grad.reshape((2,) * steps + (part, 4, columns // 4))
        parts = jnp.moveaxis(parts, steps + 1, 0)
    else:
        parts = grad.reshape((2,) * steps + (4, part // 4, columns))
        parts = jnp.moveaxis(parts, steps, 0)
    parts = parts.reshape((2, 2) + parts.shape[1:])
    names = ["core", "y"] + [1 << bit for bit in reversed(range(steps))]
    for name in order(steps):
        dim = names.index(name)
        if name == "core":
            parts = halve(parts, dim, "seq", 1)
        elif name == "y":
            parts = halve(parts, dim, "seq", 2)
        else:
            parts = halve(parts, dim, "dp", name)
        names.pop(dim)
    parts = join(parts[None], 0, "seq", 2)
    parts = join(parts[None], 0, "seq", 1)
    parts = parts.reshape((4,) + parts.shape[2:]).astype(jnp.float32)
    if columns % 512 == 0:
        return jnp.moveaxis(parts, 0, 1).reshape(part, columns)
    return parts.reshape(part, columns)


def x_first(steps):
    return ["core"] + [1 << bit for bit in range(steps)] + ["y"]


def y_first(steps):
    return ["core", "y"] + [1 << bit for bit in range(steps)]


def z_first(steps):
    return ["core"] + [1 << bit for bit in range(1, steps)] + [1, "y"]


def reduce_vector(values):
    dp = lax.axis_size("dp")
    steps = dp.bit_length() - 1
    values = values + swap(values, "seq", 1)
    values = values + swap(values, "seq", 2)
    values = values.reshape((2,) * steps + values.shape[1:])
    for bit in reversed(range(steps)):
        mine = own_bit("dp", 1 << bit)
        received = swap(pick(values, 0, 1 - mine), "dp", 1 << bit)
        values = pick(values, 0, mine) + received
    return values


def any_places(
    patches,
    targets,
    mask_order,
    mask_count,
    attend_gain,
    attend_shift,
    joint_weight,
    query_bias,
    value_bias,
    output_weight,
    output_bias,
    feed_gain,
    feed_shift,
    expand_weight,
    expand_bias,
    reduce_weight,
    reduce_bias,
    pixel_weight,
    pixel_bias,
    mask_token,
):
    images, quarter, features = patches.shape
    dp = lax.axis_size("dp")
    near = images // 2
    rows_one = 2 * quarter
    row_count = near * rows_one
    place_y = own_bit("seq", 2)

    def own_and_far(values):
        parts = values.reshape((2, near) + values.shape[1:])
        return pick(parts, 0, place_y), swap(pick(parts, 0, 1 - place_y), "seq", 2)

    def line(vector):
        return vector.astype(F32)[None, :]

    masked_here = mask_order < mask_count[:, None]
    embedded_here = jnp.where(masked_here[:, :, None], mask_token[None, None, :], patches)
    embedded_own, embedded_far = own_and_far(embedded_here)
    mask = jnp.concatenate(own_and_far(masked_here.astype(jnp.int32)), axis=1)
    mask = mask.astype(F32)[:, :, None]
    count_sum = jnp.sum(mask_count)
    for bit in range(dp.bit_length() - 1):
        count_sum = count_sum + swap(count_sum, "dp", 1 << bit)
    inverse = 1.0 / (count_sum.astype(F32) * PIXELS)
    target_own, target_far = own_and_far(targets)
    joint_bias = jnp.concatenate(
        [line(query_bias), jnp.zeros((1, features), F32), line(value_bias)], axis=1
    )
    biases = jnp.concatenate(
        [
            line(vector)
            for vector in (output_bias, feed_gain, feed_shift, reduce_bias, pixel_bias)
        ]
        + [jnp.zeros((3, features), F32)],
        axis=0,
    )
    embedded, joint = project(
        embedded_own, embedded_far, line(attend_gain), line(attend_shift), joint_weight, joint_bias
    )
    pairs_far = swap(joint[:, 1:], "seq", 1)
    mixed, probs = attend(joint, pairs_far)
    (
        input_two,
        activated,
        after_low,
        grad_pred,
        grad_branch,
        grad_expand,
        grad_out,
        grad_attn,
        grad_mixed,
        sums_two,
    ) = rows_step(
        inverse.reshape(1, 1),
        embedded,
        mixed,
        mask,
        target_own,
        target_far,
        output_weight,
        expand_weight,
        reduce_weight,
        pixel_weight,
        biases,
        line(expand_bias),
    )

    def flat(values):
        return values.reshape(row_count, values.shape[-1])

    reduce_weight_grad = outer(flat(activated), flat(grad_branch))
    expand_weight_grad = outer(flat(input_two), flat(grad_expand))
    pixel_weight_grad = outer(flat(after_low), flat(grad_pred))
    output_weight_grad = outer(flat(mixed), flat(grad_out))
    square_grads = jnp.concatenate([pixel_weight_grad, output_weight_grad], axis=1)
    grad_query, grad_own, grad_far = attend_back(joint, pairs_far, probs, grad_mixed)
    received = swap(grad_far, "seq", 1)
    input_one, grad_joint, patch_near, patch_far, sums_one = project_back(
        grad_query,
        grad_own,
        received,
        embedded,
        grad_attn,
        mask,
        line(attend_gain),
        line(attend_shift),
        joint_weight,
    )
    grad_joint = grad_joint.reshape(3, row_count, features)
    joint_weight_grad = jnp.concatenate(
        [outer(flat(input_one), grad_joint[part]) for part in range(3)], axis=1
    )
    patch_far = swap(patch_far, "seq", 2).astype(F32)
    patch_grad = jnp.concatenate(
        [
            jnp.where(place_y == 0, patch_near, patch_far),
            jnp.where(place_y == 0, patch_far, patch_near),
        ],
        axis=0,
    )
    hidden = expand_bias.shape[0]
    vectors = (
        sums_one[0],
        sums_one[1],
        sums_one[2],
        sums_one[3],
        sums_two[4],
        sums_two[2],
        sums_two[3],
        sums_two[6 : 6 + hidden // features].reshape(hidden),
        sums_two[1],
        sums_two[0],
        sums_one[4],
    )
    loss_part = jnp.sum(sums_two[5]) * inverse
    lengths = [vector.shape[0] // dp for vector in vectors]
    packed = jnp.concatenate(
        [vector.reshape(dp, -1) for vector in vectors]
        + [jnp.broadcast_to(loss_part[None, None], (dp, 1))],
        axis=1,
    )
    packed = reduce_vector(packed)
    loss_value = packed[-1]
    cuts, start = [], 0
    for length in lengths:
        cuts.append(packed[start : start + length])
        start += length
    (
        attend_gain_grad,
        attend_shift_grad,
        query_bias_grad,
        value_bias_grad,
        output_bias_grad,
        feed_gain_grad,
        feed_shift_grad,
        expand_bias_grad,
        reduce_bias_grad,
        pixel_bias_grad,
        mask_token_grad,
    ) = cuts
    reduce_weight_grad = reduce_rows(reduce_weight_grad, x_first)
    expand_weight_grad = reduce_rows(expand_weight_grad, y_first)
    square_grads = reduce_rows(square_grads, z_first)
    joint_weight_grad = reduce_rows(joint_weight_grad, x_first)
    return (
        loss_value,
        attend_gain_grad,
        attend_shift_grad,
        joint_weight_grad,
        query_bias_grad,
        value_bias_grad,
        square_grads[:, PIXELS:],
        output_bias_grad,
        feed_gain_grad,
        feed_shift_grad,
        expand_weight_grad,
        expand_bias_grad,
        reduce_weight_grad,
        reduce_bias_grad,
        square_grads[:, :PIXELS],
        pixel_bias_grad,
        mask_token_grad,
        patch_grad,
    )


MESH = pl.DeviceIdType.MESH


def places():
    data, seq = lax.axis_index("dp"), lax.axis_index("seq")
    x, low, high = lax.rem(data, 2), lax.rem(lax.div(data, 2), 2), lax.div(data, 4)
    core, y = lax.rem(seq, 2), lax.div(seq, 2)
    return {
        "x": (x, {"dp": data + 1 - 2 * x}),
        "low": (low, {"dp": data + 2 - 4 * low}),
        "high": (high, {"dp": data + 4 - 8 * high}),
        "y": (y, {"seq": seq + 2 - 4 * y}),
        "core": (core, {"seq": seq + 1 - 2 * core}),
    }


def greet(where):
    barrier = pltpu.get_barrier_semaphore()
    for _, partner in where.values():
        pl.semaphore_signal(barrier, inc=1, device_id=partner, device_id_type=MESH)
    pl.semaphore_wait(barrier, len(where))


def remote(source, target, send, receive, partner):
    return pltpu.make_async_remote_copy(
        src_ref=source,
        dst_ref=target,
        send_sem=send,
        recv_sem=receive,
        device_id=partner,
        device_id_type=MESH,
    )


NAMES = ("high", "low", "x", "y")


def names_of(order):
    halved = [token for token in order if token in NAMES]
    return tuple(halved + [name for name in NAMES if name not in halved])


def stage_shapes(names, order, tail):
    names, shapes = list(names), []
    for token in order:
        if token == "Gy":
            names = ["y"]
        elif token == "Gcore":
            names = ["core"] + names
        elif token[0] != "+":
            names.remove(token)
        shapes.append((2,) * len(names) + tail)
    return shapes


def for_each(dims, body):
    outer = max(dims - 2, 0)
    inner = list(itertools.product(range(2), repeat=dims - outer))
    if outer == 0:
        for spot in inner:
            body(spot)
        return

    def one(place, carry):
        first = tuple(lax.rem(lax.div(place, 2 ** (outer - 1 - dim)), 2) for dim in range(outer))
        for spot in inner:
            body(first + spot)
        return carry

    lax.fori_loop(0, 2**outer, one, 0)


def add_up(target, place, other):
    target[place] = target[place] + other


class Chain:
    def __init__(self, where, start, names, order, buffers, send, receive, base, swapped=None):
        self.where, self.order = dict(where), order
        if swapped is not None:
            (first, partner_first), (second, partner_second) = (where[name] for name in swapped)
            core = where["core"][0]

            def chosen(zero, one):
                return zero + core * (one - zero)

            for name, place, ours, other in (
                (swapped[0], (first, second), partner_first, partner_second),
                (swapped[1], (second, first), partner_second, partner_first),
            ):
                here = {"dp": lax.axis_index("dp"), "seq": lax.axis_index("seq")}
                ours, other = {**here, **ours}, {**here, **other}
                partner = {axis: chosen(ours[axis], other[axis]) for axis in here}
                self.where[name] = (chosen(*place), partner)
        self.plain = where
        self.refs = [start] + list(buffers)
        self.send, self.receive, self.base = send, receive, base
        self.names = [list(names)]
        for token in order:
            names = list(self.names[-1])
            if token == "Gy":
                names = ["y"]
            elif token == "Gcore":
                names = ["core"] + names
            elif token[0] != "+":
                names.remove(token)
            self.names.append(names)

    def copy(self, stage):
        token = self.order[stage]
        source, target = self.refs[stage], self.refs[stage + 1]
        if token[0] == "+":
            _, partner = self.plain[token[1:]]
        elif token[0] == "G":
            place, partner = self.plain[token[1:]]
            target = target.at[place]
        else:
            place, partner = self.where[token]
            dim = self.names[stage].index(token)
            source = source.at[(slice(None),) * dim + (1 - place,)]
        spot = self.base + stage
        return remote(source, target, self.send.at[spot], self.receive.at[spot], partner)

    def start(self, stage):
        self.copy(stage).start()

    def finish(self, stage):
        self.copy(stage).wait()
        token = self.order[stage]
        source, target = self.refs[stage], self.refs[stage + 1]
        if token[0] == "G":
            place, _ = self.plain[token[1:]]
            target[place] = source[...]
            return
        dim = None
        if token[0] != "+":
            place, _ = self.where[token]
            dim = self.names[stage].index(token)

        def one(spot):
            origin = spot if dim is None else spot[:dim] + (place,) + spot[dim:]
            add_up(target, spot if spot else Ellipsis, source[origin if origin else Ellipsis])

        for_each(len(self.names[stage + 1]), one)

    def turn(self, stage):
        if stage > 0:
            self.finish(stage - 1)
        if stage < len(self.order):
            self.start(stage)


Y_FIRST = ("y", "x", "low", "high", "Gy", "Gcore")
Y_THEN_LOW = ("y", "low", "x", "high", "Gy", "Gcore")
X_FIRST = ("x", "low", "high", "+y", "Gcore")
SUMS_ORDER = ("+core", "+y", "+x", "+low", "+high")
MOST = 6
TILE_ORDERS = (
    Y_FIRST,
    Y_FIRST,
    Y_THEN_LOW,
    X_FIRST,
    Y_FIRST,
    Y_FIRST,
    X_FIRST,
    Y_THEN_LOW,
    Y_FIRST,
    Y_THEN_LOW,
    Y_FIRST,
    X_FIRST,
    X_FIRST,
)
TILE_SWAPS = (
    ("x", "y"),
    ("x", "y"),
    ("y", "low"),
    ("x", "low"),
    ("x", "y"),
    ("x", "y"),
    ("x", "low"),
    ("y", "low"),
    ("x", "y"),
    ("y", "low"),
    ("x", "y"),
    ("x", "low"),
    ("x", "low"),
)
TILES = len(TILE_ORDERS)
TILE_STEPS = (0, 1, 2, 3, 4, 5, 6, 7, 8, 10, 15, 19, 22)
TURNS = {
    2: ((0, 0),),
    3: ((1, 0),),
    4: ((2, 0), (0, 1),),
    5: ((3, 0),),
    6: ((1, 1), (4, 0),),
    7: ((0, 2), (2, 1), (5, 0),),
    8: ((1, 2), (3, 1), (6, 0),),
    9: ((0, 3), (7, 0),),
    10: ((1, 3), (2, 2), (4, 1), (8, 0),),
    11: ((0, 4), (5, 1), (13, 0),),
    12: ((1, 4), (3, 2), (13, 1), (9, 0),),
    13: ((0, 5), (2, 3),),
    14: ((0, 6), (6, 1), (7, 1), (1, 5), (4, 2),),
    15: ((1, 6), (2, 4), (3, 3), (13, 2),),
    16: ((5, 2),),
    17: ((2, 5), (4, 3), (13, 3), (8, 1), (10, 0),),
    18: ((2, 6), (3, 4), (6, 2), (7, 2), (9, 1), (5, 3),),
    19: ((3, 5), (4, 4), (13, 4),),
    20: ((7, 3), (8, 2),),
    21: ((4, 5), (5, 4), (9, 2), (10, 1), (11, 0),),
    22: ((4, 6), (13, 5), (6, 3), (8, 3),),
    23: ((5, 5), (7, 4), (9, 3),),
    24: ((6, 4), (8, 4), (10, 2), (12, 0), (5, 6), (6, 5), (7, 5), (11, 1),),
    25: ((9, 4),),
}
LAST_TURNS = (
    (14, 0),
    (8, 5),
    (10, 3),
    (7, 6),
    (14, 1),
    (8, 6),
    (10, 4),
    (9, 5),
    (11, 2),
    (14, 2),
    (9, 6),
    (12, 1),
    (14, 3),
    (10, 5),
    (11, 3),
    (12, 2),
    (14, 4),
    (10, 6),
    (14, 5),
    (12, 3),
    (11, 4),
    (11, 5),
    (12, 4),
    (12, 5),
)


def chain_scratch(cases):
    scratch, counts = [], []
    for names, order, tail, dtype in cases:
        shapes = stage_shapes(names, order, tail)
        scratch += [pltpu.VMEM(shape, dtype) for shape in shapes]
        counts.append(len(shapes))
    return scratch, counts


def split_list(values, counts):
    parts, start = [], 0
    for count in counts:
        parts.append(values[start : start + count])
        start += count
    return parts


GAIN_ONE, SHIFT_ONE, QUERY, VALUE, OUTPUT, GAIN_TWO, SHIFT_TWO, REDUCE, PIXEL, TOKEN, EXPAND = range(11)
FRONT_OWN = 6
FRONT_FAR = 9
FRONT_ATTEND = 12
FRONT_PAIRS = 2


def lines_kernel(*refs):
    out = refs[-1]
    row = 0
    for ref in refs[:-1]:
        for start in range(0, ref.shape[0], WIDE):
            out[row : row + 1] = ref[start : start + WIDE].astype(F32).reshape(1, WIDE)
            row += 1


def stack_lines(*vectors):
    return pl.pallas_call(
        lines_kernel,
        in_specs=[pl.BlockSpec(memory_space=pltpu.VMEM)] * len(vectors),
        out_specs=pl.BlockSpec(memory_space=pltpu.VMEM),
        out_shape=jax.ShapeDtypeStruct((16, WIDE), F32),
        cost_estimate=cost(1e4, 1e5),
        name="stack_lines",
    )(*vectors)


def column_of(line):
    count = line.shape[1]
    down = lax.broadcasted_iota(jnp.int32, (count, count), 0)
    along = lax.broadcasted_iota(jnp.int32, (count, count), 1)
    return jnp.sum(jnp.where(down == along, jnp.broadcast_to(line, (count, count)), 0.0), axis=1, keepdims=True)


def front_kernel(
    parts, counts, rows_in, targets_in, orders_in, lines, weight_in, pixel_in, expand_in, output_in,
    embedded_out, input_out, joint_out, pairs_out, mixed_out, probs_out, masks_out, target_out, expand_out,
    embedded, inputs, masks, order_far, joint, pairs, weight, pixel, expand, output,
    local, far_send, far_receive, send, receive,
):
    images, heads = joint.shape[:2]
    quarter = rows_in.shape[2]
    where = {name: places()[name] for name in ("core", "y")}
    sibling = where["core"][1]
    y, other = where["y"]
    step = pl.program_id(0)
    near_half, far_half = pl.ds(0, quarter), pl.ds(quarter, quarter)

    def pair_copy(image):
        return remote(
            joint.at[image, :, pl.ds(1, 2)], pairs.at[image], send.at[image], receive.at[image], sibling
        )

    def far_copy(index, source, target):
        return remote(source, target, far_send.at[index], far_receive.at[index], other)

    order_copy = far_copy(0, orders_in.at[1 - y], order_far)
    row_copies = [
        far_copy(1 + image, rows_in.at[1 - y, image], embedded.at[image, far_half]) for image in range(images)
    ]
    target_copies = [
        far_copy(1 + images + image, targets_in.at[1 - y, image], target_out.at[image, far_half])
        for image in range(images)
    ]
    own_copy = pltpu.make_async_copy(rows_in.at[y], embedded.at[:, near_half], local.at[0])
    target_copy = pltpu.make_async_copy(targets_in.at[y], target_out.at[:, near_half], local.at[1])
    loads = [
        pltpu.make_async_copy(source, target, local.at[2 + index])
        for index, (source, target) in enumerate(
            ((pixel_in, pixel), (expand_in, expand), (output_in, output), (weight_in, weight))
        )
    ]

    @pl.when(step == 0)
    def _():
        own_copy.start()
        greet(where)
        order_copy.start()
        for copy in row_copies + loads:
            copy.start()
        target_copy.start()
        loads[0].wait()
        expand_out[0] = pixel[...]

    @pl.when(step == parts + 1)
    def _():
        loads[2].wait()
        expand_out[0] = output[...]

    for part in range(parts):

        @pl.when(step == 1 + part)
        def _(part=part):
            if part == 0:
                loads[1].wait()
            span = weight.shape[0] // 8
            starts = [place * parts * span + part * span for place in range(8)]
            expand_out[0] = jnp.concatenate([expand[:, start : start + span] for start in starts], axis=1)

    def project(image, start, order):
        block = pl.ds(start, quarter)
        mask = column_of((order < counts[y * images + image]).astype(F32))
        masks[image, block] = mask
        token = lines[TOKEN : TOKEN + 1].astype(BF16)
        rows = jnp.where(mask > 0.5, token, embedded[image, block])
        embedded[image, block] = rows
        normed, _ = normalize(rows.astype(F32))
        gain, shift = lines[GAIN_ONE : GAIN_ONE + 1], lines[SHIFT_ONE : SHIFT_ONE + 1]
        low = (normed * gain + shift).astype(BF16)
        inputs[image, block] = low
        for part, bias in ((1, None), (2, lines[VALUE : VALUE + 1]), (0, lines[QUERY : QUERY + 1])):
            total = dot(low, weight[:, part * WIDE : (part + 1) * WIDE])
            total = (total if bias is None else total + bias).astype(BF16)
            for pair in range(heads):
                joint[image, pair, part, block] = total[:, pair * PAIR : (pair + 1) * PAIR]

    @pl.when((step >= FRONT_OWN) & (step < FRONT_FAR))
    def _():
        @pl.when(step == FRONT_OWN)
        def _():
            own_copy.wait()
            loads[3].wait()

        image = step - FRONT_OWN
        project(image, 0, orders_in[y, image, 0:1, :quarter])

    @pl.when((step >= FRONT_FAR) & (step < FRONT_ATTEND))
    def _():
        for index in range(images):

            @pl.when(step == FRONT_FAR + index)
            def _(index=index):
                if index == 0:
                    order_copy.wait()
                row_copies[index].wait()
                target_copies[index].start()

        image = step - FRONT_FAR
        project(image, quarter, order_far[image, 0:1, :quarter])
        pair_copy(image).start()
        embedded_out[0] = embedded[image]
        input_out[0] = inputs[image]
        joint_out[0] = joint[image]
        masks_out[0] = masks[image]

    def attend(image, pair, index):
        queries = side_by_side(joint[image, pair, 0] * jnp.asarray(HEAD_DIM**-0.5, BF16))
        keys_in = jnp.concatenate([joint[image, pair, 1], pairs[image, pair, 0]], axis=0)
        values_in = jnp.concatenate([joint[image, pair, 2], pairs[image, pair, 1]], axis=0)
        pairs_out[0, index] = pairs[image, pair]
        scores = dot_nt(keys_in, queries)
        exponent = jnp.exp(scores - jnp.max(scores, axis=0, keepdims=True))
        total = jnp.sum(exponent, axis=0, keepdims=True)
        probs = (exponent * (1.0 / total)).astype(BF16)
        probs_out[0, index] = probs
        mixed = merge_turned(dot_tn(values_in, probs)).astype(BF16)
        mixed_out[0, :, index * PAIR : (index + 1) * PAIR] = mixed

    @pl.when(step >= FRONT_ATTEND)
    def _():
        place = step - FRONT_ATTEND
        turns = heads // FRONT_PAIRS
        image, turn = lax.div(place, turns), lax.rem(place, turns)

        @pl.when(turn == 0)
        def _():
            pair_copy(image).wait()

        for index in range(FRONT_PAIRS):
            attend(image, turn * FRONT_PAIRS + index, index)

    @pl.when(step == pl.num_programs(0) - 1)
    def _():
        for copy in target_copies:
            copy.wait()
        target_copy.wait()


def merge_turned(stacked):
    rows = stacked.shape[1] // 2
    down = lax.broadcasted_iota(jnp.int32, (PAIR, rows), 0)
    return jnp.where(down < HEAD_DIM, stacked[:, :rows], stacked[:, rows:]).T


def front(counts, rows_in, targets_in, orders_in, lines, weight, pixel, expand, output):
    near, quarter, width = rows_in.shape[1:]
    rows, heads = 2 * quarter, width // PAIR
    parts = expand.shape[1] // width

    def image(step):
        return jnp.clip(step - FRONT_FAR, 0, near - 1)

    turns = heads // FRONT_PAIRS

    def spot(step):
        place = jnp.maximum(step - FRONT_ATTEND, 0)
        return lax.div(place, turns), lax.rem(place, turns)

    block = pl.BlockSpec((1, rows, width), lambda s: (image(s), 0, 0))
    return pl.pallas_call(
        partial(front_kernel, parts),
        grid=(FRONT_ATTEND + near * turns,),
        in_specs=[
            pl.BlockSpec(memory_space=pltpu.SMEM),
            pl.BlockSpec(memory_space=pl.ANY),
            pl.BlockSpec(memory_space=pl.ANY),
            fixed(orders_in.shape),
            fixed(lines.shape),
        ]
        + [pl.BlockSpec(memory_space=pl.ANY)] * 4,
        out_specs=[
            block,
            block,
            pl.BlockSpec((1, heads, 3, rows, PAIR), lambda s: (image(s), 0, 0, 0, 0)),
            pl.BlockSpec((1, FRONT_PAIRS, 2, rows, PAIR), lambda s: spot(s) + (0, 0, 0)),
            pl.BlockSpec((1, rows, FRONT_PAIRS * PAIR), lambda s: (spot(s)[0], 0, spot(s)[1])),
            pl.BlockSpec((1, FRONT_PAIRS, 2 * rows, 2 * rows), lambda s: spot(s) + (0, 0)),
            pl.BlockSpec((1, rows, 1), lambda s: (image(s), 0, 0)),
            pl.BlockSpec(memory_space=pl.ANY),
            pl.BlockSpec((1, width, width), lambda s: (jnp.minimum(s, parts + 1), 0, 0)),
        ],
        out_shape=[
            jax.ShapeDtypeStruct((near, rows, width), BF16),
            jax.ShapeDtypeStruct((near, rows, width), BF16),
            jax.ShapeDtypeStruct((near, heads, 3, rows, PAIR), BF16),
            jax.ShapeDtypeStruct((near, heads, 2, rows, PAIR), BF16),
            jax.ShapeDtypeStruct((near, rows, width), BF16),
            jax.ShapeDtypeStruct((near, heads, 2 * rows, 2 * rows), BF16),
            jax.ShapeDtypeStruct((near, rows, 1), F32),
            jax.ShapeDtypeStruct((near, rows, width), BF16),
            jax.ShapeDtypeStruct((parts + 2, width, width), BF16),
        ],
        scratch_shapes=[
            pltpu.VMEM((near, rows, width), BF16),
            pltpu.VMEM((near, rows, width), BF16),
            pltpu.VMEM((near, rows, 1), F32),
            pltpu.VMEM(orders_in.shape[1:], jnp.int32),
            pltpu.VMEM((near, heads, 3, rows, PAIR), BF16),
            pltpu.VMEM((near, heads, 2, rows, PAIR), BF16),
            pltpu.VMEM(weight.shape, BF16),
            pltpu.VMEM(pixel.shape, BF16),
            pltpu.VMEM(expand.shape, BF16),
            pltpu.VMEM(output.shape, BF16),
            pltpu.SemaphoreType.DMA((6,)),
            pltpu.SemaphoreType.DMA((1 + 2 * near,)),
            pltpu.SemaphoreType.DMA((1 + 2 * near,)),
            pltpu.SemaphoreType.DMA((near,)),
            pltpu.SemaphoreType.DMA((near,)),
        ],
        compiler_params=pltpu.CompilerParams(
            vmem_limit_bytes=60 * MIB, collective_id=1, has_side_effects=True
        ),
        cost_estimate=cost(5e9, 40e6),
        name="front",
    )(counts, rows_in, targets_in, orders_in, lines, weight, pixel, expand, output)


def middle_kernel(
    embedded_in, mixed, mask_in, target_in, weights, reduce, lines,
    lefts, rights, input_out, scaling_out, sums_out, low, total, biases,
):
    parts = reduce.shape[1]
    span = reduce.shape[2]
    width = weights.shape[1]
    mask = mask_in[0]

    @pl.when(pl.program_id(0) == 0)
    def _():
        sums_out[...] = jnp.zeros_like(sums_out)
        for part in range(parts):
            pieces = []
            for place in range(8):
                row, start = divmod((place * parts + part) * span, width)
                pieces.append(lines[EXPAND + row : EXPAND + row + 1, start : start + span])
            biases[part] = jnp.concatenate(pieces, axis=1)

    after_attn = embedded_in[0].astype(F32) + dot(mixed[0], weights[parts + 1]) + lines[OUTPUT : OUTPUT + 1]
    lefts[0, parts + 1] = mixed[0]
    normed, scaling = normalize(after_attn)
    rights[0, parts + 1] = normed.astype(BF16)
    scaling_out[0] = scaling
    low[...] = (normed * lines[GAIN_TWO : GAIN_TWO + 1] + lines[SHIFT_TWO : SHIFT_TWO + 1]).astype(BF16)
    input_out[0] = low[...]
    total[...] = after_attn + lines[REDUCE : REDUCE + 1]

    def one(part, carry):
        active, rate = gelu_both(dot(low[...], weights[1 + part]) + biases[part])
        active = active.astype(BF16)
        lefts[0, 1 + part] = active
        rights[0, 1 + part] = rate.astype(BF16)
        total[...] += dot(active, reduce[:, part].reshape(width, width))
        return carry

    for part in range(parts):
        one(part, 0)
    after_low = total[...].astype(BF16)
    lefts[0, 0] = after_low
    errors = dot(after_low, weights[0]) + lines[PIXEL : PIXEL + 1] - target_in[0].astype(F32)
    square = errors * errors + 1.0
    root = lax.rsqrt(square)
    grad_pred = (mask * errors * root).astype(BF16)
    rights[0, 0] = grad_pred
    sums_out[0:1] += column_sums(grad_pred)
    sums_out[5:6] += jnp.sum((square * root - 1.0) * mask, axis=0, keepdims=True)
    sums_out[10:11] += jnp.sum(jnp.broadcast_to(mask, errors.shape), axis=0, keepdims=True)


def middle(embedded, mixed, mask, targets, weights, reduce, lines):
    near, rows, width = embedded.shape
    parts = reduce.shape[1]
    block = pl.BlockSpec((1, rows, width), lambda i: (i, 0, 0))
    column = pl.BlockSpec((1, rows, 1), lambda i: (i, 0, 0))
    stack = pl.BlockSpec((1, parts + 2, rows, width), lambda i: (i, 0, 0, 0))
    return pl.pallas_call(
        middle_kernel,
        grid=(near,),
        in_specs=[
            block,
            block,
            column,
            block,
            fixed((parts + 2, width, width)),
            fixed(reduce.shape),
            fixed(lines.shape),
        ],
        out_specs=[stack, stack, block, column, fixed_out((16, width))],
        out_shape=[
            jax.ShapeDtypeStruct((near, parts + 2, rows, width), BF16),
            jax.ShapeDtypeStruct((near, parts + 2, rows, width), BF16),
            jax.ShapeDtypeStruct((near, rows, width), BF16),
            jax.ShapeDtypeStruct((near, rows, 1), F32),
            jax.ShapeDtypeStruct((16, width), F32),
        ],
        scratch_shapes=[
            pltpu.VMEM((rows, width), BF16),
            pltpu.VMEM((rows, width), F32),
            pltpu.VMEM((parts, 1, width), F32),
        ],
        compiler_params=params(60),
        cost_estimate=cost(2 * near * rows * width * width * (2 * parts + 2), 40e6),
        name="middle",
    )(embedded, mixed, mask, targets, weights, reduce, lines)


HIGH_ROWS = 4 * 96


def spread_half(result, target, high, start, names, swapped):
    for low in range(2):
        for x in range(2):
            for y in range(2):
                at = (low * 2 + x) * 96 + start
                piece = result[at : at + HALF, y * 384 : (y + 1) * 384]
                spot = {"high": high, "low": low, "x": x, "y": y}
                if swapped is not None:
                    first, second = swapped
                    spot[first], spot[second] = spot[second], spot[first]
                target[tuple(spot[name] for name in names)] = piece.astype(BF16)


HALF = 48
SLOTS = 4
KEPT = 10
FIRST_ATTEND = 11
GROUP_STEPS = (15, 19, 22)
FIRST_NORM = 23


def back_kernel(
    counts, left, right, weights, reduce, query, key, value, input_two, scaling_two, input_one, joint, pairs, probs_in, lines, sums_in,
    embedded_in, mask_in, *rest,
):
    (
        done_out,
        near_out,
        far_out,
        sums_out,
        late_out,
        done,
        done_sent,
        branch,
        wide,
        grad_in,
        upstream,
        own_pairs,
        give_pairs,
        got_pairs,
        far_give,
        sums,
        late,
        keep,
        give,
        got,
        send,
        receive,
        core_send,
        core_receive,
        pair_send,
        pair_receive,
        far_send,
        far_receive,
    ) = rest[:28]
    buffers = split_list(rest[28:], counts)
    where = places()
    core, sibling = where["core"]
    step = pl.program_id(0)
    images, rows, width = input_two.shape
    every = images * rows
    quarter = rows // 2
    heads = width // PAIR
    first_gain, second_gain = lines[GAIN_ONE : GAIN_ONE + 1], lines[GAIN_TWO : GAIN_TWO + 1]
    chains = [
        Chain(where, keep.at[unit % KEPT], names_of(order), order, list(buffers[unit]) + [done.at[unit]], send, receive, MOST * unit, TILE_SWAPS[unit])
        for unit, order in enumerate(TILE_ORDERS)
    ]
    chains.append(Chain(where, sums, (), SUMS_ORDER, buffers[TILES], send, receive, MOST * TILES))
    chains.append(Chain(where, late, (), SUMS_ORDER, buffers[TILES + 1], send, receive, MOST * TILES + MOST))

    def core_copy(unit):
        slot = lax.rem(unit, SLOTS)
        return remote(give.at[slot], got.at[slot], core_send.at[unit], core_receive.at[unit], sibling)

    def pair_copy(place, second):
        image = lax.rem(place, 3)
        slot = lax.rem((lax.div(place, 6) * 3 + image) * 2 + second, SLOTS)
        return remote(
            give_pairs.at[slot], got_pairs.at[place], pair_send.at[place], pair_receive.at[place], sibling
        )

    def far_copy(image):
        return remote(
            far_give.at[image], far_out.at[image], far_send.at[image], far_receive.at[image], where["y"][1]
        )

    def core_sum(unit):
        core_copy(unit).wait()
        for_each(4, lambda spot: add_up(keep.at[unit % KEPT], spot, got[(unit % SLOTS,) + spot]))

    def done_copy(unit):
        return pltpu.make_async_copy(done.at[unit], done_out.at[unit], done_sent.at[unit])

    def turn(unit, stage):
        if unit < TILES and stage == 0:
            core_sum(unit)
        chains[unit].turn(stage)
        if stage == len(chains[unit].order) and unit < TILES:
            done_copy(unit).start()

    def tile(unit, lines_of, value, forms):
        def one(high):
            columns = slice(high * HIGH_ROWS, (high + 1) * HIGH_ROWS)
            result = dot_tn(lines_of(columns).reshape(every, HIGH_ROWS), value)
            for half in range(2):
                for names, swapped, chosen in forms:
                    swapped = swapped if half == 1 else None

                    @pl.when(jnp.logical_and(core == half, chosen))
                    def _(half=half, names=names, swapped=swapped):
                        spread_half(result, keep.at[lax.rem(unit, KEPT)], high, half * HALF, names, swapped)

                    @pl.when(jnp.logical_and(core != half, chosen))
                    def _(half=half, names=names, swapped=swapped):
                        spread_half(result, give.at[lax.rem(unit, SLOTS)], high, half * HALF, names, swapped)

        for high in range(2):
            one(high)
        core_copy(unit).start()

    def forms_of(units, unit):
        forms = {}
        for other in units:
            form = (names_of(TILE_ORDERS[other]), TILE_SWAPS[other])
            forms.setdefault(form, []).append(unit == other)
        if len(forms) == 1:
            return [form + (True,) for form in forms]
        return [form + (functools.reduce(jnp.logical_or, asked),) for form, asked in forms.items()]

    def flat(ref):
        return ref[...].reshape(every, ref.shape[-1])

    def left_lines(columns):
        return left[:, 0, :, columns]

    @pl.when(step == 0)
    def _():
        greet(where)
        sums[...] = sums_in[...]
        late[...] = jnp.zeros_like(late)
        grad_in[...] = jnp.zeros_like(grad_in)

    for at, turns in TURNS.items():

        @pl.when(step == at)
        def _(turns=turns):
            for unit, stage in turns:
                turn(unit, stage)

    @pl.when(step == 0)
    def _():
        tile(0, left_lines, right[:, 0].reshape(every, width), forms_of((0,), 0))

        def one(image):
            low = dot_nt(right[image, 0], weights[0]).astype(BF16)
            branch[image] = low
            sums[1:2] += column_sums(low)
        for image in range(images):
            one(image)

    @pl.when((step > 0) & (step < 9) & (lax.rem(step, 2) == 1))
    def _():
        tile(step, left_lines, flat(branch), forms_of((1, 3, 5, 7), step))
        row = pl.ds(6 + lax.div(step, 2), 1)

        def one(image):
            low = dot_nt(branch[image], reduce[:, 0].reshape(width, width)) * right[image, 0].astype(F32)
            low = low.astype(BF16)
            wide[image] = low
            sums[row] += column_sums(low)
        for image in range(images):
            one(image)

    @pl.when((step > 0) & (step < 9) & (lax.rem(step, 2) == 0))
    def _():
        tile(step, lambda columns: input_two[:, :, columns], flat(wide), forms_of((2, 4, 6, 8), step))
        fresh = jnp.where(step == 2, 0.0, 1.0)

        def one(image):
            grad_in[image] = grad_in[image] * fresh + dot_nt(wide[image], weights[0])
        for image in range(images):
            one(image)

    @pl.when(step == 9)
    def _():
        def one(image):
            normed = right[image, 0].astype(F32)
            grad = grad_in[image]
            low = branch[image].astype(F32) + normalize_back(grad, normed, scaling_two[image], second_gain)
            low = low.astype(BF16)
            branch[image] = low
            sums[2:3] += column_sums(grad * normed)
            sums[3:4] += column_sums(grad)
            sums[4:5] += column_sums(low)
            mixed = dot_nt(low, weights[0]).astype(BF16)
            for pair in range(heads):
                upstream[image, pair] = mixed[:, pair * PAIR : (pair + 1) * PAIR]
        for image in range(images):
            one(image)

    @pl.when(step == 10)
    def _():
        tile(9, left_lines, flat(branch), forms_of((9,), 9))

    def attend_back(group, image, second, inside, order):
        place = group * 6 + inside

        @pl.when(order >= SLOTS)
        def _():
            before = order - SLOTS
            pair_copy(lax.div(before, 6) * 6 + second * 3 + lax.rem(lax.div(before, 2), 3), second).wait_send()

        scale = HEAD_DIM**-0.5
        target = own_pairs.at[lax.rem(group, 2), inside]
        away = give_pairs.at[lax.rem(order, SLOTS)]
        queries = side_by_side(joint[0, second, 0])
        keys_in = jnp.concatenate([joint[0, second, 1], pairs[0, second, 0]], axis=0)
        values_in = jnp.concatenate([joint[0, second, 2], pairs[0, second, 1]], axis=0)
        grad_mixed = side_by_side(upstream[image, group * 2 + second])
        probs = probs_in[0, second]
        grad_probs = dot_nt(values_in, grad_mixed)
        broad = probs.astype(F32)
        weighted = broad * grad_probs
        inner = jnp.sum(weighted, axis=0, keepdims=True)
        grad_scores = (weighted - broad * inner).astype(BF16)
        grad_values = dot(probs, grad_mixed).astype(BF16)
        grad_keys = (dot(grad_scores, queries) * scale).astype(BF16)
        target[0] = (merge_turned(dot_tn(keys_in, grad_scores)) * scale).astype(BF16)
        target[1] = grad_keys[:rows]
        target[2] = grad_values[:rows]
        away[0] = grad_keys[rows:]
        away[1] = grad_values[rows:]
        pair_copy(place, second).start()

    attends = (step >= FIRST_ATTEND) & (step < GROUP_STEPS[2]) & (step != GROUP_STEPS[0]) & (step != GROUP_STEPS[1])

    @pl.when(attends)
    def _():
        group, image = attend_place(step)
        for second in range(2):
            inside = second * 3 + image
            attend_back(group, image, second, inside, (group * 3 + image) * 2 + second)

    @pl.when((step == GROUP_STEPS[0]) | (step == GROUP_STEPS[1]) | (step == GROUP_STEPS[2]))
    def _():
        group = jnp.where(step == GROUP_STEPS[0], 0, jnp.where(step == GROUP_STEPS[1], 1, 2))
        slot = lax.rem(group, 2)
        for inside in range(6):
            pair_copy(group * 6 + inside, inside // 3).wait_recv()
            image, second = inside % 3, inside // 3
            for part in range(3):
                piece = own_pairs[slot, inside, part]
                if part > 0:
                    piece = piece.astype(F32) + got_pairs[group * 6 + inside, part - 1].astype(F32)
                start = part * 2 * PAIR + second * PAIR
                wide[image, :, start : start + PAIR] = piece.astype(BF16)
        tile(10 + group, lambda columns: input_one[:, :, columns], flat(wide), forms_of((10, 11, 12), 10 + group))
        columns = jnp.concatenate([query[...], key[...], value[...]], axis=1)
        fresh = jnp.where(group == 0, 0.0, 1.0)
        row = pl.ds(5 + group, 1)

        def one(image):
            late[row] += column_sums(wide[image])
            grad_in[image] = grad_in[image] * fresh + dot_nt(wide[image], columns)
        for image in range(images):
            one(image)

    @pl.when(step >= FIRST_NORM)
    def _():
        image = step - FIRST_NORM
        mask = mask_in[0]
        normed, scaling = normalize(embedded_in[0].astype(F32))
        grad = grad_in[image]
        total = branch[image].astype(F32) + normalize_back(grad, normed, scaling, first_gain)
        kept = total * (1.0 - mask)
        near_out[0] = kept[:quarter]
        far_give[image] = kept[quarter:].astype(BF16)
        far_copy(image).start()
        late[0:1] += column_sums(grad * normed)
        late[1:2] += column_sums(grad)
        late[2:3] += column_sums(total * mask)

    @pl.when(step == pl.num_programs(0) - 1)
    def _():
        for unit, stage in LAST_TURNS:
            turn(unit, stage)
        for image in range(images):
            far_copy(image).wait()
        for unit in range(TILES):
            done_copy(unit).wait()
        for image in range(1, 3):
            for second in range(2):
                pair_copy(12 + second * 3 + image, second).wait_send()
        sums_out[...] = chains[TILES].refs[-1][...]
        late_out[...] = chains[TILES + 1].refs[-1][...]


def attend_place(step):
    place = step - FIRST_ATTEND
    for at in GROUP_STEPS[:2]:
        place = place - jnp.where(step > at, 1, 0)
    place = jnp.clip(place, 0, 8)
    return lax.div(place, 3), lax.rem(place, 3)


def back(
    lefts, rights, weights, reduce, joint_weight, input_two, scaling_two, input_one, joint, pairs, probs, lines, sums, embedded, mask
):
    near, slots, rows, width = lefts.shape
    quarter = rows // 2
    heads = width // PAIR

    def slot(step):
        return jnp.minimum(lax.div(step + 1, 2), slots - 1)

    def part(step):
        return jnp.clip(lax.div(step - 1, 2), 0, slots - 3)

    def group(step):
        return jnp.where(step > GROUP_STEPS[0], 1, 0) + jnp.where(step > GROUP_STEPS[1], 1, 0)

    def columns(which):
        return pl.BlockSpec((width, 2 * PAIR), lambda s: (0, which * 3 + group(s)))

    def spot(step):
        group, image = attend_place(step)
        return image, group

    def image(step):
        return jnp.maximum(step - FIRST_NORM, 0)

    cases = [(names_of(order), order, (HALF, 384), BF16) for order in TILE_ORDERS]
    cases.append(((), SUMS_ORDER, sums.shape, F32))
    cases.append(((), SUMS_ORDER, (8, width), F32))
    buffers, counts = chain_scratch(cases)
    kept, start = [], 0
    for index, count in enumerate(counts):
        kept += buffers[start : start + count - (index < TILES)]
        start += count
    buffers, counts = kept, [count - (index < TILES) for index, count in enumerate(counts)]
    whole = (2, 2, 2, 2, HALF, 384)
    stack = pl.BlockSpec((near, 1, rows, width), lambda s: (0, slot(s), 0, 0))
    return pl.pallas_call(
        partial(back_kernel, counts),
        grid=(FIRST_NORM + near,),
        in_specs=[
            stack,
            stack,
            pl.BlockSpec((1, width, width), lambda s: (slot(s), 0, 0)),
            pl.BlockSpec((8, 1, reduce.shape[2], width), lambda s: (0, part(s), 0, 0)),
            columns(0),
            columns(1),
            columns(2),
            fixed((near, rows, width)),
            fixed((near, rows, 1)),
            fixed((near, rows, width)),
            pl.BlockSpec((1, 2, 3, rows, PAIR), lambda s: spot(s) + (0, 0, 0)),
            pl.BlockSpec((1, 2, 2, rows, PAIR), lambda s: spot(s) + (0, 0, 0)),
            pl.BlockSpec((1, 2, 2 * rows, 2 * rows), lambda s: spot(s) + (0, 0)),
            fixed(lines.shape),
            fixed(sums.shape),
            pl.BlockSpec((1, rows, width), lambda s: (image(s), 0, 0)),
            pl.BlockSpec((1, rows, 1), lambda s: (image(s), 0, 0)),
        ],
        out_specs=[
            pl.BlockSpec(memory_space=pl.ANY),
            pl.BlockSpec((1, quarter, width), lambda s: (image(s), 0, 0)),
            pl.BlockSpec(memory_space=pl.ANY),
            fixed_out(sums.shape),
            fixed_out((8, width)),
        ],
        out_shape=[
            jax.ShapeDtypeStruct((TILES, 2, 2, HALF, 384), BF16),
            jax.ShapeDtypeStruct((near, quarter, width), F32),
            jax.ShapeDtypeStruct((near, quarter, width), BF16),
            jax.ShapeDtypeStruct(sums.shape, F32),
            jax.ShapeDtypeStruct((8, width), F32),
        ],
        scratch_shapes=[
            pltpu.VMEM((TILES, 2, 2, HALF, 384), BF16),
            pltpu.SemaphoreType.DMA((TILES,)),
            pltpu.VMEM((near, rows, width), BF16),
            pltpu.VMEM((near, rows, width), BF16),
            pltpu.VMEM((near, rows, width), F32),
            pltpu.VMEM((near, heads, rows, PAIR), BF16),
            pltpu.VMEM((2, 6, 3, rows, PAIR), BF16),
            pltpu.VMEM((SLOTS, 2, rows, PAIR), BF16),
            pltpu.VMEM((near * heads, 2, rows, PAIR), BF16),
            pltpu.VMEM((near, quarter, width), BF16),
            pltpu.VMEM(sums.shape, F32),
            pltpu.VMEM((8, width), F32),
            pltpu.VMEM((KEPT,) + whole, BF16),
            pltpu.VMEM((SLOTS,) + whole, BF16),
            pltpu.VMEM((SLOTS,) + whole, BF16),
            pltpu.SemaphoreType.DMA((MOST * (TILES + 2),)),
            pltpu.SemaphoreType.DMA((MOST * (TILES + 2),)),
            pltpu.SemaphoreType.DMA((TILES,)),
            pltpu.SemaphoreType.DMA((TILES,)),
            pltpu.SemaphoreType.DMA((near * heads,)),
            pltpu.SemaphoreType.DMA((near * heads,)),
            pltpu.SemaphoreType.DMA((near,)),
            pltpu.SemaphoreType.DMA((near,)),
        ]
        + buffers,
        compiler_params=pltpu.CompilerParams(
            vmem_limit_bytes=60 * MIB, collective_id=2, has_side_effects=True
        ),
        cost_estimate=cost(40e9, 60e6),
        name="back",
    )(
        lefts, rights, weights, reduce, joint_weight, joint_weight, joint_weight, input_two,
        scaling_two, input_one, joint, pairs, probs, lines, sums, embedded, mask,
    )


def emit_kernel(parts, done, near_in, far_in, sums, late, *outs):
    (
        loss, attend_gain, attend_shift, joint, query_bias, value_bias, output, output_bias, feed_gain,
        feed_shift, expand, expand_bias, reduce, reduce_bias, pixel, pixel_bias, token, patch,
    ) = outs
    data, y = lax.axis_index("dp"), lax.div(lax.axis_index("seq"), 2)
    inverse = 1.0 / (sums[10:11] * PIXELS)
    loss[0] = jnp.sum(sums[5:6] * inverse)
    wide_inverse = inverse[:, :384]

    def piece(unit, core, half):
        return done[unit, core, half].astype(F32) * wide_inverse

    def square(unit):
        return [
            jnp.concatenate([piece(unit, core, half) for half in range(2)], axis=1) for core in range(2)
        ]

    for unit, target in ((0, pixel), (2 * parts + 1, output)):
        for core, lines in enumerate(square(unit)):
            target[core * HALF : (core + 1) * HALF] = lines
    expands = []
    for part in range(parts):
        for core, lines in enumerate(square(1 + 2 * part)):
            start = part * 2 * HALF + core * HALF
            reduce[start : start + HALF] = lines
        expands.append(square(2 + 2 * part))
    span = 2 * HALF
    for core in range(2):
        for d in range(8):
            lines = [expands[part][core][:, d * span : (d + 1) * span] for part in range(parts)]
            expand[core * HALF : (core + 1) * HALF, d * 4 * span : (d + 1) * 4 * span] = jnp.concatenate(
                lines, axis=1
            )
    for group in range(3):
        for core, lines in enumerate(square(2 * parts + 2 + group)):
            for part in range(3):
                start = part * WIDE + group * 2 * PAIR
                joint[core * HALF : (core + 1) * HALF, start : start + 2 * PAIR] = lines[
                    :, part * 2 * PAIR : (part + 1) * 2 * PAIR
                ]

    def own_cut(lines):
        shift = lax.rem(WIDE - data * span, WIDE)
        return pltpu.roll(lines, shift, axis=1)[:, :span]

    early = own_cut(sums[...] * inverse)
    later = own_cut(late[...] * inverse)
    queries = jnp.concatenate([late[5 + group : 6 + group, : 2 * PAIR] for group in range(3)], axis=1)
    values = jnp.concatenate([late[5 + group : 6 + group, 4 * PAIR :] for group in range(3)], axis=1)
    both = jnp.concatenate([queries, values] + [jnp.zeros((6, WIDE), F32)], axis=0)
    both = own_cut(both * inverse)
    for target, lines, row in (
        (attend_gain, later, 0),
        (attend_shift, later, 1),
        (query_bias, both, 0),
        (value_bias, both, 1),
        (output_bias, early, 4),
        (feed_gain, early, 2),
        (feed_shift, early, 3),
        (reduce_bias, early, 1),
        (pixel_bias, early, 0),
        (token, later, 2),
    ):
        target[...] = lines[row : row + 1]
    expand_bias[...] = jnp.concatenate([early[6 + part : 7 + part] for part in range(parts)], axis=1)
    images = near_in.shape[0]
    for image in range(images):
        patch[y * images + image] = near_in[image] * inverse
        patch[(1 - y) * images + image] = far_in[image].astype(F32) * inverse


def emit(parts, done, near_in, far_in, sums, late):
    images, quarter, width = near_in.shape
    hidden = parts * width

    def out(*shape):
        return jax.ShapeDtypeStruct(shape, F32)

    small = out(1, 96)
    outs = [
        out(1), small, small, out(96, 3 * width), small, small, out(96, width), small, small,
        small, out(96, hidden), out(1, hidden // 8), out(hidden // 8, width), small, out(96, width), small, small,
        out(2 * images, quarter, width),
    ]
    whole = pl.BlockSpec(memory_space=pltpu.VMEM)
    return pl.pallas_call(
        partial(emit_kernel, parts),
        in_specs=[whole] * 5,
        out_specs=[pl.BlockSpec(memory_space=pltpu.SMEM)] + [whole] * (len(outs) - 1),
        out_shape=outs,
        compiler_params=params(60),
        cost_estimate=cost(1e6, 12e6),
        name="emit",
    )(done, near_in, far_in, sums, late)


def eight_places(
    patches,
    targets,
    mask_order,
    mask_count,
    attend_gain,
    attend_shift,
    joint_weight,
    query_bias,
    value_bias,
    output_weight,
    output_bias,
    feed_gain,
    feed_shift,
    expand_weight,
    expand_bias,
    reduce_weight,
    reduce_bias,
    pixel_weight,
    pixel_bias,
    mask_token,
):
    images, quarter, features = patches.shape
    near = images // 2
    place_y = own_bit("seq", 2)
    hidden = expand_bias.shape[0]
    parts = hidden // features

    def halves(values):
        return values.reshape((2, near) + values.shape[1:])

    lines = stack_lines(
        attend_gain,
        attend_shift,
        query_bias,
        value_bias,
        output_bias,
        feed_gain,
        feed_shift,
        reduce_bias,
        pixel_bias,
        mask_token,
        expand_bias,
    )
    orders = jnp.pad(mask_order[:, None, :], ((0, 0), (0, 7), (0, 256 - quarter)))
    reduce_parts = reduce_weight.reshape(8, parts, hidden // (8 * parts), features)
    embedded, input_one, joint, pairs, mixed, probs, mask, targets_here, weights = front(
        mask_count,
        halves(patches),
        halves(targets),
        halves(orders),
        lines,
        joint_weight,
        pixel_weight,
        expand_weight,
        output_weight,
    )
    lefts, rights, input_two, scaling_two, sums = middle(
        embedded, mixed, mask, targets_here, weights, reduce_parts, lines
    )
    done, patch_near, patch_far, sums, late = back(
        lefts,
        rights,
        weights,
        reduce_parts,
        joint_weight,
        input_two,
        scaling_two,
        input_one,
        joint,
        pairs,
        probs,
        lines,
        sums,
        embedded,
        mask,
    )
    outs = emit(parts, done, patch_near, patch_far, sums, late)
    flat = {0: (), 1: (-1,), 2: (-1,), 4: (-1,), 5: (-1,), 7: (-1,), 8: (-1,), 9: (-1,), 11: (-1,)}
    flat.update({13: (-1,), 15: (-1,), 16: (-1,)})
    return tuple(
        out.reshape(flat[index]) if index in flat else out for index, out in enumerate(outs)
    )


def on_device(*arguments):
    if lax.axis_size("dp") == 8 and lax.axis_size("seq") == 4:
        return eight_places(*arguments)
    return any_places(*arguments)


def solution(mesh):
    placed = (
        P("dp", "seq", None),
        P("dp", "seq", None),
        P("dp", "seq"),
        P("dp"),
        P(),
        P(),
        P(),
        P(),
        P(),
        P(),
        P(),
        P(),
        P(),
        P(),
        P(),
        P(),
        P(),
        P(),
        P(),
        P(),
    )
    return jax.shard_map(
        on_device,
        mesh=mesh,
        in_specs=placed,
        out_specs=(
            P(),
            P("dp"),
            P("dp"),
            P("dp", None),
            P("dp"),
            P("dp"),
            P("dp", None),
            P("dp"),
            P("dp"),
            P("dp"),
            P("dp", None),
            P("dp"),
            P("dp", None),
            P("dp"),
            P("dp", None),
            P("dp"),
            P("dp"),
            P("dp", "seq", None),
        ),
        check_vma=False,
    )
```

```python
import functools
import itertools
from functools import partial

import jax
import jax.numpy as jnp
from jax import lax
from jax.experimental import pallas as pl
from jax.experimental.pallas import tpu as pltpu
from jax.sharding import PartitionSpec as P

HEADS = 12
HEAD_DIM = 64
PIXELS = 768
WIDE = 768
PAIR = 2 * HEAD_DIM
MIB = 1 << 20
F32 = jnp.float32
BF16 = jnp.bfloat16


def dot(left, right):
    return jnp.dot(left, right, preferred_element_type=F32)


def dot_nt(left, right):
    return lax.dot_general(left, right, (((1,), (1,)), ((), ())), preferred_element_type=F32)


def dot_tn(left, right):
    return lax.dot_general(left, right, (((0,), (0,)), ((), ())), preferred_element_type=F32)


def normalize(inputs):
    centre = inputs - jnp.mean(inputs, axis=-1, keepdims=True)
    scaling = lax.rsqrt(jnp.mean(centre * centre, axis=-1, keepdims=True) + 1e-06)
    return (centre * scaling, scaling)


def normalize_back(upstream, normed, scaling, gain):
    scaled = upstream * gain
    return scaling * (
        scaled
        - jnp.mean(scaled, axis=-1, keepdims=True)
        - normed * jnp.mean(scaled * normed, axis=-1, keepdims=True)
    )


def column_sums(values):
    return jnp.sum(values.astype(F32), axis=0, keepdims=True)


def gelu_both(inputs):
    bell = jnp.exp(inputs * inputs * -0.5)
    base_of = 1.0 + (0.3275911 * 0.7071067811865476) * jnp.abs(inputs)
    inner = pl.reciprocal(base_of, approx=True)
    inner = inner * (2.0 - base_of * inner)
    series = inner * (
        0.254829592
        + inner * (-0.284496736 + inner * (1.421413741 + inner * (-1.453152027 + inner * 1.061405429)))
    )
    tail = 0.5 * series * bell
    below = jnp.where(inputs < 0.0, tail, 1.0 - tail)
    return (inputs * below, below + inputs * bell * 0.3989422804014327)


def params(limit):
    return pltpu.CompilerParams(vmem_limit_bytes=limit * MIB)


def fixed(shape):
    zeros = (0,) * len(shape)
    return pl.BlockSpec(shape, lambda *place: zeros, pipeline_mode=pl.Buffered(1))


def cost(flops, moved):
    return pl.CostEstimate(flops=int(flops), bytes_accessed=int(moved), transcendentals=0)


def project_kernel(own, far, gain, shift, weight, bias, embedded_out, joint_out):
    embedded = jnp.concatenate([own[0], far[0]], axis=0)
    embedded_out[0] = embedded
    normed, _ = normalize(embedded.astype(F32))
    low = (normed * gain[...] + shift[...]).astype(BF16)
    for part in range(3):
        cut = slice(part * WIDE, (part + 1) * WIDE)
        joint_out[0, part] = (dot(low, weight[:, cut]) + bias[:, cut]).astype(BF16)


def project(own, far, gain, shift, weight, bias):
    near, quarter, width = own.shape
    rows = 2 * quarter
    return pl.pallas_call(
        project_kernel,
        grid=(near,),
        in_specs=[
            pl.BlockSpec((1, quarter, width), lambda i: (i, 0, 0)),
            pl.BlockSpec((1, quarter, width), lambda i: (i, 0, 0)),
            fixed((1, width)),
            fixed((1, width)),
            fixed((width, 3 * width)),
            fixed((1, 3 * width)),
        ],
        out_specs=[
            pl.BlockSpec((1, rows, width), lambda i: (i, 0, 0)),
            pl.BlockSpec((1, 3, rows, width), lambda i: (i, 0, 0, 0)),
        ],
        out_shape=[
            jax.ShapeDtypeStruct((near, rows, width), BF16),
            jax.ShapeDtypeStruct((near, 3, rows, width), BF16),
        ],
        compiler_params=params(32),
        cost_estimate=cost(2 * near * rows * width * 3 * width, 12e6),
        name="project",
    )(own, far, gain, shift, weight, bias)


def side_by_side(pair):
    lanes = lax.broadcasted_iota(jnp.int32, pair.shape, 1)
    zero = jnp.zeros_like(pair)
    first = jnp.where(lanes < HEAD_DIM, pair, zero)
    second = jnp.where(lanes < HEAD_DIM, zero, pair)
    return jnp.concatenate([first, second], axis=0)


def merge_heads(stacked):
    rows = stacked.shape[0] // 2
    lanes = lax.broadcasted_iota(jnp.int32, (rows, PAIR), 1)
    return jnp.where(lanes < HEAD_DIM, stacked[:rows], stacked[rows:])


def attend_kernel(own, far, mixed_out, probs_out):
    queries = side_by_side(own[0, 0] * jnp.asarray(HEAD_DIM**-0.5, BF16))
    keys_in = jnp.concatenate([own[0, 1], far[0, 0]], axis=0)
    values_in = jnp.concatenate([own[0, 2], far[0, 1]], axis=0)
    scores = dot_nt(queries, keys_in)
    exponent = jnp.exp(scores - jnp.max(scores, axis=-1, keepdims=True))
    total = jnp.sum(exponent, axis=-1, keepdims=True)
    probs = (exponent * (1.0 / total)).astype(BF16)
    probs_out[0, 0] = probs
    mixed_out[0] = merge_heads(dot(probs, values_in)).astype(BF16)


def attend(joint, pairs_far):
    near, _, rows, width = joint.shape
    keys_count = 2 * rows
    pairs = width // PAIR
    return pl.pallas_call(
        attend_kernel,
        grid=(near, pairs),
        in_specs=[
            pl.BlockSpec((1, 3, rows, PAIR), lambda i, h: (i, 0, 0, h)),
            pl.BlockSpec((1, 2, rows, PAIR), lambda i, h: (i, 0, 0, h)),
        ],
        out_specs=[
            pl.BlockSpec((1, rows, PAIR), lambda i, h: (i, 0, h)),
            pl.BlockSpec((1, 1, 2 * rows, keys_count), lambda i, h: (i, h, 0, 0)),
        ],
        out_shape=[
            jax.ShapeDtypeStruct((near, rows, width), BF16),
            jax.ShapeDtypeStruct((near, pairs, 2 * rows, keys_count), BF16),
        ],
        compiler_params=params(32),
        cost_estimate=cost(8 * near * rows * keys_count * width, 20e6),
        name="attend",
    )(joint, pairs_far)


def attend_back_kernel(own, far, probs_in, upstream, query_out, own_out, far_out):
    rows = own.shape[2]
    scale = HEAD_DIM**-0.5
    queries = side_by_side(own[0, 0])
    keys_in = jnp.concatenate([own[0, 1], far[0, 0]], axis=0)
    values_in = jnp.concatenate([own[0, 2], far[0, 1]], axis=0)
    grad_mixed = side_by_side(upstream[0])
    probs = probs_in[0, 0]
    grad_probs = dot_nt(grad_mixed, values_in)
    wide = probs.astype(F32)
    weighted = wide * grad_probs
    inner = jnp.sum(weighted, axis=-1, keepdims=True)
    grad_scores = (weighted - wide * inner).astype(BF16)
    query_out[0] = (merge_heads(dot(grad_scores, keys_in)) * scale).astype(BF16)
    grad_values = dot_tn(probs, grad_mixed).astype(BF16)
    grad_keys = (dot_tn(grad_scores, queries) * scale).astype(BF16)
    own_out[0, 0] = grad_keys[:rows]
    own_out[0, 1] = grad_values[:rows]
    far_out[0, 0] = grad_keys[rows:]
    far_out[0, 1] = grad_values[rows:]


def attend_back(joint, pairs_far, probs, upstream):
    near, _, rows, width = joint.shape
    keys_count = 2 * rows
    pairs = width // PAIR
    two = pl.BlockSpec((1, 2, rows, PAIR), lambda i, h: (i, 0, 0, h))
    one = pl.BlockSpec((1, rows, PAIR), lambda i, h: (i, 0, h))
    return pl.pallas_call(
        attend_back_kernel,
        grid=(near, pairs),
        in_specs=[
            pl.BlockSpec((1, 3, rows, PAIR), lambda i, h: (i, 0, 0, h)),
            two,
            pl.BlockSpec((1, 1, 2 * rows, keys_count), lambda i, h: (i, h, 0, 0)),
            one,
        ],
        out_specs=[one, two, two],
        out_shape=[
            jax.ShapeDtypeStruct((near, rows, width), BF16),
            jax.ShapeDtypeStruct((near, 2, rows, width), BF16),
            jax.ShapeDtypeStruct((near, 2, rows, width), BF16),
        ],
        compiler_params=params(32),
        cost_estimate=cost(16 * near * rows * keys_count * width, 25e6),
        name="attend_back",
    )(joint, pairs_far, probs, upstream)


def rows_kernel(
    hidden,
    inverse,
    embedded_in,
    mixed,
    mask_in,
    target_own,
    target_far,
    output_weight,
    expand_weight,
    reduce_weight,
    pixel_weight,
    biases,
    expand_bias,
    input_out,
    active_out,
    after_out,
    pred_out,
    branch_out,
    expand_out,
    low_out,
    attn_out,
    mixed_out,
    sums_out,
    slope,
):
    output_bias, gain, shift, reduce_bias, pixel_bias = (biases[row : row + 1] for row in range(5))
    mask = mask_in[0]
    after_attn = embedded_in[0].astype(F32) + dot(mixed[0], output_weight[...]) + output_bias
    normed, scaling = normalize(after_attn)
    low = (normed * gain + shift).astype(BF16)
    input_out[0] = low
    total = after_attn + reduce_bias
    for start in range(0, hidden, WIDE):
        cut = slice(start, start + WIDE)
        active, rate = gelu_both(dot(low, expand_weight[:, cut]) + expand_bias[:, cut])
        active = active.astype(BF16)
        active_out[0, :, cut] = active
        slope[:, cut] = rate.astype(slope.dtype)
        total += dot(active, reduce_weight[cut, :])
    after_low = total.astype(BF16)
    after_out[0] = after_low
    target = jnp.concatenate([target_own[0], target_far[0]], axis=0).astype(F32)
    errors = dot(after_low, pixel_weight[...]) + pixel_bias - target
    square = errors * errors + 1.0
    root = lax.rsqrt(square)
    channel = jnp.sum((square * root - 1.0) * mask, axis=0, keepdims=True)
    grad_pred = (mask * errors * root * inverse[0, 0]).astype(BF16)
    pred_out[0] = grad_pred
    grad_mlp = dot_nt(grad_pred, pixel_weight[...])
    branch = grad_mlp.astype(BF16)
    branch_out[0] = branch
    grad_in = jnp.zeros_like(grad_mlp)
    expand_sums = []
    for start in range(0, hidden, WIDE):
        cut = slice(start, start + WIDE)
        grad_expand = dot_nt(branch, reduce_weight[cut, :]) * slope[:, cut].astype(F32)
        grad_expand = grad_expand.astype(BF16)
        expand_out[0, :, cut] = grad_expand
        expand_sums.append(column_sums(grad_expand))
        grad_in += dot_nt(grad_expand, expand_weight[:, cut])
    grad_attn = grad_mlp + normalize_back(grad_in, normed, scaling, gain)
    attn_out[0] = grad_attn
    grad_low = grad_attn.astype(BF16)
    low_out[0] = grad_low
    mixed_out[0] = dot_nt(grad_low, output_weight[...]).astype(BF16)
    sums = [
        column_sums(grad_pred),
        column_sums(branch),
        column_sums(grad_in * normed),
        column_sums(grad_in),
        column_sums(grad_low),
        channel,
    ] + expand_sums

    @pl.when(pl.program_id(0) == 0)
    def _():
        sums_out[...] = jnp.zeros_like(sums_out)

    for row, line in enumerate(sums):
        sums_out[row : row + 1] += line


def rows_step(
    inverse,
    embedded,
    mixed,
    mask,
    target_own,
    target_far,
    output_weight,
    expand_weight,
    reduce_weight,
    pixel_weight,
    biases,
    expand_bias,
):
    near, rows, width = embedded.shape
    quarter = target_own.shape[1]
    hidden = expand_weight.shape[1]
    block = pl.BlockSpec((1, rows, width), lambda i: (i, 0, 0))
    half = pl.BlockSpec((1, quarter, width), lambda i: (i, 0, 0))
    long = pl.BlockSpec((1, rows, hidden), lambda i: (i, 0, 0))
    narrow = jax.ShapeDtypeStruct((near, rows, width), BF16)
    broad = jax.ShapeDtypeStruct((near, rows, hidden), BF16)
    return pl.pallas_call(
        partial(rows_kernel, hidden),
        grid=(near,),
        in_specs=[
            pl.BlockSpec(memory_space=pltpu.SMEM),
            block,
            block,
            pl.BlockSpec((1, rows, 1), lambda i: (i, 0, 0)),
            half,
            half,
            fixed((width, width)),
            fixed((width, hidden)),
            fixed((hidden, width)),
            fixed((width, width)),
            fixed((8, width)),
            fixed((1, hidden)),
        ],
        out_specs=[block, long, block, block, block, long, block, block, block, fixed_out((16, width))],
        out_shape=[
            narrow,
            broad,
            narrow,
            narrow,
            narrow,
            broad,
            narrow,
            jax.ShapeDtypeStruct((near, rows, width), F32),
            narrow,
            jax.ShapeDtypeStruct((16, width), F32),
        ],
        scratch_shapes=[pltpu.VMEM((rows, hidden), F32)],
        compiler_params=params(56),
        cost_estimate=cost(4 * near * rows * width * (2 * width + 2 * hidden), 40e6),
        name="rows_step",
    )(
        inverse,
        embedded,
        mixed,
        mask,
        target_own,
        target_far,
        output_weight,
        expand_weight,
        reduce_weight,
        pixel_weight,
        biases,
        expand_bias,
    )


def fixed_out(shape):
    zeros = (0,) * len(shape)
    return pl.BlockSpec(shape, lambda *place: zeros)


def outer_kernel(left_moves, left, right, out, turned):
    if left_moves:
        out[...] = dot_tn(left[...], right[...]).astype(out.dtype)
        return

    @pl.when(pl.program_id(0) == 0)
    def _():
        turned[...] = left[...].T

    out[...] = dot(turned[...], right[...]).astype(out.dtype)


def outer(left, right):
    rows, tall = left.shape
    broad = right.shape[1]
    left_moves = tall > broad
    if left_moves:
        grid, specs = tall // WIDE, [
            pl.BlockSpec((rows, WIDE), lambda i: (0, i)),
            fixed((rows, broad)),
        ]
        out_spec = pl.BlockSpec((WIDE, broad), lambda i: (i, 0))
    else:
        grid, specs = broad // WIDE, [
            fixed((rows, tall)),
            pl.BlockSpec((rows, WIDE), lambda i: (0, i)),
        ]
        out_spec = pl.BlockSpec((tall, WIDE), lambda i: (0, i))
    return pl.pallas_call(
        partial(outer_kernel, left_moves),
        grid=(grid,),
        in_specs=specs,
        out_specs=out_spec,
        out_shape=jax.ShapeDtypeStruct((tall, broad), BF16),
        scratch_shapes=[pltpu.VMEM((WIDE, rows), BF16)],
        compiler_params=params(32),
        cost_estimate=cost(2 * rows * tall * broad, 2 * (rows * (tall + broad) + tall * broad)),
        name="outer",
    )(left, right)


def project_back_kernel(
    query, own, received, embedded_in, attn, mask_in, gain, shift, weight,
    input_out, joint_out, near_out, far_out, sums_out,
):
    quarter = near_out.shape[1]
    mask = mask_in[0]
    embedded = embedded_in[0].astype(F32)
    normed, scaling = normalize(embedded)
    input_out[0] = (normed * gain[...] + shift[...]).astype(BF16)
    grad_query = query[0]
    grad_key = (own[0, 0].astype(F32) + received[0, 0].astype(F32)).astype(BF16)
    grad_value = (own[0, 1].astype(F32) + received[0, 1].astype(F32)).astype(BF16)
    grad_in = None
    for part, grad in enumerate((grad_query, grad_key, grad_value)):
        joint_out[part, 0] = grad
        term = dot_nt(grad, weight[:, part * WIDE : (part + 1) * WIDE])
        grad_in = term if grad_in is None else grad_in + term
    grad_embedded = attn[0] + normalize_back(grad_in, normed, scaling, gain[...])
    kept = grad_embedded * (1.0 - mask)
    near_out[0] = kept[:quarter]
    far_out[0] = kept[quarter:].astype(BF16)
    sums = [
        column_sums(grad_in * normed),
        column_sums(grad_in),
        column_sums(grad_query),
        column_sums(grad_value),
        column_sums(grad_embedded * mask),
    ]

    @pl.when(pl.program_id(0) == 0)
    def _():
        sums_out[...] = jnp.zeros_like(sums_out)

    for row, line in enumerate(sums):
        sums_out[row : row + 1] += line


def project_back(query, own, received, embedded, attn, mask, gain, shift, weight):
    near, rows, width = embedded.shape
    quarter = rows // 2
    block = pl.BlockSpec((1, rows, width), lambda i: (i, 0, 0))
    half = pl.BlockSpec((1, quarter, width), lambda i: (i, 0, 0))
    two = pl.BlockSpec((1, 2, rows, width), lambda i: (i, 0, 0, 0))
    return pl.pallas_call(
        project_back_kernel,
        grid=(near,),
        in_specs=[
            block,
            two,
            two,
            block,
            block,
            pl.BlockSpec((1, rows, 1), lambda i: (i, 0, 0)),
            fixed((1, width)),
            fixed((1, width)),
            fixed((width, 3 * width)),
        ],
        out_specs=[
            block,
            pl.BlockSpec((3, 1, rows, width), lambda i: (0, i, 0, 0)),
            half,
            half,
            fixed_out((8, width)),
        ],
        out_shape=[
            jax.ShapeDtypeStruct((near, rows, width), BF16),
            jax.ShapeDtypeStruct((3, near, rows, width), BF16),
            jax.ShapeDtypeStruct((near, quarter, width), F32),
            jax.ShapeDtypeStruct((near, quarter, width), BF16),
            jax.ShapeDtypeStruct((8, width), F32),
        ],
        compiler_params=params(40),
        cost_estimate=cost(2 * near * rows * width * 3 * width, 20e6),
        name="project_back",
    )(query, own, received, embedded, attn, mask, gain, shift, weight)


def swap(values, axis, bit):
    size = lax.axis_size(axis)
    return lax.ppermute(values, axis, [(place, place ^ bit) for place in range(size)])


def own_bit(axis, bit):
    return (lax.axis_index(axis) // bit) % 2


def pick(values, dim, which):
    return lax.dynamic_index_in_dim(values, which, dim, keepdims=False)


def add_in(kept, received):
    return (kept.astype(jnp.float32) + received.astype(jnp.float32)).astype(kept.dtype)


def halve(values, dim, axis, bit):
    mine = own_bit(axis, bit)
    received = swap(pick(values, dim, 1 - mine), axis, bit)
    return add_in(pick(values, dim, mine), received)


def join(values, dim, axis, bit):
    mine = own_bit(axis, bit)
    received = swap(values, axis, bit)
    first = jnp.where(mine == 0, values, received)
    second = jnp.where(mine == 0, received, values)
    return jnp.concatenate([first, second], axis=dim)


def reduce_rows(grad, order):
    dp = lax.axis_size("dp")
    rows, columns = grad.shape
    steps = dp.bit_length() - 1
    part = rows // dp
    if columns % 512 == 0:
        tail = (1, 2, part, 2, columns // 4, 2)
        parts = grad.reshape((2,) * steps + (part, 4, columns // 4))
        parts = jnp.moveaxis(parts, steps + 1, 0)
    else:
        parts = grad.reshape((2,) * steps + (4, part // 4, columns))
        parts = jnp.moveaxis(parts, steps, 0)
    parts = parts.reshape((2, 2) + parts.shape[1:])
    names = ["core", "y"] + [1 << bit for bit in reversed(range(steps))]
    for name in order(steps):
        dim = names.index(name)
        if name == "core":
            parts = halve(parts, dim, "seq", 1)
        elif name == "y":
            parts = halve(parts, dim, "seq", 2)
        else:
            parts = halve(parts, dim, "dp", name)
        names.pop(dim)
    parts = join(parts[None], 0, "seq", 2)
    parts = join(parts[None], 0, "seq", 1)
    parts = parts.reshape((4,) + parts.shape[2:]).astype(jnp.float32)
    if columns % 512 == 0:
        return jnp.moveaxis(parts, 0, 1).reshape(part, columns)
    return parts.reshape(part, columns)


def x_first(steps):
    return ["core"] + [1 << bit for bit in range(steps)] + ["y"]


def y_first(steps):
    return ["core", "y"] + [1 << bit for bit in range(steps)]


def z_first(steps):
    return ["core"] + [1 << bit for bit in range(1, steps)] + [1, "y"]


def reduce_vector(values):
    dp = lax.axis_size("dp")
    steps = dp.bit_length() - 1
    values = values + swap(values, "seq", 1)
    values = values + swap(values, "seq", 2)
    values = values.reshape((2,) * steps + values.shape[1:])
    for bit in reversed(range(steps)):
        mine = own_bit("dp", 1 << bit)
        received = swap(pick(values, 0, 1 - mine), "dp", 1 << bit)
        values = pick(values, 0, mine) + received
    return values


def any_places(
    patches,
    targets,
    mask_order,
    mask_count,
    attend_gain,
    attend_shift,
    joint_weight,
    query_bias,
    value_bias,
    output_weight,
    output_bias,
    feed_gain,
    feed_shift,
    expand_weight,
    expand_bias,
    reduce_weight,
    reduce_bias,
    pixel_weight,
    pixel_bias,
    mask_token,
):
    images, quarter, features = patches.shape
    dp = lax.axis_size("dp")
    near = images // 2
    rows_one = 2 * quarter
    row_count = near * rows_one
    place_y = own_bit("seq", 2)

    def own_and_far(values):
        parts = values.reshape((2, near) + values.shape[1:])
        return pick(parts, 0, place_y), swap(pick(parts, 0, 1 - place_y), "seq", 2)

    def line(vector):
        return vector.astype(F32)[None, :]

    masked_here = mask_order < mask_count[:, None]
    embedded_here = jnp.where(masked_here[:, :, None], mask_token[None, None, :], patches)
    embedded_own, embedded_far = own_and_far(embedded_here)
    mask = jnp.concatenate(own_and_far(masked_here.astype(jnp.int32)), axis=1)
    mask = mask.astype(F32)[:, :, None]
    count_sum = jnp.sum(mask_count)
    for bit in range(dp.bit_length() - 1):
        count_sum = count_sum + swap(count_sum, "dp", 1 << bit)
    inverse = 1.0 / (count_sum.astype(F32) * PIXELS)
    target_own, target_far = own_and_far(targets)
    joint_bias = jnp.concatenate(
        [line(query_bias), jnp.zeros((1, features), F32), line(value_bias)], axis=1
    )
    biases = jnp.concatenate(
        [
            line(vector)
            for vector in (output_bias, feed_gain, feed_shift, reduce_bias, pixel_bias)
        ]
        + [jnp.zeros((3, features), F32)],
        axis=0,
    )
    embedded, joint = project(
        embedded_own, embedded_far, line(attend_gain), line(attend_shift), joint_weight, joint_bias
    )
    pairs_far = swap(joint[:, 1:], "seq", 1)
    mixed, probs = attend(joint, pairs_far)
    (
        input_two,
        activated,
        after_low,
        grad_pred,
        grad_branch,
        grad_expand,
        grad_out,
        grad_attn,
        grad_mixed,
        sums_two,
    ) = rows_step(
        inverse.reshape(1, 1),
        embedded,
        mixed,
        mask,
        target_own,
        target_far,
        output_weight,
        expand_weight,
        reduce_weight,
        pixel_weight,
        biases,
        line(expand_bias),
    )

    def flat(values):
        return values.reshape(row_count, values.shape[-1])

    reduce_weight_grad = outer(flat(activated), flat(grad_branch))
    expand_weight_grad = outer(flat(input_two), flat(grad_expand))
    pixel_weight_grad = outer(flat(after_low), flat(grad_pred))
    output_weight_grad = outer(flat(mixed), flat(grad_out))
    square_grads = jnp.concatenate([pixel_weight_grad, output_weight_grad], axis=1)
    grad_query, grad_own, grad_far = attend_back(joint, pairs_far, probs, grad_mixed)
    received = swap(grad_far, "seq", 1)
    input_one, grad_joint, patch_near, patch_far, sums_one = project_back(
        grad_query,
        grad_own,
        received,
        embedded,
        grad_attn,
        mask,
        line(attend_gain),
        line(attend_shift),
        joint_weight,
    )
    grad_joint = grad_joint.reshape(3, row_count, features)
    joint_weight_grad = jnp.concatenate(
        [outer(flat(input_one), grad_joint[part]) for part in range(3)], axis=1
    )
    patch_far = swap(patch_far, "seq", 2).astype(F32)
    patch_grad = jnp.concatenate(
        [
            jnp.where(place_y == 0, patch_near, patch_far),
            jnp.where(place_y == 0, patch_far, patch_near),
        ],
        axis=0,
    )
    hidden = expand_bias.shape[0]
    vectors = (
        sums_one[0],
        sums_one[1],
        sums_one[2],
        sums_one[3],
        sums_two[4],
        sums_two[2],
        sums_two[3],
        sums_two[6 : 6 + hidden // features].reshape(hidden),
        sums_two[1],
        sums_two[0],
        sums_one[4],
    )
    loss_part = jnp.sum(sums_two[5]) * inverse
    lengths = [vector.shape[0] // dp for vector in vectors]
    packed = jnp.concatenate(
        [vector.reshape(dp, -1) for vector in vectors]
        + [jnp.broadcast_to(loss_part[None, None], (dp, 1))],
        axis=1,
    )
    packed = reduce_vector(packed)
    loss_value = packed[-1]
    cuts, start = [], 0
    for length in lengths:
        cuts.append(packed[start : start + length])
        start += length
    (
        attend_gain_grad,
        attend_shift_grad,
        query_bias_grad,
        value_bias_grad,
        output_bias_grad,
        feed_gain_grad,
        feed_shift_grad,
        expand_bias_grad,
        reduce_bias_grad,
        pixel_bias_grad,
        mask_token_grad,
    ) = cuts
    reduce_weight_grad = reduce_rows(reduce_weight_grad, x_first)
    expand_weight_grad = reduce_rows(expand_weight_grad, y_first)
    square_grads = reduce_rows(square_grads, z_first)
    joint_weight_grad = reduce_rows(joint_weight_grad, x_first)
    return (
        loss_value,
        attend_gain_grad,
        attend_shift_grad,
        joint_weight_grad,
        query_bias_grad,
        value_bias_grad,
        square_grads[:, PIXELS:],
        output_bias_grad,
        feed_gain_grad,
        feed_shift_grad,
        expand_weight_grad,
        expand_bias_grad,
        reduce_weight_grad,
        reduce_bias_grad,
        square_grads[:, :PIXELS],
        pixel_bias_grad,
        mask_token_grad,
        patch_grad,
    )


MESH = pl.DeviceIdType.MESH


def places():
    data, seq = lax.axis_index("dp"), lax.axis_index("seq")
    x, low, high = lax.rem(data, 2), lax.rem(lax.div(data, 2), 2), lax.div(data, 4)
    core, y = lax.rem(seq, 2), lax.div(seq, 2)
    return {
        "x": (x, {"dp": data + 1 - 2 * x}),
        "low": (low, {"dp": data + 2 - 4 * low}),
        "high": (high, {"dp": data + 4 - 8 * high}),
        "y": (y, {"seq": seq + 2 - 4 * y}),
        "core": (core, {"seq": seq + 1 - 2 * core}),
    }


def greet(where):
    barrier = pltpu.get_barrier_semaphore()
    for _, partner in where.values():
        pl.semaphore_signal(barrier, inc=1, device_id=partner, device_id_type=MESH)
    pl.semaphore_wait(barrier, len(where))


def remote(source, target, send, receive, partner):
    return pltpu.make_async_remote_copy(
        src_ref=source,
        dst_ref=target,
        send_sem=send,
        recv_sem=receive,
        device_id=partner,
        device_id_type=MESH,
    )


NAMES = ("high", "low", "x", "y")


def names_of(order):
    halved = [token for token in order if token in NAMES]
    return tuple(halved + [name for name in NAMES if name not in halved])


def stage_shapes(names, order, tail):
    names, shapes = list(names), []
    for token in order:
        if token == "Gy":
            names = ["y"]
        elif token == "Gcore":
            names = ["core"] + names
        elif token[0] != "+":
            names.remove(token)
        shapes.append((2,) * len(names) + tail)
    return shapes


def for_each(dims, body):
    outer = max(dims - 2, 0)
    inner = list(itertools.product(range(2), repeat=dims - outer))
    if outer == 0:
        for spot in inner:
            body(spot)
        return

    def one(place, carry):
        first = tuple(lax.rem(lax.div(place, 2 ** (outer - 1 - dim)), 2) for dim in range(outer))
        for spot in inner:
            body(first + spot)
        return carry

    lax.fori_loop(0, 2**outer, one, 0)


def add_up(target, place, other):
    target[place] = target[place] + other


class Chain:
    def __init__(self, where, start, names, order, buffers, send, receive, base, swapped=None):
        self.where, self.order = dict(where), order
        if swapped is not None:
            (first, partner_first), (second, partner_second) = (where[name] for name in swapped)
            core = where["core"][0]

            def chosen(zero, one):
                return zero + core * (one - zero)

            for name, place, ours, other in (
                (swapped[0], (first, second), partner_first, partner_second),
                (swapped[1], (second, first), partner_second, partner_first),
            ):
                here = {"dp": lax.axis_index("dp"), "seq": lax.axis_index("seq")}
                ours, other = {**here, **ours}, {**here, **other}
                partner = {axis: chosen(ours[axis], other[axis]) for axis in here}
                self.where[name] = (chosen(*place), partner)
        self.plain = where
        self.refs = [start] + list(buffers)
        self.send, self.receive, self.base = send, receive, base
        self.names = [list(names)]
        for token in order:
            names = list(self.names[-1])
            if token == "Gy":
                names = ["y"]
            elif token == "Gcore":
                names = ["core"] + names
            elif token[0] != "+":
                names.remove(token)
            self.names.append(names)

    def copy(self, stage):
        token = self.order[stage]
        source, target = self.refs[stage], self.refs[stage + 1]
        if token[0] == "+":
            _, partner = self.plain[token[1:]]
        elif token[0] == "G":
            place, partner = self.plain[token[1:]]
            target = target.at[place]
        else:
            place, partner = self.where[token]
            dim = self.names[stage].index(token)
            source = source.at[(slice(None),) * dim + (1 - place,)]
        spot = self.base + stage
        return remote(source, target, self.send.at[spot], self.receive.at[spot], partner)

    def start(self, stage):
        self.copy(stage).start()

    def finish(self, stage):
        self.copy(stage).wait()
        token = self.order[stage]
        source, target = self.refs[stage], self.refs[stage + 1]
        if token[0] == "G":
            place, _ = self.plain[token[1:]]
            target[place] = source[...]
            return
        dim = None
        if token[0] != "+":
            place, _ = self.where[token]
            dim = self.names[stage].index(token)

        def one(spot):
            origin = spot if dim is None else spot[:dim] + (place,) + spot[dim:]
            add_up(target, spot if spot else Ellipsis, source[origin if origin else Ellipsis])

        for_each(len(self.names[stage + 1]), one)

    def turn(self, stage):
        if stage > 0:
            self.finish(stage - 1)
        if stage < len(self.order):
            self.start(stage)


Y_FIRST = ("y", "x", "low", "high", "Gy", "Gcore")
Y_THEN_LOW = ("y", "low", "x", "high", "Gy", "Gcore")
X_FIRST = ("x", "low", "high", "+y", "Gcore")
SUMS_ORDER = ("+core", "+y", "+x", "+low", "+high")
MOST = 6
TILE_ORDERS = (
    Y_FIRST,
    X_FIRST,
    Y_THEN_LOW,
    Y_FIRST,
    Y_THEN_LOW,
    X_FIRST,
    Y_FIRST,
    X_FIRST,
    Y_THEN_LOW,
    Y_FIRST,
    Y_FIRST,
    Y_FIRST,
    X_FIRST,
)
TILE_SWAPS = (
    ("x", "y"),
    ("x", "low"),
    ("y", "low"),
    ("x", "y"),
    ("y", "low"),
    ("x", "low"),
    ("x", "y"),
    ("x", "low"),
    ("y", "low"),
    ("x", "y"),
    ("x", "y"),
    ("x", "y"),
    ("x", "low"),
)
TILES = len(TILE_ORDERS)
TILE_STEPS = (0, 1, 2, 3, 4, 5, 6, 7, 8, 9, 14, 18, 21)
TURNS = {
    2: ((0, 0),),
    3: ((1, 0),),
    4: ((0, 1), (2, 0),),
    5: ((1, 1), (3, 0),),
    6: ((0, 2), (4, 0),),
    7: ((1, 2), (2, 1), (3, 1), (5, 0),),
    8: ((0, 3), (6, 0),),
    9: ((1, 3), (3, 2), (7, 0),),
    10: ((0, 4), (1, 4), (2, 2), (4, 1), (6, 1), (8, 0), (13, 0), (3, 3),),
    11: ((1, 5), (5, 1), (13, 1), (9, 0), (0, 5),),
    12: ((0, 6), (3, 4), (2, 3), (7, 1),),
    13: ((4, 2), (6, 2), (13, 2),),
    14: ((3, 5), (2, 4), (5, 2),),
    15: ((3, 6), (2, 5), (4, 3), (6, 3), (13, 3), (7, 2), (8, 1), (9, 1),),
    16: ((2, 6), (5, 3), (10, 0),),
    18: ((4, 4), (5, 4), (6, 4), (13, 4), (7, 3), (8, 2), (9, 2),),
    19: ((4, 5), (5, 5), (6, 5), (13, 5), (8, 3), (10, 1),),
    20: ((4, 6), (6, 6), (7, 4), (9, 3), (11, 0),),
    21: ((7, 5), (8, 4), (10, 2),),
    22: ((8, 5), (9, 4), (10, 3), (11, 1),),
}
LAST_TURNS = (
    (14, 0),
    (8, 6),
    (9, 5),
    (10, 4),
    (11, 2),
    (14, 1),
    (9, 6),
    (11, 3),
    (14, 2),
    (10, 5),
    (12, 1),
    (10, 6),
    (14, 3),
    (11, 4),
    (12, 2),
    (14, 4),
    (11, 5),
    (14, 5),
    (11, 6),
    (12, 3),
    (12, 4),
    (12, 5),
)


def chain_scratch(cases):
    scratch, counts = [], []
    for names, order, tail, dtype in cases:
        shapes = stage_shapes(names, order, tail)
        scratch += [pltpu.VMEM(shape, dtype) for shape in shapes]
        counts.append(len(shapes))
    return scratch, counts


def split_list(values, counts):
    parts, start = [], 0
    for count in counts:
        parts.append(values[start : start + count])
        start += count
    return parts


GAIN_ONE, SHIFT_ONE, QUERY, VALUE, OUTPUT, GAIN_TWO, SHIFT_TWO, REDUCE, PIXEL, TOKEN, EXPAND = range(11)
FRONT_OWN = 9
FRONT_FAR = 12
FRONT_ATTEND = 15
FRONT_PAIRS = 2


def lines_kernel(*refs):
    out = refs[-1]
    row = 0
    for ref in refs[:-1]:
        for start in range(0, ref.shape[0], WIDE):
            out[row : row + 1] = ref[start : start + WIDE].astype(F32).reshape(1, WIDE)
            row += 1


def stack_lines(*vectors):
    return pl.pallas_call(
        lines_kernel,
        in_specs=[pl.BlockSpec(memory_space=pltpu.VMEM)] * len(vectors),
        out_specs=pl.BlockSpec(memory_space=pltpu.VMEM),
        out_shape=jax.ShapeDtypeStruct((16, WIDE), F32),
        cost_estimate=cost(1e4, 1e5),
        name="stack_lines",
    )(*vectors)


def column_of(line):
    count = line.shape[1]
    down = lax.broadcasted_iota(jnp.int32, (count, count), 0)
    along = lax.broadcasted_iota(jnp.int32, (count, count), 1)
    return jnp.sum(jnp.where(down == along, jnp.broadcast_to(line, (count, count)), 0.0), axis=1, keepdims=True)


def front_kernel(
    parts, counts, rows_in, targets_in, orders_in, lines, weight_in, pixel_in, expand_in, output_in,
    embedded_out, input_out, joint_out, pairs_out, mixed_out, probs_out, masks_out, target_out, expand_out,
    embedded, inputs, masks, order_far, joint, pairs, weight, pixel, expand, output,
    local, far_send, far_receive, send, receive,
):
    images, heads = joint.shape[:2]
    quarter = rows_in.shape[2]
    where = {name: places()[name] for name in ("core", "y")}
    sibling = where["core"][1]
    y, other = where["y"]
    step = pl.program_id(0)
    near_half, far_half = pl.ds(0, quarter), pl.ds(quarter, quarter)

    def pair_copy(image):
        return remote(
            joint.at[image, :, pl.ds(1, 2)], pairs.at[image], send.at[image], receive.at[image], sibling
        )

    def far_copy(index, source, target):
        return remote(source, target, far_send.at[index], far_receive.at[index], other)

    order_copy = far_copy(0, orders_in, order_far)
    row_copies = [
        far_copy(1 + image, rows_in.at[1 - y, image], embedded.at[image, far_half]) for image in range(images)
    ]
    target_copies = [
        far_copy(1 + images + image, targets_in.at[1 - y, image], target_out.at[image, far_half])
        for image in range(images)
    ]
    own_copy = pltpu.make_async_copy(rows_in.at[y], embedded.at[:, near_half], local.at[0])
    target_copy = pltpu.make_async_copy(targets_in.at[y], target_out.at[:, near_half], local.at[1])
    loads = [
        pltpu.make_async_copy(source, target, local.at[2 + index])
        for index, (source, target) in enumerate(
            ((pixel_in, pixel), (expand_in, expand), (output_in, output), (weight_in, weight))
        )
    ]

    @pl.when(step == 0)
    def _():
        own_copy.start()
        greet(where)
        order_copy.start()
        for copy in row_copies + loads:
            copy.start()
        target_copy.start()
        loads[0].wait()
        expand_out[0] = pixel[...]

    @pl.when(step == parts + 1)
    def _():
        loads[2].wait()
        expand_out[0] = output[...]

    for part in range(parts):

        @pl.when(step == 1 + part)
        def _(part=part):
            if part == 0:
                loads[1].wait()
            span = weight.shape[0] // 8
            starts = [place * parts * span + part * span for place in range(8)]
            expand_out[0] = jnp.concatenate([expand[:, start : start + span] for start in starts], axis=1)

    for group in range(3):

        @pl.when(step == parts + 2 + group)
        def _(group=group):
            if group == 0:
                loads[3].wait()
            starts = [part * WIDE + group * 2 * PAIR for part in range(3)]
            expand_out[0] = jnp.concatenate([weight[:, start : start + 2 * PAIR] for start in starts], axis=1)

    def project(image, start, order):
        block = pl.ds(start, quarter)
        mask = column_of((order < counts[y * images + image]).astype(F32))
        masks[image, block] = mask
        token = lines[TOKEN : TOKEN + 1].astype(BF16)
        rows = jnp.where(mask > 0.5, token, embedded[image, block])
        embedded[image, block] = rows
        normed, _ = normalize(rows.astype(F32))
        gain, shift = lines[GAIN_ONE : GAIN_ONE + 1], lines[SHIFT_ONE : SHIFT_ONE + 1]
        low = (normed * gain + shift).astype(BF16)
        inputs[image, block] = low
        for part, bias in ((1, None), (2, lines[VALUE : VALUE + 1]), (0, lines[QUERY : QUERY + 1])):
            total = dot(low, weight[:, part * WIDE : (part + 1) * WIDE])
            total = (total if bias is None else total + bias).astype(BF16)
            for pair in range(heads):
                joint[image, pair, part, block] = total[:, pair * PAIR : (pair + 1) * PAIR]

    @pl.when((step >= FRONT_OWN) & (step < FRONT_FAR))
    def _():
        @pl.when(step == FRONT_OWN)
        def _():
            own_copy.wait()

        image = step - FRONT_OWN
        project(image, 0, orders_in[pl.ds(y * images + image, 1)])

    @pl.when((step >= FRONT_FAR) & (step < FRONT_ATTEND))
    def _():
        for index in range(images):

            @pl.when(step == FRONT_FAR + index)
            def _(index=index):
                if index == 0:
                    order_copy.wait()
                row_copies[index].wait()
                target_copies[index].start()

        image = step - FRONT_FAR
        project(image, quarter, order_far[pl.ds(y * images + image, 1)])
        pair_copy(image).start()
        embedded_out[0] = embedded[image]
        input_out[0] = inputs[image]
        joint_out[0] = joint[image]
        masks_out[0] = masks[image]

    def attend(image, pair, index):
        queries = side_by_side(joint[image, pair, 0] * jnp.asarray(HEAD_DIM**-0.5, BF16))
        keys_in = jnp.concatenate([joint[image, pair, 1], pairs[image, pair, 0]], axis=0)
        values_in = jnp.concatenate([joint[image, pair, 2], pairs[image, pair, 1]], axis=0)
        pairs_out[0, index] = pairs[image, pair]
        scores = dot_nt(keys_in, queries)
        exponent = jnp.exp(scores - jnp.max(scores, axis=0, keepdims=True))
        total = jnp.sum(exponent, axis=0, keepdims=True)
        probs = (exponent * (1.0 / total)).astype(BF16)
        probs_out[0, index] = probs
        mixed = merge_turned(dot_tn(values_in, probs)).astype(BF16)
        mixed_out[0, :, index * PAIR : (index + 1) * PAIR] = mixed

    @pl.when(step >= FRONT_ATTEND)
    def _():
        place = step - FRONT_ATTEND
        turns = heads // FRONT_PAIRS
        image, turn = lax.div(place, turns), lax.rem(place, turns)

        @pl.when(turn == 0)
        def _():
            pair_copy(image).wait()

        for index in range(FRONT_PAIRS):
            attend(image, turn * FRONT_PAIRS + index, index)

    @pl.when(step == pl.num_programs(0) - 1)
    def _():
        for copy in target_copies:
            copy.wait()
        target_copy.wait()


def merge_turned(stacked):
    rows = stacked.shape[1] // 2
    down = lax.broadcasted_iota(jnp.int32, (PAIR, rows), 0)
    return jnp.where(down < HEAD_DIM, stacked[:, :rows], stacked[:, rows:]).T


def front(counts, rows_in, targets_in, orders_in, lines, weight, pixel, expand, output):
    near, quarter, width = rows_in.shape[1:]
    rows, heads = 2 * quarter, width // PAIR
    parts = expand.shape[1] // width

    def image(step):
        return jnp.clip(step - FRONT_FAR, 0, near - 1)

    turns = heads // FRONT_PAIRS

    def spot(step):
        place = jnp.maximum(step - FRONT_ATTEND, 0)
        return lax.div(place, turns), lax.rem(place, turns)

    block = pl.BlockSpec((1, rows, width), lambda s: (image(s), 0, 0))
    return pl.pallas_call(
        partial(front_kernel, parts),
        grid=(FRONT_ATTEND + near * turns,),
        in_specs=[
            pl.BlockSpec(memory_space=pltpu.SMEM),
            pl.BlockSpec(memory_space=pl.ANY),
            pl.BlockSpec(memory_space=pl.ANY),
            fixed(orders_in.shape),
            fixed(lines.shape),
        ]
        + [pl.BlockSpec(memory_space=pl.ANY)] * 4,
        out_specs=[
            block,
            block,
            pl.BlockSpec((1, heads, 3, rows, PAIR), lambda s: (image(s), 0, 0, 0, 0)),
            pl.BlockSpec((1, FRONT_PAIRS, 2, rows, PAIR), lambda s: spot(s) + (0, 0, 0)),
            pl.BlockSpec((1, rows, FRONT_PAIRS * PAIR), lambda s: (spot(s)[0], 0, spot(s)[1])),
            pl.BlockSpec((1, FRONT_PAIRS, 2 * rows, 2 * rows), lambda s: spot(s) + (0, 0)),
            pl.BlockSpec((1, rows, 1), lambda s: (image(s), 0, 0)),
            pl.BlockSpec(memory_space=pl.ANY),
            pl.BlockSpec((1, width, width), lambda s: (jnp.minimum(s, parts + 4), 0, 0)),
        ],
        out_shape=[
            jax.ShapeDtypeStruct((near, rows, width), BF16),
            jax.ShapeDtypeStruct((near, rows, width), BF16),
            jax.ShapeDtypeStruct((near, heads, 3, rows, PAIR), BF16),
            jax.ShapeDtypeStruct((near, heads, 2, rows, PAIR), BF16),
            jax.ShapeDtypeStruct((near, rows, width), BF16),
            jax.ShapeDtypeStruct((near, heads, 2 * rows, 2 * rows), BF16),
            jax.ShapeDtypeStruct((near, rows, 1), F32),
            jax.ShapeDtypeStruct((near, rows, width), BF16),
            jax.ShapeDtypeStruct((parts + 5, width, width), BF16),
        ],
        scratch_shapes=[
            pltpu.VMEM((near, rows, width), BF16),
            pltpu.VMEM((near, rows, width), BF16),
            pltpu.VMEM((near, rows, 1), F32),
            pltpu.VMEM(orders_in.shape, jnp.int32),
            pltpu.VMEM((near, heads, 3, rows, PAIR), BF16),
            pltpu.VMEM((near, heads, 2, rows, PAIR), BF16),
            pltpu.VMEM(weight.shape, BF16),
            pltpu.VMEM(pixel.shape, BF16),
            pltpu.VMEM(expand.shape, BF16),
            pltpu.VMEM(output.shape, BF16),
            pltpu.SemaphoreType.DMA((6,)),
            pltpu.SemaphoreType.DMA((1 + 2 * near,)),
            pltpu.SemaphoreType.DMA((1 + 2 * near,)),
            pltpu.SemaphoreType.DMA((near,)),
            pltpu.SemaphoreType.DMA((near,)),
        ],
        compiler_params=pltpu.CompilerParams(
            vmem_limit_bytes=60 * MIB, collective_id=1, has_side_effects=True
        ),
        cost_estimate=cost(5e9, 40e6),
        name="front",
    )(counts, rows_in, targets_in, orders_in, lines, weight, pixel, expand, output)


def middle_kernel(
    embedded_in, mixed, mask_in, target_in, weights, reduce, lines,
    sides, input_out, scaling_out, sums_out, low, total, biases,
):
    parts = reduce.shape[1]
    span = reduce.shape[2]
    width = weights.shape[1]
    mask = mask_in[0]

    @pl.when(pl.program_id(0) == 0)
    def _():
        sums_out[...] = jnp.zeros_like(sums_out)
        for part in range(parts):
            pieces = []
            for place in range(8):
                row, start = divmod((place * parts + part) * span, width)
                pieces.append(lines[EXPAND + row : EXPAND + row + 1, start : start + span])
            biases[part] = jnp.concatenate(pieces, axis=1)

    after_attn = embedded_in[0].astype(F32) + dot(mixed[0], weights[parts + 1]) + lines[OUTPUT : OUTPUT + 1]
    sides[0, 0, parts + 1] = mixed[0]
    normed, scaling = normalize(after_attn)
    sides[0, 1, parts + 1] = normed.astype(BF16)
    scaling_out[0] = scaling
    low[...] = (normed * lines[GAIN_TWO : GAIN_TWO + 1] + lines[SHIFT_TWO : SHIFT_TWO + 1]).astype(BF16)
    input_out[0] = low[...]
    total[...] = after_attn + lines[REDUCE : REDUCE + 1]

    def one(part, carry):
        active, rate = gelu_both(dot(low[...], weights[1 + part]) + biases[part])
        active = active.astype(BF16)
        sides[0, 0, 1 + part] = active
        sides[0, 1, 1 + part] = rate.astype(BF16)
        total[...] += dot(active, reduce[:, part].reshape(width, width))
        return carry

    for part in range(parts):
        one(part, 0)
    after_low = total[...].astype(BF16)
    sides[0, 0, 0] = after_low
    errors = dot(after_low, weights[0]) + lines[PIXEL : PIXEL + 1] - target_in[0].astype(F32)
    square = errors * errors + 1.0
    root = lax.rsqrt(square)
    grad_pred = (mask * errors * root).astype(BF16)
    sides[0, 1, 0] = grad_pred
    sums_out[0:1] += column_sums(grad_pred)
    sums_out[5:6] += jnp.sum((square * root - 1.0) * mask, axis=0, keepdims=True)
    sums_out[10:11] += jnp.sum(jnp.broadcast_to(mask, errors.shape), axis=0, keepdims=True)


def middle(embedded, mixed, mask, targets, weights, reduce, lines):
    near, rows, width = embedded.shape
    parts = reduce.shape[1]
    block = pl.BlockSpec((1, rows, width), lambda i: (i, 0, 0))
    column = pl.BlockSpec((1, rows, 1), lambda i: (i, 0, 0))
    stack = pl.BlockSpec((1, 2, parts + 2, rows, width), lambda i: (i, 0, 0, 0, 0))
    return pl.pallas_call(
        middle_kernel,
        grid=(near,),
        in_specs=[
            block,
            block,
            column,
            block,
            fixed((parts + 2, width, width)),
            fixed(reduce.shape),
            fixed(lines.shape),
        ],
        out_specs=[stack, block, column, fixed_out((16, width))],
        out_shape=[
            jax.ShapeDtypeStruct((near, 2, parts + 2, rows, width), BF16),
            jax.ShapeDtypeStruct((near, rows, width), BF16),
            jax.ShapeDtypeStruct((near, rows, 1), F32),
            jax.ShapeDtypeStruct((16, width), F32),
        ],
        scratch_shapes=[
            pltpu.VMEM((rows, width), BF16),
            pltpu.VMEM((rows, width), F32),
            pltpu.VMEM((parts, 1, width), F32),
        ],
        compiler_params=params(60),
        cost_estimate=cost(2 * near * rows * width * width * (2 * parts + 2), 40e6),
        name="middle",
    )(embedded, mixed, mask, targets, weights, reduce, lines)


HIGH_ROWS = 4 * 96


def spread_half(result, target, high, start, names, swapped):
    for low in range(2):
        for x in range(2):
            for y in range(2):
                at = (low * 2 + x) * 96 + start
                piece = result[at : at + HALF, y * 384 : (y + 1) * 384]
                spot = {"high": high, "low": low, "x": x, "y": y}
                if swapped is not None:
                    first, second = swapped
                    spot[first], spot[second] = spot[second], spot[first]
                target[tuple(spot[name] for name in names)] = piece.astype(BF16)


HALF = 48
SLOTS = 4
KEPT = 10
FIRST_ATTEND = 10
GROUP_STEPS = (14, 18, 21)
FIRST_NORM = 22


def back_kernel(
    counts, sides, weights, reduce, input_two, scaling_two, input_one, joint, pairs, probs_in, lines, sums_in,
    embedded_in, mask_in, *rest,
):
    (
        done_out,
        near_out,
        far_out,
        sums_out,
        late_out,
        done,
        done_sent,
        branch,
        wide,
        grad_in,
        upstream,
        own_pairs,
        give_pairs,
        got_pairs,
        far_give,
        sums,
        late,
        keep,
        give,
        got,
        send,
        receive,
        core_send,
        core_receive,
        pair_send,
        pair_receive,
        far_send,
        far_receive,
    ) = rest[:28]
    buffers = split_list(rest[28:], counts)
    where = places()
    core, sibling = where["core"]
    step = pl.program_id(0)
    images, rows, width = input_two.shape
    every = images * rows
    quarter = rows // 2
    heads = width // PAIR
    first_gain, second_gain = lines[GAIN_ONE : GAIN_ONE + 1], lines[GAIN_TWO : GAIN_TWO + 1]
    chains = [
        Chain(where, keep.at[unit % KEPT], names_of(order), order, list(buffers[unit]) + [done.at[unit]], send, receive, MOST * unit, TILE_SWAPS[unit])
        for unit, order in enumerate(TILE_ORDERS)
    ]
    chains.append(Chain(where, sums, (), SUMS_ORDER, buffers[TILES], send, receive, MOST * TILES))
    chains.append(Chain(where, late, (), SUMS_ORDER, buffers[TILES + 1], send, receive, MOST * TILES + MOST))

    def core_copy(unit):
        slot = lax.rem(unit, SLOTS)
        return remote(give.at[slot], got.at[slot], core_send.at[unit], core_receive.at[unit], sibling)

    def pair_copy(place, second):
        image = lax.rem(place, 3)
        slot = lax.rem((lax.div(place, 6) * 3 + image) * 2 + second, SLOTS)
        return remote(
            give_pairs.at[slot], got_pairs.at[place], pair_send.at[place], pair_receive.at[place], sibling
        )

    def far_copy(image):
        return remote(
            far_give.at[image], far_out.at[image], far_send.at[image], far_receive.at[image], where["y"][1]
        )

    def core_sum(unit):
        core_copy(unit).wait()
        for_each(4, lambda spot: add_up(keep.at[unit % KEPT], spot, got[(unit % SLOTS,) + spot]))

    def done_copy(unit):
        return pltpu.make_async_copy(done.at[unit], done_out.at[unit], done_sent.at[unit])

    def turn(unit, stage):
        if unit < TILES and stage == 0:
            core_sum(unit)
        chains[unit].turn(stage)
        if stage == len(chains[unit].order) and unit < TILES:
            done_copy(unit).start()

    def tile(unit, lines_of, value, forms):
        def one(high):
            columns = slice(high * HIGH_ROWS, (high + 1) * HIGH_ROWS)
            result = dot_tn(lines_of(columns).reshape(every, HIGH_ROWS), value)
            for half in range(2):
                for names, swapped, chosen in forms:
                    swapped = swapped if half == 1 else None

                    @pl.when(jnp.logical_and(core == half, chosen))
                    def _(half=half, names=names, swapped=swapped):
                        spread_half(result, keep.at[lax.rem(unit, KEPT)], high, half * HALF, names, swapped)

                    @pl.when(jnp.logical_and(core != half, chosen))
                    def _(half=half, names=names, swapped=swapped):
                        spread_half(result, give.at[lax.rem(unit, SLOTS)], high, half * HALF, names, swapped)

        for high in range(2):
            one(high)
        core_copy(unit).start()

    def forms_of(units, unit):
        forms = {}
        for other in units:
            form = (names_of(TILE_ORDERS[other]), TILE_SWAPS[other])
            forms.setdefault(form, []).append(unit == other)
        if len(forms) == 1:
            return [form + (True,) for form in forms]
        return [form + (functools.reduce(jnp.logical_or, asked),) for form, asked in forms.items()]

    def flat(ref):
        return ref[...].reshape(every, ref.shape[-1])

    def left_lines(columns):
        return sides[:, 0, 0, :, columns]

    @pl.when(step == 0)
    def _():
        greet(where)
        sums[...] = sums_in[...]
        late[...] = jnp.zeros_like(late)
        grad_in[...] = jnp.zeros_like(grad_in)

    for at, turns in TURNS.items():

        @pl.when(step == at)
        def _(turns=turns):
            for unit, stage in turns:
                turn(unit, stage)

    @pl.when(step == 0)
    def _():
        tile(0, left_lines, sides[:, 1, 0].reshape(every, width), forms_of((0,), 0))

        def one(image):
            low = dot_nt(sides[image, 1, 0], weights[0]).astype(BF16)
            branch[image] = low
            sums[1:2] += column_sums(low)
        for image in range(images):
            one(image)

    @pl.when((step > 0) & (step < 9) & (lax.rem(step, 2) == 1))
    def _():
        tile(step, left_lines, flat(branch), forms_of((1, 3, 5, 7), step))
        row = pl.ds(6 + lax.div(step, 2), 1)

        def one(image):
            low = dot_nt(branch[image], reduce[:, 0].reshape(width, width)) * sides[image, 1, 0].astype(F32)
            low = low.astype(BF16)
            wide[image] = low
            sums[row] += column_sums(low)
        for image in range(images):
            one(image)

    @pl.when((step > 0) & (step < 9) & (lax.rem(step, 2) == 0))
    def _():
        tile(step, lambda columns: input_two[:, :, columns], flat(wide), forms_of((2, 4, 6, 8), step))
        fresh = jnp.where(step == 2, 0.0, 1.0)

        def one(image):
            grad_in[image] = grad_in[image] * fresh + dot_nt(wide[image], weights[0])
        for image in range(images):
            one(image)

    @pl.when(step == 9)
    def _():
        def one(image):
            normed = sides[image, 1, 0].astype(F32)
            grad = grad_in[image]
            low = branch[image].astype(F32) + normalize_back(grad, normed, scaling_two[image], second_gain)
            low = low.astype(BF16)
            branch[image] = low
            sums[2:3] += column_sums(grad * normed)
            sums[3:4] += column_sums(grad)
            sums[4:5] += column_sums(low)
            mixed = dot_nt(low, weights[0]).astype(BF16)
            for pair in range(heads):
                upstream[image, pair] = mixed[:, pair * PAIR : (pair + 1) * PAIR]
        for image in range(images):
            one(image)

        tile(9, left_lines, flat(branch), forms_of((9,), 9))

    def attend_back(group, image, second, inside, order):
        place = group * 6 + inside

        @pl.when(order >= SLOTS)
        def _():
            before = order - SLOTS
            pair_copy(lax.div(before, 6) * 6 + second * 3 + lax.rem(lax.div(before, 2), 3), second).wait_send()

        scale = HEAD_DIM**-0.5
        target = own_pairs.at[lax.rem(group, 2), inside]
        away = give_pairs.at[lax.rem(order, SLOTS)]
        queries = side_by_side(joint[0, second, 0])
        keys_in = jnp.concatenate([joint[0, second, 1], pairs[0, second, 0]], axis=0)
        values_in = jnp.concatenate([joint[0, second, 2], pairs[0, second, 1]], axis=0)
        grad_mixed = side_by_side(upstream[image, group * 2 + second])
        probs = probs_in[0, second]
        grad_probs = dot_nt(values_in, grad_mixed)
        broad = probs.astype(F32)
        weighted = broad * grad_probs
        inner = jnp.sum(weighted, axis=0, keepdims=True)
        grad_scores = (weighted - broad * inner).astype(BF16)
        grad_values = dot(probs, grad_mixed).astype(BF16)
        grad_keys = (dot(grad_scores, queries) * scale).astype(BF16)
        target[0] = (merge_turned(dot_tn(keys_in, grad_scores)) * scale).astype(BF16)
        target[1] = grad_keys[:rows]
        target[2] = grad_values[:rows]
        away[0] = grad_keys[rows:]
        away[1] = grad_values[rows:]
        pair_copy(place, second).start()

    attends = (step >= FIRST_ATTEND) & (step < GROUP_STEPS[2]) & (step != GROUP_STEPS[0]) & (step != GROUP_STEPS[1])

    @pl.when(attends)
    def _():
        group, image = attend_place(step)
        for second in range(2):
            inside = second * 3 + image
            attend_back(group, image, second, inside, (group * 3 + image) * 2 + second)

    @pl.when((step == GROUP_STEPS[0]) | (step == GROUP_STEPS[1]) | (step == GROUP_STEPS[2]))
    def _():
        group = jnp.where(step == GROUP_STEPS[0], 0, jnp.where(step == GROUP_STEPS[1], 1, 2))
        slot = lax.rem(group, 2)
        for inside in range(6):
            pair_copy(group * 6 + inside, inside // 3).wait_recv()
            image, second = inside % 3, inside // 3
            for part in range(3):
                piece = own_pairs[slot, inside, part]
                if part > 0:
                    piece = piece.astype(F32) + got_pairs[group * 6 + inside, part - 1].astype(F32)
                start = part * 2 * PAIR + second * PAIR
                wide[image, :, start : start + PAIR] = piece.astype(BF16)
        tile(10 + group, lambda columns: input_one[:, :, columns], flat(wide), forms_of((10, 11, 12), 10 + group))
        fresh = jnp.where(group == 0, 0.0, 1.0)
        row = pl.ds(5 + group, 1)

        def one(image):
            late[row] += column_sums(wide[image])
            grad_in[image] = grad_in[image] * fresh + dot_nt(wide[image], weights[0])
        for image in range(images):
            one(image)

    @pl.when(step == FIRST_NORM)
    def _():
        for image in range(images):
            mask = mask_in[image]
            normed, scaling = normalize(embedded_in[image].astype(F32))
            grad = grad_in[image]
            total = branch[image].astype(F32) + normalize_back(grad, normed, scaling, first_gain)
            kept = total * (1.0 - mask)
            far_give[image] = kept[quarter:].astype(BF16)
            far_copy(image).start()
            near_out[image] = kept[:quarter]
            late[0:1] += column_sums(grad * normed)
            late[1:2] += column_sums(grad)
            late[2:3] += column_sums(total * mask)
            if image == 0:
                turn(TILES - 1, 0)

    @pl.when(step == pl.num_programs(0) - 1)
    def _():
        for unit, stage in LAST_TURNS:
            turn(unit, stage)
        for image in range(images):
            far_copy(image).wait()
        for unit in range(TILES):
            done_copy(unit).wait()
        for image in range(1, 3):
            for second in range(2):
                pair_copy(12 + second * 3 + image, second).wait_send()
        sums_out[...] = chains[TILES].refs[-1][...]
        late_out[...] = chains[TILES + 1].refs[-1][...]


def attend_place(step):
    place = step - FIRST_ATTEND
    for at in GROUP_STEPS[:2]:
        place = place - jnp.where(step > at, 1, 0)
    place = jnp.clip(place, 0, 8)
    return lax.div(place, 3), lax.rem(place, 3)


def back(
    sides, weights, reduce, input_two, scaling_two, input_one, joint, pairs, probs, lines, sums, embedded, mask
):
    near, _, slots, rows, width = sides.shape
    quarter = rows // 2
    heads = width // PAIR

    def slot(step):
        return jnp.minimum(lax.div(step + 1, 2), slots - 1)

    def part(step):
        return jnp.clip(lax.div(step - 1, 2), 0, slots - 3)

    def weight(step):
        late = slots + jnp.where(step > GROUP_STEPS[0], 1, 0) + jnp.where(step > GROUP_STEPS[1], 1, 0)
        return jnp.where(step < FIRST_ATTEND, slot(step), late)

    def spot(step):
        group, image = attend_place(step)
        return image, group

    cases = [(names_of(order), order, (HALF, 384), BF16) for order in TILE_ORDERS]
    cases.append(((), SUMS_ORDER, sums.shape, F32))
    cases.append(((), SUMS_ORDER, (8, width), F32))
    buffers, counts = chain_scratch(cases)
    kept, start = [], 0
    for index, count in enumerate(counts):
        kept += buffers[start : start + count - (index < TILES)]
        start += count
    buffers, counts = kept, [count - (index < TILES) for index, count in enumerate(counts)]
    whole = (2, 2, 2, 2, HALF, 384)
    stack = pl.BlockSpec((near, 2, 1, rows, width), lambda s: (0, 0, slot(s), 0, 0))
    return pl.pallas_call(
        partial(back_kernel, counts),
        grid=(FIRST_NORM + 1,),
        in_specs=[
            stack,
            pl.BlockSpec((1, width, width), lambda s: (weight(s), 0, 0)),
            pl.BlockSpec((8, 1, reduce.shape[2], width), lambda s: (0, part(s), 0, 0)),
            fixed((near, rows, width)),
            fixed((near, rows, 1)),
            fixed((near, rows, width)),
            pl.BlockSpec((1, 2, 3, rows, PAIR), lambda s: spot(s) + (0, 0, 0)),
            pl.BlockSpec((1, 2, 2, rows, PAIR), lambda s: spot(s) + (0, 0, 0)),
            pl.BlockSpec((1, 2, 2 * rows, 2 * rows), lambda s: spot(s) + (0, 0)),
            fixed(lines.shape),
            fixed(sums.shape),
            fixed((near, rows, width)),
            fixed((near, rows, 1)),
        ],
        out_specs=[
            pl.BlockSpec(memory_space=pl.ANY),
            fixed((near, quarter, width)),
            pl.BlockSpec(memory_space=pl.ANY),
            fixed_out(sums.shape),
            fixed_out((8, width)),
        ],
        out_shape=[
            jax.ShapeDtypeStruct((TILES, 2, 2, HALF, 384), BF16),
            jax.ShapeDtypeStruct((near, quarter, width), F32),
            jax.ShapeDtypeStruct((near, quarter, width), BF16),
            jax.ShapeDtypeStruct(sums.shape, F32),
            jax.ShapeDtypeStruct((8, width), F32),
        ],
        scratch_shapes=[
            pltpu.VMEM((TILES, 2, 2, HALF, 384), BF16),
            pltpu.SemaphoreType.DMA((TILES,)),
            pltpu.VMEM((near, rows, width), BF16),
            pltpu.VMEM((near, rows, width), BF16),
            pltpu.VMEM((near, rows, width), F32),
            pltpu.VMEM((near, heads, rows, PAIR), BF16),
            pltpu.VMEM((2, 6, 3, rows, PAIR), BF16),
            pltpu.VMEM((SLOTS, 2, rows, PAIR), BF16),
            pltpu.VMEM((near * heads, 2, rows, PAIR), BF16),
            pltpu.VMEM((near, quarter, width), BF16),
            pltpu.VMEM(sums.shape, F32),
            pltpu.VMEM((8, width), F32),
            pltpu.VMEM((KEPT,) + whole, BF16),
            pltpu.VMEM((SLOTS,) + whole, BF16),
            pltpu.VMEM((SLOTS,) + whole, BF16),
            pltpu.SemaphoreType.DMA((MOST * (TILES + 2),)),
            pltpu.SemaphoreType.DMA((MOST * (TILES + 2),)),
            pltpu.SemaphoreType.DMA((TILES,)),
            pltpu.SemaphoreType.DMA((TILES,)),
            pltpu.SemaphoreType.DMA((near * heads,)),
            pltpu.SemaphoreType.DMA((near * heads,)),
            pltpu.SemaphoreType.DMA((near,)),
            pltpu.SemaphoreType.DMA((near,)),
        ]
        + buffers,
        compiler_params=pltpu.CompilerParams(
            vmem_limit_bytes=60 * MIB, collective_id=2, has_side_effects=True
        ),
        cost_estimate=cost(40e9, 60e6),
        name="back",
    )(
        sides, weights, reduce, input_two,
        scaling_two, input_one, joint, pairs, probs, lines, sums, embedded, mask,
    )


def emit_kernel(parts, done, near_in, far_in, sums, late, *outs):
    (
        loss, attend_gain, attend_shift, joint, query_bias, value_bias, output, output_bias, feed_gain,
        feed_shift, expand, expand_bias, reduce, reduce_bias, pixel, pixel_bias, token, patch,
    ) = outs
    data, y = lax.axis_index("dp"), lax.div(lax.axis_index("seq"), 2)
    inverse = 1.0 / (sums[10:11] * PIXELS)
    loss[0] = jnp.sum(sums[5:6] * inverse)
    wide_inverse = inverse[:, :384]

    def piece(unit, core, half):
        return done[unit, core, half].astype(F32) * wide_inverse

    def square(unit):
        return [
            jnp.concatenate([piece(unit, core, half) for half in range(2)], axis=1) for core in range(2)
        ]

    for unit, target in ((0, pixel), (2 * parts + 1, output)):
        for core, lines in enumerate(square(unit)):
            target[core * HALF : (core + 1) * HALF] = lines
    expands = []
    for part in range(parts):
        for core, lines in enumerate(square(1 + 2 * part)):
            start = part * 2 * HALF + core * HALF
            reduce[start : start + HALF] = lines
        expands.append(square(2 + 2 * part))
    span = 2 * HALF
    for core in range(2):
        for d in range(8):
            lines = [expands[part][core][:, d * span : (d + 1) * span] for part in range(parts)]
            expand[core * HALF : (core + 1) * HALF, d * 4 * span : (d + 1) * 4 * span] = jnp.concatenate(
                lines, axis=1
            )
    for group in range(3):
        for core, lines in enumerate(square(2 * parts + 2 + group)):
            for part in range(3):
                start = part * WIDE + group * 2 * PAIR
                joint[core * HALF : (core + 1) * HALF, start : start + 2 * PAIR] = lines[
                    :, part * 2 * PAIR : (part + 1) * 2 * PAIR
                ]

    def own_cut(lines):
        shift = lax.rem(WIDE - data * span, WIDE)
        return pltpu.roll(lines, shift, axis=1)[:, :span]

    early = own_cut(sums[...] * inverse)
    later = own_cut(late[...] * inverse)
    queries = jnp.concatenate([late[5 + group : 6 + group, : 2 * PAIR] for group in range(3)], axis=1)
    values = jnp.concatenate([late[5 + group : 6 + group, 4 * PAIR :] for group in range(3)], axis=1)
    both = jnp.concatenate([queries, values] + [jnp.zeros((6, WIDE), F32)], axis=0)
    both = own_cut(both * inverse)
    for target, lines, row in (
        (attend_gain, later, 0),
        (attend_shift, later, 1),
        (query_bias, both, 0),
        (value_bias, both, 1),
        (output_bias, early, 4),
        (feed_gain, early, 2),
        (feed_shift, early, 3),
        (reduce_bias, early, 1),
        (pixel_bias, early, 0),
        (token, later, 2),
    ):
        target[...] = lines[row : row + 1]
    joined = jnp.concatenate([early[6 + part : 7 + part] for part in range(parts)], axis=1)
    expand_bias[...] = joined.reshape(joined.shape[1])
    images = near_in.shape[0]
    for image in range(images):
        patch[y * images + image] = near_in[image] * inverse
        patch[(1 - y) * images + image] = far_in[image].astype(F32) * inverse


def emit(parts, done, near_in, far_in, sums, late):
    images, quarter, width = near_in.shape
    hidden = parts * width

    def out(*shape):
        return jax.ShapeDtypeStruct(shape, F32)

    small = out(1, 96)
    outs = [
        out(1), small, small, out(96, 3 * width), small, small, out(96, width), small, small,
        small, out(96, hidden), out(hidden // 8), out(hidden // 8, width), small, out(96, width), small, small,
        out(2 * images, quarter, width),
    ]
    whole = pl.BlockSpec(memory_space=pltpu.VMEM)
    return pl.pallas_call(
        partial(emit_kernel, parts),
        in_specs=[whole] * 5,
        out_specs=[pl.BlockSpec(memory_space=pltpu.SMEM)] + [whole] * (len(outs) - 1),
        out_shape=outs,
        compiler_params=params(60),
        cost_estimate=cost(1e6, 12e6),
        name="emit",
    )(done, near_in, far_in, sums, late)


def eight_places(
    patches,
    targets,
    mask_order,
    mask_count,
    attend_gain,
    attend_shift,
    joint_weight,
    query_bias,
    value_bias,
    output_weight,
    output_bias,
    feed_gain,
    feed_shift,
    expand_weight,
    expand_bias,
    reduce_weight,
    reduce_bias,
    pixel_weight,
    pixel_bias,
    mask_token,
):
    images, quarter, features = patches.shape
    near = images // 2
    place_y = own_bit("seq", 2)
    hidden = expand_bias.shape[0]
    parts = hidden // features

    def halves(values):
        return values.reshape((2, near) + values.shape[1:])

    lines = stack_lines(
        attend_gain,
        attend_shift,
        query_bias,
        value_bias,
        output_bias,
        feed_gain,
        feed_shift,
        reduce_bias,
        pixel_bias,
        mask_token,
        expand_bias,
    )
    reduce_parts = reduce_weight.reshape(8, parts, hidden // (8 * parts), features)
    embedded, input_one, joint, pairs, mixed, probs, mask, targets_here, weights = front(
        mask_count,
        halves(patches),
        halves(targets),
        mask_order,
        lines,
        joint_weight,
        pixel_weight,
        expand_weight,
        output_weight,
    )
    sides, input_two, scaling_two, sums = middle(
        embedded, mixed, mask, targets_here, weights, reduce_parts, lines
    )
    done, patch_near, patch_far, sums, late = back(
        sides,
        weights,
        reduce_parts,
        input_two,
        scaling_two,
        input_one,
        joint,
        pairs,
        probs,
        lines,
        sums,
        embedded,
        mask,
    )
    outs = emit(parts, done, patch_near, patch_far, sums, late)
    flat = {0: (), 1: (-1,), 2: (-1,), 4: (-1,), 5: (-1,), 7: (-1,), 8: (-1,), 9: (-1,), 11: (-1,)}
    flat.update({13: (-1,), 15: (-1,), 16: (-1,)})
    return tuple(
        out.reshape(flat[index]) if index in flat else out for index, out in enumerate(outs)
    )


def on_device(*arguments):
    if lax.axis_size("dp") == 8 and lax.axis_size("seq") == 4:
        return eight_places(*arguments)
    return any_places(*arguments)


def solution(mesh):
    placed = (
        P("dp", "seq", None),
        P("dp", "seq", None),
        P("dp", "seq"),
        P("dp"),
        P(),
        P(),
        P(),
        P(),
        P(),
        P(),
        P(),
        P(),
        P(),
        P(),
        P(),
        P(),
        P(),
        P(),
        P(),
        P(),
    )
    return jax.shard_map(
        on_device,
        mesh=mesh,
        in_specs=placed,
        out_specs=(
            P(),
            P("dp"),
            P("dp"),
            P("dp", None),
            P("dp"),
            P("dp"),
            P("dp", None),
            P("dp"),
            P("dp"),
            P("dp"),
            P("dp", None),
            P("dp"),
            P("dp", None),
            P("dp"),
            P("dp", None),
            P("dp"),
            P("dp"),
            P("dp", "seq", None),
        ),
        check_vma=False,
    )
```

```python
import functools
import itertools
from functools import partial

import jax
import jax.numpy as jnp
from jax import lax
from jax.experimental import pallas as pl
from jax.experimental.pallas import tpu as pltpu
from jax.sharding import PartitionSpec as P

HEADS = 12
HEAD_DIM = 64
PIXELS = 768
WIDE = 768
PAIR = 2 * HEAD_DIM
MIB = 1 << 20
F32 = jnp.float32
BF16 = jnp.bfloat16


def dot(left, right):
    return jnp.dot(left, right, preferred_element_type=F32)


def dot_nt(left, right):
    return lax.dot_general(left, right, (((1,), (1,)), ((), ())), preferred_element_type=F32)


def dot_tn(left, right):
    return lax.dot_general(left, right, (((0,), (0,)), ((), ())), preferred_element_type=F32)


def normalize(inputs):
    centre = inputs - jnp.mean(inputs, axis=-1, keepdims=True)
    scaling = lax.rsqrt(jnp.mean(centre * centre, axis=-1, keepdims=True) + 1e-06)
    return (centre * scaling, scaling)


def normalize_back(upstream, normed, scaling, gain):
    scaled = upstream * gain
    return scaling * (
        scaled
        - jnp.mean(scaled, axis=-1, keepdims=True)
        - normed * jnp.mean(scaled * normed, axis=-1, keepdims=True)
    )


def column_sums(values):
    return jnp.sum(values.astype(F32), axis=0, keepdims=True)


def gelu_both(inputs):
    bell = jnp.exp2(inputs * inputs * (-0.5 * 1.4426950408889634))
    base_of = 1.0 + (0.3275911 * 0.7071067811865476) * jnp.abs(inputs)
    inner = pl.reciprocal(base_of, approx=True)
    inner = inner * (2.0 - base_of * inner)
    series = 0.5 * 1.453152027 - inner * (0.5 * 1.061405429)
    series = 0.5 * 1.421413741 - inner * series
    series = 0.5 * 0.284496736 - inner * series
    series = 0.5 * 0.254829592 - inner * series
    tail = series * inner * bell
    below = jnp.where(inputs < 0.0, tail, 1.0 - tail)
    return (inputs * below, below + inputs * bell * 0.3989422804014327)


def params(limit):
    return pltpu.CompilerParams(vmem_limit_bytes=limit * MIB)


def fixed(shape):
    zeros = (0,) * len(shape)
    return pl.BlockSpec(shape, lambda *place: zeros, pipeline_mode=pl.Buffered(1))


def cost(flops, moved):
    return pl.CostEstimate(flops=int(flops), bytes_accessed=int(moved), transcendentals=0)


def project_kernel(own, far, gain, shift, weight, bias, embedded_out, joint_out):
    embedded = jnp.concatenate([own[0], far[0]], axis=0)
    embedded_out[0] = embedded
    normed, _ = normalize(embedded.astype(F32))
    low = (normed * gain[...] + shift[...]).astype(BF16)
    for part in range(3):
        cut = slice(part * WIDE, (part + 1) * WIDE)
        joint_out[0, part] = (dot(low, weight[:, cut]) + bias[:, cut]).astype(BF16)


def project(own, far, gain, shift, weight, bias):
    near, quarter, width = own.shape
    rows = 2 * quarter
    return pl.pallas_call(
        project_kernel,
        grid=(near,),
        in_specs=[
            pl.BlockSpec((1, quarter, width), lambda i: (i, 0, 0)),
            pl.BlockSpec((1, quarter, width), lambda i: (i, 0, 0)),
            fixed((1, width)),
            fixed((1, width)),
            fixed((width, 3 * width)),
            fixed((1, 3 * width)),
        ],
        out_specs=[
            pl.BlockSpec((1, rows, width), lambda i: (i, 0, 0)),
            pl.BlockSpec((1, 3, rows, width), lambda i: (i, 0, 0, 0)),
        ],
        out_shape=[
            jax.ShapeDtypeStruct((near, rows, width), BF16),
            jax.ShapeDtypeStruct((near, 3, rows, width), BF16),
        ],
        compiler_params=params(32),
        cost_estimate=cost(2 * near * rows * width * 3 * width, 12e6),
        name="project",
    )(own, far, gain, shift, weight, bias)


def side_by_side(pair):
    lanes = lax.broadcasted_iota(jnp.int32, pair.shape, 1)
    zero = jnp.zeros_like(pair)
    first = jnp.where(lanes < HEAD_DIM, pair, zero)
    second = jnp.where(lanes < HEAD_DIM, zero, pair)
    return jnp.concatenate([first, second], axis=0)


def merge_heads(stacked):
    rows = stacked.shape[0] // 2
    lanes = lax.broadcasted_iota(jnp.int32, (rows, PAIR), 1)
    return jnp.where(lanes < HEAD_DIM, stacked[:rows], stacked[rows:])


def attend_kernel(own, far, mixed_out, probs_out):
    queries = side_by_side(own[0, 0] * jnp.asarray(HEAD_DIM**-0.5, BF16))
    keys_in = jnp.concatenate([own[0, 1], far[0, 0]], axis=0)
    values_in = jnp.concatenate([own[0, 2], far[0, 1]], axis=0)
    scores = dot_nt(queries, keys_in)
    exponent = jnp.exp(scores - jnp.max(scores, axis=-1, keepdims=True))
    total = jnp.sum(exponent, axis=-1, keepdims=True)
    probs = (exponent * (1.0 / total)).astype(BF16)
    probs_out[0, 0] = probs
    mixed_out[0] = merge_heads(dot(probs, values_in)).astype(BF16)


def attend(joint, pairs_far):
    near, _, rows, width = joint.shape
    keys_count = 2 * rows
    pairs = width // PAIR
    return pl.pallas_call(
        attend_kernel,
        grid=(near, pairs),
        in_specs=[
            pl.BlockSpec((1, 3, rows, PAIR), lambda i, h: (i, 0, 0, h)),
            pl.BlockSpec((1, 2, rows, PAIR), lambda i, h: (i, 0, 0, h)),
        ],
        out_specs=[
            pl.BlockSpec((1, rows, PAIR), lambda i, h: (i, 0, h)),
            pl.BlockSpec((1, 1, 2 * rows, keys_count), lambda i, h: (i, h, 0, 0)),
        ],
        out_shape=[
            jax.ShapeDtypeStruct((near, rows, width), BF16),
            jax.ShapeDtypeStruct((near, pairs, 2 * rows, keys_count), BF16),
        ],
        compiler_params=params(32),
        cost_estimate=cost(8 * near * rows * keys_count * width, 20e6),
        name="attend",
    )(joint, pairs_far)


def attend_back_kernel(own, far, probs_in, upstream, query_out, own_out, far_out):
    rows = own.shape[2]
    scale = HEAD_DIM**-0.5
    queries = side_by_side(own[0, 0])
    keys_in = jnp.concatenate([own[0, 1], far[0, 0]], axis=0)
    values_in = jnp.concatenate([own[0, 2], far[0, 1]], axis=0)
    grad_mixed = side_by_side(upstream[0])
    probs = probs_in[0, 0]
    grad_probs = dot_nt(grad_mixed, values_in)
    wide = probs.astype(F32)
    weighted = wide * grad_probs
    inner = jnp.sum(weighted, axis=-1, keepdims=True)
    grad_scores = (weighted - wide * inner).astype(BF16)
    query_out[0] = (merge_heads(dot(grad_scores, keys_in)) * scale).astype(BF16)
    grad_values = dot_tn(probs, grad_mixed).astype(BF16)
    grad_keys = (dot_tn(grad_scores, queries) * scale).astype(BF16)
    own_out[0, 0] = grad_keys[:rows]
    own_out[0, 1] = grad_values[:rows]
    far_out[0, 0] = grad_keys[rows:]
    far_out[0, 1] = grad_values[rows:]


def attend_back(joint, pairs_far, probs, upstream):
    near, _, rows, width = joint.shape
    keys_count = 2 * rows
    pairs = width // PAIR
    two = pl.BlockSpec((1, 2, rows, PAIR), lambda i, h: (i, 0, 0, h))
    one = pl.BlockSpec((1, rows, PAIR), lambda i, h: (i, 0, h))
    return pl.pallas_call(
        attend_back_kernel,
        grid=(near, pairs),
        in_specs=[
            pl.BlockSpec((1, 3, rows, PAIR), lambda i, h: (i, 0, 0, h)),
            two,
            pl.BlockSpec((1, 1, 2 * rows, keys_count), lambda i, h: (i, h, 0, 0)),
            one,
        ],
        out_specs=[one, two, two],
        out_shape=[
            jax.ShapeDtypeStruct((near, rows, width), BF16),
            jax.ShapeDtypeStruct((near, 2, rows, width), BF16),
            jax.ShapeDtypeStruct((near, 2, rows, width), BF16),
        ],
        compiler_params=params(32),
        cost_estimate=cost(16 * near * rows * keys_count * width, 25e6),
        name="attend_back",
    )(joint, pairs_far, probs, upstream)


def rows_kernel(
    hidden,
    inverse,
    embedded_in,
    mixed,
    mask_in,
    target_own,
    target_far,
    output_weight,
    expand_weight,
    reduce_weight,
    pixel_weight,
    biases,
    expand_bias,
    input_out,
    active_out,
    after_out,
    pred_out,
    branch_out,
    expand_out,
    low_out,
    attn_out,
    mixed_out,
    sums_out,
    slope,
):
    output_bias, gain, shift, reduce_bias, pixel_bias = (biases[row : row + 1] for row in range(5))
    mask = mask_in[0]
    after_attn = embedded_in[0].astype(F32) + dot(mixed[0], output_weight[...]) + output_bias
    normed, scaling = normalize(after_attn)
    low = (normed * gain + shift).astype(BF16)
    input_out[0] = low
    total = after_attn + reduce_bias
    for start in range(0, hidden, WIDE):
        cut = slice(start, start + WIDE)
        active, rate = gelu_both(dot(low, expand_weight[:, cut]) + expand_bias[:, cut])
        active = active.astype(BF16)
        active_out[0, :, cut] = active
        slope[:, cut] = rate.astype(slope.dtype)
        total += dot(active, reduce_weight[cut, :])
    after_low = total.astype(BF16)
    after_out[0] = after_low
    target = jnp.concatenate([target_own[0], target_far[0]], axis=0).astype(F32)
    errors = dot(after_low, pixel_weight[...]) + pixel_bias - target
    square = errors * errors + 1.0
    root = lax.rsqrt(square)
    channel = jnp.sum((square * root - 1.0) * mask, axis=0, keepdims=True)
    grad_pred = (mask * errors * root * inverse[0, 0]).astype(BF16)
    pred_out[0] = grad_pred
    grad_mlp = dot_nt(grad_pred, pixel_weight[...])
    branch = grad_mlp.astype(BF16)
    branch_out[0] = branch
    grad_in = jnp.zeros_like(grad_mlp)
    expand_sums = []
    for start in range(0, hidden, WIDE):
        cut = slice(start, start + WIDE)
        grad_expand = dot_nt(branch, reduce_weight[cut, :]) * slope[:, cut].astype(F32)
        grad_expand = grad_expand.astype(BF16)
        expand_out[0, :, cut] = grad_expand
        expand_sums.append(column_sums(grad_expand))
        grad_in += dot_nt(grad_expand, expand_weight[:, cut])
    grad_attn = grad_mlp + normalize_back(grad_in, normed, scaling, gain)
    attn_out[0] = grad_attn
    grad_low = grad_attn.astype(BF16)
    low_out[0] = grad_low
    mixed_out[0] = dot_nt(grad_low, output_weight[...]).astype(BF16)
    sums = [
        column_sums(grad_pred),
        column_sums(branch),
        column_sums(grad_in * normed),
        column_sums(grad_in),
        column_sums(grad_low),
        channel,
    ] + expand_sums

    @pl.when(pl.program_id(0) == 0)
    def _():
        sums_out[...] = jnp.zeros_like(sums_out)

    for row, line in enumerate(sums):
        sums_out[row : row + 1] += line


def rows_step(
    inverse,
    embedded,
    mixed,
    mask,
    target_own,
    target_far,
    output_weight,
    expand_weight,
    reduce_weight,
    pixel_weight,
    biases,
    expand_bias,
):
    near, rows, width = embedded.shape
    quarter = target_own.shape[1]
    hidden = expand_weight.shape[1]
    block = pl.BlockSpec((1, rows, width), lambda i: (i, 0, 0))
    half = pl.BlockSpec((1, quarter, width), lambda i: (i, 0, 0))
    long = pl.BlockSpec((1, rows, hidden), lambda i: (i, 0, 0))
    narrow = jax.ShapeDtypeStruct((near, rows, width), BF16)
    broad = jax.ShapeDtypeStruct((near, rows, hidden), BF16)
    return pl.pallas_call(
        partial(rows_kernel, hidden),
        grid=(near,),
        in_specs=[
            pl.BlockSpec(memory_space=pltpu.SMEM),
            block,
            block,
            pl.BlockSpec((1, rows, 1), lambda i: (i, 0, 0)),
            half,
            half,
            fixed((width, width)),
            fixed((width, hidden)),
            fixed((hidden, width)),
            fixed((width, width)),
            fixed((8, width)),
            fixed((1, hidden)),
        ],
        out_specs=[block, long, block, block, block, long, block, block, block, fixed_out((16, width))],
        out_shape=[
            narrow,
            broad,
            narrow,
            narrow,
            narrow,
            broad,
            narrow,
            jax.ShapeDtypeStruct((near, rows, width), F32),
            narrow,
            jax.ShapeDtypeStruct((16, width), F32),
        ],
        scratch_shapes=[pltpu.VMEM((rows, hidden), F32)],
        compiler_params=params(56),
        cost_estimate=cost(4 * near * rows * width * (2 * width + 2 * hidden), 40e6),
        name="rows_step",
    )(
        inverse,
        embedded,
        mixed,
        mask,
        target_own,
        target_far,
        output_weight,
        expand_weight,
        reduce_weight,
        pixel_weight,
        biases,
        expand_bias,
    )


def fixed_out(shape):
    zeros = (0,) * len(shape)
    return pl.BlockSpec(shape, lambda *place: zeros)


def outer_kernel(left_moves, left, right, out, turned):
    if left_moves:
        out[...] = dot_tn(left[...], right[...]).astype(out.dtype)
        return

    @pl.when(pl.program_id(0) == 0)
    def _():
        turned[...] = left[...].T

    out[...] = dot(turned[...], right[...]).astype(out.dtype)


def outer(left, right):
    rows, tall = left.shape
    broad = right.shape[1]
    left_moves = tall > broad
    if left_moves:
        grid, specs = tall // WIDE, [
            pl.BlockSpec((rows, WIDE), lambda i: (0, i)),
            fixed((rows, broad)),
        ]
        out_spec = pl.BlockSpec((WIDE, broad), lambda i: (i, 0))
    else:
        grid, specs = broad // WIDE, [
            fixed((rows, tall)),
            pl.BlockSpec((rows, WIDE), lambda i: (0, i)),
        ]
        out_spec = pl.BlockSpec((tall, WIDE), lambda i: (0, i))
    return pl.pallas_call(
        partial(outer_kernel, left_moves),
        grid=(grid,),
        in_specs=specs,
        out_specs=out_spec,
        out_shape=jax.ShapeDtypeStruct((tall, broad), BF16),
        scratch_shapes=[pltpu.VMEM((WIDE, rows), BF16)],
        compiler_params=params(32),
        cost_estimate=cost(2 * rows * tall * broad, 2 * (rows * (tall + broad) + tall * broad)),
        name="outer",
    )(left, right)


def project_back_kernel(
    query, own, received, embedded_in, attn, mask_in, gain, shift, weight,
    input_out, joint_out, near_out, far_out, sums_out,
):
    quarter = near_out.shape[1]
    mask = mask_in[0]
    embedded = embedded_in[0].astype(F32)
    normed, scaling = normalize(embedded)
    input_out[0] = (normed * gain[...] + shift[...]).astype(BF16)
    grad_query = query[0]
    grad_key = (own[0, 0].astype(F32) + received[0, 0].astype(F32)).astype(BF16)
    grad_value = (own[0, 1].astype(F32) + received[0, 1].astype(F32)).astype(BF16)
    grad_in = None
    for part, grad in enumerate((grad_query, grad_key, grad_value)):
        joint_out[part, 0] = grad
        term = dot_nt(grad, weight[:, part * WIDE : (part + 1) * WIDE])
        grad_in = term if grad_in is None else grad_in + term
    grad_embedded = attn[0] + normalize_back(grad_in, normed, scaling, gain[...])
    kept = grad_embedded * (1.0 - mask)
    near_out[0] = kept[:quarter]
    far_out[0] = kept[quarter:].astype(BF16)
    sums = [
        column_sums(grad_in * normed),
        column_sums(grad_in),
        column_sums(grad_query),
        column_sums(grad_value),
        column_sums(grad_embedded * mask),
    ]

    @pl.when(pl.program_id(0) == 0)
    def _():
        sums_out[...] = jnp.zeros_like(sums_out)

    for row, line in enumerate(sums):
        sums_out[row : row + 1] += line


def project_back(query, own, received, embedded, attn, mask, gain, shift, weight):
    near, rows, width = embedded.shape
    quarter = rows // 2
    block = pl.BlockSpec((1, rows, width), lambda i: (i, 0, 0))
    half = pl.BlockSpec((1, quarter, width), lambda i: (i, 0, 0))
    two = pl.BlockSpec((1, 2, rows, width), lambda i: (i, 0, 0, 0))
    return pl.pallas_call(
        project_back_kernel,
        grid=(near,),
        in_specs=[
            block,
            two,
            two,
            block,
            block,
            pl.BlockSpec((1, rows, 1), lambda i: (i, 0, 0)),
            fixed((1, width)),
            fixed((1, width)),
            fixed((width, 3 * width)),
        ],
        out_specs=[
            block,
            pl.BlockSpec((3, 1, rows, width), lambda i: (0, i, 0, 0)),
            half,
            half,
            fixed_out((8, width)),
        ],
        out_shape=[
            jax.ShapeDtypeStruct((near, rows, width), BF16),
            jax.ShapeDtypeStruct((3, near, rows, width), BF16),
            jax.ShapeDtypeStruct((near, quarter, width), F32),
            jax.ShapeDtypeStruct((near, quarter, width), BF16),
            jax.ShapeDtypeStruct((8, width), F32),
        ],
        compiler_params=params(40),
        cost_estimate=cost(2 * near * rows * width * 3 * width, 20e6),
        name="project_back",
    )(query, own, received, embedded, attn, mask, gain, shift, weight)


def swap(values, axis, bit):
    size = lax.axis_size(axis)
    return lax.ppermute(values, axis, [(place, place ^ bit) for place in range(size)])


def own_bit(axis, bit):
    return (lax.axis_index(axis) // bit) % 2


def pick(values, dim, which):
    return lax.dynamic_index_in_dim(values, which, dim, keepdims=False)


def add_in(kept, received):
    return (kept.astype(jnp.float32) + received.astype(jnp.float32)).astype(kept.dtype)


def halve(values, dim, axis, bit):
    mine = own_bit(axis, bit)
    received = swap(pick(values, dim, 1 - mine), axis, bit)
    return add_in(pick(values, dim, mine), received)


def join(values, dim, axis, bit):
    mine = own_bit(axis, bit)
    received = swap(values, axis, bit)
    first = jnp.where(mine == 0, values, received)
    second = jnp.where(mine == 0, received, values)
    return jnp.concatenate([first, second], axis=dim)


def reduce_rows(grad, order):
    dp = lax.axis_size("dp")
    rows, columns = grad.shape
    steps = dp.bit_length() - 1
    part = rows // dp
    if columns % 512 == 0:
        tail = (1, 2, part, 2, columns // 4, 2)
        parts = grad.reshape((2,) * steps + (part, 4, columns // 4))
        parts = jnp.moveaxis(parts, steps + 1, 0)
    else:
        parts = grad.reshape((2,) * steps + (4, part // 4, columns))
        parts = jnp.moveaxis(parts, steps, 0)
    parts = parts.reshape((2, 2) + parts.shape[1:])
    names = ["core", "y"] + [1 << bit for bit in reversed(range(steps))]
    for name in order(steps):
        dim = names.index(name)
        if name == "core":
            parts = halve(parts, dim, "seq", 1)
        elif name == "y":
            parts = halve(parts, dim, "seq", 2)
        else:
            parts = halve(parts, dim, "dp", name)
        names.pop(dim)
    parts = join(parts[None], 0, "seq", 2)
    parts = join(parts[None], 0, "seq", 1)
    parts = parts.reshape((4,) + parts.shape[2:]).astype(jnp.float32)
    if columns % 512 == 0:
        return jnp.moveaxis(parts, 0, 1).reshape(part, columns)
    return parts.reshape(part, columns)


def x_first(steps):
    return ["core"] + [1 << bit for bit in range(steps)] + ["y"]


def y_first(steps):
    return ["core", "y"] + [1 << bit for bit in range(steps)]


def z_first(steps):
    return ["core"] + [1 << bit for bit in range(1, steps)] + [1, "y"]


def reduce_vector(values):
    dp = lax.axis_size("dp")
    steps = dp.bit_length() - 1
    values = values + swap(values, "seq", 1)
    values = values + swap(values, "seq", 2)
    values = values.reshape((2,) * steps + values.shape[1:])
    for bit in reversed(range(steps)):
        mine = own_bit("dp", 1 << bit)
        received = swap(pick(values, 0, 1 - mine), "dp", 1 << bit)
        values = pick(values, 0, mine) + received
    return values


def any_places(
    patches,
    targets,
    mask_order,
    mask_count,
    attend_gain,
    attend_shift,
    joint_weight,
    query_bias,
    value_bias,
    output_weight,
    output_bias,
    feed_gain,
    feed_shift,
    expand_weight,
    expand_bias,
    reduce_weight,
    reduce_bias,
    pixel_weight,
    pixel_bias,
    mask_token,
):
    images, quarter, features = patches.shape
    dp = lax.axis_size("dp")
    near = images // 2
    rows_one = 2 * quarter
    row_count = near * rows_one
    place_y = own_bit("seq", 2)

    def own_and_far(values):
        parts = values.reshape((2, near) + values.shape[1:])
        return pick(parts, 0, place_y), swap(pick(parts, 0, 1 - place_y), "seq", 2)

    def line(vector):
        return vector.astype(F32)[None, :]

    masked_here = mask_order < mask_count[:, None]
    embedded_here = jnp.where(masked_here[:, :, None], mask_token[None, None, :], patches)
    embedded_own, embedded_far = own_and_far(embedded_here)
    mask = jnp.concatenate(own_and_far(masked_here.astype(jnp.int32)), axis=1)
    mask = mask.astype(F32)[:, :, None]
    count_sum = jnp.sum(mask_count)
    for bit in range(dp.bit_length() - 1):
        count_sum = count_sum + swap(count_sum, "dp", 1 << bit)
    inverse = 1.0 / (count_sum.astype(F32) * PIXELS)
    target_own, target_far = own_and_far(targets)
    joint_bias = jnp.concatenate(
        [line(query_bias), jnp.zeros((1, features), F32), line(value_bias)], axis=1
    )
    biases = jnp.concatenate(
        [
            line(vector)
            for vector in (output_bias, feed_gain, feed_shift, reduce_bias, pixel_bias)
        ]
        + [jnp.zeros((3, features), F32)],
        axis=0,
    )
    embedded, joint = project(
        embedded_own, embedded_far, line(attend_gain), line(attend_shift), joint_weight, joint_bias
    )
    pairs_far = swap(joint[:, 1:], "seq", 1)
    mixed, probs = attend(joint, pairs_far)
    (
        input_two,
        activated,
        after_low,
        grad_pred,
        grad_branch,
        grad_expand,
        grad_out,
        grad_attn,
        grad_mixed,
        sums_two,
    ) = rows_step(
        inverse.reshape(1, 1),
        embedded,
        mixed,
        mask,
        target_own,
        target_far,
        output_weight,
        expand_weight,
        reduce_weight,
        pixel_weight,
        biases,
        line(expand_bias),
    )

    def flat(values):
        return values.reshape(row_count, values.shape[-1])

    reduce_weight_grad = outer(flat(activated), flat(grad_branch))
    expand_weight_grad = outer(flat(input_two), flat(grad_expand))
    pixel_weight_grad = outer(flat(after_low), flat(grad_pred))
    output_weight_grad = outer(flat(mixed), flat(grad_out))
    square_grads = jnp.concatenate([pixel_weight_grad, output_weight_grad], axis=1)
    grad_query, grad_own, grad_far = attend_back(joint, pairs_far, probs, grad_mixed)
    received = swap(grad_far, "seq", 1)
    input_one, grad_joint, patch_near, patch_far, sums_one = project_back(
        grad_query,
        grad_own,
        received,
        embedded,
        grad_attn,
        mask,
        line(attend_gain),
        line(attend_shift),
        joint_weight,
    )
    grad_joint = grad_joint.reshape(3, row_count, features)
    joint_weight_grad = jnp.concatenate(
        [outer(flat(input_one), grad_joint[part]) for part in range(3)], axis=1
    )
    patch_far = swap(patch_far, "seq", 2).astype(F32)
    patch_grad = jnp.concatenate(
        [
            jnp.where(place_y == 0, patch_near, patch_far),
            jnp.where(place_y == 0, patch_far, patch_near),
        ],
        axis=0,
    )
    hidden = expand_bias.shape[0]
    vectors = (
        sums_one[0],
        sums_one[1],
        sums_one[2],
        sums_one[3],
        sums_two[4],
        sums_two[2],
        sums_two[3],
        sums_two[6 : 6 + hidden // features].reshape(hidden),
        sums_two[1],
        sums_two[0],
        sums_one[4],
    )
    loss_part = jnp.sum(sums_two[5]) * inverse
    lengths = [vector.shape[0] // dp for vector in vectors]
    packed = jnp.concatenate(
        [vector.reshape(dp, -1) for vector in vectors]
        + [jnp.broadcast_to(loss_part[None, None], (dp, 1))],
        axis=1,
    )
    packed = reduce_vector(packed)
    loss_value = packed[-1]
    cuts, start = [], 0
    for length in lengths:
        cuts.append(packed[start : start + length])
        start += length
    (
        attend_gain_grad,
        attend_shift_grad,
        query_bias_grad,
        value_bias_grad,
        output_bias_grad,
        feed_gain_grad,
        feed_shift_grad,
        expand_bias_grad,
        reduce_bias_grad,
        pixel_bias_grad,
        mask_token_grad,
    ) = cuts
    reduce_weight_grad = reduce_rows(reduce_weight_grad, x_first)
    expand_weight_grad = reduce_rows(expand_weight_grad, y_first)
    square_grads = reduce_rows(square_grads, z_first)
    joint_weight_grad = reduce_rows(joint_weight_grad, x_first)
    return (
        loss_value,
        attend_gain_grad,
        attend_shift_grad,
        joint_weight_grad,
        query_bias_grad,
        value_bias_grad,
        square_grads[:, PIXELS:],
        output_bias_grad,
        feed_gain_grad,
        feed_shift_grad,
        expand_weight_grad,
        expand_bias_grad,
        reduce_weight_grad,
        reduce_bias_grad,
        square_grads[:, :PIXELS],
        pixel_bias_grad,
        mask_token_grad,
        patch_grad,
    )


MESH = pl.DeviceIdType.MESH


def places():
    data, seq = lax.axis_index("dp"), lax.axis_index("seq")
    x, low, high = lax.rem(data, 2), lax.rem(lax.div(data, 2), 2), lax.div(data, 4)
    core, y = lax.rem(seq, 2), lax.div(seq, 2)
    return {
        "x": (x, {"dp": data + 1 - 2 * x}),
        "low": (low, {"dp": data + 2 - 4 * low}),
        "high": (high, {"dp": data + 4 - 8 * high}),
        "y": (y, {"seq": seq + 2 - 4 * y}),
        "core": (core, {"seq": seq + 1 - 2 * core}),
    }


def greet(where):
    barrier = pltpu.get_barrier_semaphore()
    for _, partner in where.values():
        pl.semaphore_signal(barrier, inc=1, device_id=partner, device_id_type=MESH)
    pl.semaphore_wait(barrier, len(where))


def remote(source, target, send, receive, partner):
    return pltpu.make_async_remote_copy(
        src_ref=source,
        dst_ref=target,
        send_sem=send,
        recv_sem=receive,
        device_id=partner,
        device_id_type=MESH,
    )


NAMES = ("high", "low", "x", "y")


def names_of(order):
    halved = [token for token in order if token in NAMES]
    return tuple(halved + [name for name in NAMES if name not in halved])


def stage_shapes(names, order, tail):
    names, shapes = list(names), []
    for token in order:
        if token == "Gy":
            names = ["y"]
        elif token == "Gcore":
            names = ["core"] + names
        elif token[0] != "+":
            names.remove(token)
        shapes.append((2,) * len(names) + tail)
    return shapes


def for_each(dims, body):
    outer = max(dims - 2, 0)
    inner = list(itertools.product(range(2), repeat=dims - outer))
    if outer == 0:
        for spot in inner:
            body(spot)
        return

    def one(place, carry):
        first = tuple(lax.rem(lax.div(place, 2 ** (outer - 1 - dim)), 2) for dim in range(outer))
        for spot in inner:
            body(first + spot)
        return carry

    lax.fori_loop(0, 2**outer, one, 0)


def add_up(target, place, other):
    target[place] = target[place] + other


class Chain:
    def __init__(self, where, start, names, order, buffers, send, receive, base, swapped=None):
        self.where, self.order = dict(where), order
        if swapped is not None:
            (first, partner_first), (second, partner_second) = (where[name] for name in swapped)
            core = where["core"][0]

            def chosen(zero, one):
                return zero + core * (one - zero)

            for name, place, ours, other in (
                (swapped[0], (first, second), partner_first, partner_second),
                (swapped[1], (second, first), partner_second, partner_first),
            ):
                here = {"dp": lax.axis_index("dp"), "seq": lax.axis_index("seq")}
                ours, other = {**here, **ours}, {**here, **other}
                partner = {axis: chosen(ours[axis], other[axis]) for axis in here}
                self.where[name] = (chosen(*place), partner)
        self.plain = where
        self.refs = [start] + list(buffers)
        self.send, self.receive, self.base = send, receive, base
        self.names = [list(names)]
        for token in order:
            names = list(self.names[-1])
            if token == "Gy":
                names = ["y"]
            elif token == "Gcore":
                names = ["core"] + names
            elif token[0] != "+":
                names.remove(token)
            self.names.append(names)

    def copy(self, stage):
        token = self.order[stage]
        source, target = self.refs[stage], self.refs[stage + 1]
        if token[0] == "+":
            _, partner = self.plain[token[1:]]
        elif token[0] == "G":
            place, partner = self.plain[token[1:]]
            target = target.at[place]
        else:
            place, partner = self.where[token]
            dim = self.names[stage].index(token)
            source = source.at[(slice(None),) * dim + (1 - place,)]
        spot = self.base + stage
        return remote(source, target, self.send.at[spot], self.receive.at[spot], partner)

    def start(self, stage):
        self.copy(stage).start()

    def finish(self, stage):
        self.copy(stage).wait()
        token = self.order[stage]
        source, target = self.refs[stage], self.refs[stage + 1]
        if token[0] == "G":
            place, _ = self.plain[token[1:]]
            target[place] = source[...]
            return
        dim = None
        if token[0] != "+":
            place, _ = self.where[token]
            dim = self.names[stage].index(token)

        def one(spot):
            origin = spot if dim is None else spot[:dim] + (place,) + spot[dim:]
            add_up(target, spot if spot else Ellipsis, source[origin if origin else Ellipsis])

        for_each(len(self.names[stage + 1]), one)

    def turn(self, stage):
        if stage > 0:
            self.finish(stage - 1)
        if stage < len(self.order):
            self.start(stage)


Y_FIRST = ("y", "x", "low", "high", "Gy", "Gcore")
Y_THEN_LOW = ("y", "low", "x", "high", "Gy", "Gcore")
X_FIRST = ("x", "low", "high", "+y", "Gcore")
SUMS_ORDER = ("+core", "+y", "+x", "+low", "+high")
MOST = 6
TILE_ORDERS = (
    Y_FIRST,
    X_FIRST,
    Y_THEN_LOW,
    Y_FIRST,
    Y_THEN_LOW,
    X_FIRST,
    Y_FIRST,
    X_FIRST,
    Y_THEN_LOW,
    Y_FIRST,
    Y_FIRST,
    Y_FIRST,
    X_FIRST,
)
TILE_SWAPS = (
    ("x", "y"),
    ("x", "low"),
    ("y", "low"),
    ("x", "y"),
    ("y", "low"),
    ("x", "low"),
    ("x", "y"),
    ("x", "low"),
    ("y", "low"),
    ("x", "y"),
    ("x", "y"),
    ("x", "y"),
    ("x", "low"),
)
TILES = len(TILE_ORDERS)
TILE_STEPS = (0, 1, 2, 3, 4, 5, 6, 7, 8, 9, 14, 18, 21)
TURNS = {
    2: ((0, 0),),
    3: ((1, 0),),
    4: ((0, 1), (2, 0),),
    5: ((1, 1), (3, 0),),
    6: ((0, 2), (4, 0),),
    7: ((1, 2), (2, 1), (3, 1), (5, 0),),
    8: ((0, 3), (6, 0),),
    9: ((1, 3), (3, 2), (7, 0),),
    10: ((0, 4), (1, 4), (2, 2), (4, 1), (6, 1), (8, 0), (13, 0), (3, 3),),
    11: ((1, 5), (5, 1), (13, 1), (9, 0), (0, 5),),
    12: ((0, 6), (3, 4), (2, 3), (7, 1),),
    13: ((4, 2), (6, 2), (13, 2),),
    14: ((3, 5), (2, 4), (5, 2),),
    15: ((3, 6), (2, 5), (4, 3), (6, 3), (13, 3), (7, 2), (8, 1), (9, 1),),
    16: ((2, 6), (5, 3), (10, 0),),
    18: ((4, 4), (5, 4), (6, 4), (13, 4), (7, 3), (8, 2), (9, 2),),
    19: ((4, 5), (5, 5), (6, 5), (13, 5), (8, 3), (10, 1),),
    20: ((4, 6), (6, 6), (7, 4), (9, 3), (11, 0),),
    21: ((7, 5), (8, 4), (10, 2),),
    22: ((8, 5), (9, 4), (10, 3), (11, 1),),
}
LAST_TURNS = (
    (14, 0),
    (8, 6),
    (9, 5),
    (10, 4),
    (11, 2),
    (14, 1),
    (9, 6),
    (11, 3),
    (14, 2),
    (10, 5),
    (12, 1),
    (10, 6),
    (14, 3),
    (11, 4),
    (12, 2),
    (14, 4),
    (11, 5),
    (14, 5),
    (11, 6),
    (12, 3),
    (12, 4),
    (12, 5),
)


def chain_scratch(cases):
    scratch, counts = [], []
    for names, order, tail, dtype in cases:
        shapes = stage_shapes(names, order, tail)
        scratch += [pltpu.VMEM(shape, dtype) for shape in shapes]
        counts.append(len(shapes))
    return scratch, counts


def split_list(values, counts):
    parts, start = [], 0
    for count in counts:
        parts.append(values[start : start + count])
        start += count
    return parts


GAIN_ONE, SHIFT_ONE, QUERY, VALUE, OUTPUT, GAIN_TWO, SHIFT_TWO, REDUCE, PIXEL, TOKEN, EXPAND = range(11)
FRONT_OWN = 9
FRONT_FAR = 12
FRONT_ATTEND = 15
FRONT_PAIRS = 3


def lines_kernel(*refs):
    out = refs[-1]
    row = 0
    for ref in refs[:-1]:
        for start in range(0, ref.shape[0], WIDE):
            out[row : row + 1] = ref[start : start + WIDE].astype(F32).reshape(1, WIDE)
            row += 1


def stack_lines(*vectors):
    return pl.pallas_call(
        lines_kernel,
        in_specs=[pl.BlockSpec(memory_space=pltpu.VMEM)] * len(vectors),
        out_specs=pl.BlockSpec(memory_space=pltpu.VMEM),
        out_shape=jax.ShapeDtypeStruct((16, WIDE), F32),
        cost_estimate=cost(1e4, 1e5),
        name="stack_lines",
    )(*vectors)


def column_of(line):
    count = line.shape[1]
    down = lax.broadcasted_iota(jnp.int32, (count, count), 0)
    along = lax.broadcasted_iota(jnp.int32, (count, count), 1)
    return jnp.sum(jnp.where(down == along, jnp.broadcast_to(line, (count, count)), 0.0), axis=1, keepdims=True)


def front_kernel(
    parts, counts, rows_in, targets_in, orders_in, lines, weight_in, pixel_in, expand_in, output_in,
    embedded_out, input_out, joint_out, pairs_out, mixed_out, probs_out, masks_out, target_out, expand_out,
    embedded, inputs, masks, order_far, joint, pairs, weight, pixel, expand, output,
    local, far_send, far_receive, send, receive,
):
    images, heads = joint.shape[:2]
    quarter = rows_in.shape[2]
    where = {name: places()[name] for name in ("core", "y")}
    sibling = where["core"][1]
    y, other = where["y"]
    step = pl.program_id(0)
    near_half, far_half = pl.ds(0, quarter), pl.ds(quarter, quarter)

    def pair_copy(image):
        return remote(
            joint.at[image, :, pl.ds(1, 2)], pairs.at[image], send.at[image], receive.at[image], sibling
        )

    def far_copy(index, source, target):
        return remote(source, target, far_send.at[index], far_receive.at[index], other)

    order_copy = far_copy(0, orders_in, order_far)
    row_copies = [
        far_copy(1 + image, rows_in.at[1 - y, image], embedded.at[image, far_half]) for image in range(images)
    ]
    target_copies = [
        far_copy(1 + images + image, targets_in.at[1 - y, image], target_out.at[image, far_half])
        for image in range(images)
    ]
    own_copy = pltpu.make_async_copy(rows_in.at[y], embedded.at[:, near_half], local.at[0])
    target_copy = pltpu.make_async_copy(targets_in.at[y], target_out.at[:, near_half], local.at[1])
    loads = [
        pltpu.make_async_copy(source, target, local.at[2 + index])
        for index, (source, target) in enumerate(
            ((pixel_in, pixel), (expand_in, expand), (output_in, output), (weight_in, weight))
        )
    ]

    @pl.when(step == 0)
    def _():
        own_copy.start()
        greet(where)
        order_copy.start()
        for copy in row_copies + loads:
            copy.start()
        target_copy.start()
        loads[0].wait()
        expand_out[0] = pixel[...]

    @pl.when(step == parts + 1)
    def _():
        loads[2].wait()
        expand_out[0] = output[...]

    for part in range(parts):

        @pl.when(step == 1 + part)
        def _(part=part):
            if part == 0:
                loads[1].wait()
            span = weight.shape[0] // 8
            starts = [place * parts * span + part * span for place in range(8)]
            expand_out[0] = jnp.concatenate([expand[:, start : start + span] for start in starts], axis=1)

    for group in range(3):

        @pl.when(step == parts + 2 + group)
        def _(group=group):
            if group == 0:
                loads[3].wait()
            starts = [part * WIDE + group * 2 * PAIR for part in range(3)]
            expand_out[0] = jnp.concatenate([weight[:, start : start + 2 * PAIR] for start in starts], axis=1)

    def project(image, start, order):
        block = pl.ds(start, quarter)
        mask = column_of((order < counts[y * images + image]).astype(F32))
        masks[image, block] = mask
        token = lines[TOKEN : TOKEN + 1].astype(BF16)
        rows = jnp.where(mask > 0.5, token, embedded[image, block])
        embedded[image, block] = rows
        normed, _ = normalize(rows.astype(F32))
        gain, shift = lines[GAIN_ONE : GAIN_ONE + 1], lines[SHIFT_ONE : SHIFT_ONE + 1]
        low = (normed * gain + shift).astype(BF16)
        inputs[image, block] = low
        for part, bias in ((1, None), (2, lines[VALUE : VALUE + 1]), (0, lines[QUERY : QUERY + 1])):
            total = dot(low, weight[:, part * WIDE : (part + 1) * WIDE])
            total = (total if bias is None else total + bias).astype(BF16)
            for pair in range(heads):
                joint[image, pair, part, block] = total[:, pair * PAIR : (pair + 1) * PAIR]

    @pl.when((step >= FRONT_OWN) & (step < FRONT_FAR))
    def _():
        @pl.when(step == FRONT_OWN)
        def _():
            own_copy.wait()

        image = step - FRONT_OWN
        project(image, 0, orders_in[pl.ds(y * images + image, 1)])

    @pl.when((step >= FRONT_FAR) & (step < FRONT_ATTEND))
    def _():
        for index in range(images):

            @pl.when(step == FRONT_FAR + index)
            def _(index=index):
                if index == 0:
                    order_copy.wait()
                row_copies[index].wait()
                target_copies[index].start()

        image = step - FRONT_FAR
        project(image, quarter, order_far[pl.ds(y * images + image, 1)])
        pair_copy(image).start()
        embedded_out[0] = embedded[image]
        input_out[0] = inputs[image]
        joint_out[0] = joint[image]
        masks_out[0] = masks[image]

    def attend(image, pair, index):
        queries = side_by_side(joint[image, pair, 0] * jnp.asarray(HEAD_DIM**-0.5, BF16))
        keys_in = jnp.concatenate([joint[image, pair, 1], pairs[image, pair, 0]], axis=0)
        values_in = jnp.concatenate([joint[image, pair, 2], pairs[image, pair, 1]], axis=0)
        pairs_out[0, index] = pairs[image, pair]
        scores = dot_nt(keys_in, queries)
        exponent = jnp.exp(scores - jnp.max(scores, axis=0, keepdims=True))
        total = jnp.sum(exponent, axis=0, keepdims=True)
        probs = (exponent * (1.0 / total)).astype(BF16)
        probs_out[0, index] = probs
        mixed = merge_turned(dot_tn(values_in, probs)).astype(BF16)
        mixed_out[0, :, index * PAIR : (index + 1) * PAIR] = mixed

    @pl.when(step >= FRONT_ATTEND)
    def _():
        place = step - FRONT_ATTEND
        turns = heads // FRONT_PAIRS
        image, turn = lax.div(place, turns), lax.rem(place, turns)

        @pl.when(turn == 0)
        def _():
            pair_copy(image).wait()

        for index in range(FRONT_PAIRS):
            attend(image, turn * FRONT_PAIRS + index, index)

    @pl.when(step == pl.num_programs(0) - 1)
    def _():
        for copy in target_copies:
            copy.wait()
        target_copy.wait()


def merge_turned(stacked):
    rows = stacked.shape[1] // 2
    down = lax.broadcasted_iota(jnp.int32, (PAIR, rows), 0)
    return jnp.where(down < HEAD_DIM, stacked[:, :rows], stacked[:, rows:]).T


def front(counts, rows_in, targets_in, orders_in, lines, weight, pixel, expand, output):
    near, quarter, width = rows_in.shape[1:]
    rows, heads = 2 * quarter, width // PAIR
    parts = expand.shape[1] // width

    def image(step):
        return jnp.clip(step - FRONT_FAR, 0, near - 1)

    turns = heads // FRONT_PAIRS

    def spot(step):
        place = jnp.maximum(step - FRONT_ATTEND, 0)
        return lax.div(place, turns), lax.rem(place, turns)

    block = pl.BlockSpec((1, rows, width), lambda s: (image(s), 0, 0))
    return pl.pallas_call(
        partial(front_kernel, parts),
        grid=(FRONT_ATTEND + near * turns,),
        in_specs=[
            pl.BlockSpec(memory_space=pltpu.SMEM),
            pl.BlockSpec(memory_space=pl.ANY),
            pl.BlockSpec(memory_space=pl.ANY),
            fixed(orders_in.shape),
            fixed(lines.shape),
        ]
        + [pl.BlockSpec(memory_space=pl.ANY)] * 4,
        out_specs=[
            block,
            block,
            pl.BlockSpec((1, heads, 3, rows, PAIR), lambda s: (image(s), 0, 0, 0, 0)),
            pl.BlockSpec((1, FRONT_PAIRS, 2, rows, PAIR), lambda s: spot(s) + (0, 0, 0)),
            pl.BlockSpec((1, rows, FRONT_PAIRS * PAIR), lambda s: (spot(s)[0], 0, spot(s)[1])),
            pl.BlockSpec((1, FRONT_PAIRS, 2 * rows, 2 * rows), lambda s: spot(s) + (0, 0)),
            pl.BlockSpec((1, rows, 1), lambda s: (image(s), 0, 0)),
            pl.BlockSpec(memory_space=pl.ANY),
            pl.BlockSpec((1, width, width), lambda s: (jnp.minimum(s, parts + 4), 0, 0)),
        ],
        out_shape=[
            jax.ShapeDtypeStruct((near, rows, width), BF16),
            jax.ShapeDtypeStruct((near, rows, width), BF16),
            jax.ShapeDtypeStruct((near, heads, 3, rows, PAIR), BF16),
            jax.ShapeDtypeStruct((near, heads, 2, rows, PAIR), BF16),
            jax.ShapeDtypeStruct((near, rows, width), BF16),
            jax.ShapeDtypeStruct((near, heads, 2 * rows, 2 * rows), BF16),
            jax.ShapeDtypeStruct((near, rows, 1), F32),
            jax.ShapeDtypeStruct((near, rows, width), BF16),
            jax.ShapeDtypeStruct((parts + 5, width, width), BF16),
        ],
        scratch_shapes=[
            pltpu.VMEM((near, rows, width), BF16),
            pltpu.VMEM((near, rows, width), BF16),
            pltpu.VMEM((near, rows, 1), F32),
            pltpu.VMEM(orders_in.shape, jnp.int32),
            pltpu.VMEM((near, heads, 3, rows, PAIR), BF16),
            pltpu.VMEM((near, heads, 2, rows, PAIR), BF16),
            pltpu.VMEM(weight.shape, BF16),
            pltpu.VMEM(pixel.shape, BF16),
            pltpu.VMEM(expand.shape, BF16),
            pltpu.VMEM(output.shape, BF16),
            pltpu.SemaphoreType.DMA((6,)),
            pltpu.SemaphoreType.DMA((1 + 2 * near,)),
            pltpu.SemaphoreType.DMA((1 + 2 * near,)),
            pltpu.SemaphoreType.DMA((near,)),
            pltpu.SemaphoreType.DMA((near,)),
        ],
        compiler_params=pltpu.CompilerParams(
            vmem_limit_bytes=60 * MIB, collective_id=1, has_side_effects=True
        ),
        cost_estimate=cost(5e9, 40e6),
        name="front",
    )(counts, rows_in, targets_in, orders_in, lines, weight, pixel, expand, output)


def middle_kernel(
    embedded_in, mixed, mask_in, target_in, weights, reduce, lines,
    sides, input_out, scaling_out, sums_out, low, total, biases,
):
    parts = reduce.shape[1]
    span = reduce.shape[2]
    width = weights.shape[1]
    mask = mask_in[0]

    @pl.when(pl.program_id(0) == 0)
    def _():
        sums_out[...] = jnp.zeros_like(sums_out)
        for part in range(parts):
            pieces = []
            for place in range(8):
                row, start = divmod((place * parts + part) * span, width)
                pieces.append(lines[EXPAND + row : EXPAND + row + 1, start : start + span])
            biases[part] = jnp.concatenate(pieces, axis=1)

    after_attn = embedded_in[0].astype(F32) + dot(mixed[0], weights[parts + 1]) + lines[OUTPUT : OUTPUT + 1]
    sides[0, 0, parts + 1] = mixed[0]
    normed, scaling = normalize(after_attn)
    sides[0, 1, parts + 1] = normed.astype(BF16)
    scaling_out[0] = scaling
    low[...] = (normed * lines[GAIN_TWO : GAIN_TWO + 1] + lines[SHIFT_TWO : SHIFT_TWO + 1]).astype(BF16)
    input_out[0] = low[...]
    total[...] = after_attn + lines[REDUCE : REDUCE + 1]

    def one(part, carry):
        active, rate = gelu_both(dot(low[...], weights[1 + part]) + biases[part])
        active = active.astype(BF16)
        sides[0, 0, 1 + part] = active
        sides[0, 1, 1 + part] = rate.astype(BF16)
        total[...] += dot(active, reduce[:, part].reshape(width, width))
        return carry

    for part in range(parts):
        one(part, 0)
    after_low = total[...].astype(BF16)
    sides[0, 0, 0] = after_low
    errors = dot(after_low, weights[0]) + lines[PIXEL : PIXEL + 1] - target_in[0].astype(F32)
    square = errors * errors + 1.0
    root = lax.rsqrt(square)
    grad_pred = (mask * errors * root).astype(BF16)
    sides[0, 1, 0] = grad_pred
    sums_out[0:1] += column_sums(grad_pred)
    sums_out[5:6] += jnp.sum((square * root - 1.0) * mask, axis=0, keepdims=True)
    sums_out[10:11] += jnp.sum(jnp.broadcast_to(mask, errors.shape), axis=0, keepdims=True)


def middle(embedded, mixed, mask, targets, weights, reduce, lines):
    near, rows, width = embedded.shape
    parts = reduce.shape[1]
    block = pl.BlockSpec((1, rows, width), lambda i: (i, 0, 0))
    column = pl.BlockSpec((1, rows, 1), lambda i: (i, 0, 0))
    stack = pl.BlockSpec((1, 2, parts + 2, rows, width), lambda i: (i, 0, 0, 0, 0))
    return pl.pallas_call(
        middle_kernel,
        grid=(near,),
        in_specs=[
            block,
            block,
            column,
            block,
            fixed((parts + 2, width, width)),
            fixed(reduce.shape),
            fixed(lines.shape),
        ],
        out_specs=[stack, block, column, fixed_out((16, width))],
        out_shape=[
            jax.ShapeDtypeStruct((near, 2, parts + 2, rows, width), BF16),
            jax.ShapeDtypeStruct((near, rows, width), BF16),
            jax.ShapeDtypeStruct((near, rows, 1), F32),
            jax.ShapeDtypeStruct((16, width), F32),
        ],
        scratch_shapes=[
            pltpu.VMEM((rows, width), BF16),
            pltpu.VMEM((rows, width), F32),
            pltpu.VMEM((parts, 1, width), F32),
        ],
        compiler_params=params(60),
        cost_estimate=cost(2 * near * rows * width * width * (2 * parts + 2), 40e6),
        name="middle",
    )(embedded, mixed, mask, targets, weights, reduce, lines)


HIGH_ROWS = 4 * 96


def spread_half(result, target, high, start, names, swapped):
    for low in range(2):
        for x in range(2):
            for y in range(2):
                at = (low * 2 + x) * 96 + start
                piece = result[at : at + HALF, y * 384 : (y + 1) * 384]
                spot = {"high": high, "low": low, "x": x, "y": y}
                if swapped is not None:
                    first, second = swapped
                    spot[first], spot[second] = spot[second], spot[first]
                target[tuple(spot[name] for name in names)] = piece.astype(BF16)


HALF = 48
SLOTS = 4
KEPT = 10
FIRST_ATTEND = 10
GROUP_STEPS = (14, 18, 21)
FIRST_NORM = 22


def back_kernel(
    counts, sides, weights, reduce, input_two, scaling_two, input_one, joint, pairs, probs_in, lines, sums_in,
    embedded_in, mask_in, *rest,
):
    (
        done_out,
        near_out,
        far_out,
        sums_out,
        late_out,
        done,
        done_sent,
        branch,
        wide,
        grad_in,
        upstream,
        own_pairs,
        give_pairs,
        got_pairs,
        far_give,
        sums,
        late,
        keep,
        give,
        got,
        send,
        receive,
        core_send,
        core_receive,
        pair_send,
        pair_receive,
        far_send,
        far_receive,
    ) = rest[:28]
    buffers = split_list(rest[28:], counts)
    where = places()
    core, sibling = where["core"]
    step = pl.program_id(0)
    images, rows, width = input_two.shape
    every = images * rows
    quarter = rows // 2
    heads = width // PAIR
    first_gain, second_gain = lines[GAIN_ONE : GAIN_ONE + 1], lines[GAIN_TWO : GAIN_TWO + 1]
    chains = [
        Chain(where, keep.at[unit % KEPT], names_of(order), order, list(buffers[unit]) + [done.at[unit]], send, receive, MOST * unit, TILE_SWAPS[unit])
        for unit, order in enumerate(TILE_ORDERS)
    ]
    chains.append(Chain(where, sums, (), SUMS_ORDER, buffers[TILES], send, receive, MOST * TILES))
    chains.append(Chain(where, late, (), SUMS_ORDER, buffers[TILES + 1], send, receive, MOST * TILES + MOST))

    def core_copy(unit):
        slot = lax.rem(unit, SLOTS)
        return remote(give.at[slot], got.at[slot], core_send.at[unit], core_receive.at[unit], sibling)

    def pair_copy(place, second):
        image = lax.rem(place, 3)
        slot = lax.rem((lax.div(place, 6) * 3 + image) * 2 + second, SLOTS)
        return remote(
            give_pairs.at[slot], got_pairs.at[place], pair_send.at[place], pair_receive.at[place], sibling
        )

    def far_copy(image):
        return remote(
            far_give.at[image], far_out.at[image], far_send.at[image], far_receive.at[image], where["y"][1]
        )

    def core_sum(unit):
        core_copy(unit).wait()
        for_each(4, lambda spot: add_up(keep.at[unit % KEPT], spot, got[(unit % SLOTS,) + spot]))

    def done_copy(unit):
        return pltpu.make_async_copy(done.at[unit], done_out.at[unit], done_sent.at[unit])

    def turn(unit, stage):
        if unit < TILES and stage == 0:
            core_sum(unit)
        chains[unit].turn(stage)
        if stage == len(chains[unit].order) and unit < TILES:
            done_copy(unit).start()

    def tile(unit, lines_of, value, forms):
        def one(high):
            columns = slice(high * HIGH_ROWS, (high + 1) * HIGH_ROWS)
            result = dot_tn(lines_of(columns).reshape(every, HIGH_ROWS), value)
            for half in range(2):
                for names, swapped, chosen in forms:
                    swapped = swapped if half == 1 else None

                    @pl.when(jnp.logical_and(core == half, chosen))
                    def _(half=half, names=names, swapped=swapped):
                        spread_half(result, keep.at[lax.rem(unit, KEPT)], high, half * HALF, names, swapped)

                    @pl.when(jnp.logical_and(core != half, chosen))
                    def _(half=half, names=names, swapped=swapped):
                        spread_half(result, give.at[lax.rem(unit, SLOTS)], high, half * HALF, names, swapped)

        for high in range(2):
            one(high)
        core_copy(unit).start()

    def forms_of(units, unit):
        forms = {}
        for other in units:
            form = (names_of(TILE_ORDERS[other]), TILE_SWAPS[other])
            forms.setdefault(form, []).append(unit == other)
        if len(forms) == 1:
            return [form + (True,) for form in forms]
        return [form + (functools.reduce(jnp.logical_or, asked),) for form, asked in forms.items()]

    def flat(ref):
        return ref[...].reshape(every, ref.shape[-1])

    def left_lines(columns):
        return sides[:, 0, 0, :, columns]

    @pl.when(step == 0)
    def _():
        greet(where)
        sums[...] = sums_in[...]
        late[...] = jnp.zeros_like(late)
        grad_in[...] = jnp.zeros_like(grad_in)

    for at, turns in TURNS.items():

        @pl.when(step == at)
        def _(turns=turns):
            for unit, stage in turns:
                turn(unit, stage)

    @pl.when(step == 0)
    def _():
        tile(0, left_lines, sides[:, 1, 0].reshape(every, width), forms_of((0,), 0))

        def one(image):
            low = dot_nt(sides[image, 1, 0], weights[0]).astype(BF16)
            branch[image] = low
            sums[1:2] += column_sums(low)
        for image in range(images):
            one(image)

    @pl.when((step > 0) & (step < 9) & (lax.rem(step, 2) == 1))
    def _():
        tile(step, left_lines, flat(branch), forms_of((1, 3, 5, 7), step))
        row = pl.ds(6 + lax.div(step, 2), 1)

        def one(image):
            low = dot_nt(branch[image], reduce[:, 0].reshape(width, width)) * sides[image, 1, 0].astype(F32)
            low = low.astype(BF16)
            wide[image] = low
            sums[row] += column_sums(low)
        for image in range(images):
            one(image)

    @pl.when((step > 0) & (step < 9) & (lax.rem(step, 2) == 0))
    def _():
        tile(step, lambda columns: input_two[:, :, columns], flat(wide), forms_of((2, 4, 6, 8), step))
        fresh = jnp.where(step == 2, 0.0, 1.0)

        def one(image):
            grad_in[image] = grad_in[image] * fresh + dot_nt(wide[image], weights[0])
        for image in range(images):
            one(image)

    @pl.when(step == 9)
    def _():
        def one(image):
            normed = sides[image, 1, 0].astype(F32)
            grad = grad_in[image]
            low = branch[image].astype(F32) + normalize_back(grad, normed, scaling_two[image], second_gain)
            low = low.astype(BF16)
            branch[image] = low
            sums[2:3] += column_sums(grad * normed)
            sums[3:4] += column_sums(grad)
            sums[4:5] += column_sums(low)
            mixed = dot_nt(low, weights[0]).astype(BF16)
            for pair in range(heads):
                upstream[image, pair] = mixed[:, pair * PAIR : (pair + 1) * PAIR]
        for image in range(images):
            one(image)

        tile(9, left_lines, flat(branch), forms_of((9,), 9))

    def attend_back(group, image, second, inside, order):
        place = group * 6 + inside

        @pl.when(order >= SLOTS)
        def _():
            before = order - SLOTS
            pair_copy(lax.div(before, 6) * 6 + second * 3 + lax.rem(lax.div(before, 2), 3), second).wait_send()

        scale = HEAD_DIM**-0.5
        target = own_pairs.at[lax.rem(group, 2), inside]
        away = give_pairs.at[lax.rem(order, SLOTS)]
        queries = side_by_side(joint[0, second, 0])
        keys_in = jnp.concatenate([joint[0, second, 1], pairs[0, second, 0]], axis=0)
        values_in = jnp.concatenate([joint[0, second, 2], pairs[0, second, 1]], axis=0)
        grad_mixed = side_by_side(upstream[image, group * 2 + second])
        probs = probs_in[0, second]
        grad_probs = dot_nt(values_in, grad_mixed)
        broad = probs.astype(F32)
        weighted = broad * grad_probs
        inner = jnp.sum(weighted, axis=0, keepdims=True)
        grad_scores = (weighted - broad * inner).astype(BF16)
        grad_values = dot(probs, grad_mixed).astype(BF16)
        grad_keys = (dot(grad_scores, queries) * scale).astype(BF16)
        target[0] = (merge_turned(dot_tn(keys_in, grad_scores)) * scale).astype(BF16)
        target[1] = grad_keys[:rows]
        target[2] = grad_values[:rows]
        away[0] = grad_keys[rows:]
        away[1] = grad_values[rows:]
        pair_copy(place, second).start()

    attends = (step >= FIRST_ATTEND) & (step < GROUP_STEPS[2]) & (step != GROUP_STEPS[0]) & (step != GROUP_STEPS[1])

    @pl.when(attends)
    def _():
        group, image = attend_place(step)
        for second in range(2):
            inside = second * 3 + image
            attend_back(group, image, second, inside, (group * 3 + image) * 2 + second)

    @pl.when((step == GROUP_STEPS[0]) | (step == GROUP_STEPS[1]) | (step == GROUP_STEPS[2]))
    def _():
        group = jnp.where(step == GROUP_STEPS[0], 0, jnp.where(step == GROUP_STEPS[1], 1, 2))
        slot = lax.rem(group, 2)
        for inside in range(6):
            pair_copy(group * 6 + inside, inside // 3).wait_recv()
            image, second = inside % 3, inside // 3
            for part in range(3):
                piece = own_pairs[slot, inside, part]
                if part > 0:
                    piece = piece.astype(F32) + got_pairs[group * 6 + inside, part - 1].astype(F32)
                start = part * 2 * PAIR + second * PAIR
                wide[image, :, start : start + PAIR] = piece.astype(BF16)
        tile(10 + group, lambda columns: input_one[:, :, columns], flat(wide), forms_of((10, 11, 12), 10 + group))
        fresh = jnp.where(group == 0, 0.0, 1.0)
        row = pl.ds(5 + group, 1)

        def one(image):
            late[row] += column_sums(wide[image])
            grad_in[image] = grad_in[image] * fresh + dot_nt(wide[image], weights[0])
        for image in range(images):
            one(image)

    @pl.when(step == FIRST_NORM)
    def _():
        for image in range(images):
            mask = mask_in[image]
            normed, scaling = normalize(embedded_in[image].astype(F32))
            grad = grad_in[image]
            total = branch[image].astype(F32) + normalize_back(grad, normed, scaling, first_gain)
            kept = total * (1.0 - mask)
            far_give[image] = kept[quarter:].astype(BF16)
            far_copy(image).start()
            near_out[image] = kept[:quarter]
            late[0:1] += column_sums(grad * normed)
            late[1:2] += column_sums(grad)
            late[2:3] += column_sums(total * mask)
            if image == 0:
                turn(TILES - 1, 0)

    @pl.when(step == pl.num_programs(0) - 1)
    def _():
        for unit, stage in LAST_TURNS:
            turn(unit, stage)
        for image in range(images):
            far_copy(image).wait()
        for unit in range(TILES):
            done_copy(unit).wait()
        for image in range(1, 3):
            for second in range(2):
                pair_copy(12 + second * 3 + image, second).wait_send()
        sums_out[...] = chains[TILES].refs[-1][...]
        late_out[...] = chains[TILES + 1].refs[-1][...]


def attend_place(step):
    place = step - FIRST_ATTEND
    for at in GROUP_STEPS[:2]:
        place = place - jnp.where(step > at, 1, 0)
    place = jnp.clip(place, 0, 8)
    return lax.div(place, 3), lax.rem(place, 3)


def back(
    sides, weights, reduce, input_two, scaling_two, input_one, joint, pairs, probs, lines, sums, embedded, mask
):
    near, _, slots, rows, width = sides.shape
    quarter = rows // 2
    heads = width // PAIR

    def slot(step):
        return jnp.minimum(lax.div(step + 1, 2), slots - 1)

    def part(step):
        return jnp.clip(lax.div(step - 1, 2), 0, slots - 3)

    def weight(step):
        late = slots + jnp.where(step > GROUP_STEPS[0], 1, 0) + jnp.where(step > GROUP_STEPS[1], 1, 0)
        return jnp.where(step < FIRST_ATTEND, slot(step), late)

    def spot(step):
        group, image = attend_place(step)
        return image, group

    cases = [(names_of(order), order, (HALF, 384), BF16) for order in TILE_ORDERS]
    cases.append(((), SUMS_ORDER, sums.shape, F32))
    cases.append(((), SUMS_ORDER, (8, width), F32))
    buffers, counts = chain_scratch(cases)
    kept, start = [], 0
    for index, count in enumerate(counts):
        kept += buffers[start : start + count - (index < TILES)]
        start += count
    buffers, counts = kept, [count - (index < TILES) for index, count in enumerate(counts)]
    whole = (2, 2, 2, 2, HALF, 384)
    stack = pl.BlockSpec((near, 2, 1, rows, width), lambda s: (0, 0, slot(s), 0, 0))
    return pl.pallas_call(
        partial(back_kernel, counts),
        grid=(FIRST_NORM + 1,),
        in_specs=[
            stack,
            pl.BlockSpec((1, width, width), lambda s: (weight(s), 0, 0)),
            pl.BlockSpec((8, 1, reduce.shape[2], width), lambda s: (0, part(s), 0, 0)),
            fixed((near, rows, width)),
            fixed((near, rows, 1)),
            fixed((near, rows, width)),
            pl.BlockSpec((1, 2, 3, rows, PAIR), lambda s: spot(s) + (0, 0, 0)),
            pl.BlockSpec((1, 2, 2, rows, PAIR), lambda s: spot(s) + (0, 0, 0)),
            pl.BlockSpec((1, 2, 2 * rows, 2 * rows), lambda s: spot(s) + (0, 0)),
            fixed(lines.shape),
            fixed(sums.shape),
            fixed((near, rows, width)),
            fixed((near, rows, 1)),
        ],
        out_specs=[
            pl.BlockSpec(memory_space=pl.ANY),
            fixed((near, quarter, width)),
            pl.BlockSpec(memory_space=pl.ANY),
            fixed_out(sums.shape),
            fixed_out((8, width)),
        ],
        out_shape=[
            jax.ShapeDtypeStruct((TILES, 2, 2, HALF, 384), BF16),
            jax.ShapeDtypeStruct((near, quarter, width), F32),
            jax.ShapeDtypeStruct((near, quarter, width), BF16),
            jax.ShapeDtypeStruct(sums.shape, F32),
            jax.ShapeDtypeStruct((8, width), F32),
        ],
        scratch_shapes=[
            pltpu.VMEM((TILES, 2, 2, HALF, 384), BF16),
            pltpu.SemaphoreType.DMA((TILES,)),
            pltpu.VMEM((near, rows, width), BF16),
            pltpu.VMEM((near, rows, width), BF16),
            pltpu.VMEM((near, rows, width), F32),
            pltpu.VMEM((near, heads, rows, PAIR), BF16),
            pltpu.VMEM((2, 6, 3, rows, PAIR), BF16),
            pltpu.VMEM((SLOTS, 2, rows, PAIR), BF16),
            pltpu.VMEM((near * heads, 2, rows, PAIR), BF16),
            pltpu.VMEM((near, quarter, width), BF16),
            pltpu.VMEM(sums.shape, F32),
            pltpu.VMEM((8, width), F32),
            pltpu.VMEM((KEPT,) + whole, BF16),
            pltpu.VMEM((SLOTS,) + whole, BF16),
            pltpu.VMEM((SLOTS,) + whole, BF16),
            pltpu.SemaphoreType.DMA((MOST * (TILES + 2),)),
            pltpu.SemaphoreType.DMA((MOST * (TILES + 2),)),
            pltpu.SemaphoreType.DMA((TILES,)),
            pltpu.SemaphoreType.DMA((TILES,)),
            pltpu.SemaphoreType.DMA((near * heads,)),
            pltpu.SemaphoreType.DMA((near * heads,)),
            pltpu.SemaphoreType.DMA((near,)),
            pltpu.SemaphoreType.DMA((near,)),
        ]
        + buffers,
        compiler_params=pltpu.CompilerParams(
            vmem_limit_bytes=60 * MIB, collective_id=2, has_side_effects=True
        ),
        cost_estimate=cost(40e9, 60e6),
        name="back",
    )(
        sides, weights, reduce, input_two,
        scaling_two, input_one, joint, pairs, probs, lines, sums, embedded, mask,
    )


def emit_kernel(parts, done, near_in, far_in, sums, late, *outs):
    patch = outs[-1]
    data, y = lax.axis_index("dp"), lax.div(lax.axis_index("seq"), 2)
    inverse = 1.0 / (sums[10:11] * PIXELS)
    patch[y, 0] = near_in[0] * inverse
    patch[1 - y, 0] = far_in[0].astype(F32) * inverse
    pl.when(pl.program_id(0) == 0)(lambda: emit_weights(parts, data, inverse, done, sums, late, outs))


def emit_weights(parts, data, inverse, done, sums, late, outs):
    (
        loss, attend_gain, attend_shift, joint, query_bias, value_bias, output, output_bias, feed_gain,
        feed_shift, expand, expand_bias, reduce, reduce_bias, pixel, pixel_bias, token, _,
    ) = outs
    loss[0] = jnp.sum(sums[5:6] * inverse)
    wide_inverse = inverse[:, :384]

    def piece(unit, core, half):
        return done[unit, core, half].astype(F32) * wide_inverse

    def square(unit):
        return [
            jnp.concatenate([piece(unit, core, half) for half in range(2)], axis=1) for core in range(2)
        ]

    for unit, target in ((0, pixel), (2 * parts + 1, output)):
        for core, lines in enumerate(square(unit)):
            target[core * HALF : (core + 1) * HALF] = lines
    expands = []
    for part in range(parts):
        for core, lines in enumerate(square(1 + 2 * part)):
            start = part * 2 * HALF + core * HALF
            reduce[start : start + HALF] = lines
        expands.append(square(2 + 2 * part))
    span = 2 * HALF
    for core in range(2):
        for d in range(8):
            lines = [expands[part][core][:, d * span : (d + 1) * span] for part in range(parts)]
            expand[core * HALF : (core + 1) * HALF, d * 4 * span : (d + 1) * 4 * span] = jnp.concatenate(
                lines, axis=1
            )
    for group in range(3):
        for core, lines in enumerate(square(2 * parts + 2 + group)):
            for part in range(3):
                start = part * WIDE + group * 2 * PAIR
                joint[core * HALF : (core + 1) * HALF, start : start + 2 * PAIR] = lines[
                    :, part * 2 * PAIR : (part + 1) * 2 * PAIR
                ]

    def own_cut(lines):
        shift = lax.rem(WIDE - data * span, WIDE)
        return pltpu.roll(lines, shift, axis=1)[:, :span]

    early = own_cut(sums[...] * inverse)
    later = own_cut(late[...] * inverse)
    queries = jnp.concatenate([late[5 + group : 6 + group, : 2 * PAIR] for group in range(3)], axis=1)
    values = jnp.concatenate([late[5 + group : 6 + group, 4 * PAIR :] for group in range(3)], axis=1)
    both = jnp.concatenate([queries, values] + [jnp.zeros((6, WIDE), F32)], axis=0)
    both = own_cut(both * inverse)
    for target, lines, row in (
        (attend_gain, later, 0),
        (attend_shift, later, 1),
        (query_bias, both, 0),
        (value_bias, both, 1),
        (output_bias, early, 4),
        (feed_gain, early, 2),
        (feed_shift, early, 3),
        (reduce_bias, early, 1),
        (pixel_bias, early, 0),
        (token, later, 2),
    ):
        target[...] = lines[row : row + 1]
    expand_bias[...] = jnp.concatenate([early[6 + part : 7 + part] for part in range(parts)], axis=1)


def emit(parts, done, near_in, far_in, sums, late):
    images, quarter, width = near_in.shape
    hidden = parts * width

    def out(*shape):
        return jax.ShapeDtypeStruct(shape, F32)

    small = out(1, 96)
    outs = [
        out(1), small, small, out(96, 3 * width), small, small, out(96, width), small, small,
        small, out(96, hidden), out(1, hidden // 8), out(hidden // 8, width), small, out(96, width), small, small,
        out(2, images, quarter, width),
    ]
    half = pl.BlockSpec((1, quarter, width), lambda i: (i, 0, 0))
    outs_specs = [pl.BlockSpec(memory_space=pltpu.SMEM)] + [fixed(leaf.shape) for leaf in outs[1:-1]]
    return pl.pallas_call(
        partial(emit_kernel, parts),
        grid=(images,),
        in_specs=[fixed(done.shape), half, half, fixed(sums.shape), fixed(late.shape)],
        out_specs=outs_specs + [pl.BlockSpec((2, 1, quarter, width), lambda i: (0, i, 0, 0))],
        out_shape=outs,
        compiler_params=params(60),
        cost_estimate=cost(1e6, 12e6),
        name="emit",
    )(done, near_in, far_in, sums, late)


def eight_places(
    patches,
    targets,
    mask_order,
    mask_count,
    attend_gain,
    attend_shift,
    joint_weight,
    query_bias,
    value_bias,
    output_weight,
    output_bias,
    feed_gain,
    feed_shift,
    expand_weight,
    expand_bias,
    reduce_weight,
    reduce_bias,
    pixel_weight,
    pixel_bias,
    mask_token,
):
    images, quarter, features = patches.shape
    near = images // 2
    place_y = own_bit("seq", 2)
    hidden = expand_bias.shape[0]
    parts = hidden // features

    def halves(values):
        return values.reshape((2, near) + values.shape[1:])

    lines = stack_lines(
        attend_gain,
        attend_shift,
        query_bias,
        value_bias,
        output_bias,
        feed_gain,
        feed_shift,
        reduce_bias,
        pixel_bias,
        mask_token,
        expand_bias,
    )
    reduce_parts = reduce_weight.reshape(8, parts, hidden // (8 * parts), features)
    embedded, input_one, joint, pairs, mixed, probs, mask, targets_here, weights = front(
        mask_count,
        halves(patches),
        halves(targets),
        mask_order,
        lines,
        joint_weight,
        pixel_weight,
        expand_weight,
        output_weight,
    )
    sides, input_two, scaling_two, sums = middle(
        embedded, mixed, mask, targets_here, weights, reduce_parts, lines
    )
    done, patch_near, patch_far, sums, late = back(
        sides,
        weights,
        reduce_parts,
        input_two,
        scaling_two,
        input_one,
        joint,
        pairs,
        probs,
        lines,
        sums,
        embedded,
        mask,
    )
    outs = list(emit(parts, done, patch_near, patch_far, sums, late))
    outs[-1] = outs[-1].reshape(images, quarter, features)
    flat = {0: (), 1: (-1,), 2: (-1,), 4: (-1,), 5: (-1,), 7: (-1,), 8: (-1,), 9: (-1,), 11: (-1,)}
    flat.update({13: (-1,), 15: (-1,), 16: (-1,)})
    return tuple(
        out.reshape(flat[index]) if index in flat else out for index, out in enumerate(outs)
    )


def on_device(*arguments):
    if lax.axis_size("dp") == 8 and lax.axis_size("seq") == 4:
        return eight_places(*arguments)
    return any_places(*arguments)


def solution(mesh):
    placed = (
        P("dp", "seq", None),
        P("dp", "seq", None),
        P("dp", "seq"),
        P("dp"),
        P(),
        P(),
        P(),
        P(),
        P(),
        P(),
        P(),
        P(),
        P(),
        P(),
        P(),
        P(),
        P(),
        P(),
        P(),
        P(),
    )
    return jax.shard_map(
        on_device,
        mesh=mesh,
        in_specs=placed,
        out_specs=(
            P(),
            P("dp"),
            P("dp"),
            P("dp", None),
            P("dp"),
            P("dp"),
            P("dp", None),
            P("dp"),
            P("dp"),
            P("dp"),
            P("dp", None),
            P("dp"),
            P("dp", None),
            P("dp"),
            P("dp", None),
            P("dp"),
            P("dp"),
            P("dp", "seq", None),
        ),
        check_vma=False,
    )
```

```python
import functools
import itertools
from functools import partial

import jax
import jax.numpy as jnp
from jax import lax
from jax.experimental import pallas as pl
from jax.experimental.pallas import tpu as pltpu
from jax.sharding import PartitionSpec as P

HEADS = 12
HEAD_DIM = 64
PIXELS = 768
WIDE = 768
PAIR = 2 * HEAD_DIM
MIB = 1 << 20
F32 = jnp.float32
BF16 = jnp.bfloat16


def dot(left, right):
    return jnp.dot(left, right, preferred_element_type=F32)


def dot_nt(left, right):
    return lax.dot_general(left, right, (((1,), (1,)), ((), ())), preferred_element_type=F32)


def dot_tn(left, right):
    return lax.dot_general(left, right, (((0,), (0,)), ((), ())), preferred_element_type=F32)


def normalize(inputs):
    centre = inputs - jnp.mean(inputs, axis=-1, keepdims=True)
    scaling = lax.rsqrt(jnp.mean(centre * centre, axis=-1, keepdims=True) + 1e-06)
    return (centre * scaling, scaling)


def normalize_back(upstream, normed, scaling, gain):
    scaled = upstream * gain
    return scaling * (
        scaled
        - jnp.mean(scaled, axis=-1, keepdims=True)
        - normed * jnp.mean(scaled * normed, axis=-1, keepdims=True)
    )


def column_sums(values):
    return jnp.sum(values.astype(F32), axis=0, keepdims=True)


def gelu_both(inputs):
    bell = jnp.exp2(inputs * inputs * (-0.5 * 1.4426950408889634))
    base_of = 1.0 + (0.3275911 * 0.7071067811865476) * jnp.abs(inputs)
    inner = pl.reciprocal(base_of, approx=True)
    inner = inner * (2.0 - base_of * inner)
    series = 0.5 * 1.453152027 - inner * (0.5 * 1.061405429)
    series = 0.5 * 1.421413741 - inner * series
    series = 0.5 * 0.284496736 - inner * series
    series = 0.5 * 0.254829592 - inner * series
    tail = series * inner * bell
    below = jnp.where(inputs < 0.0, tail, 1.0 - tail)
    return (inputs * below, below + inputs * bell * 0.3989422804014327)


def params(limit):
    return pltpu.CompilerParams(vmem_limit_bytes=limit * MIB)


def fixed(shape):
    zeros = (0,) * len(shape)
    return pl.BlockSpec(shape, lambda *place: zeros, pipeline_mode=pl.Buffered(1))


def cost(flops, moved):
    return pl.CostEstimate(flops=int(flops), bytes_accessed=int(moved), transcendentals=0)


def project_kernel(own, far, gain, shift, weight, bias, embedded_out, joint_out):
    embedded = jnp.concatenate([own[0], far[0]], axis=0)
    embedded_out[0] = embedded
    normed, _ = normalize(embedded.astype(F32))
    low = (normed * gain[...] + shift[...]).astype(BF16)
    for part in range(3):
        cut = slice(part * WIDE, (part + 1) * WIDE)
        joint_out[0, part] = (dot(low, weight[:, cut]) + bias[:, cut]).astype(BF16)


def project(own, far, gain, shift, weight, bias):
    near, quarter, width = own.shape
    rows = 2 * quarter
    return pl.pallas_call(
        project_kernel,
        grid=(near,),
        in_specs=[
            pl.BlockSpec((1, quarter, width), lambda i: (i, 0, 0)),
            pl.BlockSpec((1, quarter, width), lambda i: (i, 0, 0)),
            fixed((1, width)),
            fixed((1, width)),
            fixed((width, 3 * width)),
            fixed((1, 3 * width)),
        ],
        out_specs=[
            pl.BlockSpec((1, rows, width), lambda i: (i, 0, 0)),
            pl.BlockSpec((1, 3, rows, width), lambda i: (i, 0, 0, 0)),
        ],
        out_shape=[
            jax.ShapeDtypeStruct((near, rows, width), BF16),
            jax.ShapeDtypeStruct((near, 3, rows, width), BF16),
        ],
        compiler_params=params(32),
        cost_estimate=cost(2 * near * rows * width * 3 * width, 12e6),
        name="project",
    )(own, far, gain, shift, weight, bias)


def side_by_side(pair):
    lanes = lax.broadcasted_iota(jnp.int32, pair.shape, 1)
    zero = jnp.zeros_like(pair)
    first = jnp.where(lanes < HEAD_DIM, pair, zero)
    second = jnp.where(lanes < HEAD_DIM, zero, pair)
    return jnp.concatenate([first, second], axis=0)


def merge_heads(stacked):
    rows = stacked.shape[0] // 2
    lanes = lax.broadcasted_iota(jnp.int32, (rows, PAIR), 1)
    return jnp.where(lanes < HEAD_DIM, stacked[:rows], stacked[rows:])


def attend_kernel(own, far, mixed_out, probs_out):
    queries = side_by_side(own[0, 0] * jnp.asarray(HEAD_DIM**-0.5, BF16))
    keys_in = jnp.concatenate([own[0, 1], far[0, 0]], axis=0)
    values_in = jnp.concatenate([own[0, 2], far[0, 1]], axis=0)
    scores = dot_nt(queries, keys_in)
    exponent = jnp.exp(scores - jnp.max(scores, axis=-1, keepdims=True))
    total = jnp.sum(exponent, axis=-1, keepdims=True)
    probs = (exponent * (1.0 / total)).astype(BF16)
    probs_out[0, 0] = probs
    mixed_out[0] = merge_heads(dot(probs, values_in)).astype(BF16)


def attend(joint, pairs_far):
    near, _, rows, width = joint.shape
    keys_count = 2 * rows
    pairs = width // PAIR
    return pl.pallas_call(
        attend_kernel,
        grid=(near, pairs),
        in_specs=[
            pl.BlockSpec((1, 3, rows, PAIR), lambda i, h: (i, 0, 0, h)),
            pl.BlockSpec((1, 2, rows, PAIR), lambda i, h: (i, 0, 0, h)),
        ],
        out_specs=[
            pl.BlockSpec((1, rows, PAIR), lambda i, h: (i, 0, h)),
            pl.BlockSpec((1, 1, 2 * rows, keys_count), lambda i, h: (i, h, 0, 0)),
        ],
        out_shape=[
            jax.ShapeDtypeStruct((near, rows, width), BF16),
            jax.ShapeDtypeStruct((near, pairs, 2 * rows, keys_count), BF16),
        ],
        compiler_params=params(32),
        cost_estimate=cost(8 * near * rows * keys_count * width, 20e6),
        name="attend",
    )(joint, pairs_far)


def attend_back_kernel(own, far, probs_in, upstream, query_out, own_out, far_out):
    rows = own.shape[2]
    scale = HEAD_DIM**-0.5
    queries = side_by_side(own[0, 0])
    keys_in = jnp.concatenate([own[0, 1], far[0, 0]], axis=0)
    values_in = jnp.concatenate([own[0, 2], far[0, 1]], axis=0)
    grad_mixed = side_by_side(upstream[0])
    probs = probs_in[0, 0]
    grad_probs = dot_nt(grad_mixed, values_in)
    wide = probs.astype(F32)
    weighted = wide * grad_probs
    inner = jnp.sum(weighted, axis=-1, keepdims=True)
    grad_scores = (weighted - wide * inner).astype(BF16)
    query_out[0] = (merge_heads(dot(grad_scores, keys_in)) * scale).astype(BF16)
    grad_values = dot_tn(probs, grad_mixed).astype(BF16)
    grad_keys = (dot_tn(grad_scores, queries) * scale).astype(BF16)
    own_out[0, 0] = grad_keys[:rows]
    own_out[0, 1] = grad_values[:rows]
    far_out[0, 0] = grad_keys[rows:]
    far_out[0, 1] = grad_values[rows:]


def attend_back(joint, pairs_far, probs, upstream):
    near, _, rows, width = joint.shape
    keys_count = 2 * rows
    pairs = width // PAIR
    two = pl.BlockSpec((1, 2, rows, PAIR), lambda i, h: (i, 0, 0, h))
    one = pl.BlockSpec((1, rows, PAIR), lambda i, h: (i, 0, h))
    return pl.pallas_call(
        attend_back_kernel,
        grid=(near, pairs),
        in_specs=[
            pl.BlockSpec((1, 3, rows, PAIR), lambda i, h: (i, 0, 0, h)),
            two,
            pl.BlockSpec((1, 1, 2 * rows, keys_count), lambda i, h: (i, h, 0, 0)),
            one,
        ],
        out_specs=[one, two, two],
        out_shape=[
            jax.ShapeDtypeStruct((near, rows, width), BF16),
            jax.ShapeDtypeStruct((near, 2, rows, width), BF16),
            jax.ShapeDtypeStruct((near, 2, rows, width), BF16),
        ],
        compiler_params=params(32),
        cost_estimate=cost(16 * near * rows * keys_count * width, 25e6),
        name="attend_back",
    )(joint, pairs_far, probs, upstream)


def rows_kernel(
    hidden,
    inverse,
    embedded_in,
    mixed,
    mask_in,
    target_own,
    target_far,
    output_weight,
    expand_weight,
    reduce_weight,
    pixel_weight,
    biases,
    expand_bias,
    input_out,
    active_out,
    after_out,
    pred_out,
    branch_out,
    expand_out,
    low_out,
    attn_out,
    mixed_out,
    sums_out,
    slope,
):
    output_bias, gain, shift, reduce_bias, pixel_bias = (biases[row : row + 1] for row in range(5))
    mask = mask_in[0]
    after_attn = embedded_in[0].astype(F32) + dot(mixed[0], output_weight[...]) + output_bias
    normed, scaling = normalize(after_attn)
    low = (normed * gain + shift).astype(BF16)
    input_out[0] = low
    total = after_attn + reduce_bias
    for start in range(0, hidden, WIDE):
        cut = slice(start, start + WIDE)
        active, rate = gelu_both(dot(low, expand_weight[:, cut]) + expand_bias[:, cut])
        active = active.astype(BF16)
        active_out[0, :, cut] = active
        slope[:, cut] = rate.astype(slope.dtype)
        total += dot(active, reduce_weight[cut, :])
    after_low = total.astype(BF16)
    after_out[0] = after_low
    target = jnp.concatenate([target_own[0], target_far[0]], axis=0).astype(F32)
    errors = dot(after_low, pixel_weight[...]) + pixel_bias - target
    square = errors * errors + 1.0
    root = lax.rsqrt(square)
    channel = jnp.sum((square * root - 1.0) * mask, axis=0, keepdims=True)
    grad_pred = (mask * errors * root * inverse[0, 0]).astype(BF16)
    pred_out[0] = grad_pred
    grad_mlp = dot_nt(grad_pred, pixel_weight[...])
    branch = grad_mlp.astype(BF16)
    branch_out[0] = branch
    grad_in = jnp.zeros_like(grad_mlp)
    expand_sums = []
    for start in range(0, hidden, WIDE):
        cut = slice(start, start + WIDE)
        grad_expand = dot_nt(branch, reduce_weight[cut, :]) * slope[:, cut].astype(F32)
        grad_expand = grad_expand.astype(BF16)
        expand_out[0, :, cut] = grad_expand
        expand_sums.append(column_sums(grad_expand))
        grad_in += dot_nt(grad_expand, expand_weight[:, cut])
    grad_attn = grad_mlp + normalize_back(grad_in, normed, scaling, gain)
    attn_out[0] = grad_attn
    grad_low = grad_attn.astype(BF16)
    low_out[0] = grad_low
    mixed_out[0] = dot_nt(grad_low, output_weight[...]).astype(BF16)
    sums = [
        column_sums(grad_pred),
        column_sums(branch),
        column_sums(grad_in * normed),
        column_sums(grad_in),
        column_sums(grad_low),
        channel,
    ] + expand_sums

    @pl.when(pl.program_id(0) == 0)
    def _():
        sums_out[...] = jnp.zeros_like(sums_out)

    for row, line in enumerate(sums):
        sums_out[row : row + 1] += line


def rows_step(
    inverse,
    embedded,
    mixed,
    mask,
    target_own,
    target_far,
    output_weight,
    expand_weight,
    reduce_weight,
    pixel_weight,
    biases,
    expand_bias,
):
    near, rows, width = embedded.shape
    quarter = target_own.shape[1]
    hidden = expand_weight.shape[1]
    block = pl.BlockSpec((1, rows, width), lambda i: (i, 0, 0))
    half = pl.BlockSpec((1, quarter, width), lambda i: (i, 0, 0))
    long = pl.BlockSpec((1, rows, hidden), lambda i: (i, 0, 0))
    narrow = jax.ShapeDtypeStruct((near, rows, width), BF16)
    broad = jax.ShapeDtypeStruct((near, rows, hidden), BF16)
    return pl.pallas_call(
        partial(rows_kernel, hidden),
        grid=(near,),
        in_specs=[
            pl.BlockSpec(memory_space=pltpu.SMEM),
            block,
            block,
            pl.BlockSpec((1, rows, 1), lambda i: (i, 0, 0)),
            half,
            half,
            fixed((width, width)),
            fixed((width, hidden)),
            fixed((hidden, width)),
            fixed((width, width)),
            fixed((8, width)),
            fixed((1, hidden)),
        ],
        out_specs=[block, long, block, block, block, long, block, block, block, fixed_out((16, width))],
        out_shape=[
            narrow,
            broad,
            narrow,
            narrow,
            narrow,
            broad,
            narrow,
            jax.ShapeDtypeStruct((near, rows, width), F32),
            narrow,
            jax.ShapeDtypeStruct((16, width), F32),
        ],
        scratch_shapes=[pltpu.VMEM((rows, hidden), F32)],
        compiler_params=params(56),
        cost_estimate=cost(4 * near * rows * width * (2 * width + 2 * hidden), 40e6),
        name="rows_step",
    )(
        inverse,
        embedded,
        mixed,
        mask,
        target_own,
        target_far,
        output_weight,
        expand_weight,
        reduce_weight,
        pixel_weight,
        biases,
        expand_bias,
    )


def fixed_out(shape):
    zeros = (0,) * len(shape)
    return pl.BlockSpec(shape, lambda *place: zeros)


def outer_kernel(left_moves, left, right, out, turned):
    if left_moves:
        out[...] = dot_tn(left[...], right[...]).astype(out.dtype)
        return

    @pl.when(pl.program_id(0) == 0)
    def _():
        turned[...] = left[...].T

    out[...] = dot(turned[...], right[...]).astype(out.dtype)


def outer(left, right):
    rows, tall = left.shape
    broad = right.shape[1]
    left_moves = tall > broad
    if left_moves:
        grid, specs = tall // WIDE, [
            pl.BlockSpec((rows, WIDE), lambda i: (0, i)),
            fixed((rows, broad)),
        ]
        out_spec = pl.BlockSpec((WIDE, broad), lambda i: (i, 0))
    else:
        grid, specs = broad // WIDE, [
            fixed((rows, tall)),
            pl.BlockSpec((rows, WIDE), lambda i: (0, i)),
        ]
        out_spec = pl.BlockSpec((tall, WIDE), lambda i: (0, i))
    return pl.pallas_call(
        partial(outer_kernel, left_moves),
        grid=(grid,),
        in_specs=specs,
        out_specs=out_spec,
        out_shape=jax.ShapeDtypeStruct((tall, broad), BF16),
        scratch_shapes=[pltpu.VMEM((WIDE, rows), BF16)],
        compiler_params=params(32),
        cost_estimate=cost(2 * rows * tall * broad, 2 * (rows * (tall + broad) + tall * broad)),
        name="outer",
    )(left, right)


def project_back_kernel(
    query, own, received, embedded_in, attn, mask_in, gain, shift, weight,
    input_out, joint_out, near_out, far_out, sums_out,
):
    quarter = near_out.shape[1]
    mask = mask_in[0]
    embedded = embedded_in[0].astype(F32)
    normed, scaling = normalize(embedded)
    input_out[0] = (normed * gain[...] + shift[...]).astype(BF16)
    grad_query = query[0]
    grad_key = (own[0, 0].astype(F32) + received[0, 0].astype(F32)).astype(BF16)
    grad_value = (own[0, 1].astype(F32) + received[0, 1].astype(F32)).astype(BF16)
    grad_in = None
    for part, grad in enumerate((grad_query, grad_key, grad_value)):
        joint_out[part, 0] = grad
        term = dot_nt(grad, weight[:, part * WIDE : (part + 1) * WIDE])
        grad_in = term if grad_in is None else grad_in + term
    grad_embedded = attn[0] + normalize_back(grad_in, normed, scaling, gain[...])
    kept = grad_embedded * (1.0 - mask)
    near_out[0] = kept[:quarter]
    far_out[0] = kept[quarter:].astype(BF16)
    sums = [
        column_sums(grad_in * normed),
        column_sums(grad_in),
        column_sums(grad_query),
        column_sums(grad_value),
        column_sums(grad_embedded * mask),
    ]

    @pl.when(pl.program_id(0) == 0)
    def _():
        sums_out[...] = jnp.zeros_like(sums_out)

    for row, line in enumerate(sums):
        sums_out[row : row + 1] += line


def project_back(query, own, received, embedded, attn, mask, gain, shift, weight):
    near, rows, width = embedded.shape
    quarter = rows // 2
    block = pl.BlockSpec((1, rows, width), lambda i: (i, 0, 0))
    half = pl.BlockSpec((1, quarter, width), lambda i: (i, 0, 0))
    two = pl.BlockSpec((1, 2, rows, width), lambda i: (i, 0, 0, 0))
    return pl.pallas_call(
        project_back_kernel,
        grid=(near,),
        in_specs=[
            block,
            two,
            two,
            block,
            block,
            pl.BlockSpec((1, rows, 1), lambda i: (i, 0, 0)),
            fixed((1, width)),
            fixed((1, width)),
            fixed((width, 3 * width)),
        ],
        out_specs=[
            block,
            pl.BlockSpec((3, 1, rows, width), lambda i: (0, i, 0, 0)),
            half,
            half,
            fixed_out((8, width)),
        ],
        out_shape=[
            jax.ShapeDtypeStruct((near, rows, width), BF16),
            jax.ShapeDtypeStruct((3, near, rows, width), BF16),
            jax.ShapeDtypeStruct((near, quarter, width), F32),
            jax.ShapeDtypeStruct((near, quarter, width), BF16),
            jax.ShapeDtypeStruct((8, width), F32),
        ],
        compiler_params=params(40),
        cost_estimate=cost(2 * near * rows * width * 3 * width, 20e6),
        name="project_back",
    )(query, own, received, embedded, attn, mask, gain, shift, weight)


def swap(values, axis, bit):
    size = lax.axis_size(axis)
    return lax.ppermute(values, axis, [(place, place ^ bit) for place in range(size)])


def own_bit(axis, bit):
    return (lax.axis_index(axis) // bit) % 2


def pick(values, dim, which):
    return lax.dynamic_index_in_dim(values, which, dim, keepdims=False)


def add_in(kept, received):
    return (kept.astype(jnp.float32) + received.astype(jnp.float32)).astype(kept.dtype)


def halve(values, dim, axis, bit):
    mine = own_bit(axis, bit)
    received = swap(pick(values, dim, 1 - mine), axis, bit)
    return add_in(pick(values, dim, mine), received)


def join(values, dim, axis, bit):
    mine = own_bit(axis, bit)
    received = swap(values, axis, bit)
    first = jnp.where(mine == 0, values, received)
    second = jnp.where(mine == 0, received, values)
    return jnp.concatenate([first, second], axis=dim)


def reduce_rows(grad, order):
    dp = lax.axis_size("dp")
    rows, columns = grad.shape
    steps = dp.bit_length() - 1
    part = rows // dp
    if columns % 512 == 0:
        tail = (1, 2, part, 2, columns // 4, 2)
        parts = grad.reshape((2,) * steps + (part, 4, columns // 4))
        parts = jnp.moveaxis(parts, steps + 1, 0)
    else:
        parts = grad.reshape((2,) * steps + (4, part // 4, columns))
        parts = jnp.moveaxis(parts, steps, 0)
    parts = parts.reshape((2, 2) + parts.shape[1:])
    names = ["core", "y"] + [1 << bit for bit in reversed(range(steps))]
    for name in order(steps):
        dim = names.index(name)
        if name == "core":
            parts = halve(parts, dim, "seq", 1)
        elif name == "y":
            parts = halve(parts, dim, "seq", 2)
        else:
            parts = halve(parts, dim, "dp", name)
        names.pop(dim)
    parts = join(parts[None], 0, "seq", 2)
    parts = join(parts[None], 0, "seq", 1)
    parts = parts.reshape((4,) + parts.shape[2:]).astype(jnp.float32)
    if columns % 512 == 0:
        return jnp.moveaxis(parts, 0, 1).reshape(part, columns)
    return parts.reshape(part, columns)


def x_first(steps):
    return ["core"] + [1 << bit for bit in range(steps)] + ["y"]


def y_first(steps):
    return ["core", "y"] + [1 << bit for bit in range(steps)]


def z_first(steps):
    return ["core"] + [1 << bit for bit in range(1, steps)] + [1, "y"]


def reduce_vector(values):
    dp = lax.axis_size("dp")
    steps = dp.bit_length() - 1
    values = values + swap(values, "seq", 1)
    values = values + swap(values, "seq", 2)
    values = values.reshape((2,) * steps + values.shape[1:])
    for bit in reversed(range(steps)):
        mine = own_bit("dp", 1 << bit)
        received = swap(pick(values, 0, 1 - mine), "dp", 1 << bit)
        values = pick(values, 0, mine) + received
    return values


def any_places(
    patches,
    targets,
    mask_order,
    mask_count,
    attend_gain,
    attend_shift,
    joint_weight,
    query_bias,
    value_bias,
    output_weight,
    output_bias,
    feed_gain,
    feed_shift,
    expand_weight,
    expand_bias,
    reduce_weight,
    reduce_bias,
    pixel_weight,
    pixel_bias,
    mask_token,
):
    images, quarter, features = patches.shape
    dp = lax.axis_size("dp")
    near = images // 2
    rows_one = 2 * quarter
    row_count = near * rows_one
    place_y = own_bit("seq", 2)

    def own_and_far(values):
        parts = values.reshape((2, near) + values.shape[1:])
        return pick(parts, 0, place_y), swap(pick(parts, 0, 1 - place_y), "seq", 2)

    def line(vector):
        return vector.astype(F32)[None, :]

    masked_here = mask_order < mask_count[:, None]
    embedded_here = jnp.where(masked_here[:, :, None], mask_token[None, None, :], patches)
    embedded_own, embedded_far = own_and_far(embedded_here)
    mask = jnp.concatenate(own_and_far(masked_here.astype(jnp.int32)), axis=1)
    mask = mask.astype(F32)[:, :, None]
    count_sum = jnp.sum(mask_count)
    for bit in range(dp.bit_length() - 1):
        count_sum = count_sum + swap(count_sum, "dp", 1 << bit)
    inverse = 1.0 / (count_sum.astype(F32) * PIXELS)
    target_own, target_far = own_and_far(targets)
    joint_bias = jnp.concatenate(
        [line(query_bias), jnp.zeros((1, features), F32), line(value_bias)], axis=1
    )
    biases = jnp.concatenate(
        [
            line(vector)
            for vector in (output_bias, feed_gain, feed_shift, reduce_bias, pixel_bias)
        ]
        + [jnp.zeros((3, features), F32)],
        axis=0,
    )
    embedded, joint = project(
        embedded_own, embedded_far, line(attend_gain), line(attend_shift), joint_weight, joint_bias
    )
    pairs_far = swap(joint[:, 1:], "seq", 1)
    mixed, probs = attend(joint, pairs_far)
    (
        input_two,
        activated,
        after_low,
        grad_pred,
        grad_branch,
        grad_expand,
        grad_out,
        grad_attn,
        grad_mixed,
        sums_two,
    ) = rows_step(
        inverse.reshape(1, 1),
        embedded,
        mixed,
        mask,
        target_own,
        target_far,
        output_weight,
        expand_weight,
        reduce_weight,
        pixel_weight,
        biases,
        line(expand_bias),
    )

    def flat(values):
        return values.reshape(row_count, values.shape[-1])

    reduce_weight_grad = outer(flat(activated), flat(grad_branch))
    expand_weight_grad = outer(flat(input_two), flat(grad_expand))
    pixel_weight_grad = outer(flat(after_low), flat(grad_pred))
    output_weight_grad = outer(flat(mixed), flat(grad_out))
    square_grads = jnp.concatenate([pixel_weight_grad, output_weight_grad], axis=1)
    grad_query, grad_own, grad_far = attend_back(joint, pairs_far, probs, grad_mixed)
    received = swap(grad_far, "seq", 1)
    input_one, grad_joint, patch_near, patch_far, sums_one = project_back(
        grad_query,
        grad_own,
        received,
        embedded,
        grad_attn,
        mask,
        line(attend_gain),
        line(attend_shift),
        joint_weight,
    )
    grad_joint = grad_joint.reshape(3, row_count, features)
    joint_weight_grad = jnp.concatenate(
        [outer(flat(input_one), grad_joint[part]) for part in range(3)], axis=1
    )
    patch_far = swap(patch_far, "seq", 2).astype(F32)
    patch_grad = jnp.concatenate(
        [
            jnp.where(place_y == 0, patch_near, patch_far),
            jnp.where(place_y == 0, patch_far, patch_near),
        ],
        axis=0,
    )
    hidden = expand_bias.shape[0]
    vectors = (
        sums_one[0],
        sums_one[1],
        sums_one[2],
        sums_one[3],
        sums_two[4],
        sums_two[2],
        sums_two[3],
        sums_two[6 : 6 + hidden // features].reshape(hidden),
        sums_two[1],
        sums_two[0],
        sums_one[4],
    )
    loss_part = jnp.sum(sums_two[5]) * inverse
    lengths = [vector.shape[0] // dp for vector in vectors]
    packed = jnp.concatenate(
        [vector.reshape(dp, -1) for vector in vectors]
        + [jnp.broadcast_to(loss_part[None, None], (dp, 1))],
        axis=1,
    )
    packed = reduce_vector(packed)
    loss_value = packed[-1]
    cuts, start = [], 0
    for length in lengths:
        cuts.append(packed[start : start + length])
        start += length
    (
        attend_gain_grad,
        attend_shift_grad,
        query_bias_grad,
        value_bias_grad,
        output_bias_grad,
        feed_gain_grad,
        feed_shift_grad,
        expand_bias_grad,
        reduce_bias_grad,
        pixel_bias_grad,
        mask_token_grad,
    ) = cuts
    reduce_weight_grad = reduce_rows(reduce_weight_grad, x_first)
    expand_weight_grad = reduce_rows(expand_weight_grad, y_first)
    square_grads = reduce_rows(square_grads, z_first)
    joint_weight_grad = reduce_rows(joint_weight_grad, x_first)
    return (
        loss_value,
        attend_gain_grad,
        attend_shift_grad,
        joint_weight_grad,
        query_bias_grad,
        value_bias_grad,
        square_grads[:, PIXELS:],
        output_bias_grad,
        feed_gain_grad,
        feed_shift_grad,
        expand_weight_grad,
        expand_bias_grad,
        reduce_weight_grad,
        reduce_bias_grad,
        square_grads[:, :PIXELS],
        pixel_bias_grad,
        mask_token_grad,
        patch_grad,
    )


MESH = pl.DeviceIdType.MESH


def places():
    data, seq = lax.axis_index("dp"), lax.axis_index("seq")
    x, low, high = lax.rem(data, 2), lax.rem(lax.div(data, 2), 2), lax.div(data, 4)
    core, y = lax.rem(seq, 2), lax.div(seq, 2)
    return {
        "x": (x, {"dp": data + 1 - 2 * x}),
        "low": (low, {"dp": data + 2 - 4 * low}),
        "high": (high, {"dp": data + 4 - 8 * high}),
        "y": (y, {"seq": seq + 2 - 4 * y}),
        "core": (core, {"seq": seq + 1 - 2 * core}),
    }


def greet(where):
    barrier = pltpu.get_barrier_semaphore()
    for _, partner in where.values():
        pl.semaphore_signal(barrier, inc=1, device_id=partner, device_id_type=MESH)
    pl.semaphore_wait(barrier, len(where))


def remote(source, target, send, receive, partner):
    return pltpu.make_async_remote_copy(
        src_ref=source,
        dst_ref=target,
        send_sem=send,
        recv_sem=receive,
        device_id=partner,
        device_id_type=MESH,
    )


NAMES = ("high", "low", "x", "y")


def names_of(order):
    halved = [token for token in order if token in NAMES]
    return tuple(halved + [name for name in NAMES if name not in halved])


def stage_shapes(names, order, tail):
    names, shapes = list(names), []
    for token in order:
        if token == "Gy":
            names = ["y"]
        elif token == "Gcore":
            names = ["core"] + names
        elif token[0] != "+":
            names.remove(token)
        shapes.append((2,) * len(names) + tail)
    return shapes


def for_each(dims, body):
    outer = max(dims - 2, 0)
    inner = list(itertools.product(range(2), repeat=dims - outer))
    if outer == 0:
        for spot in inner:
            body(spot)
        return

    def one(place, carry):
        first = tuple(lax.rem(lax.div(place, 2 ** (outer - 1 - dim)), 2) for dim in range(outer))
        for spot in inner:
            body(first + spot)
        return carry

    lax.fori_loop(0, 2**outer, one, 0)


def add_up(target, place, other):
    target[place] = target[place] + other


class Chain:
    def __init__(self, where, start, names, order, buffers, send, receive, base, swapped=None):
        self.where, self.order = dict(where), order
        if swapped is not None:
            (first, partner_first), (second, partner_second) = (where[name] for name in swapped)
            core = where["core"][0]

            def chosen(zero, one):
                return zero + core * (one - zero)

            for name, place, ours, other in (
                (swapped[0], (first, second), partner_first, partner_second),
                (swapped[1], (second, first), partner_second, partner_first),
            ):
                here = {"dp": lax.axis_index("dp"), "seq": lax.axis_index("seq")}
                ours, other = {**here, **ours}, {**here, **other}
                partner = {axis: chosen(ours[axis], other[axis]) for axis in here}
                self.where[name] = (chosen(*place), partner)
        self.plain = where
        self.refs = [start] + list(buffers)
        self.send, self.receive, self.base = send, receive, base
        self.names = [list(names)]
        for token in order:
            names = list(self.names[-1])
            if token == "Gy":
                names = ["y"]
            elif token == "Gcore":
                names = ["core"] + names
            elif token[0] != "+":
                names.remove(token)
            self.names.append(names)

    def copy(self, stage):
        token = self.order[stage]
        source, target = self.refs[stage], self.refs[stage + 1]
        if token[0] == "+":
            _, partner = self.plain[token[1:]]
        elif token[0] == "G":
            place, partner = self.plain[token[1:]]
            target = target.at[place]
        else:
            place, partner = self.where[token]
            dim = self.names[stage].index(token)
            source = source.at[(slice(None),) * dim + (1 - place,)]
        spot = self.base + stage
        return remote(source, target, self.send.at[spot], self.receive.at[spot], partner)

    def start(self, stage):
        self.copy(stage).start()

    def finish(self, stage):
        self.copy(stage).wait()
        token = self.order[stage]
        source, target = self.refs[stage], self.refs[stage + 1]
        if token[0] == "G":
            place, _ = self.plain[token[1:]]
            target[place] = source[...]
            return
        dim = None
        if token[0] != "+":
            place, _ = self.where[token]
            dim = self.names[stage].index(token)

        def one(spot):
            origin = spot if dim is None else spot[:dim] + (place,) + spot[dim:]
            add_up(target, spot if spot else Ellipsis, source[origin if origin else Ellipsis])

        for_each(len(self.names[stage + 1]), one)

    def turn(self, stage):
        if stage > 0:
            self.finish(stage - 1)
        if stage < len(self.order):
            self.start(stage)


Y_FIRST = ("y", "x", "low", "high", "Gy", "Gcore")
Y_THEN_LOW = ("y", "low", "x", "high", "Gy", "Gcore")
X_FIRST = ("x", "low", "high", "+y", "Gcore")
SUMS_ORDER = ("+core", "+y", "+x", "+low", "+high")
MOST = 6
TILE_ORDERS = (
    Y_FIRST,
    X_FIRST,
    Y_THEN_LOW,
    Y_FIRST,
    Y_THEN_LOW,
    X_FIRST,
    Y_FIRST,
    X_FIRST,
    Y_THEN_LOW,
    Y_FIRST,
    Y_FIRST,
    Y_FIRST,
    X_FIRST,
)
TILE_SWAPS = (
    ("x", "y"),
    ("x", "low"),
    ("y", "low"),
    ("x", "y"),
    ("y", "low"),
    ("x", "low"),
    ("x", "y"),
    ("x", "low"),
    ("y", "low"),
    ("x", "y"),
    ("x", "y"),
    ("x", "y"),
    ("x", "low"),
)
TILES = len(TILE_ORDERS)
TILE_STEPS = (0, 1, 2, 3, 4, 5, 6, 7, 8, 9, 14, 18, 21)
TURNS = {
    2: ((0, 0),),
    3: ((1, 0),),
    4: ((0, 1), (2, 0),),
    5: ((1, 1), (3, 0),),
    6: ((0, 2), (4, 0),),
    7: ((1, 2), (2, 1), (3, 1), (5, 0),),
    8: ((0, 3), (6, 0),),
    9: ((1, 3), (3, 2), (7, 0),),
    10: ((0, 4), (1, 4), (2, 2), (4, 1), (6, 1), (8, 0), (13, 0), (3, 3),),
    11: ((1, 5), (5, 1), (13, 1), (9, 0), (0, 5),),
    12: ((0, 6), (3, 4), (2, 3), (7, 1),),
    13: ((4, 2), (6, 2), (13, 2),),
    14: ((3, 5), (2, 4), (5, 2),),
    15: ((3, 6), (2, 5), (4, 3), (6, 3), (13, 3), (7, 2), (8, 1), (9, 1),),
    16: ((2, 6), (5, 3), (10, 0),),
    18: ((4, 4), (5, 4), (6, 4), (13, 4), (7, 3), (8, 2), (9, 2),),
    19: ((4, 5), (5, 5), (6, 5), (13, 5), (8, 3), (10, 1),),
    20: ((4, 6), (6, 6), (7, 4), (9, 3), (11, 0),),
    21: ((7, 5), (8, 4), (10, 2),),
    22: ((8, 5), (9, 4), (10, 3), (11, 1),),
}
LAST_TURNS = (
    (14, 0),
    (8, 6),
    (9, 5),
    (10, 4),
    (11, 2),
    (14, 1),
    (9, 6),
    (11, 3),
    (14, 2),
    (10, 5),
    (12, 1),
    (10, 6),
    (14, 3),
    (11, 4),
    (12, 2),
    (14, 4),
    (11, 5),
    (14, 5),
    (11, 6),
    (12, 3),
    (12, 4),
    (12, 5),
)


def chain_scratch(cases):
    scratch, counts = [], []
    for names, order, tail, dtype in cases:
        shapes = stage_shapes(names, order, tail)
        scratch += [pltpu.VMEM(shape, dtype) for shape in shapes]
        counts.append(len(shapes))
    return scratch, counts


def split_list(values, counts):
    parts, start = [], 0
    for count in counts:
        parts.append(values[start : start + count])
        start += count
    return parts


GAIN_ONE, SHIFT_ONE, QUERY, VALUE, OUTPUT, GAIN_TWO, SHIFT_TWO, REDUCE, PIXEL, TOKEN, EXPAND = range(11)
FRONT_OWN = 9
FRONT_FAR = 12
FRONT_ATTEND = 15
FRONT_PAIRS = 3


def lines_kernel(*refs):
    out = refs[-1]
    row = 0
    for ref in refs[:-1]:
        for start in range(0, ref.shape[0], WIDE):
            out[row : row + 1] = ref[start : start + WIDE].astype(F32).reshape(1, WIDE)
            row += 1


def stack_lines(*vectors):
    return pl.pallas_call(
        lines_kernel,
        in_specs=[pl.BlockSpec(memory_space=pltpu.VMEM)] * len(vectors),
        out_specs=pl.BlockSpec(memory_space=pltpu.VMEM),
        out_shape=jax.ShapeDtypeStruct((16, WIDE), F32),
        cost_estimate=cost(1e4, 1e5),
        name="stack_lines",
    )(*vectors)


def column_of(line):
    count = line.shape[1]
    down = lax.broadcasted_iota(jnp.int32, (count, count), 0)
    along = lax.broadcasted_iota(jnp.int32, (count, count), 1)
    return jnp.sum(jnp.where(down == along, jnp.broadcast_to(line, (count, count)), 0.0), axis=1, keepdims=True)


def front_kernel(
    parts, counts, rows_in, targets_in, orders_in, lines, weight_in, pixel_in, expand_in, output_in,
    embedded_out, input_out, joint_out, pairs_out, mixed_out, probs_out, masks_out, target_out, expand_out,
    embedded, inputs, masks, order_far, joint, pairs, weight, pixel, expand, output,
    local, far_send, far_receive, send, receive,
):
    images, heads = joint.shape[:2]
    quarter = rows_in.shape[2]
    where = {name: places()[name] for name in ("core", "y")}
    sibling = where["core"][1]
    y, other = where["y"]
    step = pl.program_id(0)
    near_half, far_half = pl.ds(0, quarter), pl.ds(quarter, quarter)

    def pair_copy(image):
        return remote(
            joint.at[image, :, pl.ds(1, 2)], pairs.at[image], send.at[image], receive.at[image], sibling
        )

    def far_copy(index, source, target):
        return remote(source, target, far_send.at[index], far_receive.at[index], other)

    order_copy = far_copy(0, orders_in.at[1 - y], order_far)
    row_copies = [
        far_copy(1 + image, rows_in.at[1 - y, image], embedded.at[image, far_half]) for image in range(images)
    ]
    target_copies = [
        far_copy(1 + images + image, targets_in.at[1 - y, image], target_out.at[image, far_half])
        for image in range(images)
    ]
    own_copy = pltpu.make_async_copy(rows_in.at[y], embedded.at[:, near_half], local.at[0])
    target_copy = pltpu.make_async_copy(targets_in.at[y], target_out.at[:, near_half], local.at[1])
    loads = [
        pltpu.make_async_copy(source, target, local.at[2 + index])
        for index, (source, target) in enumerate(
            ((pixel_in, pixel), (expand_in, expand), (output_in, output), (weight_in, weight))
        )
    ]

    @pl.when(step == 0)
    def _():
        own_copy.start()
        greet(where)
        order_copy.start()
        for copy in row_copies + loads:
            copy.start()
        target_copy.start()
        loads[0].wait()
        expand_out[0] = pixel[...]

    @pl.when(step == parts + 1)
    def _():
        loads[2].wait()
        expand_out[0] = output[...]

    for part in range(parts):

        @pl.when(step == 1 + part)
        def _(part=part):
            if part == 0:
                loads[1].wait()
            span = weight.shape[0] // 8
            starts = [place * parts * span + part * span for place in range(8)]
            expand_out[0] = jnp.concatenate([expand[:, start : start + span] for start in starts], axis=1)

    for group in range(3):

        @pl.when(step == parts + 2 + group)
        def _(group=group):
            if group == 0:
                loads[3].wait()
            starts = [part * WIDE + group * 2 * PAIR for part in range(3)]
            expand_out[0] = jnp.concatenate([weight[:, start : start + 2 * PAIR] for start in starts], axis=1)

    def project(image, start, order):
        block = pl.ds(start, quarter)
        mask = column_of((order < counts[y * images + image]).astype(F32))
        masks[image, block] = mask
        token = lines[TOKEN : TOKEN + 1].astype(BF16)
        rows = jnp.where(mask > 0.5, token, embedded[image, block])
        embedded[image, block] = rows
        normed, _ = normalize(rows.astype(F32))
        gain, shift = lines[GAIN_ONE : GAIN_ONE + 1], lines[SHIFT_ONE : SHIFT_ONE + 1]
        low = (normed * gain + shift).astype(BF16)
        inputs[image, block] = low
        for part, bias in ((1, None), (2, lines[VALUE : VALUE + 1]), (0, lines[QUERY : QUERY + 1])):
            total = dot(low, weight[:, part * WIDE : (part + 1) * WIDE])
            total = (total if bias is None else total + bias).astype(BF16)
            for pair in range(heads):
                joint[image, pair, part, block] = total[:, pair * PAIR : (pair + 1) * PAIR]

    @pl.when((step >= FRONT_OWN) & (step < FRONT_FAR))
    def _():
        @pl.when(step == FRONT_OWN)
        def _():
            own_copy.wait()

        image = step - FRONT_OWN
        project(image, 0, orders_in[y, image, 0:1, :quarter])

    @pl.when((step >= FRONT_FAR) & (step < FRONT_ATTEND))
    def _():
        for index in range(images):

            @pl.when(step == FRONT_FAR + index)
            def _(index=index):
                if index == 0:
                    order_copy.wait()
                row_copies[index].wait()
                target_copies[index].start()

        image = step - FRONT_FAR
        project(image, quarter, order_far[image, 0:1, :quarter])
        pair_copy(image).start()
        embedded_out[0] = embedded[image]
        input_out[0] = inputs[image]
        joint_out[0] = joint[image]
        masks_out[0] = masks[image]

    def attend(image, pair, index):
        queries = side_by_side(joint[image, pair, 0] * jnp.asarray(HEAD_DIM**-0.5, BF16))
        keys_in = jnp.concatenate([joint[image, pair, 1], pairs[image, pair, 0]], axis=0)
        values_in = jnp.concatenate([joint[image, pair, 2], pairs[image, pair, 1]], axis=0)
        pairs_out[0, index] = pairs[image, pair]
        scores = dot_nt(keys_in, queries)
        exponent = jnp.exp(scores - jnp.max(scores, axis=0, keepdims=True))
        total = jnp.sum(exponent, axis=0, keepdims=True)
        probs = (exponent * (1.0 / total)).astype(BF16)
        probs_out[0, index] = probs
        mixed = merge_turned(dot_tn(values_in, probs)).astype(BF16)
        mixed_out[0, :, index * PAIR : (index + 1) * PAIR] = mixed

    @pl.when(step >= FRONT_ATTEND)
    def _():
        place = step - FRONT_ATTEND
        turns = heads // FRONT_PAIRS
        image, turn = lax.div(place, turns), lax.rem(place, turns)

        @pl.when(turn == 0)
        def _():
            pair_copy(image).wait()

        for index in range(FRONT_PAIRS):
            attend(image, turn * FRONT_PAIRS + index, index)

    @pl.when(step == pl.num_programs(0) - 1)
    def _():
        for copy in target_copies:
            copy.wait()
        target_copy.wait()


def merge_turned(stacked):
    rows = stacked.shape[1] // 2
    down = lax.broadcasted_iota(jnp.int32, (PAIR, rows), 0)
    return jnp.where(down < HEAD_DIM, stacked[:, :rows], stacked[:, rows:]).T


def front(counts, rows_in, targets_in, orders_in, lines, weight, pixel, expand, output):
    near, quarter, width = rows_in.shape[1:]
    rows, heads = 2 * quarter, width // PAIR
    parts = expand.shape[1] // width

    def image(step):
        return jnp.clip(step - FRONT_FAR, 0, near - 1)

    turns = heads // FRONT_PAIRS

    def spot(step):
        place = jnp.maximum(step - FRONT_ATTEND, 0)
        return lax.div(place, turns), lax.rem(place, turns)

    block = pl.BlockSpec((1, rows, width), lambda s: (image(s), 0, 0))
    return pl.pallas_call(
        partial(front_kernel, parts),
        grid=(FRONT_ATTEND + near * turns,),
        in_specs=[
            pl.BlockSpec(memory_space=pltpu.SMEM),
            pl.BlockSpec(memory_space=pl.ANY),
            pl.BlockSpec(memory_space=pl.ANY),
            fixed(orders_in.shape),
            fixed(lines.shape),
        ]
        + [pl.BlockSpec(memory_space=pl.ANY)] * 4,
        out_specs=[
            block,
            block,
            pl.BlockSpec((1, heads, 3, rows, PAIR), lambda s: (image(s), 0, 0, 0, 0)),
            pl.BlockSpec((1, FRONT_PAIRS, 2, rows, PAIR), lambda s: spot(s) + (0, 0, 0)),
            pl.BlockSpec((1, rows, FRONT_PAIRS * PAIR), lambda s: (spot(s)[0], 0, spot(s)[1])),
            pl.BlockSpec((1, FRONT_PAIRS, 2 * rows, 2 * rows), lambda s: spot(s) + (0, 0)),
            pl.BlockSpec((1, rows, 1), lambda s: (image(s), 0, 0)),
            pl.BlockSpec(memory_space=pl.ANY),
            pl.BlockSpec((1, width, width), lambda s: (jnp.minimum(s, parts + 4), 0, 0)),
        ],
        out_shape=[
            jax.ShapeDtypeStruct((near, rows, width), BF16),
            jax.ShapeDtypeStruct((near, rows, width), BF16),
            jax.ShapeDtypeStruct((near, heads, 3, rows, PAIR), BF16),
            jax.ShapeDtypeStruct((near, heads, 2, rows, PAIR), BF16),
            jax.ShapeDtypeStruct((near, rows, width), BF16),
            jax.ShapeDtypeStruct((near, heads, 2 * rows, 2 * rows), BF16),
            jax.ShapeDtypeStruct((near, rows, 1), F32),
            jax.ShapeDtypeStruct((near, rows, width), BF16),
            jax.ShapeDtypeStruct((parts + 5, width, width), BF16),
        ],
        scratch_shapes=[
            pltpu.VMEM((near, rows, width), BF16),
            pltpu.VMEM((near, rows, width), BF16),
            pltpu.VMEM((near, rows, 1), F32),
            pltpu.VMEM(orders_in.shape[1:], jnp.int32),
            pltpu.VMEM((near, heads, 3, rows, PAIR), BF16),
            pltpu.VMEM((near, heads, 2, rows, PAIR), BF16),
            pltpu.VMEM(weight.shape, BF16),
            pltpu.VMEM(pixel.shape, BF16),
            pltpu.VMEM(expand.shape, BF16),
            pltpu.VMEM(output.shape, BF16),
            pltpu.SemaphoreType.DMA((6,)),
            pltpu.SemaphoreType.DMA((1 + 2 * near,)),
            pltpu.SemaphoreType.DMA((1 + 2 * near,)),
            pltpu.SemaphoreType.DMA((near,)),
            pltpu.SemaphoreType.DMA((near,)),
        ],
        compiler_params=pltpu.CompilerParams(
            vmem_limit_bytes=60 * MIB, collective_id=1, has_side_effects=True
        ),
        cost_estimate=cost(5e9, 40e6),
        name="front",
    )(counts, rows_in, targets_in, orders_in, lines, weight, pixel, expand, output)


def middle_kernel(
    embedded_in, mixed, mask_in, target_in, weights, reduce, lines,
    sides, input_out, scaling_out, sums_out, low, total, biases,
):
    parts = reduce.shape[1]
    span = reduce.shape[2]
    width = weights.shape[1]
    mask = mask_in[0]

    @pl.when(pl.program_id(0) == 0)
    def _():
        sums_out[...] = jnp.zeros_like(sums_out)
        for part in range(parts):
            pieces = []
            for place in range(8):
                row, start = divmod((place * parts + part) * span, width)
                pieces.append(lines[EXPAND + row : EXPAND + row + 1, start : start + span])
            biases[part] = jnp.concatenate(pieces, axis=1)

    after_attn = embedded_in[0].astype(F32) + dot(mixed[0], weights[parts + 1]) + lines[OUTPUT : OUTPUT + 1]
    sides[0, 0, parts + 1] = mixed[0]
    normed, scaling = normalize(after_attn)
    sides[0, 1, parts + 1] = normed.astype(BF16)
    scaling_out[0] = scaling
    low[...] = (normed * lines[GAIN_TWO : GAIN_TWO + 1] + lines[SHIFT_TWO : SHIFT_TWO + 1]).astype(BF16)
    input_out[0] = low[...]
    total[...] = after_attn + lines[REDUCE : REDUCE + 1]

    def one(part, carry):
        active, rate = gelu_both(dot(low[...], weights[1 + part]) + biases[part])
        active = active.astype(BF16)
        sides[0, 0, 1 + part] = active
        sides[0, 1, 1 + part] = rate.astype(BF16)
        total[...] += dot(active, reduce[:, part].reshape(width, width))
        return carry

    for part in range(parts):
        one(part, 0)
    after_low = total[...].astype(BF16)
    sides[0, 0, 0] = after_low
    errors = dot(after_low, weights[0]) + lines[PIXEL : PIXEL + 1] - target_in[0].astype(F32)
    square = errors * errors + 1.0
    root = lax.rsqrt(square)
    grad_pred = (mask * errors * root).astype(BF16)
    sides[0, 1, 0] = grad_pred
    sums_out[0:1] += column_sums(grad_pred)
    sums_out[5:6] += jnp.sum((square * root - 1.0) * mask, axis=0, keepdims=True)
    sums_out[10:11] += jnp.sum(jnp.broadcast_to(mask, errors.shape), axis=0, keepdims=True)


def middle(embedded, mixed, mask, targets, weights, reduce, lines):
    near, rows, width = embedded.shape
    parts = reduce.shape[1]
    block = pl.BlockSpec((1, rows, width), lambda i: (i, 0, 0))
    column = pl.BlockSpec((1, rows, 1), lambda i: (i, 0, 0))
    stack = pl.BlockSpec((1, 2, parts + 2, rows, width), lambda i: (i, 0, 0, 0, 0))
    return pl.pallas_call(
        middle_kernel,
        grid=(near,),
        in_specs=[
            block,
            block,
            column,
            block,
            fixed((parts + 2, width, width)),
            fixed(reduce.shape),
            fixed(lines.shape),
        ],
        out_specs=[stack, block, column, fixed_out((16, width))],
        out_shape=[
            jax.ShapeDtypeStruct((near, 2, parts + 2, rows, width), BF16),
            jax.ShapeDtypeStruct((near, rows, width), BF16),
            jax.ShapeDtypeStruct((near, rows, 1), F32),
            jax.ShapeDtypeStruct((16, width), F32),
        ],
        scratch_shapes=[
            pltpu.VMEM((rows, width), BF16),
            pltpu.VMEM((rows, width), F32),
            pltpu.VMEM((parts, 1, width), F32),
        ],
        compiler_params=params(60),
        cost_estimate=cost(2 * near * rows * width * width * (2 * parts + 2), 40e6),
        name="middle",
    )(embedded, mixed, mask, targets, weights, reduce, lines)


HIGH_ROWS = 4 * 96


def spread_half(result, target, high, start, names, swapped):
    for low in range(2):
        for x in range(2):
            for y in range(2):
                at = (low * 2 + x) * 96 + start
                piece = result[at : at + HALF, y * 384 : (y + 1) * 384]
                spot = {"high": high, "low": low, "x": x, "y": y}
                if swapped is not None:
                    first, second = swapped
                    spot[first], spot[second] = spot[second], spot[first]
                target[tuple(spot[name] for name in names)] = piece.astype(BF16)


HALF = 48
SLOTS = 4
KEPT = 10
FIRST_ATTEND = 10
GROUP_STEPS = (14, 18, 21)
FIRST_NORM = 22


def back_kernel(
    counts, sides, weights, reduce, input_two, scaling_two, input_one, joint, pairs, probs_in, lines, sums_in,
    embedded_in, mask_in, *rest,
):
    (
        done_out,
        near_out,
        far_out,
        sums_out,
        late_out,
        done,
        done_sent,
        branch,
        wide,
        grad_in,
        upstream,
        own_pairs,
        give_pairs,
        got_pairs,
        far_give,
        sums,
        late,
        keep,
        give,
        got,
        send,
        receive,
        core_send,
        core_receive,
        pair_send,
        pair_receive,
        far_send,
        far_receive,
    ) = rest[:28]
    buffers = split_list(rest[28:], counts)
    where = places()
    core, sibling = where["core"]
    step = pl.program_id(0)
    images, rows, width = input_two.shape
    every = images * rows
    quarter = rows // 2
    heads = width // PAIR
    first_gain, second_gain = lines[GAIN_ONE : GAIN_ONE + 1], lines[GAIN_TWO : GAIN_TWO + 1]
    chains = [
        Chain(where, keep.at[unit % KEPT], names_of(order), order, list(buffers[unit]) + [done.at[unit]], send, receive, MOST * unit, TILE_SWAPS[unit])
        for unit, order in enumerate(TILE_ORDERS)
    ]
    chains.append(Chain(where, sums, (), SUMS_ORDER, buffers[TILES], send, receive, MOST * TILES))
    chains.append(Chain(where, late, (), SUMS_ORDER, buffers[TILES + 1], send, receive, MOST * TILES + MOST))

    def core_copy(unit):
        slot = lax.rem(unit, SLOTS)
        return remote(give.at[slot], got.at[slot], core_send.at[unit], core_receive.at[unit], sibling)

    def pair_copy(place, second):
        image = lax.rem(place, 3)
        slot = lax.rem((lax.div(place, 6) * 3 + image) * 2 + second, SLOTS)
        return remote(
            give_pairs.at[slot], got_pairs.at[place], pair_send.at[place], pair_receive.at[place], sibling
        )

    def far_copy(image):
        return remote(
            far_give.at[image], far_out.at[image], far_send.at[image], far_receive.at[image], where["y"][1]
        )

    def core_sum(unit):
        core_copy(unit).wait()
        for_each(4, lambda spot: add_up(keep.at[unit % KEPT], spot, got[(unit % SLOTS,) + spot]))

    def done_copy(unit):
        return pltpu.make_async_copy(done.at[unit], done_out.at[unit], done_sent.at[unit])

    def turn(unit, stage):
        if unit < TILES and stage == 0:
            core_sum(unit)
        chains[unit].turn(stage)
        if stage == len(chains[unit].order) and unit < TILES:
            done_copy(unit).start()

    def tile(unit, lines_of, value, forms):
        def one(high):
            columns = slice(high * HIGH_ROWS, (high + 1) * HIGH_ROWS)
            result = dot_tn(lines_of(columns).reshape(every, HIGH_ROWS), value)
            for half in range(2):
                for names, swapped, chosen in forms:
                    swapped = swapped if half == 1 else None

                    @pl.when(jnp.logical_and(core == half, chosen))
                    def _(half=half, names=names, swapped=swapped):
                        spread_half(result, keep.at[lax.rem(unit, KEPT)], high, half * HALF, names, swapped)

                    @pl.when(jnp.logical_and(core != half, chosen))
                    def _(half=half, names=names, swapped=swapped):
                        spread_half(result, give.at[lax.rem(unit, SLOTS)], high, half * HALF, names, swapped)

        for high in range(2):
            one(high)
        core_copy(unit).start()

    def forms_of(units, unit):
        forms = {}
        for other in units:
            form = (names_of(TILE_ORDERS[other]), TILE_SWAPS[other])
            forms.setdefault(form, []).append(unit == other)
        if len(forms) == 1:
            return [form + (True,) for form in forms]
        return [form + (functools.reduce(jnp.logical_or, asked),) for form, asked in forms.items()]

    def flat(ref):
        return ref[...].reshape(every, ref.shape[-1])

    def left_lines(columns):
        return sides[:, 0, 0, :, columns]

    @pl.when(step == 0)
    def _():
        greet(where)
        sums[...] = sums_in[...]
        late[...] = jnp.zeros_like(late)
        grad_in[...] = jnp.zeros_like(grad_in)

    for at, turns in TURNS.items():

        @pl.when(step == at)
        def _(turns=turns):
            for unit, stage in turns:
                turn(unit, stage)

    @pl.when(step == 0)
    def _():
        tile(0, left_lines, sides[:, 1, 0].reshape(every, width), forms_of((0,), 0))

        def one(image):
            low = dot_nt(sides[image, 1, 0], weights[0]).astype(BF16)
            branch[image] = low
            sums[1:2] += column_sums(low)
        for image in range(images):
            one(image)

    @pl.when((step > 0) & (step < 9) & (lax.rem(step, 2) == 1))
    def _():
        tile(step, left_lines, flat(branch), forms_of((1, 3, 5, 7), step))
        row = pl.ds(6 + lax.div(step, 2), 1)

        def one(image):
            low = dot_nt(branch[image], reduce[:, 0].reshape(width, width)) * sides[image, 1, 0].astype(F32)
            low = low.astype(BF16)
            wide[image] = low
            sums[row] += column_sums(low)
        for image in range(images):
            one(image)

    @pl.when((step > 0) & (step < 9) & (lax.rem(step, 2) == 0))
    def _():
        tile(step, lambda columns: input_two[:, :, columns], flat(wide), forms_of((2, 4, 6, 8), step))
        fresh = jnp.where(step == 2, 0.0, 1.0)

        def one(image):
            grad_in[image] = grad_in[image] * fresh + dot_nt(wide[image], weights[0])
        for image in range(images):
            one(image)

    @pl.when(step == 9)
    def _():
        def one(image):
            normed = sides[image, 1, 0].astype(F32)
            grad = grad_in[image]
            low = branch[image].astype(F32) + normalize_back(grad, normed, scaling_two[image], second_gain)
            low = low.astype(BF16)
            branch[image] = low
            sums[2:3] += column_sums(grad * normed)
            sums[3:4] += column_sums(grad)
            sums[4:5] += column_sums(low)
            mixed = dot_nt(low, weights[0]).astype(BF16)
            for pair in range(heads):
                upstream[image, pair] = mixed[:, pair * PAIR : (pair + 1) * PAIR]
        for image in range(images):
            one(image)

        tile(9, left_lines, flat(branch), forms_of((9,), 9))

    def attend_back(group, image, second, inside, order):
        place = group * 6 + inside

        @pl.when(order >= SLOTS)
        def _():
            before = order - SLOTS
            pair_copy(lax.div(before, 6) * 6 + second * 3 + lax.rem(lax.div(before, 2), 3), second).wait_send()

        scale = HEAD_DIM**-0.5
        target = own_pairs.at[lax.rem(group, 2), inside]
        away = give_pairs.at[lax.rem(order, SLOTS)]
        queries = side_by_side(joint[0, second, 0])
        keys_in = jnp.concatenate([joint[0, second, 1], pairs[0, second, 0]], axis=0)
        values_in = jnp.concatenate([joint[0, second, 2], pairs[0, second, 1]], axis=0)
        grad_mixed = side_by_side(upstream[image, group * 2 + second])
        probs = probs_in[0, second]
        grad_probs = dot_nt(values_in, grad_mixed)
        broad = probs.astype(F32)
        weighted = broad * grad_probs
        inner = jnp.sum(weighted, axis=0, keepdims=True)
        grad_scores = (weighted - broad * inner).astype(BF16)
        grad_values = dot(probs, grad_mixed).astype(BF16)
        grad_keys = (dot(grad_scores, queries) * scale).astype(BF16)
        target[0] = (merge_turned(dot_tn(keys_in, grad_scores)) * scale).astype(BF16)
        target[1] = grad_keys[:rows]
        target[2] = grad_values[:rows]
        away[0] = grad_keys[rows:]
        away[1] = grad_values[rows:]
        pair_copy(place, second).start()

    attends = (step >= FIRST_ATTEND) & (step < GROUP_STEPS[2]) & (step != GROUP_STEPS[0]) & (step != GROUP_STEPS[1])

    @pl.when(attends)
    def _():
        group, image = attend_place(step)
        for second in range(2):
            inside = second * 3 + image
            attend_back(group, image, second, inside, (group * 3 + image) * 2 + second)

    @pl.when((step == GROUP_STEPS[0]) | (step == GROUP_STEPS[1]) | (step == GROUP_STEPS[2]))
    def _():
        group = jnp.where(step == GROUP_STEPS[0], 0, jnp.where(step == GROUP_STEPS[1], 1, 2))
        slot = lax.rem(group, 2)
        for inside in range(6):
            pair_copy(group * 6 + inside, inside // 3).wait_recv()
            image, second = inside % 3, inside // 3
            for part in range(3):
                piece = own_pairs[slot, inside, part]
                if part > 0:
                    piece = piece.astype(F32) + got_pairs[group * 6 + inside, part - 1].astype(F32)
                start = part * 2 * PAIR + second * PAIR
                wide[image, :, start : start + PAIR] = piece.astype(BF16)
        tile(10 + group, lambda columns: input_one[:, :, columns], flat(wide), forms_of((10, 11, 12), 10 + group))
        fresh = jnp.where(group == 0, 0.0, 1.0)
        row = pl.ds(5 + group, 1)

        def one(image):
            late[row] += column_sums(wide[image])
            grad_in[image] = grad_in[image] * fresh + dot_nt(wide[image], weights[0])
        for image in range(images):
            one(image)

    @pl.when(step == FIRST_NORM)
    def _():
        for image in range(images):
            mask = mask_in[image]
            normed, scaling = normalize(embedded_in[image].astype(F32))
            grad = grad_in[image]
            total = branch[image].astype(F32) + normalize_back(grad, normed, scaling, first_gain)
            kept = total * (1.0 - mask)
            far_give[image] = kept[quarter:].astype(BF16)
            far_copy(image).start()
            near_out[image] = kept[:quarter]
            late[0:1] += column_sums(grad * normed)
            late[1:2] += column_sums(grad)
            late[2:3] += column_sums(total * mask)
            if image == 0:
                turn(TILES - 1, 0)

    @pl.when(step == pl.num_programs(0) - 1)
    def _():
        for unit, stage in LAST_TURNS:
            turn(unit, stage)
        for image in range(images):
            far_copy(image).wait()
        for unit in range(TILES):
            done_copy(unit).wait()
        for image in range(1, 3):
            for second in range(2):
                pair_copy(12 + second * 3 + image, second).wait_send()
        sums_out[...] = chains[TILES].refs[-1][...]
        late_out[...] = chains[TILES + 1].refs[-1][...]


def attend_place(step):
    place = step - FIRST_ATTEND
    for at in GROUP_STEPS[:2]:
        place = place - jnp.where(step > at, 1, 0)
    place = jnp.clip(place, 0, 8)
    return lax.div(place, 3), lax.rem(place, 3)


def back(
    sides, weights, reduce, input_two, scaling_two, input_one, joint, pairs, probs, lines, sums, embedded, mask
):
    near, _, slots, rows, width = sides.shape
    quarter = rows // 2
    heads = width // PAIR

    def slot(step):
        return jnp.minimum(lax.div(step + 1, 2), slots - 1)

    def part(step):
        return jnp.clip(lax.div(step - 1, 2), 0, slots - 3)

    def weight(step):
        late = slots + jnp.where(step > GROUP_STEPS[0], 1, 0) + jnp.where(step > GROUP_STEPS[1], 1, 0)
        return jnp.where(step < FIRST_ATTEND, slot(step), late)

    def spot(step):
        group, image = attend_place(step)
        return image, group

    cases = [(names_of(order), order, (HALF, 384), BF16) for order in TILE_ORDERS]
    cases.append(((), SUMS_ORDER, sums.shape, F32))
    cases.append(((), SUMS_ORDER, (8, width), F32))
    buffers, counts = chain_scratch(cases)
    kept, start = [], 0
    for index, count in enumerate(counts):
        kept += buffers[start : start + count - (index < TILES)]
        start += count
    buffers, counts = kept, [count - (index < TILES) for index, count in enumerate(counts)]
    whole = (2, 2, 2, 2, HALF, 384)
    stack = pl.BlockSpec((near, 2, 1, rows, width), lambda s: (0, 0, slot(s), 0, 0))
    return pl.pallas_call(
        partial(back_kernel, counts),
        grid=(FIRST_NORM + 1,),
        in_specs=[
            stack,
            pl.BlockSpec((1, width, width), lambda s: (weight(s), 0, 0)),
            pl.BlockSpec((8, 1, reduce.shape[2], width), lambda s: (0, part(s), 0, 0)),
            fixed((near, rows, width)),
            fixed((near, rows, 1)),
            fixed((near, rows, width)),
            pl.BlockSpec((1, 2, 3, rows, PAIR), lambda s: spot(s) + (0, 0, 0)),
            pl.BlockSpec((1, 2, 2, rows, PAIR), lambda s: spot(s) + (0, 0, 0)),
            pl.BlockSpec((1, 2, 2 * rows, 2 * rows), lambda s: spot(s) + (0, 0)),
            fixed(lines.shape),
            fixed(sums.shape),
            fixed((near, rows, width)),
            fixed((near, rows, 1)),
        ],
        out_specs=[
            pl.BlockSpec(memory_space=pl.ANY),
            fixed((near, quarter, width)),
            pl.BlockSpec(memory_space=pl.ANY),
            fixed_out(sums.shape),
            fixed_out((8, width)),
        ],
        out_shape=[
            jax.ShapeDtypeStruct((TILES, 2, 2, HALF, 384), BF16),
            jax.ShapeDtypeStruct((near, quarter, width), F32),
            jax.ShapeDtypeStruct((near, quarter, width), BF16),
            jax.ShapeDtypeStruct(sums.shape, F32),
            jax.ShapeDtypeStruct((8, width), F32),
        ],
        scratch_shapes=[
            pltpu.VMEM((TILES, 2, 2, HALF, 384), BF16),
            pltpu.SemaphoreType.DMA((TILES,)),
            pltpu.VMEM((near, rows, width), BF16),
            pltpu.VMEM((near, rows, width), BF16),
            pltpu.VMEM((near, rows, width), F32),
            pltpu.VMEM((near, heads, rows, PAIR), BF16),
            pltpu.VMEM((2, 6, 3, rows, PAIR), BF16),
            pltpu.VMEM((SLOTS, 2, rows, PAIR), BF16),
            pltpu.VMEM((near * heads, 2, rows, PAIR), BF16),
            pltpu.VMEM((near, quarter, width), BF16),
            pltpu.VMEM(sums.shape, F32),
            pltpu.VMEM((8, width), F32),
            pltpu.VMEM((KEPT,) + whole, BF16),
            pltpu.VMEM((SLOTS,) + whole, BF16),
            pltpu.VMEM((SLOTS,) + whole, BF16),
            pltpu.SemaphoreType.DMA((MOST * (TILES + 2),)),
            pltpu.SemaphoreType.DMA((MOST * (TILES + 2),)),
            pltpu.SemaphoreType.DMA((TILES,)),
            pltpu.SemaphoreType.DMA((TILES,)),
            pltpu.SemaphoreType.DMA((near * heads,)),
            pltpu.SemaphoreType.DMA((near * heads,)),
            pltpu.SemaphoreType.DMA((near,)),
            pltpu.SemaphoreType.DMA((near,)),
        ]
        + buffers,
        compiler_params=pltpu.CompilerParams(
            vmem_limit_bytes=60 * MIB, collective_id=2, has_side_effects=True
        ),
        cost_estimate=cost(40e9, 60e6),
        name="back",
    )(
        sides, weights, reduce, input_two,
        scaling_two, input_one, joint, pairs, probs, lines, sums, embedded, mask,
    )


def emit_kernel(parts, done, near_in, far_in, sums, late, *outs):
    (
        loss, attend_gain, attend_shift, joint, query_bias, value_bias, output, output_bias, feed_gain,
        feed_shift, expand, expand_bias, reduce, reduce_bias, pixel, pixel_bias, token, patch,
    ) = outs
    data, y = lax.axis_index("dp"), lax.div(lax.axis_index("seq"), 2)
    inverse = 1.0 / (sums[10:11] * PIXELS)
    loss[0] = jnp.sum(sums[5:6] * inverse)
    wide_inverse = inverse[:, :384]

    def piece(unit, core, half):
        return done[unit, core, half].astype(F32) * wide_inverse

    def square(unit):
        return [
            jnp.concatenate([piece(unit, core, half) for half in range(2)], axis=1) for core in range(2)
        ]

    for unit, target in ((0, pixel), (2 * parts + 1, output)):
        for core, lines in enumerate(square(unit)):
            target[core * HALF : (core + 1) * HALF] = lines
    expands = []
    for part in range(parts):
        for core, lines in enumerate(square(1 + 2 * part)):
            start = part * 2 * HALF + core * HALF
            reduce[start : start + HALF] = lines
        expands.append(square(2 + 2 * part))
    span = 2 * HALF
    for core in range(2):
        for d in range(8):
            lines = [expands[part][core][:, d * span : (d + 1) * span] for part in range(parts)]
            expand[core * HALF : (core + 1) * HALF, d * 4 * span : (d + 1) * 4 * span] = jnp.concatenate(
                lines, axis=1
            )
    for group in range(3):
        for core, lines in enumerate(square(2 * parts + 2 + group)):
            for part in range(3):
                start = part * WIDE + group * 2 * PAIR
                joint[core * HALF : (core + 1) * HALF, start : start + 2 * PAIR] = lines[
                    :, part * 2 * PAIR : (part + 1) * 2 * PAIR
                ]

    def own_cut(lines):
        shift = lax.rem(WIDE - data * span, WIDE)
        return pltpu.roll(lines, shift, axis=1)[:, :span]

    early = own_cut(sums[...] * inverse)
    later = own_cut(late[...] * inverse)
    queries = jnp.concatenate([late[5 + group : 6 + group, : 2 * PAIR] for group in range(3)], axis=1)
    values = jnp.concatenate([late[5 + group : 6 + group, 4 * PAIR :] for group in range(3)], axis=1)
    both = jnp.concatenate([queries, values] + [jnp.zeros((6, WIDE), F32)], axis=0)
    both = own_cut(both * inverse)
    for target, lines, row in (
        (attend_gain, later, 0),
        (attend_shift, later, 1),
        (query_bias, both, 0),
        (value_bias, both, 1),
        (output_bias, early, 4),
        (feed_gain, early, 2),
        (feed_shift, early, 3),
        (reduce_bias, early, 1),
        (pixel_bias, early, 0),
        (token, later, 2),
    ):
        target[...] = lines[row : row + 1]
    expand_bias[...] = jnp.concatenate([early[6 + part : 7 + part] for part in range(parts)], axis=1)
    images = near_in.shape[0]
    for image in range(images):
        patch[y * images + image] = near_in[image] * inverse
        patch[(1 - y) * images + image] = far_in[image].astype(F32) * inverse


def emit(parts, done, near_in, far_in, sums, late):
    images, quarter, width = near_in.shape
    hidden = parts * width

    def out(*shape):
        return jax.ShapeDtypeStruct(shape, F32)

    small = out(1, 96)
    outs = [
        out(1), small, small, out(96, 3 * width), small, small, out(96, width), small, small,
        small, out(96, hidden), out(1, hidden // 8), out(hidden // 8, width), small, out(96, width), small, small,
        out(2 * images, quarter, width),
    ]
    whole = pl.BlockSpec(memory_space=pltpu.VMEM)
    return pl.pallas_call(
        partial(emit_kernel, parts),
        in_specs=[whole] * 5,
        out_specs=[pl.BlockSpec(memory_space=pltpu.SMEM)] + [whole] * (len(outs) - 1),
        out_shape=outs,
        compiler_params=params(60),
        cost_estimate=cost(1e6, 12e6),
        name="emit",
    )(done, near_in, far_in, sums, late)


def eight_places(
    patches,
    targets,
    mask_order,
    mask_count,
    attend_gain,
    attend_shift,
    joint_weight,
    query_bias,
    value_bias,
    output_weight,
    output_bias,
    feed_gain,
    feed_shift,
    expand_weight,
    expand_bias,
    reduce_weight,
    reduce_bias,
    pixel_weight,
    pixel_bias,
    mask_token,
):
    images, quarter, features = patches.shape
    near = images // 2
    place_y = own_bit("seq", 2)
    hidden = expand_bias.shape[0]
    parts = hidden // features

    def halves(values):
        return values.reshape((2, near) + values.shape[1:])

    lines = stack_lines(
        attend_gain,
        attend_shift,
        query_bias,
        value_bias,
        output_bias,
        feed_gain,
        feed_shift,
        reduce_bias,
        pixel_bias,
        mask_token,
        expand_bias,
    )
    orders = jnp.pad(mask_order[:, None, :], ((0, 0), (0, 7), (0, 256 - quarter)))
    reduce_parts = reduce_weight.reshape(8, parts, hidden // (8 * parts), features)
    embedded, input_one, joint, pairs, mixed, probs, mask, targets_here, weights = front(
        mask_count,
        halves(patches),
        halves(targets),
        halves(orders),
        lines,
        joint_weight,
        pixel_weight,
        expand_weight,
        output_weight,
    )
    sides, input_two, scaling_two, sums = middle(
        embedded, mixed, mask, targets_here, weights, reduce_parts, lines
    )
    done, patch_near, patch_far, sums, late = back(
        sides,
        weights,
        reduce_parts,
        input_two,
        scaling_two,
        input_one,
        joint,
        pairs,
        probs,
        lines,
        sums,
        embedded,
        mask,
    )
    outs = emit(parts, done, patch_near, patch_far, sums, late)
    flat = {0: (), 1: (-1,), 2: (-1,), 4: (-1,), 5: (-1,), 7: (-1,), 8: (-1,), 9: (-1,), 11: (-1,)}
    flat.update({13: (-1,), 15: (-1,), 16: (-1,)})
    return tuple(
        out.reshape(flat[index]) if index in flat else out for index, out in enumerate(outs)
    )


def on_device(*arguments):
    if lax.axis_size("dp") == 8 and lax.axis_size("seq") == 4:
        return eight_places(*arguments)
    return any_places(*arguments)


def solution(mesh):
    placed = (
        P("dp", "seq", None),
        P("dp", "seq", None),
        P("dp", "seq"),
        P("dp"),
        P(),
        P(),
        P(),
        P(),
        P(),
        P(),
        P(),
        P(),
        P(),
        P(),
        P(),
        P(),
        P(),
        P(),
        P(),
        P(),
    )
    return jax.shard_map(
        on_device,
        mesh=mesh,
        in_specs=placed,
        out_specs=(
            P(),
            P("dp"),
            P("dp"),
            P("dp", None),
            P("dp"),
            P("dp"),
            P("dp", None),
            P("dp"),
            P("dp"),
            P("dp"),
            P("dp", None),
            P("dp"),
            P("dp", None),
            P("dp"),
            P("dp", None),
            P("dp"),
            P("dp"),
            P("dp", "seq", None),
        ),
        check_vma=False,
    )
```

```python
import functools
import itertools
from functools import partial

import jax
import jax.numpy as jnp
from jax import lax
from jax.experimental import pallas as pl
from jax.experimental.pallas import tpu as pltpu
from jax.sharding import PartitionSpec as P

HEADS = 12
HEAD_DIM = 64
PIXELS = 768
WIDE = 768
PAIR = 2 * HEAD_DIM
MIB = 1 << 20
F32 = jnp.float32
BF16 = jnp.bfloat16


def dot(left, right):
    return jnp.dot(left, right, preferred_element_type=F32)


def dot_nt(left, right):
    return lax.dot_general(left, right, (((1,), (1,)), ((), ())), preferred_element_type=F32)


def dot_tn(left, right):
    return lax.dot_general(left, right, (((0,), (0,)), ((), ())), preferred_element_type=F32)


def normalize(inputs):
    centre = inputs - jnp.mean(inputs, axis=-1, keepdims=True)
    scaling = lax.rsqrt(jnp.mean(centre * centre, axis=-1, keepdims=True) + 1e-06)
    return (centre * scaling, scaling)


def normalize_back(upstream, normed, scaling, gain):
    scaled = upstream * gain
    return scaling * (
        scaled
        - jnp.mean(scaled, axis=-1, keepdims=True)
        - normed * jnp.mean(scaled * normed, axis=-1, keepdims=True)
    )


def column_sums(values):
    return jnp.sum(values.astype(F32), axis=0, keepdims=True)


def gelu_both(inputs):
    bell = jnp.exp2(inputs * inputs * (-0.5 * 1.4426950408889634))
    base_of = 1.0 + (0.3275911 * 0.7071067811865476) * jnp.abs(inputs)
    inner = pl.reciprocal(base_of, approx=True)
    inner = inner * (2.0 - base_of * inner)
    series = 0.5 * 1.453152027 - inner * (0.5 * 1.061405429)
    series = 0.5 * 1.421413741 - inner * series
    series = 0.5 * 0.284496736 - inner * series
    series = 0.5 * 0.254829592 - inner * series
    tail = series * inner * bell
    below = jnp.where(inputs < 0.0, tail, 1.0 - tail)
    return (inputs * below, below + inputs * bell * 0.3989422804014327)


def params(limit):
    return pltpu.CompilerParams(vmem_limit_bytes=limit * MIB)


def fixed(shape):
    zeros = (0,) * len(shape)
    return pl.BlockSpec(shape, lambda *place: zeros, pipeline_mode=pl.Buffered(1))


def cost(flops, moved):
    return pl.CostEstimate(flops=int(flops), bytes_accessed=int(moved), transcendentals=0)


def project_kernel(own, far, gain, shift, weight, bias, embedded_out, joint_out):
    embedded = jnp.concatenate([own[0], far[0]], axis=0)
    embedded_out[0] = embedded
    normed, _ = normalize(embedded.astype(F32))
    low = (normed * gain[...] + shift[...]).astype(BF16)
    for part in range(3):
        cut = slice(part * WIDE, (part + 1) * WIDE)
        joint_out[0, part] = (dot(low, weight[:, cut]) + bias[:, cut]).astype(BF16)


def project(own, far, gain, shift, weight, bias):
    near, quarter, width = own.shape
    rows = 2 * quarter
    return pl.pallas_call(
        project_kernel,
        grid=(near,),
        in_specs=[
            pl.BlockSpec((1, quarter, width), lambda i: (i, 0, 0)),
            pl.BlockSpec((1, quarter, width), lambda i: (i, 0, 0)),
            fixed((1, width)),
            fixed((1, width)),
            fixed((width, 3 * width)),
            fixed((1, 3 * width)),
        ],
        out_specs=[
            pl.BlockSpec((1, rows, width), lambda i: (i, 0, 0)),
            pl.BlockSpec((1, 3, rows, width), lambda i: (i, 0, 0, 0)),
        ],
        out_shape=[
            jax.ShapeDtypeStruct((near, rows, width), BF16),
            jax.ShapeDtypeStruct((near, 3, rows, width), BF16),
        ],
        compiler_params=params(32),
        cost_estimate=cost(2 * near * rows * width * 3 * width, 12e6),
        name="project",
    )(own, far, gain, shift, weight, bias)


def side_by_side(pair):
    lanes = lax.broadcasted_iota(jnp.int32, pair.shape, 1)
    zero = jnp.zeros_like(pair)
    first = jnp.where(lanes < HEAD_DIM, pair, zero)
    second = jnp.where(lanes < HEAD_DIM, zero, pair)
    return jnp.concatenate([first, second], axis=0)


def merge_heads(stacked):
    rows = stacked.shape[0] // 2
    lanes = lax.broadcasted_iota(jnp.int32, (rows, PAIR), 1)
    return jnp.where(lanes < HEAD_DIM, stacked[:rows], stacked[rows:])


def attend_kernel(own, far, mixed_out, probs_out):
    queries = side_by_side(own[0, 0] * jnp.asarray(HEAD_DIM**-0.5, BF16))
    keys_in = jnp.concatenate([own[0, 1], far[0, 0]], axis=0)
    values_in = jnp.concatenate([own[0, 2], far[0, 1]], axis=0)
    scores = dot_nt(queries, keys_in)
    exponent = jnp.exp(scores - jnp.max(scores, axis=-1, keepdims=True))
    total = jnp.sum(exponent, axis=-1, keepdims=True)
    probs = (exponent * (1.0 / total)).astype(BF16)
    probs_out[0, 0] = probs
    mixed_out[0] = merge_heads(dot(probs, values_in)).astype(BF16)


def attend(joint, pairs_far):
    near, _, rows, width = joint.shape
    keys_count = 2 * rows
    pairs = width // PAIR
    return pl.pallas_call(
        attend_kernel,
        grid=(near, pairs),
        in_specs=[
            pl.BlockSpec((1, 3, rows, PAIR), lambda i, h: (i, 0, 0, h)),
            pl.BlockSpec((1, 2, rows, PAIR), lambda i, h: (i, 0, 0, h)),
        ],
        out_specs=[
            pl.BlockSpec((1, rows, PAIR), lambda i, h: (i, 0, h)),
            pl.BlockSpec((1, 1, 2 * rows, keys_count), lambda i, h: (i, h, 0, 0)),
        ],
        out_shape=[
            jax.ShapeDtypeStruct((near, rows, width), BF16),
            jax.ShapeDtypeStruct((near, pairs, 2 * rows, keys_count), BF16),
        ],
        compiler_params=params(32),
        cost_estimate=cost(8 * near * rows * keys_count * width, 20e6),
        name="attend",
    )(joint, pairs_far)


def attend_back_kernel(own, far, probs_in, upstream, query_out, own_out, far_out):
    rows = own.shape[2]
    scale = HEAD_DIM**-0.5
    queries = side_by_side(own[0, 0])
    keys_in = jnp.concatenate([own[0, 1], far[0, 0]], axis=0)
    values_in = jnp.concatenate([own[0, 2], far[0, 1]], axis=0)
    grad_mixed = side_by_side(upstream[0])
    probs = probs_in[0, 0]
    grad_probs = dot_nt(grad_mixed, values_in)
    wide = probs.astype(F32)
    weighted = wide * grad_probs
    inner = jnp.sum(weighted, axis=-1, keepdims=True)
    grad_scores = (weighted - wide * inner).astype(BF16)
    query_out[0] = (merge_heads(dot(grad_scores, keys_in)) * scale).astype(BF16)
    grad_values = dot_tn(probs, grad_mixed).astype(BF16)
    grad_keys = (dot_tn(grad_scores, queries) * scale).astype(BF16)
    own_out[0, 0] = grad_keys[:rows]
    own_out[0, 1] = grad_values[:rows]
    far_out[0, 0] = grad_keys[rows:]
    far_out[0, 1] = grad_values[rows:]


def attend_back(joint, pairs_far, probs, upstream):
    near, _, rows, width = joint.shape
    keys_count = 2 * rows
    pairs = width // PAIR
    two = pl.BlockSpec((1, 2, rows, PAIR), lambda i, h: (i, 0, 0, h))
    one = pl.BlockSpec((1, rows, PAIR), lambda i, h: (i, 0, h))
    return pl.pallas_call(
        attend_back_kernel,
        grid=(near, pairs),
        in_specs=[
            pl.BlockSpec((1, 3, rows, PAIR), lambda i, h: (i, 0, 0, h)),
            two,
            pl.BlockSpec((1, 1, 2 * rows, keys_count), lambda i, h: (i, h, 0, 0)),
            one,
        ],
        out_specs=[one, two, two],
        out_shape=[
            jax.ShapeDtypeStruct((near, rows, width), BF16),
            jax.ShapeDtypeStruct((near, 2, rows, width), BF16),
            jax.ShapeDtypeStruct((near, 2, rows, width), BF16),
        ],
        compiler_params=params(32),
        cost_estimate=cost(16 * near * rows * keys_count * width, 25e6),
        name="attend_back",
    )(joint, pairs_far, probs, upstream)


def rows_kernel(
    hidden,
    inverse,
    embedded_in,
    mixed,
    mask_in,
    target_own,
    target_far,
    output_weight,
    expand_weight,
    reduce_weight,
    pixel_weight,
    biases,
    expand_bias,
    input_out,
    active_out,
    after_out,
    pred_out,
    branch_out,
    expand_out,
    low_out,
    attn_out,
    mixed_out,
    sums_out,
    slope,
):
    output_bias, gain, shift, reduce_bias, pixel_bias = (biases[row : row + 1] for row in range(5))
    mask = mask_in[0]
    after_attn = embedded_in[0].astype(F32) + dot(mixed[0], output_weight[...]) + output_bias
    normed, scaling = normalize(after_attn)
    low = (normed * gain + shift).astype(BF16)
    input_out[0] = low
    total = after_attn + reduce_bias
    for start in range(0, hidden, WIDE):
        cut = slice(start, start + WIDE)
        active, rate = gelu_both(dot(low, expand_weight[:, cut]) + expand_bias[:, cut])
        active = active.astype(BF16)
        active_out[0, :, cut] = active
        slope[:, cut] = rate.astype(slope.dtype)
        total += dot(active, reduce_weight[cut, :])
    after_low = total.astype(BF16)
    after_out[0] = after_low
    target = jnp.concatenate([target_own[0], target_far[0]], axis=0).astype(F32)
    errors = dot(after_low, pixel_weight[...]) + pixel_bias - target
    square = errors * errors + 1.0
    root = lax.rsqrt(square)
    channel = jnp.sum((square * root - 1.0) * mask, axis=0, keepdims=True)
    grad_pred = (mask * errors * root * inverse[0, 0]).astype(BF16)
    pred_out[0] = grad_pred
    grad_mlp = dot_nt(grad_pred, pixel_weight[...])
    branch = grad_mlp.astype(BF16)
    branch_out[0] = branch
    grad_in = jnp.zeros_like(grad_mlp)
    expand_sums = []
    for start in range(0, hidden, WIDE):
        cut = slice(start, start + WIDE)
        grad_expand = dot_nt(branch, reduce_weight[cut, :]) * slope[:, cut].astype(F32)
        grad_expand = grad_expand.astype(BF16)
        expand_out[0, :, cut] = grad_expand
        expand_sums.append(column_sums(grad_expand))
        grad_in += dot_nt(grad_expand, expand_weight[:, cut])
    grad_attn = grad_mlp + normalize_back(grad_in, normed, scaling, gain)
    attn_out[0] = grad_attn
    grad_low = grad_attn.astype(BF16)
    low_out[0] = grad_low
    mixed_out[0] = dot_nt(grad_low, output_weight[...]).astype(BF16)
    sums = [
        column_sums(grad_pred),
        column_sums(branch),
        column_sums(grad_in * normed),
        column_sums(grad_in),
        column_sums(grad_low),
        channel,
    ] + expand_sums

    @pl.when(pl.program_id(0) == 0)
    def _():
        sums_out[...] = jnp.zeros_like(sums_out)

    for row, line in enumerate(sums):
        sums_out[row : row + 1] += line


def rows_step(
    inverse,
    embedded,
    mixed,
    mask,
    target_own,
    target_far,
    output_weight,
    expand_weight,
    reduce_weight,
    pixel_weight,
    biases,
    expand_bias,
):
    near, rows, width = embedded.shape
    quarter = target_own.shape[1]
    hidden = expand_weight.shape[1]
    block = pl.BlockSpec((1, rows, width), lambda i: (i, 0, 0))
    half = pl.BlockSpec((1, quarter, width), lambda i: (i, 0, 0))
    long = pl.BlockSpec((1, rows, hidden), lambda i: (i, 0, 0))
    narrow = jax.ShapeDtypeStruct((near, rows, width), BF16)
    broad = jax.ShapeDtypeStruct((near, rows, hidden), BF16)
    return pl.pallas_call(
        partial(rows_kernel, hidden),
        grid=(near,),
        in_specs=[
            pl.BlockSpec(memory_space=pltpu.SMEM),
            block,
            block,
            pl.BlockSpec((1, rows, 1), lambda i: (i, 0, 0)),
            half,
            half,
            fixed((width, width)),
            fixed((width, hidden)),
            fixed((hidden, width)),
            fixed((width, width)),
            fixed((8, width)),
            fixed((1, hidden)),
        ],
        out_specs=[block, long, block, block, block, long, block, block, block, fixed_out((16, width))],
        out_shape=[
            narrow,
            broad,
            narrow,
            narrow,
            narrow,
            broad,
            narrow,
            jax.ShapeDtypeStruct((near, rows, width), F32),
            narrow,
            jax.ShapeDtypeStruct((16, width), F32),
        ],
        scratch_shapes=[pltpu.VMEM((rows, hidden), F32)],
        compiler_params=params(56),
        cost_estimate=cost(4 * near * rows * width * (2 * width + 2 * hidden), 40e6),
        name="rows_step",
    )(
        inverse,
        embedded,
        mixed,
        mask,
        target_own,
        target_far,
        output_weight,
        expand_weight,
        reduce_weight,
        pixel_weight,
        biases,
        expand_bias,
    )


def fixed_out(shape):
    zeros = (0,) * len(shape)
    return pl.BlockSpec(shape, lambda *place: zeros)


def outer_kernel(left_moves, left, right, out, turned):
    if left_moves:
        out[...] = dot_tn(left[...], right[...]).astype(out.dtype)
        return

    @pl.when(pl.program_id(0) == 0)
    def _():
        turned[...] = left[...].T

    out[...] = dot(turned[...], right[...]).astype(out.dtype)


def outer(left, right):
    rows, tall = left.shape
    broad = right.shape[1]
    left_moves = tall > broad
    if left_moves:
        grid, specs = tall // WIDE, [
            pl.BlockSpec((rows, WIDE), lambda i: (0, i)),
            fixed((rows, broad)),
        ]
        out_spec = pl.BlockSpec((WIDE, broad), lambda i: (i, 0))
    else:
        grid, specs = broad // WIDE, [
            fixed((rows, tall)),
            pl.BlockSpec((rows, WIDE), lambda i: (0, i)),
        ]
        out_spec = pl.BlockSpec((tall, WIDE), lambda i: (0, i))
    return pl.pallas_call(
        partial(outer_kernel, left_moves),
        grid=(grid,),
        in_specs=specs,
        out_specs=out_spec,
        out_shape=jax.ShapeDtypeStruct((tall, broad), BF16),
        scratch_shapes=[pltpu.VMEM((WIDE, rows), BF16)],
        compiler_params=params(32),
        cost_estimate=cost(2 * rows * tall * broad, 2 * (rows * (tall + broad) + tall * broad)),
        name="outer",
    )(left, right)


def project_back_kernel(
    query, own, received, embedded_in, attn, mask_in, gain, shift, weight,
    input_out, joint_out, near_out, far_out, sums_out,
):
    quarter = near_out.shape[1]
    mask = mask_in[0]
    embedded = embedded_in[0].astype(F32)
    normed, scaling = normalize(embedded)
    input_out[0] = (normed * gain[...] + shift[...]).astype(BF16)
    grad_query = query[0]
    grad_key = (own[0, 0].astype(F32) + received[0, 0].astype(F32)).astype(BF16)
    grad_value = (own[0, 1].astype(F32) + received[0, 1].astype(F32)).astype(BF16)
    grad_in = None
    for part, grad in enumerate((grad_query, grad_key, grad_value)):
        joint_out[part, 0] = grad
        term = dot_nt(grad, weight[:, part * WIDE : (part + 1) * WIDE])
        grad_in = term if grad_in is None else grad_in + term
    grad_embedded = attn[0] + normalize_back(grad_in, normed, scaling, gain[...])
    kept = grad_embedded * (1.0 - mask)
    near_out[0] = kept[:quarter]
    far_out[0] = kept[quarter:].astype(BF16)
    sums = [
        column_sums(grad_in * normed),
        column_sums(grad_in),
        column_sums(grad_query),
        column_sums(grad_value),
        column_sums(grad_embedded * mask),
    ]

    @pl.when(pl.program_id(0) == 0)
    def _():
        sums_out[...] = jnp.zeros_like(sums_out)

    for row, line in enumerate(sums):
        sums_out[row : row + 1] += line


def project_back(query, own, received, embedded, attn, mask, gain, shift, weight):
    near, rows, width = embedded.shape
    quarter = rows // 2
    block = pl.BlockSpec((1, rows, width), lambda i: (i, 0, 0))
    half = pl.BlockSpec((1, quarter, width), lambda i: (i, 0, 0))
    two = pl.BlockSpec((1, 2, rows, width), lambda i: (i, 0, 0, 0))
    return pl.pallas_call(
        project_back_kernel,
        grid=(near,),
        in_specs=[
            block,
            two,
            two,
            block,
            block,
            pl.BlockSpec((1, rows, 1), lambda i: (i, 0, 0)),
            fixed((1, width)),
            fixed((1, width)),
            fixed((width, 3 * width)),
        ],
        out_specs=[
            block,
            pl.BlockSpec((3, 1, rows, width), lambda i: (0, i, 0, 0)),
            half,
            half,
            fixed_out((8, width)),
        ],
        out_shape=[
            jax.ShapeDtypeStruct((near, rows, width), BF16),
            jax.ShapeDtypeStruct((3, near, rows, width), BF16),
            jax.ShapeDtypeStruct((near, quarter, width), F32),
            jax.ShapeDtypeStruct((near, quarter, width), BF16),
            jax.ShapeDtypeStruct((8, width), F32),
        ],
        compiler_params=params(40),
        cost_estimate=cost(2 * near * rows * width * 3 * width, 20e6),
        name="project_back",
    )(query, own, received, embedded, attn, mask, gain, shift, weight)


def swap(values, axis, bit):
    size = lax.axis_size(axis)
    return lax.ppermute(values, axis, [(place, place ^ bit) for place in range(size)])


def own_bit(axis, bit):
    return (lax.axis_index(axis) // bit) % 2


def pick(values, dim, which):
    return lax.dynamic_index_in_dim(values, which, dim, keepdims=False)


def add_in(kept, received):
    return (kept.astype(jnp.float32) + received.astype(jnp.float32)).astype(kept.dtype)


def halve(values, dim, axis, bit):
    mine = own_bit(axis, bit)
    received = swap(pick(values, dim, 1 - mine), axis, bit)
    return add_in(pick(values, dim, mine), received)


def join(values, dim, axis, bit):
    mine = own_bit(axis, bit)
    received = swap(values, axis, bit)
    first = jnp.where(mine == 0, values, received)
    second = jnp.where(mine == 0, received, values)
    return jnp.concatenate([first, second], axis=dim)


def reduce_rows(grad, order):
    dp = lax.axis_size("dp")
    rows, columns = grad.shape
    steps = dp.bit_length() - 1
    part = rows // dp
    if columns % 512 == 0:
        tail = (1, 2, part, 2, columns // 4, 2)
        parts = grad.reshape((2,) * steps + (part, 4, columns // 4))
        parts = jnp.moveaxis(parts, steps + 1, 0)
    else:
        parts = grad.reshape((2,) * steps + (4, part // 4, columns))
        parts = jnp.moveaxis(parts, steps, 0)
    parts = parts.reshape((2, 2) + parts.shape[1:])
    names = ["core", "y"] + [1 << bit for bit in reversed(range(steps))]
    for name in order(steps):
        dim = names.index(name)
        if name == "core":
            parts = halve(parts, dim, "seq", 1)
        elif name == "y":
            parts = halve(parts, dim, "seq", 2)
        else:
            parts = halve(parts, dim, "dp", name)
        names.pop(dim)
    parts = join(parts[None], 0, "seq", 2)
    parts = join(parts[None], 0, "seq", 1)
    parts = parts.reshape((4,) + parts.shape[2:]).astype(jnp.float32)
    if columns % 512 == 0:
        return jnp.moveaxis(parts, 0, 1).reshape(part, columns)
    return parts.reshape(part, columns)


def x_first(steps):
    return ["core"] + [1 << bit for bit in range(steps)] + ["y"]


def y_first(steps):
    return ["core", "y"] + [1 << bit for bit in range(steps)]


def z_first(steps):
    return ["core"] + [1 << bit for bit in range(1, steps)] + [1, "y"]


def reduce_vector(values):
    dp = lax.axis_size("dp")
    steps = dp.bit_length() - 1
    values = values + swap(values, "seq", 1)
    values = values + swap(values, "seq", 2)
    values = values.reshape((2,) * steps + values.shape[1:])
    for bit in reversed(range(steps)):
        mine = own_bit("dp", 1 << bit)
        received = swap(pick(values, 0, 1 - mine), "dp", 1 << bit)
        values = pick(values, 0, mine) + received
    return values


def any_places(
    patches,
    targets,
    mask_order,
    mask_count,
    attend_gain,
    attend_shift,
    joint_weight,
    query_bias,
    value_bias,
    output_weight,
    output_bias,
    feed_gain,
    feed_shift,
    expand_weight,
    expand_bias,
    reduce_weight,
    reduce_bias,
    pixel_weight,
    pixel_bias,
    mask_token,
):
    images, quarter, features = patches.shape
    dp = lax.axis_size("dp")
    near = images // 2
    rows_one = 2 * quarter
    row_count = near * rows_one
    place_y = own_bit("seq", 2)

    def own_and_far(values):
        parts = values.reshape((2, near) + values.shape[1:])
        return pick(parts, 0, place_y), swap(pick(parts, 0, 1 - place_y), "seq", 2)

    def line(vector):
        return vector.astype(F32)[None, :]

    masked_here = mask_order < mask_count[:, None]
    embedded_here = jnp.where(masked_here[:, :, None], mask_token[None, None, :], patches)
    embedded_own, embedded_far = own_and_far(embedded_here)
    mask = jnp.concatenate(own_and_far(masked_here.astype(jnp.int32)), axis=1)
    mask = mask.astype(F32)[:, :, None]
    count_sum = jnp.sum(mask_count)
    for bit in range(dp.bit_length() - 1):
        count_sum = count_sum + swap(count_sum, "dp", 1 << bit)
    inverse = 1.0 / (count_sum.astype(F32) * PIXELS)
    target_own, target_far = own_and_far(targets)
    joint_bias = jnp.concatenate(
        [line(query_bias), jnp.zeros((1, features), F32), line(value_bias)], axis=1
    )
    biases = jnp.concatenate(
        [
            line(vector)
            for vector in (output_bias, feed_gain, feed_shift, reduce_bias, pixel_bias)
        ]
        + [jnp.zeros((3, features), F32)],
        axis=0,
    )
    embedded, joint = project(
        embedded_own, embedded_far, line(attend_gain), line(attend_shift), joint_weight, joint_bias
    )
    pairs_far = swap(joint[:, 1:], "seq", 1)
    mixed, probs = attend(joint, pairs_far)
    (
        input_two,
        activated,
        after_low,
        grad_pred,
        grad_branch,
        grad_expand,
        grad_out,
        grad_attn,
        grad_mixed,
        sums_two,
    ) = rows_step(
        inverse.reshape(1, 1),
        embedded,
        mixed,
        mask,
        target_own,
        target_far,
        output_weight,
        expand_weight,
        reduce_weight,
        pixel_weight,
        biases,
        line(expand_bias),
    )

    def flat(values):
        return values.reshape(row_count, values.shape[-1])

    reduce_weight_grad = outer(flat(activated), flat(grad_branch))
    expand_weight_grad = outer(flat(input_two), flat(grad_expand))
    pixel_weight_grad = outer(flat(after_low), flat(grad_pred))
    output_weight_grad = outer(flat(mixed), flat(grad_out))
    square_grads = jnp.concatenate([pixel_weight_grad, output_weight_grad], axis=1)
    grad_query, grad_own, grad_far = attend_back(joint, pairs_far, probs, grad_mixed)
    received = swap(grad_far, "seq", 1)
    input_one, grad_joint, patch_near, patch_far, sums_one = project_back(
        grad_query,
        grad_own,
        received,
        embedded,
        grad_attn,
        mask,
        line(attend_gain),
        line(attend_shift),
        joint_weight,
    )
    grad_joint = grad_joint.reshape(3, row_count, features)
    joint_weight_grad = jnp.concatenate(
        [outer(flat(input_one), grad_joint[part]) for part in range(3)], axis=1
    )
    patch_far = swap(patch_far, "seq", 2).astype(F32)
    patch_grad = jnp.concatenate(
        [
            jnp.where(place_y == 0, patch_near, patch_far),
            jnp.where(place_y == 0, patch_far, patch_near),
        ],
        axis=0,
    )
    hidden = expand_bias.shape[0]
    vectors = (
        sums_one[0],
        sums_one[1],
        sums_one[2],
        sums_one[3],
        sums_two[4],
        sums_two[2],
        sums_two[3],
        sums_two[6 : 6 + hidden // features].reshape(hidden),
        sums_two[1],
        sums_two[0],
        sums_one[4],
    )
    loss_part = jnp.sum(sums_two[5]) * inverse
    lengths = [vector.shape[0] // dp for vector in vectors]
    packed = jnp.concatenate(
        [vector.reshape(dp, -1) for vector in vectors]
        + [jnp.broadcast_to(loss_part[None, None], (dp, 1))],
        axis=1,
    )
    packed = reduce_vector(packed)
    loss_value = packed[-1]
    cuts, start = [], 0
    for length in lengths:
        cuts.append(packed[start : start + length])
        start += length
    (
        attend_gain_grad,
        attend_shift_grad,
        query_bias_grad,
        value_bias_grad,
        output_bias_grad,
        feed_gain_grad,
        feed_shift_grad,
        expand_bias_grad,
        reduce_bias_grad,
        pixel_bias_grad,
        mask_token_grad,
    ) = cuts
    reduce_weight_grad = reduce_rows(reduce_weight_grad, x_first)
    expand_weight_grad = reduce_rows(expand_weight_grad, y_first)
    square_grads = reduce_rows(square_grads, z_first)
    joint_weight_grad = reduce_rows(joint_weight_grad, x_first)
    return (
        loss_value,
        attend_gain_grad,
        attend_shift_grad,
        joint_weight_grad,
        query_bias_grad,
        value_bias_grad,
        square_grads[:, PIXELS:],
        output_bias_grad,
        feed_gain_grad,
        feed_shift_grad,
        expand_weight_grad,
        expand_bias_grad,
        reduce_weight_grad,
        reduce_bias_grad,
        square_grads[:, :PIXELS],
        pixel_bias_grad,
        mask_token_grad,
        patch_grad,
    )


MESH = pl.DeviceIdType.MESH


def places():
    data, seq = lax.axis_index("dp"), lax.axis_index("seq")
    x, low, high = lax.rem(data, 2), lax.rem(lax.div(data, 2), 2), lax.div(data, 4)
    core, y = lax.rem(seq, 2), lax.div(seq, 2)
    return {
        "x": (x, {"dp": data + 1 - 2 * x}),
        "low": (low, {"dp": data + 2 - 4 * low}),
        "high": (high, {"dp": data + 4 - 8 * high}),
        "y": (y, {"seq": seq + 2 - 4 * y}),
        "core": (core, {"seq": seq + 1 - 2 * core}),
    }


def greet(where):
    barrier = pltpu.get_barrier_semaphore()
    for _, partner in where.values():
        pl.semaphore_signal(barrier, inc=1, device_id=partner, device_id_type=MESH)
    pl.semaphore_wait(barrier, len(where))


def remote(source, target, send, receive, partner):
    return pltpu.make_async_remote_copy(
        src_ref=source,
        dst_ref=target,
        send_sem=send,
        recv_sem=receive,
        device_id=partner,
        device_id_type=MESH,
    )


NAMES = ("high", "low", "x", "y")


def names_of(order):
    halved = [token for token in order if token in NAMES]
    return tuple(halved + [name for name in NAMES if name not in halved])


def stage_shapes(names, order, tail):
    names, shapes = list(names), []
    for token in order:
        if token == "Gy":
            names = ["y"]
        elif token == "Gcore":
            names = ["core"] + names
        elif token[0] != "+":
            names.remove(token)
        shapes.append((2,) * len(names) + tail)
    return shapes


def for_each(dims, body):
    outer = max(dims - 2, 0)
    inner = list(itertools.product(range(2), repeat=dims - outer))
    if outer == 0:
        for spot in inner:
            body(spot)
        return

    def one(place, carry):
        first = tuple(lax.rem(lax.div(place, 2 ** (outer - 1 - dim)), 2) for dim in range(outer))
        for spot in inner:
            body(first + spot)
        return carry

    lax.fori_loop(0, 2**outer, one, 0)


def add_up(target, place, other):
    target[place] = target[place] + other


class Chain:
    def __init__(self, where, start, names, order, buffers, send, receive, base, swapped=None):
        self.where, self.order = dict(where), order
        if swapped is not None:
            (first, partner_first), (second, partner_second) = (where[name] for name in swapped)
            core = where["core"][0]

            def chosen(zero, one):
                return zero + core * (one - zero)

            for name, place, ours, other in (
                (swapped[0], (first, second), partner_first, partner_second),
                (swapped[1], (second, first), partner_second, partner_first),
            ):
                here = {"dp": lax.axis_index("dp"), "seq": lax.axis_index("seq")}
                ours, other = {**here, **ours}, {**here, **other}
                partner = {axis: chosen(ours[axis], other[axis]) for axis in here}
                self.where[name] = (chosen(*place), partner)
        self.plain = where
        self.refs = [start] + list(buffers)
        self.send, self.receive, self.base = send, receive, base
        self.names = [list(names)]
        for token in order:
            names = list(self.names[-1])
            if token == "Gy":
                names = ["y"]
            elif token == "Gcore":
                names = ["core"] + names
            elif token[0] != "+":
                names.remove(token)
            self.names.append(names)

    def copy(self, stage):
        token = self.order[stage]
        source, target = self.refs[stage], self.refs[stage + 1]
        if token[0] == "+":
            _, partner = self.plain[token[1:]]
        elif token[0] == "G":
            place, partner = self.plain[token[1:]]
            target = target.at[place]
        else:
            place, partner = self.where[token]
            dim = self.names[stage].index(token)
            source = source.at[(slice(None),) * dim + (1 - place,)]
        spot = self.base + stage
        return remote(source, target, self.send.at[spot], self.receive.at[spot], partner)

    def start(self, stage):
        self.copy(stage).start()

    def finish(self, stage):
        self.copy(stage).wait()
        token = self.order[stage]
        source, target = self.refs[stage], self.refs[stage + 1]
        if token[0] == "G":
            place, _ = self.plain[token[1:]]
            target[place] = source[...]
            return
        dim = None
        if token[0] != "+":
            place, _ = self.where[token]
            dim = self.names[stage].index(token)

        def one(spot):
            origin = spot if dim is None else spot[:dim] + (place,) + spot[dim:]
            add_up(target, spot if spot else Ellipsis, source[origin if origin else Ellipsis])

        for_each(len(self.names[stage + 1]), one)

    def turn(self, stage):
        if stage > 0:
            self.finish(stage - 1)
        if stage < len(self.order):
            self.start(stage)


Y_FIRST = ("y", "x", "low", "high", "Gy", "Gcore")
Y_THEN_LOW = ("y", "low", "x", "high", "Gy", "Gcore")
X_FIRST = ("x", "low", "high", "+y", "Gcore")
SUMS_ORDER = ("+core", "+y", "+x", "+low", "+high")
MOST = 6
TILE_ORDERS = (
    Y_FIRST,
    X_FIRST,
    Y_THEN_LOW,
    Y_FIRST,
    Y_THEN_LOW,
    X_FIRST,
    Y_FIRST,
    X_FIRST,
    Y_THEN_LOW,
    Y_FIRST,
    Y_FIRST,
    Y_FIRST,
    X_FIRST,
)
TILE_SWAPS = (
    ("x", "y"),
    ("x", "low"),
    ("y", "low"),
    ("x", "y"),
    ("y", "low"),
    ("x", "low"),
    ("x", "y"),
    ("x", "low"),
    ("y", "low"),
    ("x", "y"),
    ("x", "y"),
    ("x", "y"),
    ("x", "low"),
)
TILES = len(TILE_ORDERS)
TILE_STEPS = (0, 1, 2, 3, 4, 5, 6, 7, 8, 9, 14, 18, 21)
TURNS = {
    2: ((0, 0),),
    3: ((1, 0),),
    4: ((0, 1), (2, 0),),
    5: ((1, 1), (3, 0),),
    6: ((0, 2), (4, 0),),
    7: ((1, 2), (2, 1), (3, 1), (5, 0),),
    8: ((0, 3), (6, 0),),
    9: ((1, 3), (3, 2), (7, 0),),
    10: ((0, 4), (1, 4), (2, 2), (4, 1), (6, 1), (8, 0), (13, 0), (3, 3),),
    11: ((1, 5), (5, 1), (13, 1), (9, 0), (0, 5),),
    12: ((0, 6), (3, 4), (2, 3), (7, 1),),
    13: ((4, 2), (6, 2), (13, 2),),
    14: ((3, 5), (2, 4), (5, 2),),
    15: ((3, 6), (2, 5), (4, 3), (6, 3), (13, 3), (7, 2), (8, 1), (9, 1),),
    16: ((2, 6), (5, 3), (10, 0),),
    18: ((4, 4), (5, 4), (6, 4), (13, 4), (7, 3), (8, 2), (9, 2),),
    19: ((4, 5), (5, 5), (6, 5), (13, 5), (8, 3), (10, 1),),
    20: ((4, 6), (6, 6), (7, 4), (9, 3), (11, 0),),
    21: ((7, 5), (8, 4), (10, 2),),
    22: ((8, 5), (9, 4), (10, 3), (11, 1),),
}
LAST_TURNS = (
    (14, 0),
    (8, 6),
    (9, 5),
    (10, 4),
    (11, 2),
    (14, 1),
    (9, 6),
    (11, 3),
    (14, 2),
    (10, 5),
    (12, 1),
    (10, 6),
    (14, 3),
    (11, 4),
    (12, 2),
    (14, 4),
    (11, 5),
    (14, 5),
    (11, 6),
    (12, 3),
    (12, 4),
    (12, 5),
)


def chain_scratch(cases):
    scratch, counts = [], []
    for names, order, tail, dtype in cases:
        shapes = stage_shapes(names, order, tail)
        scratch += [pltpu.VMEM(shape, dtype) for shape in shapes]
        counts.append(len(shapes))
    return scratch, counts


def split_list(values, counts):
    parts, start = [], 0
    for count in counts:
        parts.append(values[start : start + count])
        start += count
    return parts


GAIN_ONE, SHIFT_ONE, QUERY, VALUE, OUTPUT, GAIN_TWO, SHIFT_TWO, REDUCE, PIXEL, TOKEN, EXPAND = range(11)
FRONT_OWN = 9
FRONT_FAR = 12
FRONT_ATTEND = 15
FRONT_PAIRS = 3


def lines_kernel(*refs):
    out = refs[-1]
    row = 0
    for ref in refs[:-1]:
        for start in range(0, ref.shape[0], WIDE):
            out[row : row + 1] = ref[start : start + WIDE].astype(F32).reshape(1, WIDE)
            row += 1


def stack_lines(*vectors):
    return pl.pallas_call(
        lines_kernel,
        in_specs=[pl.BlockSpec(memory_space=pltpu.VMEM)] * len(vectors),
        out_specs=pl.BlockSpec(memory_space=pltpu.VMEM),
        out_shape=jax.ShapeDtypeStruct((16, WIDE), F32),
        cost_estimate=cost(1e4, 1e5),
        name="stack_lines",
    )(*vectors)


def column_of(line):
    count = line.shape[1]
    down = lax.broadcasted_iota(jnp.int32, (count, count), 0)
    along = lax.broadcasted_iota(jnp.int32, (count, count), 1)
    return jnp.sum(jnp.where(down == along, jnp.broadcast_to(line, (count, count)), 0.0), axis=1, keepdims=True)


def front_kernel(
    parts, counts, rows_in, targets_in, orders_in, lines, weight_in, pixel_in, expand_in, output_in,
    embedded_out, input_out, joint_out, pairs_out, mixed_out, probs_out, masks_out, target_out, expand_out,
    embedded, inputs, masks, order_far, joint, pairs, weight, pixel, expand, output,
    local, far_send, far_receive, send, receive,
):
    images, heads = joint.shape[:2]
    quarter = rows_in.shape[2]
    where = {name: places()[name] for name in ("core", "y")}
    sibling = where["core"][1]
    y, other = where["y"]
    step = pl.program_id(0)
    near_half, far_half = pl.ds(0, quarter), pl.ds(quarter, quarter)

    def pair_copy(image):
        return remote(
            joint.at[image, :, pl.ds(1, 2)], pairs.at[image], send.at[image], receive.at[image], sibling
        )

    def far_copy(index, source, target):
        return remote(source, target, far_send.at[index], far_receive.at[index], other)

    order_copy = far_copy(0, orders_in, order_far)
    row_copies = [
        far_copy(1 + image, rows_in.at[1 - y, image], embedded.at[image, far_half]) for image in range(images)
    ]
    target_copies = [
        far_copy(1 + images + image, targets_in.at[1 - y, image], target_out.at[image, far_half])
        for image in range(images)
    ]
    own_copy = pltpu.make_async_copy(rows_in.at[y], embedded.at[:, near_half], local.at[0])
    target_copy = pltpu.make_async_copy(targets_in.at[y], target_out.at[:, near_half], local.at[1])
    loads = [
        pltpu.make_async_copy(source, target, local.at[2 + index])
        for index, (source, target) in enumerate(
            ((pixel_in, pixel), (expand_in, expand), (output_in, output), (weight_in, weight))
        )
    ]

    @pl.when(step == 0)
    def _():
        own_copy.start()
        greet(where)
        order_copy.start()
        for copy in row_copies + loads:
            copy.start()
        target_copy.start()
        loads[0].wait()
        expand_out[0] = pixel[...]

    @pl.when(step == parts + 1)
    def _():
        loads[2].wait()
        expand_out[0] = output[...]

    for part in range(parts):

        @pl.when(step == 1 + part)
        def _(part=part):
            if part == 0:
                loads[1].wait()
            span = weight.shape[0] // 8
            starts = [place * parts * span + part * span for place in range(8)]
            expand_out[0] = jnp.concatenate([expand[:, start : start + span] for start in starts], axis=1)

    for group in range(3):

        @pl.when(step == parts + 2 + group)
        def _(group=group):
            if group == 0:
                loads[3].wait()
            starts = [part * WIDE + group * 2 * PAIR for part in range(3)]
            expand_out[0] = jnp.concatenate([weight[:, start : start + 2 * PAIR] for start in starts], axis=1)

    def project(image, start, order):
        block = pl.ds(start, quarter)
        mask = column_of((order < counts[y * images + image]).astype(F32))
        masks[image, block] = mask
        token = lines[TOKEN : TOKEN + 1].astype(BF16)
        rows = jnp.where(mask > 0.5, token, embedded[image, block])
        embedded[image, block] = rows
        normed, _ = normalize(rows.astype(F32))
        gain, shift = lines[GAIN_ONE : GAIN_ONE + 1], lines[SHIFT_ONE : SHIFT_ONE + 1]
        low = (normed * gain + shift).astype(BF16)
        inputs[image, block] = low
        for part, bias in ((1, None), (2, lines[VALUE : VALUE + 1]), (0, lines[QUERY : QUERY + 1])):
            total = dot(low, weight[:, part * WIDE : (part + 1) * WIDE])
            total = (total if bias is None else total + bias).astype(BF16)
            for pair in range(heads):
                joint[image, pair, part, block] = total[:, pair * PAIR : (pair + 1) * PAIR]

    @pl.when((step >= FRONT_OWN) & (step < FRONT_FAR))
    def _():
        @pl.when(step == FRONT_OWN)
        def _():
            own_copy.wait()

        image = step - FRONT_OWN
        project(image, 0, orders_in[pl.ds(y * images + image, 1)])

    @pl.when((step >= FRONT_FAR) & (step < FRONT_ATTEND))
    def _():
        for index in range(images):

            @pl.when(step == FRONT_FAR + index)
            def _(index=index):
                if index == 0:
                    order_copy.wait()
                row_copies[index].wait()
                target_copies[index].start()

        image = step - FRONT_FAR
        project(image, quarter, order_far[pl.ds(y * images + image, 1)])
        pair_copy(image).start()
        embedded_out[0] = embedded[image]
        input_out[0] = inputs[image]
        joint_out[0] = joint[image]
        masks_out[0] = masks[image]

    def attend(image, pair, index):
        queries = side_by_side(joint[image, pair, 0] * jnp.asarray(HEAD_DIM**-0.5, BF16))
        keys_in = jnp.concatenate([joint[image, pair, 1], pairs[image, pair, 0]], axis=0)
        values_in = jnp.concatenate([joint[image, pair, 2], pairs[image, pair, 1]], axis=0)
        pairs_out[0, index] = pairs[image, pair]
        scores = dot_nt(keys_in, queries)
        exponent = jnp.exp(scores - jnp.max(scores, axis=0, keepdims=True))
        total = jnp.sum(exponent, axis=0, keepdims=True)
        probs = (exponent * (1.0 / total)).astype(BF16)
        probs_out[0, index] = probs
        mixed = merge_turned(dot_tn(values_in, probs)).astype(BF16)
        mixed_out[0, :, index * PAIR : (index + 1) * PAIR] = mixed

    @pl.when(step >= FRONT_ATTEND)
    def _():
        place = step - FRONT_ATTEND
        turns = heads // FRONT_PAIRS
        image, turn = lax.div(place, turns), lax.rem(place, turns)

        @pl.when(turn == 0)
        def _():
            pair_copy(image).wait()

        for index in range(FRONT_PAIRS):
            attend(image, turn * FRONT_PAIRS + index, index)

    @pl.when(step == pl.num_programs(0) - 1)
    def _():
        for copy in target_copies:
            copy.wait()
        target_copy.wait()


def merge_turned(stacked):
    rows = stacked.shape[1] // 2
    down = lax.broadcasted_iota(jnp.int32, (PAIR, rows), 0)
    return jnp.where(down < HEAD_DIM, stacked[:, :rows], stacked[:, rows:]).T


def front(counts, rows_in, targets_in, orders_in, lines, weight, pixel, expand, output):
    near, quarter, width = rows_in.shape[1:]
    rows, heads = 2 * quarter, width // PAIR
    parts = expand.shape[1] // width

    def image(step):
        return jnp.clip(step - FRONT_FAR, 0, near - 1)

    turns = heads // FRONT_PAIRS

    def spot(step):
        place = jnp.maximum(step - FRONT_ATTEND, 0)
        return lax.div(place, turns), lax.rem(place, turns)

    block = pl.BlockSpec((1, rows, width), lambda s: (image(s), 0, 0))
    return pl.pallas_call(
        partial(front_kernel, parts),
        grid=(FRONT_ATTEND + near * turns,),
        in_specs=[
            pl.BlockSpec(memory_space=pltpu.SMEM),
            pl.BlockSpec(memory_space=pl.ANY),
            pl.BlockSpec(memory_space=pl.ANY),
            fixed(orders_in.shape),
            fixed(lines.shape),
        ]
        + [pl.BlockSpec(memory_space=pl.ANY)] * 4,
        out_specs=[
            block,
            block,
            pl.BlockSpec((1, heads, 3, rows, PAIR), lambda s: (image(s), 0, 0, 0, 0)),
            pl.BlockSpec((1, FRONT_PAIRS, 2, rows, PAIR), lambda s: spot(s) + (0, 0, 0)),
            pl.BlockSpec((1, rows, FRONT_PAIRS * PAIR), lambda s: (spot(s)[0], 0, spot(s)[1])),
            pl.BlockSpec((1, FRONT_PAIRS, 2 * rows, 2 * rows), lambda s: spot(s) + (0, 0)),
            pl.BlockSpec((1, rows, 1), lambda s: (image(s), 0, 0)),
            pl.BlockSpec(memory_space=pl.ANY),
            pl.BlockSpec((1, width, width), lambda s: (jnp.minimum(s, parts + 4), 0, 0)),
        ],
        out_shape=[
            jax.ShapeDtypeStruct((near, rows, width), BF16),
            jax.ShapeDtypeStruct((near, rows, width), BF16),
            jax.ShapeDtypeStruct((near, heads, 3, rows, PAIR), BF16),
            jax.ShapeDtypeStruct((near, heads, 2, rows, PAIR), BF16),
            jax.ShapeDtypeStruct((near, rows, width), BF16),
            jax.ShapeDtypeStruct((near, heads, 2 * rows, 2 * rows), BF16),
            jax.ShapeDtypeStruct((near, rows, 1), F32),
            jax.ShapeDtypeStruct((near, rows, width), BF16),
            jax.ShapeDtypeStruct((parts + 5, width, width), BF16),
        ],
        scratch_shapes=[
            pltpu.VMEM((near, rows, width), BF16),
            pltpu.VMEM((near, rows, width), BF16),
            pltpu.VMEM((near, rows, 1), F32),
            pltpu.VMEM(orders_in.shape, jnp.int32),
            pltpu.VMEM((near, heads, 3, rows, PAIR), BF16),
            pltpu.VMEM((near, heads, 2, rows, PAIR), BF16),
            pltpu.VMEM(weight.shape, BF16),
            pltpu.VMEM(pixel.shape, BF16),
            pltpu.VMEM(expand.shape, BF16),
            pltpu.VMEM(output.shape, BF16),
            pltpu.SemaphoreType.DMA((6,)),
            pltpu.SemaphoreType.DMA((1 + 2 * near,)),
            pltpu.SemaphoreType.DMA((1 + 2 * near,)),
            pltpu.SemaphoreType.DMA((near,)),
            pltpu.SemaphoreType.DMA((near,)),
        ],
        compiler_params=pltpu.CompilerParams(
            vmem_limit_bytes=60 * MIB, collective_id=1, has_side_effects=True
        ),
        cost_estimate=cost(5e9, 40e6),
        name="front",
    )(counts, rows_in, targets_in, orders_in, lines, weight, pixel, expand, output)


def middle_kernel(
    embedded_in, mixed, mask_in, target_in, weights, reduce, lines,
    sides, input_out, scaling_out, sums_out, low, total, biases,
):
    parts = reduce.shape[1]
    span = reduce.shape[2]
    width = weights.shape[1]
    mask = mask_in[0]

    @pl.when(pl.program_id(0) == 0)
    def _():
        sums_out[...] = jnp.zeros_like(sums_out)
        for part in range(parts):
            pieces = []
            for place in range(8):
                row, start = divmod((place * parts + part) * span, width)
                pieces.append(lines[EXPAND + row : EXPAND + row + 1, start : start + span])
            biases[part] = jnp.concatenate(pieces, axis=1)

    after_attn = embedded_in[0].astype(F32) + dot(mixed[0], weights[parts + 1]) + lines[OUTPUT : OUTPUT + 1]
    sides[0, 0, parts + 1] = mixed[0]
    normed, scaling = normalize(after_attn)
    sides[0, 1, parts + 1] = normed.astype(BF16)
    scaling_out[0] = scaling
    low[...] = (normed * lines[GAIN_TWO : GAIN_TWO + 1] + lines[SHIFT_TWO : SHIFT_TWO + 1]).astype(BF16)
    input_out[0] = low[...]
    total[...] = after_attn + lines[REDUCE : REDUCE + 1]

    def one(part, carry):
        active, rate = gelu_both(dot(low[...], weights[1 + part]) + biases[part])
        active = active.astype(BF16)
        sides[0, 0, 1 + part] = active
        sides[0, 1, 1 + part] = rate.astype(BF16)
        total[...] += dot(active, reduce[:, part].reshape(width, width))
        return carry

    for part in range(parts):
        one(part, 0)
    after_low = total[...].astype(BF16)
    sides[0, 0, 0] = after_low
    errors = dot(after_low, weights[0]) + lines[PIXEL : PIXEL + 1] - target_in[0].astype(F32)
    square = errors * errors + 1.0
    root = lax.rsqrt(square)
    grad_pred = (mask * errors * root).astype(BF16)
    sides[0, 1, 0] = grad_pred
    sums_out[0:1] += column_sums(grad_pred)
    sums_out[5:6] += jnp.sum((square * root - 1.0) * mask, axis=0, keepdims=True)
    sums_out[10:11] += jnp.sum(jnp.broadcast_to(mask, errors.shape), axis=0, keepdims=True)


def middle(embedded, mixed, mask, targets, weights, reduce, lines):
    near, rows, width = embedded.shape
    parts = reduce.shape[1]
    block = pl.BlockSpec((1, rows, width), lambda i: (i, 0, 0))
    column = pl.BlockSpec((1, rows, 1), lambda i: (i, 0, 0))
    stack = pl.BlockSpec((1, 2, parts + 2, rows, width), lambda i: (i, 0, 0, 0, 0))
    return pl.pallas_call(
        middle_kernel,
        grid=(near,),
        in_specs=[
            block,
            block,
            column,
            block,
            fixed((parts + 2, width, width)),
            fixed(reduce.shape),
            fixed(lines.shape),
        ],
        out_specs=[stack, block, column, fixed_out((16, width))],
        out_shape=[
            jax.ShapeDtypeStruct((near, 2, parts + 2, rows, width), BF16),
            jax.ShapeDtypeStruct((near, rows, width), BF16),
            jax.ShapeDtypeStruct((near, rows, 1), F32),
            jax.ShapeDtypeStruct((16, width), F32),
        ],
        scratch_shapes=[
            pltpu.VMEM((rows, width), BF16),
            pltpu.VMEM((rows, width), F32),
            pltpu.VMEM((parts, 1, width), F32),
        ],
        compiler_params=params(60),
        cost_estimate=cost(2 * near * rows * width * width * (2 * parts + 2), 40e6),
        name="middle",
    )(embedded, mixed, mask, targets, weights, reduce, lines)


HIGH_ROWS = 4 * 96


def spread_half(result, target, high, start, names, swapped):
    for low in range(2):
        for x in range(2):
            for y in range(2):
                at = (low * 2 + x) * 96 + start
                piece = result[at : at + HALF, y * 384 : (y + 1) * 384]
                spot = {"high": high, "low": low, "x": x, "y": y}
                if swapped is not None:
                    first, second = swapped
                    spot[first], spot[second] = spot[second], spot[first]
                target[tuple(spot[name] for name in names)] = piece.astype(BF16)


HALF = 48
SLOTS = 4
KEPT = 10
FIRST_ATTEND = 10
GROUP_STEPS = (14, 18, 21)
FIRST_NORM = 22


def back_kernel(
    counts, sides, weights, reduce, input_two, scaling_two, input_one, joint, pairs, probs_in, lines, sums_in,
    embedded_in, mask_in, *rest,
):
    (
        done_out,
        near_out,
        far_out,
        sums_out,
        late_out,
        done,
        done_sent,
        branch,
        wide,
        grad_in,
        upstream,
        own_pairs,
        give_pairs,
        got_pairs,
        far_give,
        sums,
        late,
        keep,
        give,
        got,
        send,
        receive,
        core_send,
        core_receive,
        pair_send,
        pair_receive,
        far_send,
        far_receive,
    ) = rest[:28]
    buffers = split_list(rest[28:], counts)
    where = places()
    core, sibling = where["core"]
    step = pl.program_id(0)
    images, rows, width = input_two.shape
    every = images * rows
    quarter = rows // 2
    heads = width // PAIR
    first_gain, second_gain = lines[GAIN_ONE : GAIN_ONE + 1], lines[GAIN_TWO : GAIN_TWO + 1]
    chains = [
        Chain(where, keep.at[unit % KEPT], names_of(order), order, list(buffers[unit]) + [done.at[unit]], send, receive, MOST * unit, TILE_SWAPS[unit])
        for unit, order in enumerate(TILE_ORDERS)
    ]
    chains.append(Chain(where, sums, (), SUMS_ORDER, buffers[TILES], send, receive, MOST * TILES))
    chains.append(Chain(where, late, (), SUMS_ORDER, buffers[TILES + 1], send, receive, MOST * TILES + MOST))

    def core_copy(unit):
        slot = lax.rem(unit, SLOTS)
        return remote(give.at[slot], got.at[slot], core_send.at[unit], core_receive.at[unit], sibling)

    def pair_copy(place, second):
        image = lax.rem(place, 3)
        slot = lax.rem((lax.div(place, 6) * 3 + image) * 2 + second, SLOTS)
        return remote(
            give_pairs.at[slot], got_pairs.at[place], pair_send.at[place], pair_receive.at[place], sibling
        )

    def far_copy(image):
        return remote(
            far_give.at[image], far_out.at[image], far_send.at[image], far_receive.at[image], where["y"][1]
        )

    def core_sum(unit):
        core_copy(unit).wait()
        for_each(4, lambda spot: add_up(keep.at[unit % KEPT], spot, got[(unit % SLOTS,) + spot]))

    def done_copy(unit):
        return pltpu.make_async_copy(done.at[unit], done_out.at[unit], done_sent.at[unit])

    def turn(unit, stage):
        if unit < TILES and stage == 0:
            core_sum(unit)
        chains[unit].turn(stage)
        if stage == len(chains[unit].order) and unit < TILES:
            done_copy(unit).start()

    def tile(unit, lines_of, value, forms):
        def one(high):
            columns = slice(high * HIGH_ROWS, (high + 1) * HIGH_ROWS)
            result = dot_tn(lines_of(columns).reshape(every, HIGH_ROWS), value)
            for half in range(2):
                for names, swapped, chosen in forms:
                    swapped = swapped if half == 1 else None

                    @pl.when(jnp.logical_and(core == half, chosen))
                    def _(half=half, names=names, swapped=swapped):
                        spread_half(result, keep.at[lax.rem(unit, KEPT)], high, half * HALF, names, swapped)

                    @pl.when(jnp.logical_and(core != half, chosen))
                    def _(half=half, names=names, swapped=swapped):
                        spread_half(result, give.at[lax.rem(unit, SLOTS)], high, half * HALF, names, swapped)

        for high in range(2):
            one(high)
        core_copy(unit).start()

    def forms_of(units, unit):
        forms = {}
        for other in units:
            form = (names_of(TILE_ORDERS[other]), TILE_SWAPS[other])
            forms.setdefault(form, []).append(unit == other)
        if len(forms) == 1:
            return [form + (True,) for form in forms]
        return [form + (functools.reduce(jnp.logical_or, asked),) for form, asked in forms.items()]

    def flat(ref):
        return ref[...].reshape(every, ref.shape[-1])

    def left_lines(columns):
        return sides[:, 0, 0, :, columns]

    @pl.when(step == 0)
    def _():
        greet(where)
        sums[...] = sums_in[...]
        late[...] = jnp.zeros_like(late)
        grad_in[...] = jnp.zeros_like(grad_in)

    for at, turns in TURNS.items():

        @pl.when(step == at)
        def _(turns=turns):
            for unit, stage in turns:
                turn(unit, stage)

    @pl.when(step == 0)
    def _():
        tile(0, left_lines, sides[:, 1, 0].reshape(every, width), forms_of((0,), 0))

        def one(image):
            low = dot_nt(sides[image, 1, 0], weights[0]).astype(BF16)
            branch[image] = low
            sums[1:2] += column_sums(low)
        for image in range(images):
            one(image)

    @pl.when((step > 0) & (step < 9) & (lax.rem(step, 2) == 1))
    def _():
        tile(step, left_lines, flat(branch), forms_of((1, 3, 5, 7), step))
        row = pl.ds(6 + lax.div(step, 2), 1)

        def one(image):
            low = dot_nt(branch[image], reduce[:, 0].reshape(width, width)) * sides[image, 1, 0].astype(F32)
            low = low.astype(BF16)
            wide[image] = low
            sums[row] += column_sums(low)
        for image in range(images):
            one(image)

    @pl.when((step > 0) & (step < 9) & (lax.rem(step, 2) == 0))
    def _():
        tile(step, lambda columns: input_two[:, :, columns], flat(wide), forms_of((2, 4, 6, 8), step))
        fresh = jnp.where(step == 2, 0.0, 1.0)

        def one(image):
            grad_in[image] = grad_in[image] * fresh + dot_nt(wide[image], weights[0])
        for image in range(images):
            one(image)

    @pl.when(step == 9)
    def _():
        def one(image):
            normed = sides[image, 1, 0].astype(F32)
            grad = grad_in[image]
            low = branch[image].astype(F32) + normalize_back(grad, normed, scaling_two[image], second_gain)
            low = low.astype(BF16)
            branch[image] = low
            sums[2:3] += column_sums(grad * normed)
            sums[3:4] += column_sums(grad)
            sums[4:5] += column_sums(low)
            mixed = dot_nt(low, weights[0]).astype(BF16)
            for pair in range(heads):
                upstream[image, pair] = mixed[:, pair * PAIR : (pair + 1) * PAIR]
        for image in range(images):
            one(image)

        tile(9, left_lines, flat(branch), forms_of((9,), 9))

    def attend_back(group, image, second, inside, order):
        place = group * 6 + inside

        @pl.when(order >= SLOTS)
        def _():
            before = order - SLOTS
            pair_copy(lax.div(before, 6) * 6 + second * 3 + lax.rem(lax.div(before, 2), 3), second).wait_send()

        scale = HEAD_DIM**-0.5
        target = own_pairs.at[lax.rem(group, 2), inside]
        away = give_pairs.at[lax.rem(order, SLOTS)]
        queries = side_by_side(joint[0, second, 0])
        keys_in = jnp.concatenate([joint[0, second, 1], pairs[0, second, 0]], axis=0)
        values_in = jnp.concatenate([joint[0, second, 2], pairs[0, second, 1]], axis=0)
        grad_mixed = side_by_side(upstream[image, group * 2 + second])
        probs = probs_in[0, second]
        grad_probs = dot_nt(values_in, grad_mixed)
        broad = probs.astype(F32)
        weighted = broad * grad_probs
        inner = jnp.sum(weighted, axis=0, keepdims=True)
        grad_scores = (weighted - broad * inner).astype(BF16)
        grad_values = dot(probs, grad_mixed).astype(BF16)
        grad_keys = (dot(grad_scores, queries) * scale).astype(BF16)
        target[0] = (merge_turned(dot_tn(keys_in, grad_scores)) * scale).astype(BF16)
        target[1] = grad_keys[:rows]
        target[2] = grad_values[:rows]
        away[0] = grad_keys[rows:]
        away[1] = grad_values[rows:]
        pair_copy(place, second).start()

    attends = (step >= FIRST_ATTEND) & (step < GROUP_STEPS[2]) & (step != GROUP_STEPS[0]) & (step != GROUP_STEPS[1])

    @pl.when(attends)
    def _():
        group, image = attend_place(step)
        for second in range(2):
            inside = second * 3 + image
            attend_back(group, image, second, inside, (group * 3 + image) * 2 + second)

    @pl.when((step == GROUP_STEPS[0]) | (step == GROUP_STEPS[1]) | (step == GROUP_STEPS[2]))
    def _():
        group = jnp.where(step == GROUP_STEPS[0], 0, jnp.where(step == GROUP_STEPS[1], 1, 2))
        slot = lax.rem(group, 2)
        for inside in range(6):
            pair_copy(group * 6 + inside, inside // 3).wait_recv()
            image, second = inside % 3, inside // 3
            for part in range(3):
                piece = own_pairs[slot, inside, part]
                if part > 0:
                    piece = piece.astype(F32) + got_pairs[group * 6 + inside, part - 1].astype(F32)
                start = part * 2 * PAIR + second * PAIR
                wide[image, :, start : start + PAIR] = piece.astype(BF16)
        tile(10 + group, lambda columns: input_one[:, :, columns], flat(wide), forms_of((10, 11, 12), 10 + group))
        fresh = jnp.where(group == 0, 0.0, 1.0)
        row = pl.ds(5 + group, 1)

        def one(image):
            late[row] += column_sums(wide[image])
            grad_in[image] = grad_in[image] * fresh + dot_nt(wide[image], weights[0])
        for image in range(images):
            one(image)

    @pl.when(step == FIRST_NORM)
    def _():
        for image in range(images):
            mask = mask_in[image]
            normed, scaling = normalize(embedded_in[image].astype(F32))
            grad = grad_in[image]
            total = branch[image].astype(F32) + normalize_back(grad, normed, scaling, first_gain)
            kept = total * (1.0 - mask)
            far_give[image] = kept[quarter:].astype(BF16)
            far_copy(image).start()
            near_out[image] = kept[:quarter]
            late[0:1] += column_sums(grad * normed)
            late[1:2] += column_sums(grad)
            late[2:3] += column_sums(total * mask)
            if image == 0:
                turn(TILES - 1, 0)

    @pl.when(step == pl.num_programs(0) - 1)
    def _():
        for unit, stage in LAST_TURNS:
            turn(unit, stage)
        for image in range(images):
            far_copy(image).wait()
        for unit in range(TILES):
            done_copy(unit).wait()
        for image in range(1, 3):
            for second in range(2):
                pair_copy(12 + second * 3 + image, second).wait_send()
        sums_out[...] = chains[TILES].refs[-1][...]
        late_out[...] = chains[TILES + 1].refs[-1][...]


def attend_place(step):
    place = step - FIRST_ATTEND
    for at in GROUP_STEPS[:2]:
        place = place - jnp.where(step > at, 1, 0)
    place = jnp.clip(place, 0, 8)
    return lax.div(place, 3), lax.rem(place, 3)


def back(
    sides, weights, reduce, input_two, scaling_two, input_one, joint, pairs, probs, lines, sums, embedded, mask
):
    near, _, slots, rows, width = sides.shape
    quarter = rows // 2
    heads = width // PAIR

    def slot(step):
        return jnp.minimum(lax.div(step + 1, 2), slots - 1)

    def part(step):
        return jnp.clip(lax.div(step - 1, 2), 0, slots - 3)

    def weight(step):
        late = slots + jnp.where(step > GROUP_STEPS[0], 1, 0) + jnp.where(step > GROUP_STEPS[1], 1, 0)
        return jnp.where(step < FIRST_ATTEND, slot(step), late)

    def spot(step):
        group, image = attend_place(step)
        return image, group

    cases = [(names_of(order), order, (HALF, 384), BF16) for order in TILE_ORDERS]
    cases.append(((), SUMS_ORDER, sums.shape, F32))
    cases.append(((), SUMS_ORDER, (8, width), F32))
    buffers, counts = chain_scratch(cases)
    kept, start = [], 0
    for index, count in enumerate(counts):
        kept += buffers[start : start + count - (index < TILES)]
        start += count
    buffers, counts = kept, [count - (index < TILES) for index, count in enumerate(counts)]
    whole = (2, 2, 2, 2, HALF, 384)
    stack = pl.BlockSpec((near, 2, 1, rows, width), lambda s: (0, 0, slot(s), 0, 0))
    return pl.pallas_call(
        partial(back_kernel, counts),
        grid=(FIRST_NORM + 1,),
        in_specs=[
            stack,
            pl.BlockSpec((1, width, width), lambda s: (weight(s), 0, 0)),
            pl.BlockSpec((8, 1, reduce.shape[2], width), lambda s: (0, part(s), 0, 0)),
            fixed((near, rows, width)),
            fixed((near, rows, 1)),
            fixed((near, rows, width)),
            pl.BlockSpec((1, 2, 3, rows, PAIR), lambda s: spot(s) + (0, 0, 0)),
            pl.BlockSpec((1, 2, 2, rows, PAIR), lambda s: spot(s) + (0, 0, 0)),
            pl.BlockSpec((1, 2, 2 * rows, 2 * rows), lambda s: spot(s) + (0, 0)),
            fixed(lines.shape),
            fixed(sums.shape),
            fixed((near, rows, width)),
            fixed((near, rows, 1)),
        ],
        out_specs=[
            pl.BlockSpec(memory_space=pl.ANY),
            fixed((near, quarter, width)),
            pl.BlockSpec(memory_space=pl.ANY),
            fixed_out(sums.shape),
            fixed_out((8, width)),
        ],
        out_shape=[
            jax.ShapeDtypeStruct((TILES, 2, 2, HALF, 384), BF16),
            jax.ShapeDtypeStruct((near, quarter, width), F32),
            jax.ShapeDtypeStruct((near, quarter, width), BF16),
            jax.ShapeDtypeStruct(sums.shape, F32),
            jax.ShapeDtypeStruct((8, width), F32),
        ],
        scratch_shapes=[
            pltpu.VMEM((TILES, 2, 2, HALF, 384), BF16),
            pltpu.SemaphoreType.DMA((TILES,)),
            pltpu.VMEM((near, rows, width), BF16),
            pltpu.VMEM((near, rows, width), BF16),
            pltpu.VMEM((near, rows, width), F32),
            pltpu.VMEM((near, heads, rows, PAIR), BF16),
            pltpu.VMEM((2, 6, 3, rows, PAIR), BF16),
            pltpu.VMEM((SLOTS, 2, rows, PAIR), BF16),
            pltpu.VMEM((near * heads, 2, rows, PAIR), BF16),
            pltpu.VMEM((near, quarter, width), BF16),
            pltpu.VMEM(sums.shape, F32),
            pltpu.VMEM((8, width), F32),
            pltpu.VMEM((KEPT,) + whole, BF16),
            pltpu.VMEM((SLOTS,) + whole, BF16),
            pltpu.VMEM((SLOTS,) + whole, BF16),
            pltpu.SemaphoreType.DMA((MOST * (TILES + 2),)),
            pltpu.SemaphoreType.DMA((MOST * (TILES + 2),)),
            pltpu.SemaphoreType.DMA((TILES,)),
            pltpu.SemaphoreType.DMA((TILES,)),
            pltpu.SemaphoreType.DMA((near * heads,)),
            pltpu.SemaphoreType.DMA((near * heads,)),
            pltpu.SemaphoreType.DMA((near,)),
            pltpu.SemaphoreType.DMA((near,)),
        ]
        + buffers,
        compiler_params=pltpu.CompilerParams(
            vmem_limit_bytes=60 * MIB, collective_id=2, has_side_effects=True
        ),
        cost_estimate=cost(40e9, 60e6),
        name="back",
    )(
        sides, weights, reduce, input_two,
        scaling_two, input_one, joint, pairs, probs, lines, sums, embedded, mask,
    )


def emit_kernel(parts, done, near_in, far_in, sums, late, *outs):
    (
        loss, attend_gain, attend_shift, joint, query_bias, value_bias, output, output_bias, feed_gain,
        feed_shift, expand, expand_bias, reduce, reduce_bias, pixel, pixel_bias, token, patch,
    ) = outs
    data, y = lax.axis_index("dp"), lax.div(lax.axis_index("seq"), 2)
    inverse = 1.0 / (sums[10:11] * PIXELS)
    loss[0] = jnp.sum(sums[5:6] * inverse)
    wide_inverse = inverse[:, :384]

    def piece(unit, core, half):
        return done[unit, core, half].astype(F32) * wide_inverse

    def square(unit):
        return [
            jnp.concatenate([piece(unit, core, half) for half in range(2)], axis=1) for core in range(2)
        ]

    for unit, target in ((0, pixel), (2 * parts + 1, output)):
        for core, lines in enumerate(square(unit)):
            target[core * HALF : (core + 1) * HALF] = lines
    expands = []
    for part in range(parts):
        for core, lines in enumerate(square(1 + 2 * part)):
            start = part * 2 * HALF + core * HALF
            reduce[start : start + HALF] = lines
        expands.append(square(2 + 2 * part))
    span = 2 * HALF
    for core in range(2):
        for d in range(8):
            lines = [expands[part][core][:, d * span : (d + 1) * span] for part in range(parts)]
            expand[core * HALF : (core + 1) * HALF, d * 4 * span : (d + 1) * 4 * span] = jnp.concatenate(
                lines, axis=1
            )
    for group in range(3):
        for core, lines in enumerate(square(2 * parts + 2 + group)):
            for part in range(3):
                start = part * WIDE + group * 2 * PAIR
                joint[core * HALF : (core + 1) * HALF, start : start + 2 * PAIR] = lines[
                    :, part * 2 * PAIR : (part + 1) * 2 * PAIR
                ]

    def own_cut(lines):
        shift = lax.rem(WIDE - data * span, WIDE)
        return pltpu.roll(lines, shift, axis=1)[:, :span]

    early = own_cut(sums[...] * inverse)
    later = own_cut(late[...] * inverse)
    queries = jnp.concatenate([late[5 + group : 6 + group, : 2 * PAIR] for group in range(3)], axis=1)
    values = jnp.concatenate([late[5 + group : 6 + group, 4 * PAIR :] for group in range(3)], axis=1)
    both = jnp.concatenate([queries, values] + [jnp.zeros((6, WIDE), F32)], axis=0)
    both = own_cut(both * inverse)
    for target, lines, row in (
        (attend_gain, later, 0),
        (attend_shift, later, 1),
        (query_bias, both, 0),
        (value_bias, both, 1),
        (output_bias, early, 4),
        (feed_gain, early, 2),
        (feed_shift, early, 3),
        (reduce_bias, early, 1),
        (pixel_bias, early, 0),
        (token, later, 2),
    ):
        target[...] = lines[row : row + 1]
    joined = jnp.concatenate([early[6 + part : 7 + part] for part in range(parts)], axis=1)
    expand_bias[...] = joined.reshape(joined.shape[1])
    images = near_in.shape[0]
    for image in range(images):
        patch[y * images + image] = near_in[image] * inverse
        patch[(1 - y) * images + image] = far_in[image].astype(F32) * inverse


def emit(parts, done, near_in, far_in, sums, late):
    images, quarter, width = near_in.shape
    hidden = parts * width

    def out(*shape):
        return jax.ShapeDtypeStruct(shape, F32)

    small = out(1, 96)
    outs = [
        out(1), small, small, out(96, 3 * width), small, small, out(96, width), small, small,
        small, out(96, hidden), out(hidden // 8), out(hidden // 8, width), small, out(96, width), small, small,
        out(2 * images, quarter, width),
    ]
    whole = pl.BlockSpec(memory_space=pltpu.VMEM)
    return pl.pallas_call(
        partial(emit_kernel, parts),
        in_specs=[whole] * 5,
        out_specs=[pl.BlockSpec(memory_space=pltpu.SMEM)] + [whole] * (len(outs) - 1),
        out_shape=outs,
        compiler_params=params(60),
        cost_estimate=cost(1e6, 12e6),
        name="emit",
    )(done, near_in, far_in, sums, late)


def eight_places(
    patches,
    targets,
    mask_order,
    mask_count,
    attend_gain,
    attend_shift,
    joint_weight,
    query_bias,
    value_bias,
    output_weight,
    output_bias,
    feed_gain,
    feed_shift,
    expand_weight,
    expand_bias,
    reduce_weight,
    reduce_bias,
    pixel_weight,
    pixel_bias,
    mask_token,
):
    images, quarter, features = patches.shape
    near = images // 2
    place_y = own_bit("seq", 2)
    hidden = expand_bias.shape[0]
    parts = hidden // features

    def halves(values):
        return values.reshape((2, near) + values.shape[1:])

    lines = stack_lines(
        attend_gain,
        attend_shift,
        query_bias,
        value_bias,
        output_bias,
        feed_gain,
        feed_shift,
        reduce_bias,
        pixel_bias,
        mask_token,
        expand_bias,
    )
    reduce_parts = reduce_weight.reshape(8, parts, hidden // (8 * parts), features)
    embedded, input_one, joint, pairs, mixed, probs, mask, targets_here, weights = front(
        mask_count,
        halves(patches),
        halves(targets),
        mask_order,
        lines,
        joint_weight,
        pixel_weight,
        expand_weight,
        output_weight,
    )
    sides, input_two, scaling_two, sums = middle(
        embedded, mixed, mask, targets_here, weights, reduce_parts, lines
    )
    done, patch_near, patch_far, sums, late = back(
        sides,
        weights,
        reduce_parts,
        input_two,
        scaling_two,
        input_one,
        joint,
        pairs,
        probs,
        lines,
        sums,
        embedded,
        mask,
    )
    outs = emit(parts, done, patch_near, patch_far, sums, late)
    flat = {0: (), 1: (-1,), 2: (-1,), 4: (-1,), 5: (-1,), 7: (-1,), 8: (-1,), 9: (-1,), 11: (-1,)}
    flat.update({13: (-1,), 15: (-1,), 16: (-1,)})
    return tuple(
        out.reshape(flat[index]) if index in flat else out for index, out in enumerate(outs)
    )


def on_device(*arguments):
    if lax.axis_size("dp") == 8 and lax.axis_size("seq") == 4:
        return eight_places(*arguments)
    return any_places(*arguments)


def solution(mesh):
    placed = (
        P("dp", "seq", None),
        P("dp", "seq", None),
        P("dp", "seq"),
        P("dp"),
        P(),
        P(),
        P(),
        P(),
        P(),
        P(),
        P(),
        P(),
        P(),
        P(),
        P(),
        P(),
        P(),
        P(),
        P(),
        P(),
    )
    return jax.shard_map(
        on_device,
        mesh=mesh,
        in_specs=placed,
        out_specs=(
            P(),
            P("dp"),
            P("dp"),
            P("dp", None),
            P("dp"),
            P("dp"),
            P("dp", None),
            P("dp"),
            P("dp"),
            P("dp"),
            P("dp", None),
            P("dp"),
            P("dp", None),
            P("dp"),
            P("dp", None),
            P("dp"),
            P("dp"),
            P("dp", "seq", None),
        ),
        check_vma=False,
    )
```
